32 devices in a mesh: groups: 2 (over y), rows: 4 (over z), feat: 2 (over x), sub: 2 (over core).
Axes of the slice: x: 2, y: 2, z: 4, core: 2. Of those that a mesh axis runs over, the one named last changes fastest.
Arguments:
- h_input: bfloat16 [16384, 256], P(('groups', 'rows', 'feat'), 'sub'), parts along dimension 0, may hold values from -6 to 6
- inv_degree: float32 [16384], P(('groups', 'rows', 'feat')), parts along dimension 0, may hold values from 0.1 to 1
- dest_block: int32 [1024, 1], P(('groups', 'rows', 'feat')), parts along dimension 0, may hold values from 0 to 7; in each aligned block of 64 rows (0 to 63, 64 to 127, ...) at most 16 rows name the same one
- row_block: int32 [1024], P(('groups', 'rows', 'feat')), parts along dimension 0, may hold values from 0 to 7
- block_offset: int32 [1024], P(('groups', 'rows', 'feat')), parts along dimension 0, may hold values from -8 to 8
- new_tiles: bfloat16 [1024, 128, 128], P(('groups', 'rows', 'feat')), parts along dimension 0, may hold values from 0 to 0.25
- base_one: float32 [16384, 256], P(('groups', 'rows', 'feat'), 'sub'), parts along dimension 0, may hold values from -12 to 12
- affected_one: int32 [128], P(('groups', 'rows', 'feat')), parts along dimension 0, may hold values 0 or 1
- old_one: bfloat16 [16384, 256], P(('groups', 'rows', 'feat'), 'sub'), parts along dimension 0, may hold values from -6 to 6
- self_one: bfloat16 [256, 256], replicated, may hold values from -0.375 to 0.375
- neigh_one: bfloat16 [256, 256], replicated, may hold values from -0.375 to 0.375
- bias_one: float32 [256], replicated, may hold values from -3 to 3
- base_two: float32 [16384, 256], P(('groups', 'rows', 'feat'), 'sub'), parts along dimension 0, may hold values from -12 to 12
- affected_two: int32 [128], P(('groups', 'rows', 'feat')), parts along dimension 0, may hold values 0 or 1
- old_two: bfloat16 [16384, 256], P(('groups', 'rows', 'feat'), 'sub'), parts along dimension 0, may hold values from -6 to 6
- self_two: bfloat16 [256, 256], replicated, may hold values from -0.375 to 0.375
- neigh_two: bfloat16 [256, 256], replicated, may hold values from -0.375 to 0.375
- bias_two: float32 [256], replicated, may hold values from -3 to 3
Outputs:
- hidden_one: bfloat16 [16384, 256], P(('groups', 'rows', 'feat'), 'sub'), parts along dimension 0
- hidden_two: bfloat16 [16384, 256], P(('groups', 'rows', 'feat'), 'sub'), parts along dimension 0
The draws below stay inside these ranges and needn't reach their ends.
There are 2 independent parts, one for each index of `groups`. The reference program is written for one: setup_inputs(seed, part) draws one part's arguments, and reference() takes and returns one part's arrays. A program takes and returns all parts, laid end to end along the dimension named above; an argument that names none is the same for every part. Nothing has to cross between parts.
Inputs may be any that keep to these rules, and one draw needn't show every extreme that they name: `dest_block`: among the 64 entries of one device no destination appears more than 16 times, and some destination appears exactly 16 times.
All inputs are finite; a program needn't handle non-finite values. No bound on the sum of `affected_one` or of `affected_two` on one device may be relied on, other than what follows from the above.
Results may differ from the reference program's by a relative error of at most 0.0051.
Values may be sent and summed in bfloat16 or wider, within the bound.
No kernel may reach another device: no remote copies, remote signals or barrier semaphores. Data moves between devices by JAX's collectives and lax.ppermute only.
A program may use at most 64 MiB of HBM per device.

```python
import math
import jax
import jax.numpy as jnp
import numpy as np
from jax import lax

D = 256
BLK_DEV = 8
NT_DEV = 64
PEERS = 8
CAP = 16
NB = 64
V = 8192
TILES = 512


def plant(values, stream_key, least, largest):
    place = [jax.random.randint(jax.random.fold_in(stream_key, axis), (), 0, length) for axis, length in enumerate(values.shape)]
    main_axis = values.shape.index(max(values.shape))
    next_to = place[:main_axis] + [(place[main_axis] + 1) % values.shape[main_axis]] + place[main_axis + 1:]
    return values.at[tuple(place)].set(least).at[tuple(next_to)].set(largest)


def level_of(own_key, dims, pieces, smallest, top_value):
    def one(position, parts):
        steps = jax.random.uniform(jax.random.fold_in(jax.random.fold_in(own_key, 6), position), (parts,), jnp.float32, smallest / len(pieces), top_value / len(pieces))
        return jnp.repeat(jnp.exp(steps), dims[position] // parts).reshape((-1,) + (1,) * (len(dims) - position - 1))

    gain = one(*pieces[0])
    for cut in pieces[1:]:
        gain = gain * one(*cut)
    return gain


def shared_out(rng, own, number, rows, count, top, limit, skew):
    ranking = jax.random.permutation(rng, count)
    crowded, ordinary = portions_of(count, rows * top, limit, skew, True), portions_of(count, rows * top, limit, skew, False)
    places = jnp.arange(count)

    def named(tallies, offset_by):
        used = int((tallies > 0).sum())
        fixed = max(1, used // 4)
        passed = fixed + (places - fixed + offset_by * (used - fixed)) % max(1, count - fixed)
        return jnp.zeros((count,), jnp.int32).at[ranking[jnp.where(places < fixed, places, passed)]].set(jnp.asarray(tallies, jnp.int32))

    tallies = jnp.where(number % 4 == 0, named(crowded, number // 4), named(ordinary, number - number // 4 - 1))
    mixed = jax.random.permutation(jax.random.fold_in(own, 3), count)
    source_of, taker = mixed[0:count // 2 * 2:2], mixed[1:count // 2 * 2:2]
    margin = jnp.minimum(tallies[source_of] - 1, limit - tallies[taker]) // 2
    margin = jnp.where((source_of == ranking[0]) | (taker == ranking[0]) | (tallies[taker] == 0), 0, jnp.maximum(margin, 0))
    passed = jax.random.randint(jax.random.fold_in(own, 4), (count // 2,), 0, 1 << 20) % (margin + 1)
    tallies = tallies.at[source_of].add(-passed).at[taker].add(passed)
    labels = jnp.searchsorted(jnp.cumsum(tallies), jnp.arange(rows * top), side="right").astype(jnp.int32)
    grid = labels.reshape(top, rows).T
    grid = grid[jax.random.permutation(jax.random.fold_in(own, 1), rows)]
    offset_by = jax.random.randint(jax.random.fold_in(own, 2), (rows, 1), 0, top)
    return jnp.take_along_axis(grid, (jnp.arange(top)[None, :] + offset_by) % top, axis=1)


def portions_of(number_of, total, reach, slope, full):
    portions = [(1 << 20) // math.isqrt(rank ** slope) + 1 for rank in range(1, number_of + 1)]
    largest = reach if full else min(reach, max(-(-total // number_of), total * portions[0] // sum(portions)))
    least = 1 if total - largest >= number_of - 1 else 0
    given, surplus = [largest] + [least] * (number_of - 1), total - largest - least * (number_of - 1)
    while surplus > 0:
        movable = [i for i in range(1, number_of) if given[i] < largest] or [i for i in range(1, number_of) if given[i] < reach]
        pool, remaining = sum([portions[i] for i in movable]), surplus
        for i in movable:
            more = min(reach - given[i], max(1, remaining * portions[i] // pool), surplus)
            given[i] = given[i] + more
            surplus = surplus - more
    return np.array(given)


def normal_values(stream_key, shape, width, reach, cuts=(), kind=jnp.bfloat16):
    loudness = level_of(stream_key, shape, cuts, -0.22, 0.18) if cuts else 1.0
    entries = jax.random.normal(stream_key, shape, jnp.float32) * width * loudness
    return jnp.minimum(jnp.maximum(entries, -reach), reach).astype(kind)


def setup_inputs(seed: int = 0, part: int = 0) -> dict:
    splits = jax.random.split(jax.random.key(seed), 19)
    part_splits = jax.random.split(jax.random.fold_in(splits[18], part), 19)
    h_input = normal_values(part_splits[0], (V, D), 1.0, 6.0, ((0, 8), (1, 2)))
    inv_degree = jnp.clip(jnp.exp(math.log(1.0) - 2.3025851 * jax.random.uniform(part_splits[1], (V,), jnp.float32) ** level_of(part_splits[1], (V,), ((0, 8),), -0.2, 0.2)), 0.1, 1.0)
    dest_block_keys = jax.random.split(jax.random.fold_in(part_splits[2], 1), TILES // NT_DEV)
    dest_block_turns = jax.random.permutation(jax.random.fold_in(part_splits[2], 3), TILES // NT_DEV)
    dest_block = jax.vmap(lambda own, number: shared_out(jax.random.fold_in(part_splits[2], 2), own, number, NT_DEV, PEERS, 1, CAP, 2))(dest_block_keys, dest_block_turns).reshape((TILES, 1))
    row_block = plant(jax.random.randint(part_splits[3], (TILES,), 0, BLK_DEV), jax.random.fold_in(part_splits[3], 1), 0, BLK_DEV - 1).astype(jnp.int32)
    block_offset = plant(jax.random.randint(part_splits[4], (TILES,), -BLK_DEV, BLK_DEV + 1), jax.random.fold_in(part_splits[4], 1), -BLK_DEV, BLK_DEV).astype(jnp.int32)
    new_tiles = jnp.clip(0.25 * jax.random.uniform(part_splits[5], (TILES, 128, 128), jnp.float32) ** level_of(part_splits[5], (TILES, 128, 128), ((0, 8),), -0.2, 0.2), 0.0, 0.25).astype(jnp.bfloat16)
    base_one = normal_values(part_splits[6], (V, D), 2.0, 12.0, ((0, 8), (1, 2)), jnp.float32)
    affected_one = plant((jax.random.randint(part_splits[7], (NB,), 0, 4) < 3).astype(jnp.int32), jax.random.fold_in(part_splits[7], 1), 0, 1)
    old_one = normal_values(part_splits[8], (V, D), 1.0, 6.0, ((0, 8), (1, 2)))
    self_one = normal_values(splits[9], (D, D), D ** -0.5, 0.375)
    neigh_one = normal_values(splits[10], (D, D), D ** -0.5, 0.375)
    bias_one = normal_values(splits[11], (D,), 0.5, 3.0, (), jnp.float32)
    base_two = normal_values(part_splits[12], (V, D), 2.0, 12.0, ((0, 8), (1, 2)), jnp.float32)
    affected_two = plant((jax.random.randint(part_splits[13], (NB,), 0, 4) < 3).astype(jnp.int32), jax.random.fold_in(part_splits[13], 1), 0, 1)
    old_two = normal_values(part_splits[14], (V, D), 1.0, 6.0, ((0, 8), (1, 2)))
    self_two = normal_values(splits[15], (D, D), D ** -0.5, 0.375)
    neigh_two = normal_values(splits[16], (D, D), D ** -0.5, 0.375)
    bias_two = normal_values(splits[17], (D,), 0.5, 3.0, (), jnp.float32)
    return {"h_input": h_input, "inv_degree": inv_degree, "dest_block": dest_block, "row_block": row_block, "block_offset": block_offset, "new_tiles": new_tiles, "base_one": base_one, "affected_one": affected_one, "old_one": old_one, "self_one": self_one, "neigh_one": neigh_one, "bias_one": bias_one, "base_two": base_two, "affected_two": affected_two, "old_two": old_two, "self_two": self_two, "neigh_two": neigh_two, "bias_two": bias_two}


def tile_sums(h_in, rblock, cblock, new_tiles):
    nblocks = BLK_DEV * PEERS
    blocks = h_in.reshape(nblocks, 128, D)
    size = math.gcd(TILES, 256)
    steps = TILES // size

    def step(acc, items):
        rows_now, cols_now, tiles_now = items
        chosen = blocks[cols_now].astype(jnp.float32)
        prods = jnp.einsum('tij,tjf->tif', tiles_now.astype(jnp.float32), chosen, precision=lax.Precision.HIGHEST)
        return acc.at[rows_now].add(prods), None

    start = jnp.zeros((nblocks, 128, D), jnp.float32)
    acc, _ = lax.scan(step, start, (rblock.reshape(steps, size), cblock.reshape(steps, size), new_tiles.reshape(steps, size, 128, 128)))
    return acc.reshape(nblocks * 128, D)


def one_layer(h_in, inv_degree, base, rblock, cblock, new_tiles, affected, old, w_self, w_neigh, bias, use_relu):
    agg = base + tile_sums(h_in, rblock, cblock, new_tiles)
    mean = (agg * inv_degree[:, None]).astype(jnp.bfloat16)
    pre = jnp.dot(h_in, w_self, preferred_element_type=jnp.float32) + jnp.dot(mean, w_neigh, preferred_element_type=jnp.float32) + bias[None, :]
    if use_relu:
        pre = jnp.maximum(pre, 0.0)
    keep = jnp.repeat(affected, 128) > 0
    return jnp.where(keep[:, None], pre, old.astype(jnp.float32)).astype(jnp.bfloat16)


def reference(h_input, inv_degree, dest_block, row_block, block_offset, new_tiles, base_one, affected_one, old_one, self_one, neigh_one, bias_one, base_two, affected_two, old_two, self_two, neigh_two, bias_two):
    nblocks = BLK_DEV * PEERS
    rblock = (dest_block[:, 0] * BLK_DEV + row_block).astype(jnp.int32)
    cblock = jnp.mod(rblock + block_offset, nblocks).astype(jnp.int32)
    hidden_one = one_layer(h_input, inv_degree, base_one, rblock, cblock, new_tiles, affected_one, old_one, self_one, neigh_one, bias_one, True)
    hidden_two = one_layer(hidden_one, inv_degree, base_two, rblock, cblock, new_tiles, affected_two, old_two, self_two, neigh_two, bias_two, False)
    return hidden_one, hidden_two
```

```python
import functools

import jax
import jax.numpy as jnp
from jax import lax
from jax.experimental import pallas as pl
from jax.experimental.pallas import tpu as pltpu
from jax.sharding import PartitionSpec as P

PEERS = ("rows", "feat")
BLK = 128
QUAD = 4
F32 = jnp.float32
BF16 = jnp.bfloat16
ANY = pl.BlockSpec(memory_space=pl.ANY)
SMEM = pl.BlockSpec(memory_space=pltpu.SMEM)
VMEM = pl.BlockSpec(memory_space=pltpu.VMEM)
PARAMS = pltpu.CompilerParams(vmem_limit_bytes=48 * 1024 * 1024)


def gather_kernel(peers, cap, pieces, dest, row, off, tiles, *refs):
    outs, codes = refs[:pieces], refs[pieces]
    fill, source, sems = refs[pieces + 1 :]
    count = dest.shape[0]
    half = outs[0].shape[1]
    me = lax.axis_index(PEERS)
    first = pl.multiple_of(lax.axis_index("sub") * half, half)

    def clear(i, _):
        fill[i] = 0
        return 0

    lax.fori_loop(0, peers, clear, 0)

    def blank(i, _):
        codes[i] = -1
        return 0

    lax.fori_loop(0, peers * cap, blank, 0)

    def share(t):
        return tiles.at[t, pl.ds(first, half)]

    def place(t, _):
        to = dest[t]
        at = to * cap + fill[to]
        fill[to] = fill[to] + 1
        codes[at] = row[t] * 32 + off[t] + 8
        source[at] = t
        if pieces == 1:
            pltpu.make_async_copy(share(t), outs[0].at[at], sems.at[t]).start()
        return 0

    lax.fori_loop(0, count, place, 0)
    if pieces > 1:
        for k in list(range(1, peers)) + [0]:
            to = lax.rem(me + k, peers)

            def send(j, _, k=k, to=to):
                t = source[to * cap + j]
                pltpu.make_async_copy(share(t), outs[k].at[j], sems.at[t]).start()
                return 0

            lax.fori_loop(0, fill[to], send, 0)

    def finish(t, _):
        pltpu.make_async_copy(share(0), outs[0].at[0], sems.at[t]).wait()
        return 0

    lax.fori_loop(0, count, finish, 0)


def plan_kernel(nblk, codes, by_row, row_at, by_side, side_at, fill_row, fill_side):
    slots = codes.shape[0]
    nothing = slots * 32 + nblk

    def clear(i, _):
        fill_row[i] = 0
        fill_side[i] = 0
        fill_side[nblk + i] = 0
        return 0

    lax.fori_loop(0, nblk, clear, 0)

    def blank(i, _):
        by_row[i] = nothing
        by_side[i] = nothing
        return 0

    lax.fori_loop(0, by_row.shape[0], blank, 0)

    def blank_side(i, _):
        by_side[i] = nothing
        return 0

    lax.fori_loop(by_row.shape[0], by_side.shape[0], blank_side, 0)

    def groups(code):
        row = code >> 5
        col = row + (code & 31)
        own = (col >= nblk) & (col < 2 * nblk)
        return row, row + jnp.where(own, 0, nblk), col

    def tally(i, _):
        code = codes[i]

        @pl.when(code >= 0)
        def _():
            row, side, _ = groups(code)
            fill_row[row] = fill_row[row] + 1
            fill_side[side] = fill_side[side] + 1

        return 0

    lax.fori_loop(0, slots, tally, 0)

    def starts(fill, at, number):
        def step(g, now):
            at[g] = now
            need = (fill[g] + QUAD - 1) // QUAD
            fill[g] = now * QUAD
            return now + need

        at[number] = lax.fori_loop(0, number, step, jnp.int32(0))

    starts(fill_row, row_at, nblk)
    starts(fill_side, side_at, 2 * nblk)

    def place(i, _):
        code = codes[i]

        @pl.when(code >= 0)
        def _():
            row, side, col = groups(code)
            entry = i * 32 + col
            by_row[fill_row[row]] = entry
            fill_row[row] = fill_row[row] + 1
            by_side[fill_side[side]] = entry
            fill_side[side] = fill_side[side] + 1

        return 0

    lax.fori_loop(0, slots, place, 0)


def tile_copies(cap, arrived, tiles, sems):
    copies = []
    if len(arrived) == 1:
        copies.append(
            pltpu.make_async_copy(arrived[0], tiles.at[pl.ds(0, arrived[0].shape[0])], sems.at[0])
        )
    else:
        peers = len(arrived)
        me = lax.axis_index(PEERS)
        for k, ref in enumerate(arrived):
            origin = lax.rem(me + peers - k, peers)
            copies.append(
                pltpu.make_async_copy(ref, tiles.at[pl.ds(origin * cap, cap)], sems.at[k])
            )
    return copies


def tile_sums(order, begin, end, tiles, cells, base):
    def quad(q, acc):
        for pair in range(0, QUAD, 2):
            first = order[q * QUAD + pair]
            second = order[q * QUAD + pair + 1]
            weights = jnp.concatenate([tiles[first >> 5], tiles[second >> 5]], axis=1)
            chosen = jnp.concatenate([cells[first & 31], cells[second & 31]], axis=0)
            acc = acc + jnp.dot(weights, chosen, preferred_element_type=F32)
        return acc

    return lax.fori_loop(begin, end, quad, base)


def layer_one_kernel(cap, pieces, nblk, order, at, affected, *refs):
    arrived = refs[:pieces]
    mine, twin, base, inv, own, w_neigh, old, out, tiles, cells, means, sems = refs[pieces:]
    half = base.shape[1]
    sub = lax.axis_index("sub")
    width = mine.shape[2]
    copies = tile_copies(cap, arrived, tiles, sems)
    for k, (ref, side) in enumerate(((mine, sub), (twin, 1 - sub))):
        lanes = pl.ds(pl.multiple_of(side * width, width), width)
        copies.append(pltpu.make_async_copy(ref, cells.at[:, :, lanes], sems.at[pieces + k]))
    for copy in copies:
        copy.start()
    tiles[tiles.shape[0] - 1] = jnp.zeros(tiles.shape[1:], tiles.dtype)
    for copy in copies:
        copy.wait()
    for r in range(nblk):
        agg = tile_sums(order, at[r], at[r + 1], tiles, cells, base[r])
        means[r] = (agg * inv[r]).astype(BF16)
    for r in range(nblk):
        pre = own[r] + jnp.dot(means[r], w_neigh[...], preferred_element_type=F32)
        pre = jnp.maximum(pre, 0.0)
        keep = jnp.full((half, 1), affected[r], jnp.int32) > 0
        out[r] = jnp.where(keep, pre, old[r].astype(F32)).astype(BF16)


def near_kernel(cap, pieces, nblk, order, at, *refs):
    arrived = refs[:pieces]
    mine, twin, base, w_self, bias, agg, own, tiles, cells, sems = refs[pieces:]
    half = base.shape[1]
    sub = lax.axis_index("sub")
    copies = tile_copies(cap, arrived, tiles, sems)
    for k, (ref, side) in enumerate(((mine, sub), (twin, 1 - sub))):
        lines = pl.ds(pl.multiple_of(side * half, half), half)
        copies.append(
            pltpu.make_async_copy(ref, cells.at[pl.ds(nblk, nblk), lines], sems.at[pieces + k])
        )
    for copy in copies:
        copy.start()
    tiles[tiles.shape[0] - 1] = jnp.zeros(tiles.shape[1:], tiles.dtype)
    for copy in copies:
        copy.wait()
    for r in range(nblk):
        agg[r] = tile_sums(order, at[r], at[r + 1], tiles, cells, base[r])
    mine_rows = pl.ds(pl.multiple_of(sub * half, half), half)
    for r in range(nblk):
        own[r] = (
            jnp.dot(cells[nblk + r, mine_rows], w_self[...], preferred_element_type=F32) + bias[...]
        )


def far_kernel(cap, pieces, nblk, order, at, *refs):
    arrived = refs[:pieces]
    left, left_twin, right, right_twin, agg, inv, own, w_neigh, keep, send = refs[
        pieces : pieces + 10
    ]
    tiles, cells, means, sems = refs[pieces + 10 :]
    half = agg.shape[1]
    width = keep.shape[2]
    sub = lax.axis_index("sub")
    copies = tile_copies(cap, arrived, tiles, sems)
    sides = ((left, 0, sub), (left_twin, 0, 1 - sub), (right, 2, sub), (right_twin, 2, 1 - sub))
    for k, (ref, third, side) in enumerate(sides):
        lines = pl.ds(pl.multiple_of(side * half, half), half)
        copies.append(
            pltpu.make_async_copy(
                ref, cells.at[pl.ds(third * nblk, nblk), lines], sems.at[pieces + k]
            )
        )
    for copy in copies:
        copy.start()
    tiles[tiles.shape[0] - 1] = jnp.zeros(tiles.shape[1:], tiles.dtype)
    cells[nblk] = jnp.zeros(cells.shape[1:], cells.dtype)
    for copy in copies:
        copy.wait()
    for r in range(nblk):
        total = tile_sums(order, at[nblk + r], at[nblk + r + 1], tiles, cells, agg[r])
        means[r] = (total * inv[r]).astype(BF16)
    for r in range(nblk):
        pre = own[r] + jnp.dot(means[r], w_neigh[...], preferred_element_type=F32)
        low = pre[:, :width].astype(BF16)
        high = pre[:, width:].astype(BF16)
        first = jnp.full((half, 1), sub, jnp.int32) == 0
        keep[r] = jnp.where(first, low, high)
        send[r] = jnp.where(first, high, low)


def swap(x):
    return lax.ppermute(x, "sub", [(0, 1), (1, 0)])


def ring(x, step):
    peers = lax.axis_size(PEERS)
    return lax.ppermute(x, PEERS, [(i, (i + step) % peers) for i in range(peers)])


def joined(sub, mine, twin, axis):
    return jnp.where(
        sub == 0,
        jnp.concatenate([mine, twin], axis=axis),
        jnp.concatenate([twin, mine], axis=axis),
    )


def on_device(
    h_input,
    inv_degree,
    dest_block,
    row_block,
    block_offset,
    new_tiles,
    base_one,
    affected_one,
    old_one,
    self_one,
    neigh_one,
    bias_one,
    base_two,
    affected_two,
    old_two,
    self_two,
    neigh_two,
    bias_two,
):
    peers = lax.axis_size(PEERS)
    sub = lax.axis_index("sub")
    count = dest_block.shape[0]
    cap = max(2, 2 * count // peers)
    slots = peers * cap
    rows_here, width = h_input.shape
    full = width * lax.axis_size("sub")
    nblk = rows_here // BLK
    half = BLK // lax.axis_size("sub")
    pieces = peers if peers <= 16 else 1

    shape = jax.ShapeDtypeStruct
    piece = shape((slots // pieces, half, BLK), BF16)
    *packed, codes = pl.pallas_call(
        functools.partial(gather_kernel, peers, cap, pieces),
        out_shape=[piece] * pieces + [shape((slots,), jnp.int32)],
        in_specs=[SMEM, SMEM, SMEM, ANY],
        out_specs=[ANY] * pieces + [SMEM],
        scratch_shapes=[
            pltpu.SMEM((peers,), jnp.int32),
            pltpu.SMEM((slots,), jnp.int32),
            pltpu.SemaphoreType.DMA((count,)),
        ],
        compiler_params=PARAMS,
        name="gather_tiles",
    )(dest_block.reshape(count), row_block, block_offset, new_tiles)

    if pieces > 1:
        arrived = [packed[0]] + [ring(packed[k], k) for k in range(1, peers)]
    else:
        arrived = [
            lax.all_to_all(
                packed[0].reshape(peers, cap, half, BLK),
                PEERS,
                split_axis=0,
                concat_axis=0,
                tiled=True,
            ).reshape(slots, half, BLK)
        ]
    got_codes = lax.all_to_all(
        codes.reshape(peers, cap), PEERS, split_axis=0, concat_axis=0, tiled=True
    ).reshape(slots)

    len_row = slots + nblk * QUAD
    len_side = slots + 2 * nblk * QUAD
    by_row, row_at, by_side, side_at = pl.pallas_call(
        functools.partial(plan_kernel, nblk),
        out_shape=[
            shape((len_row,), jnp.int32),
            shape((nblk + 1,), jnp.int32),
            shape((len_side,), jnp.int32),
            shape((2 * nblk + 1,), jnp.int32),
        ],
        in_specs=[SMEM],
        out_specs=[SMEM] * 4,
        scratch_shapes=[pltpu.SMEM((nblk,), jnp.int32), pltpu.SMEM((2 * nblk,), jnp.int32)],
        compiler_params=PARAMS,
        cost_estimate=pl.CostEstimate(flops=0, bytes_accessed=8 << 20, transcendentals=0),
        name="plan",
    )(got_codes)

    def my_rows(x):
        return lax.dynamic_slice_in_dim(x.reshape(nblk, BLK, -1), sub * half, half, 1)

    def twin_rows(x):
        return lax.dynamic_slice_in_dim(x.reshape(nblk, BLK, -1), (1 - sub) * half, half, 1)

    def by_rows(x):
        return joined(sub, my_rows(x), swap(twin_rows(x)), 2)

    mine = jnp.concatenate([ring(h_input, 1), h_input, ring(h_input, peers - 1)], axis=0)
    twin = swap(mine)
    own_rows = joined(
        sub, my_rows(h_input), my_rows(twin[rows_here : 2 * rows_here]), 2
    )
    own_one = (
        jnp.dot(own_rows.reshape(nblk * half, full), self_one, preferred_element_type=F32)
        + bias_one[None, :]
    ).reshape(nblk, half, full)
    inv = jnp.broadcast_to(my_rows(inv_degree), (nblk, half, full))
    base_one_rows = by_rows(base_one)
    base_two_rows = by_rows(base_two)
    old_one_rows = by_rows(old_one)

    tile_scratch = pltpu.VMEM((slots + 1, half, BLK), BF16)
    cell_scratch = pltpu.VMEM((3 * nblk, BLK, full), BF16)
    mean_scratch = pltpu.VMEM((nblk, half, full), BF16)
    rows_shape = (nblk, half, full)

    hidden_rows = pl.pallas_call(
        functools.partial(layer_one_kernel, cap, pieces, nblk),
        out_shape=shape(rows_shape, BF16),
        in_specs=[SMEM] * 3 + [ANY] * (pieces + 2) + [VMEM] * 5,
        out_specs=VMEM,
        scratch_shapes=[
            tile_scratch,
            cell_scratch,
            mean_scratch,
            pltpu.SemaphoreType.DMA((pieces + 2,)),
        ],
        compiler_params=PARAMS,
        name="layer_one",
    )(
        by_row,
        row_at,
        affected_one,
        *arrived,
        mine.reshape(3 * nblk, BLK, width),
        twin.reshape(3 * nblk, BLK, width),
        base_one_rows,
        inv,
        own_one,
        neigh_one,
        old_one_rows,
    )

    hidden_twin = swap(hidden_rows)
    left = ring(hidden_rows, 1)
    right = ring(hidden_rows, peers - 1)
    left_twin = swap(left)
    right_twin = swap(right)

    agg_two, own_two = pl.pallas_call(
        functools.partial(near_kernel, cap, pieces, nblk),
        out_shape=[shape(rows_shape, F32)] * 2,
        in_specs=[SMEM] * 2 + [ANY] * (pieces + 2) + [VMEM] * 3,
        out_specs=[VMEM] * 2,
        scratch_shapes=[tile_scratch, cell_scratch, pltpu.SemaphoreType.DMA((pieces + 2,))],
        compiler_params=PARAMS,
        cost_estimate=pl.CostEstimate(flops=0, bytes_accessed=16 << 20, transcendentals=0),
        name="near",
    )(
        by_side,
        side_at,
        *arrived,
        hidden_rows,
        hidden_twin,
        base_two_rows,
        self_two,
        bias_two.reshape(1, full),
    )

    kept, sent = pl.pallas_call(
        functools.partial(far_kernel, cap, pieces, nblk),
        out_shape=[shape((nblk, half, width), BF16)] * 2,
        in_specs=[SMEM] * 2 + [ANY] * (pieces + 4) + [VMEM] * 4,
        out_specs=[VMEM] * 2,
        scratch_shapes=[
            tile_scratch,
            cell_scratch,
            mean_scratch,
            pltpu.SemaphoreType.DMA((pieces + 4,)),
        ],
        compiler_params=PARAMS,
        name="far",
    )(
        by_side,
        side_at,
        *arrived,
        left,
        left_twin,
        right,
        right_twin,
        agg_two,
        inv,
        own_two,
        neigh_two,
    )
    came = swap(sent)
    pre_two = joined(sub, kept, came, 1)
    keep_two = (affected_two > 0)[:, None, None]
    hidden_two = jnp.where(keep_two, pre_two, old_two.reshape(nblk, BLK, width))

    def my_lanes(x):
        return lax.dynamic_slice_in_dim(x, sub * width, width, 2)

    hidden_one = joined(sub, my_lanes(hidden_rows), my_lanes(hidden_twin), 1)
    return (hidden_one.reshape(rows_here, width), hidden_two.reshape(rows_here, width))


def solution(mesh):
    rows = P(("groups", "rows", "feat"))
    cells = P(("groups", "rows", "feat"), "sub")
    placed = (
        cells,
        rows,
        P(("groups", "rows", "feat"), None),
        rows,
        rows,
        P(("groups", "rows", "feat"), None, None),
        cells,
        rows,
        cells,
        P(),
        P(),
        P(),
        cells,
        rows,
        cells,
        P(),
        P(),
        P(),
    )
    return jax.shard_map(
        on_device, mesh=mesh, in_specs=placed, out_specs=(cells, cells), check_vma=False
    )
```

```python
import functools

import jax
import jax.numpy as jnp
from jax import lax
from jax.experimental import pallas as pl
from jax.experimental.pallas import tpu as pltpu
from jax.sharding import PartitionSpec as P

PEERS = ("rows", "feat")
BLK = 128
QUAD = 4
F32 = jnp.float32
BF16 = jnp.bfloat16
ANY = pl.BlockSpec(memory_space=pl.ANY)
HBM = pl.BlockSpec(memory_space=pltpu.HBM)
SMEM = pl.BlockSpec(memory_space=pltpu.SMEM)
VMEM = pl.BlockSpec(memory_space=pltpu.VMEM)
PARAMS = pltpu.CompilerParams(vmem_limit_bytes=48 * 1024 * 1024)


def first_kernel(peers, cap, lead, dest, tiles, out, source, fill, sem):
    count = dest.shape[0]
    half = out.shape[1]
    me = lax.axis_index(PEERS)
    first = pl.multiple_of(lax.axis_index("sub") * half, half)
    for to in range(min(peers, 16)):
        fill[to] = 0
    if peers > 16:

        def clear(i, _):
            fill[i] = 0
            return 0

        lax.fori_loop(16, peers, clear, 0)
    for t in range(count):
        to = dest[t]
        at = fill[to]
        fill[to] = at + 1
        source[to * cap + at] = t
    if lead is None:
        return
    to = lax.rem(me + lead, peers)

    def send(j, _):
        t = source[to * cap + j]
        pltpu.make_async_copy(tiles.at[t, pl.ds(first, half)], out.at[j], sem.at[j]).start()
        return 0

    def finish(j, _):
        pltpu.make_async_copy(tiles.at[0, pl.ds(first, half)], out.at[0], sem.at[j]).wait()
        return 0

    lax.fori_loop(0, fill[to], send, 0)
    lax.fori_loop(0, fill[to], finish, 0)


def rest_kernel(peers, cap, order, source, fill, tiles, *refs):
    outs, sems = refs[:-1], refs[-1]
    half = outs[0].shape[1]
    me = lax.axis_index(PEERS)
    first = pl.multiple_of(lax.axis_index("sub") * half, half)
    begun = []
    for n, k in enumerate(order):
        to = lax.rem(me + k, peers)

        def send(j, _, n=n, to=to):
            t = source[to * cap + j]
            pltpu.make_async_copy(
                tiles.at[t, pl.ds(first, half)], outs[n].at[j], sems.at[n, j]
            ).start()
            return 0

        lax.fori_loop(0, fill[to], send, 0)
        begun.append(fill[to])
    for n, amount in enumerate(begun):

        def finish(j, _, n=n):
            pltpu.make_async_copy(
                tiles.at[0, pl.ds(first, half)], outs[n].at[0], sems.at[n, j]
            ).wait()
            return 0

        lax.fori_loop(0, amount, finish, 0)


def sorted_kernel(peers, cap, source, fill, tiles, out, sems):
    half = out.shape[1]
    first = pl.multiple_of(lax.axis_index("sub") * half, half)

    def each(act):
        def peer(to, _):
            def slot(j, _):
                at = to * cap + j
                act(source[at], at)
                return 0

            return lax.fori_loop(0, fill[to], slot, 0)

        lax.fori_loop(0, peers, peer, 0)

    def copy(t, at):
        return pltpu.make_async_copy(tiles.at[t, pl.ds(first, half)], out.at[at], sems.at[t])

    each(lambda t, at: copy(t, at).start())
    each(lambda t, at: copy(t, at).wait())


def label_kernel(peers, cap, source, fill, row, off, codes):
    def blank(i, _):
        codes[i] = -1
        return 0

    lax.fori_loop(0, peers * cap, blank, 0)

    def peer(to, _):
        def slot(j, _):
            at = to * cap + j
            t = source[at]
            codes[at] = row[t] * 32 + off[t] + 8
            return 0

        return lax.fori_loop(0, fill[to], slot, 0)

    lax.fori_loop(0, peers, peer, 0)


def plan_kernel(peers, late, nblk, codes, by_row, row_at, by_side, side_at, fill_row, fill_side):
    slots = codes.shape[0]
    cap = slots // peers
    nothing = slots * 32 + nblk
    me = lax.axis_index(PEERS)

    def clear(i, _):
        fill_row[i] = 0
        fill_side[i] = 0
        return 0

    lax.fori_loop(0, 2 * nblk, clear, 0)

    def blank(i, _):
        by_row[i] = nothing
        by_side[i] = nothing
        return 0

    lax.fori_loop(0, by_row.shape[0], blank, 0)

    def groups(i, code):
        row = code >> 5
        col = row + (code & 31)
        own = (col >= nblk) & (col < 2 * nblk)
        step = lax.rem(me + peers - i // cap, peers)
        behind = jnp.bool_(False)
        for k in late:
            behind = behind | (step == k)
        return row + jnp.where(behind, nblk, 0), row + jnp.where(own, 0, nblk), col

    def tally(i, _):
        code = codes[i]

        @pl.when(code >= 0)
        def _():
            row, side, _ = groups(i, code)
            fill_row[row] = fill_row[row] + 1
            fill_side[side] = fill_side[side] + 1

        return 0

    lax.fori_loop(0, slots, tally, 0)

    def starts(fill, at, number):
        def step(g, now):
            at[g] = now
            need = (fill[g] + QUAD - 1) // QUAD
            fill[g] = now * QUAD
            return now + need

        at[number] = lax.fori_loop(0, number, step, jnp.int32(0))

    starts(fill_row, row_at, 2 * nblk)
    starts(fill_side, side_at, 2 * nblk)

    def place(i, _):
        code = codes[i]

        @pl.when(code >= 0)
        def _():
            row, side, col = groups(i, code)
            entry = i * 32 + col
            by_row[fill_row[row]] = entry
            fill_row[row] = fill_row[row] + 1
            by_side[fill_side[side]] = entry
            fill_side[side] = fill_side[side] + 1

        return 0

    lax.fori_loop(0, slots, place, 0)


def tile_copies(cap, steps, arrived, tiles, sems):
    if steps is None:
        whole = tiles.at[pl.ds(0, arrived[0].shape[0])]
        return [pltpu.make_async_copy(arrived[0], whole, sems.at[0])]
    me = lax.axis_index(PEERS)
    peers = lax.axis_size(PEERS)
    copies = []
    for n, (k, ref) in enumerate(zip(steps, arrived)):
        origin = lax.rem(me + peers - k, peers)
        copies.append(pltpu.make_async_copy(ref, tiles.at[pl.ds(origin * cap, cap)], sems.at[n]))
    return copies


def tile_sums(order, begin, end, tiles, cells, base):
    def quad(q, acc):
        for pair in range(0, QUAD, 2):
            first = order[q * QUAD + pair]
            second = order[q * QUAD + pair + 1]
            weights = jnp.concatenate([tiles[first >> 5], tiles[second >> 5]], axis=1)
            chosen = jnp.concatenate([cells[first & 31], cells[second & 31]], axis=0)
            acc = acc + jnp.dot(weights, chosen, preferred_element_type=F32)
        return acc

    return lax.fori_loop(begin, end, quad, base)


def early_kernel(cap, steps, pieces, nblk, order, at, *refs):
    arrived = refs[:pieces]
    mine, twin, base, agg, cells, tiles, sems = refs[pieces:]
    sub = lax.axis_index("sub")
    width = mine.shape[2]
    copies = tile_copies(cap, steps, arrived, tiles, sems)
    for k, (ref, side) in enumerate(((mine, sub), (twin, 1 - sub))):
        lanes = pl.ds(pl.multiple_of(side * width, width), width)
        copies.append(pltpu.make_async_copy(ref, cells.at[:, :, lanes], sems.at[pieces + k]))
    for copy in copies:
        copy.start()
    tiles[tiles.shape[0] - 1] = jnp.zeros(tiles.shape[1:], tiles.dtype)
    for copy in copies:
        copy.wait()
    for r in range(nblk):
        agg[r] = tile_sums(order, at[r], at[r + 1], tiles, cells, base[r])


def late_kernel(cap, steps, pieces, nblk, order, at, affected, *refs):
    arrived = refs[:pieces]
    cells, agg, inv, own, w_neigh, old, out, tiles, means, sems = refs[pieces:]
    half = agg.shape[1]
    copies = tile_copies(cap, steps, arrived, tiles, sems) if pieces else []
    for copy in copies:
        copy.start()
    tiles[tiles.shape[0] - 1] = jnp.zeros(tiles.shape[1:], tiles.dtype)
    for copy in copies:
        copy.wait()
    for r in range(nblk):
        total = tile_sums(order, at[nblk + r], at[nblk + r + 1], tiles, cells, agg[r])
        means[r] = (total * inv[r]).astype(BF16)
    for r in range(nblk):
        pre = own[r] + jnp.dot(means[r], w_neigh[...], preferred_element_type=F32)
        pre = jnp.maximum(pre, 0.0)
        keep = jnp.full((half, 1), affected[r], jnp.int32) > 0
        out[r] = jnp.where(keep, pre, old[r].astype(F32)).astype(BF16)


def near_kernel(cap, steps, pieces, nblk, order, at, *refs):
    arrived = refs[:pieces]
    mine, twin, base, w_self, bias, agg, own, tiles, cells, sems = refs[pieces:]
    half = base.shape[1]
    sub = lax.axis_index("sub")
    copies = tile_copies(cap, steps, arrived, tiles, sems)
    for k, (ref, side) in enumerate(((mine, sub), (twin, 1 - sub))):
        lines = pl.ds(pl.multiple_of(side * half, half), half)
        copies.append(
            pltpu.make_async_copy(ref, cells.at[pl.ds(nblk, nblk), lines], sems.at[pieces + k])
        )
    for copy in copies:
        copy.start()
    tiles[tiles.shape[0] - 1] = jnp.zeros(tiles.shape[1:], tiles.dtype)
    for copy in copies:
        copy.wait()
    for r in range(nblk):
        agg[r] = tile_sums(order, at[r], at[r + 1], tiles, cells, base[r])
    mine_rows = pl.ds(pl.multiple_of(sub * half, half), half)
    for r in range(nblk):
        own[r] = (
            jnp.dot(cells[nblk + r, mine_rows], w_self[...], preferred_element_type=F32) + bias[...]
        )


def far_kernel(cap, steps, pieces, nblk, order, at, *refs):
    arrived = refs[:pieces]
    left, left_twin, right, right_twin, agg, inv, own, w_neigh, keep, send = refs[
        pieces : pieces + 10
    ]
    tiles, cells, means, sems = refs[pieces + 10 :]
    half = agg.shape[1]
    width = keep.shape[2]
    sub = lax.axis_index("sub")
    copies = tile_copies(cap, steps, arrived, tiles, sems)
    sides = ((left, 0, sub), (left_twin, 0, 1 - sub), (right, 2, sub), (right_twin, 2, 1 - sub))
    for k, (ref, third, side) in enumerate(sides):
        lines = pl.ds(pl.multiple_of(side * half, half), half)
        copies.append(
            pltpu.make_async_copy(
                ref, cells.at[pl.ds(third * nblk, nblk), lines], sems.at[pieces + k]
            )
        )
    for copy in copies:
        copy.start()
    tiles[tiles.shape[0] - 1] = jnp.zeros(tiles.shape[1:], tiles.dtype)
    cells[nblk] = jnp.zeros(cells.shape[1:], cells.dtype)
    for copy in copies:
        copy.wait()
    for r in range(nblk):
        total = tile_sums(order, at[nblk + r], at[nblk + r + 1], tiles, cells, agg[r])
        means[r] = (total * inv[r]).astype(BF16)
    for r in range(nblk):
        pre = own[r] + jnp.dot(means[r], w_neigh[...], preferred_element_type=F32)
        low = pre[:, :width].astype(BF16)
        high = pre[:, width:].astype(BF16)
        first = jnp.full((half, 1), sub, jnp.int32) == 0
        keep[r] = jnp.where(first, low, high)
        send[r] = jnp.where(first, high, low)


def swap(x):
    return lax.ppermute(x, "sub", [(0, 1), (1, 0)])


def ring(x, step):
    peers = lax.axis_size(PEERS)
    return lax.ppermute(x, PEERS, [(i, (i + step) % peers) for i in range(peers)])


def joined(sub, mine, twin, axis):
    return jnp.where(
        sub == 0,
        jnp.concatenate([mine, twin], axis=axis),
        jnp.concatenate([twin, mine], axis=axis),
    )


def on_device(
    h_input,
    inv_degree,
    dest_block,
    row_block,
    block_offset,
    new_tiles,
    base_one,
    affected_one,
    old_one,
    self_one,
    neigh_one,
    bias_one,
    base_two,
    affected_two,
    old_two,
    self_two,
    neigh_two,
    bias_two,
):
    peers = lax.axis_size(PEERS)
    sub = lax.axis_index("sub")
    count = dest_block.shape[0]
    cap = max(2, 2 * count // peers)
    slots = peers * cap
    rows_here, width = h_input.shape
    full = width * lax.axis_size("sub")
    nblk = rows_here // BLK
    half = BLK // lax.axis_size("sub")
    direct = 2 < peers <= 16
    shape = jax.ShapeDtypeStruct
    after = lax.optimization_barrier

    order = sorted(range(1, peers), key=lambda k: (abs(k - peers // 2), k))
    lead = order[0] if direct else None
    piece = shape((cap, half, BLK), BF16)
    out_piece, source, fill = pl.pallas_call(
        functools.partial(first_kernel, peers, cap, lead),
        out_shape=[piece, shape((slots,), jnp.int32), shape((peers,), jnp.int32)],
        in_specs=[SMEM, HBM],
        out_specs=[HBM, SMEM, SMEM],
        scratch_shapes=[pltpu.SemaphoreType.DMA((cap,))],
        compiler_params=PARAMS,
        name="first",
    )(dest_block.reshape(count), new_tiles)

    if direct:
        others = order[1:] + [0]
        packed = pl.pallas_call(
            functools.partial(rest_kernel, peers, cap, others),
            out_shape=[piece] * len(others),
            in_specs=[SMEM, SMEM, HBM],
            out_specs=[HBM] * len(others),
            scratch_shapes=[pltpu.SemaphoreType.DMA((len(others), cap))],
            compiler_params=PARAMS,
            name="rest",
        )(source, fill, new_tiles)
        steps = order + [0]
        got = dict(zip(others, packed))
        got[lead] = out_piece
        got = {k: ring(got[k], k) if k else got[k] for k in steps}
        late = tuple(order[4:]) if peers > 4 else ()
        early = [k for k in steps if k not in late]
        arrived = [got[k] for k in steps]
        arrived_early = [got[k] for k in early]
        arrived_late = [got[k] for k in late]
        flag = got[lead]
    else:
        sent = pl.pallas_call(
            functools.partial(sorted_kernel, peers, cap),
            out_shape=shape((slots, half, BLK), BF16),
            in_specs=[SMEM, SMEM, HBM],
            out_specs=HBM,
            scratch_shapes=[pltpu.SemaphoreType.DMA((count,))],
            compiler_params=PARAMS,
            name="rest",
        )(source, fill, new_tiles)
        sent = sent.reshape(peers, cap, half, BLK)
        got = lax.all_to_all(sent, PEERS, split_axis=0, concat_axis=0, tiled=True)
        arrived = [got.reshape(slots, half, BLK)]
        steps = early = None
        late = ()
        arrived_early, arrived_late = arrived, []
        flag = source

    codes = pl.pallas_call(
        functools.partial(label_kernel, peers, cap),
        out_shape=shape((slots,), jnp.int32),
        in_specs=[SMEM] * 4,
        out_specs=SMEM,
        compiler_params=PARAMS,
        name="label",
    )(source, fill, row_block, block_offset)
    got_codes = lax.all_to_all(
        codes.reshape(peers, cap), PEERS, split_axis=0, concat_axis=0, tiled=True
    ).reshape(slots)

    length = slots + 2 * nblk * QUAD
    by_row, row_at, by_side, side_at = pl.pallas_call(
        functools.partial(plan_kernel, peers, late, nblk),
        out_shape=[shape((length,), jnp.int32), shape((2 * nblk + 1,), jnp.int32)] * 2,
        in_specs=[SMEM],
        out_specs=[SMEM] * 4,
        scratch_shapes=[pltpu.SMEM((2 * nblk,), jnp.int32)] * 2,
        compiler_params=PARAMS,
        name="plan",
    )(got_codes)

    def my_rows(x):
        return lax.dynamic_slice_in_dim(x.reshape(nblk, BLK, -1), sub * half, half, 1)

    def twin_rows(x):
        return lax.dynamic_slice_in_dim(x.reshape(nblk, BLK, -1), (1 - sub) * half, half, 1)

    h_later, base_one_later, base_two_later, old_one_later, flag = after(
        (h_input, base_one, base_two, old_one, flag)
    )
    mine = jnp.concatenate([ring(h_later, 1), h_later, ring(h_later, peers - 1)], axis=0)
    twin = swap(mine)
    own_rows = joined(sub, my_rows(h_input), my_rows(twin[rows_here : 2 * rows_here]), 2)
    own_one = (
        jnp.dot(own_rows.reshape(nblk * half, full), self_one, preferred_element_type=F32)
        + bias_one[None, :]
    ).reshape(nblk, half, full)
    inv = jnp.broadcast_to(my_rows(inv_degree), (nblk, half, full))
    bases_came = swap(jnp.concatenate([twin_rows(base_one_later), twin_rows(base_two_later)], 0))
    base_one_rows = joined(sub, my_rows(base_one), bases_came[:nblk], 2)
    base_two_rows = joined(sub, my_rows(base_two), bases_came[nblk:], 2)
    old_one_rows = joined(sub, my_rows(old_one), swap(twin_rows(old_one_later)), 2)

    tile_scratch = pltpu.VMEM((slots + 1, half, BLK), BF16)
    cell_scratch = pltpu.VMEM((3 * nblk, BLK, full), BF16)
    mean_scratch = pltpu.VMEM((nblk, half, full), BF16)
    rows_shape = (nblk, half, full)

    many = len(arrived_early)
    agg_early, cells_one = pl.pallas_call(
        functools.partial(early_kernel, cap, early, many, nblk),
        out_shape=[shape(rows_shape, F32), shape((3 * nblk, BLK, full), BF16)],
        in_specs=[SMEM] * 2 + [ANY] * (many + 2) + [VMEM],
        out_specs=[VMEM] * 2,
        scratch_shapes=[tile_scratch, pltpu.SemaphoreType.DMA((many + 2,))],
        compiler_params=PARAMS,
        cost_estimate=pl.CostEstimate(flops=0, bytes_accessed=16 << 20, transcendentals=0),
        name="early",
    )(
        by_row,
        row_at,
        *arrived_early,
        mine.reshape(3 * nblk, BLK, width),
        twin.reshape(3 * nblk, BLK, width),
        base_one_rows,
    )

    agg_early, own_one, inv, old_one_rows, base_two_rows = after(
        (agg_early, own_one, inv, old_one_rows, base_two_rows)
    )
    many = len(arrived_late)
    hidden_rows = pl.pallas_call(
        functools.partial(late_kernel, cap, late, many, nblk),
        out_shape=shape(rows_shape, BF16),
        in_specs=[SMEM] * 3 + [ANY] * many + [VMEM] * 6,
        out_specs=VMEM,
        scratch_shapes=[tile_scratch, mean_scratch, pltpu.SemaphoreType.DMA((max(1, many),))],
        compiler_params=PARAMS,
        name="late",
    )(
        by_row,
        row_at,
        affected_one,
        *arrived_late,
        cells_one,
        agg_early,
        inv,
        own_one,
        neigh_one,
        old_one_rows,
    )

    hidden_twin = swap(hidden_rows)
    left = ring(hidden_rows, 1)
    right = ring(hidden_rows, peers - 1)

    many = len(arrived)
    agg_two, own_two = pl.pallas_call(
        functools.partial(near_kernel, cap, steps, many, nblk),
        out_shape=[shape(rows_shape, F32)] * 2,
        in_specs=[SMEM] * 2 + [ANY] * (many + 2) + [VMEM] * 3,
        out_specs=[VMEM] * 2,
        scratch_shapes=[tile_scratch, cell_scratch, pltpu.SemaphoreType.DMA((many + 2,))],
        compiler_params=PARAMS,
        cost_estimate=pl.CostEstimate(flops=0, bytes_accessed=16 << 20, transcendentals=0),
        name="near",
    )(
        by_side,
        side_at,
        *arrived,
        hidden_rows,
        hidden_twin,
        base_two_rows,
        self_two,
        bias_two.reshape(1, full),
    )

    def my_lanes(x):
        return lax.dynamic_slice_in_dim(x, sub * width, width, 2)

    hidden_one = joined(sub, my_lanes(hidden_rows), my_lanes(hidden_twin), 1)

    left, right, agg_two, own_two, hidden_one = after((left, right, agg_two, own_two, hidden_one))
    left_twin = swap(left)
    right_twin = swap(right)
    kept, sent = pl.pallas_call(
        functools.partial(far_kernel, cap, steps, many, nblk),
        out_shape=[shape((nblk, half, width), BF16)] * 2,
        in_specs=[SMEM] * 2 + [ANY] * (many + 4) + [VMEM] * 4,
        out_specs=[VMEM] * 2,
        scratch_shapes=[
            tile_scratch,
            cell_scratch,
            mean_scratch,
            pltpu.SemaphoreType.DMA((many + 4,)),
        ],
        compiler_params=PARAMS,
        name="far",
    )(
        by_side,
        side_at,
        *arrived,
        left,
        left_twin,
        right,
        right_twin,
        agg_two,
        inv,
        own_two,
        neigh_two,
    )
    came = swap(sent)
    pre_two = joined(sub, kept, came, 1)
    keep_two = (affected_two > 0)[:, None, None]
    hidden_two = jnp.where(keep_two, pre_two, old_two.reshape(nblk, BLK, width))
    return (hidden_one.reshape(rows_here, width), hidden_two.reshape(rows_here, width))


def solution(mesh):
    rows = P(("groups", "rows", "feat"))
    cells = P(("groups", "rows", "feat"), "sub")
    placed = (
        cells,
        rows,
        P(("groups", "rows", "feat"), None),
        rows,
        rows,
        P(("groups", "rows", "feat"), None, None),
        cells,
        rows,
        cells,
        P(),
        P(),
        P(),
        cells,
        rows,
        cells,
        P(),
        P(),
        P(),
    )
    return jax.shard_map(
        on_device, mesh=mesh, in_specs=placed, out_specs=(cells, cells), check_vma=False
    )
```

```python
import functools

import jax
import jax.numpy as jnp
from jax import lax
from jax.experimental import pallas as pl
from jax.experimental.pallas import tpu as pltpu
from jax.sharding import PartitionSpec as P

PEERS = ("rows", "feat")
BLK = 128
QUAD = 4
F32 = jnp.float32
BF16 = jnp.bfloat16
ANY = pl.BlockSpec(memory_space=pl.ANY)
HBM = pl.BlockSpec(memory_space=pltpu.HBM)
SMEM = pl.BlockSpec(memory_space=pltpu.SMEM)
VMEM = pl.BlockSpec(memory_space=pltpu.VMEM)
PARAMS = pltpu.CompilerParams(vmem_limit_bytes=20 * 1024 * 1024)
SMALL = pltpu.CompilerParams(vmem_limit_bytes=4 * 1024 * 1024)
TINY = pl.CostEstimate(flops=0, bytes_accessed=128, transcendentals=0)


def first_kernel(peers, cap, lead, dest, tiles, out, source, fill, sem):
    count = dest.shape[0]
    half = out.shape[1]
    me = lax.axis_index(PEERS)
    first = pl.multiple_of(lax.axis_index("sub") * half, half)
    for to in range(min(peers, 16)):
        fill[to] = 0
    if peers > 16:

        def clear(i, _):
            fill[i] = 0
            return 0

        lax.fori_loop(16, peers, clear, 0)
    for t in range(count):
        to = dest[t]
        at = fill[to]
        fill[to] = at + 1
        source[to * cap + at] = t
    if lead is None:
        return
    to = lax.rem(me + lead, peers)

    def send(j, _):
        t = source[to * cap + j]
        pltpu.make_async_copy(tiles.at[t, pl.ds(first, half)], out.at[j], sem.at[j]).start()
        return 0

    def finish(j, _):
        pltpu.make_async_copy(tiles.at[0, pl.ds(first, half)], out.at[0], sem.at[j]).wait()
        return 0

    lax.fori_loop(0, fill[to], send, 0)
    lax.fori_loop(0, fill[to], finish, 0)


def rest_kernel(peers, cap, order, source, fill, tiles, *refs):
    outs, sems = refs[:-1], refs[-1]
    half = outs[0].shape[1]
    me = lax.axis_index(PEERS)
    first = pl.multiple_of(lax.axis_index("sub") * half, half)
    begun = []
    for n, k in enumerate(order):
        to = lax.rem(me + k, peers)

        def send(j, _, n=n, to=to):
            t = source[to * cap + j]
            pltpu.make_async_copy(
                tiles.at[t, pl.ds(first, half)], outs[n].at[j], sems.at[n, j]
            ).start()
            return 0

        lax.fori_loop(0, fill[to], send, 0)
        begun.append(fill[to])
    for n, amount in enumerate(begun):

        def finish(j, _, n=n):
            pltpu.make_async_copy(
                tiles.at[0, pl.ds(first, half)], outs[n].at[0], sems.at[n, j]
            ).wait()
            return 0

        lax.fori_loop(0, amount, finish, 0)


def sorted_kernel(peers, cap, source, fill, tiles, out, sems):
    half = out.shape[1]
    first = pl.multiple_of(lax.axis_index("sub") * half, half)

    def each(act):
        def peer(to, _):
            def slot(j, _):
                at = to * cap + j
                act(source[at], at)
                return 0

            return lax.fori_loop(0, fill[to], slot, 0)

        lax.fori_loop(0, peers, peer, 0)

    def copy(t, at):
        return pltpu.make_async_copy(tiles.at[t, pl.ds(first, half)], out.at[at], sems.at[t])

    each(lambda t, at: copy(t, at).start())
    each(lambda t, at: copy(t, at).wait())


def label_kernel(peers, cap, source, fill, row, off, after, codes):
    def peer(to, _):
        def slot(j, _):
            t = source[to * cap + j]
            codes[to * (cap + 1) + j] = row[t] * 32 + off[t] + 8
            return 0

        lax.fori_loop(0, fill[to], slot, 0)
        codes[to * (cap + 1) + cap] = fill[to]
        return 0

    lax.fori_loop(0, peers, peer, 0)


def turn_kernel(nblk, h, base_one, base_two, old, after, bases, halves, sems):
    half = bases.shape[1]
    other = pl.ds(pl.multiple_of((1 - lax.axis_index("sub")) * half, half), half)
    copies = [
        pltpu.make_async_copy(base_one.at[:, other], bases.at[pl.ds(0, nblk)], sems.at[0]),
        pltpu.make_async_copy(base_two.at[:, other], bases.at[pl.ds(nblk, nblk)], sems.at[1]),
        pltpu.make_async_copy(h.at[:, pl.ds(0, half)], halves.at[pl.ds(0, nblk)], sems.at[2]),
        pltpu.make_async_copy(
            h.at[:, pl.ds(half, half)], halves.at[pl.ds(nblk, nblk)], sems.at[3]
        ),
        pltpu.make_async_copy(old.at[:, other], halves.at[pl.ds(2 * nblk, nblk)], sems.at[4]),
    ]
    for copy in copies:
        copy.start()
    for copy in copies:
        copy.wait()


def plan_kernel(peers, late, nblk, codes, by_row, row_at, by_side, side_at, fill_row, fill_side):
    cap = codes.shape[0] // peers - 1
    nothing = peers * cap * 32 + nblk
    me = lax.axis_index(PEERS)
    for g in range(2 * nblk):
        fill_row[g] = 0
        fill_side[g] = 0

    def walk(act):
        def peer(origin, _):
            behind = jnp.int32(0)
            step = lax.rem(me + peers - origin, peers)
            for k in late:
                behind = behind + jnp.where(step == k, nblk, 0)

            def slot(j, _):
                code = codes[origin * (cap + 1) + j]
                row = code >> 5
                col = row + (code & 31)
                own = (col >= nblk) & (col < 2 * nblk)
                act(
                    row + behind,
                    row + jnp.where(own, 0, nblk),
                    (origin * cap + j) * 32 + col,
                )
                return 0

            return lax.fori_loop(0, codes[origin * (cap + 1) + cap], slot, 0)

        lax.fori_loop(0, peers, peer, 0)

    def tally(row, side, entry):
        fill_row[row] = fill_row[row] + 1
        fill_side[side] = fill_side[side] + 1

    def place(row, side, entry):
        to = fill_row[row]
        by_row[to] = entry
        fill_row[row] = to + 1
        to = fill_side[side]
        by_side[to] = entry
        fill_side[side] = to + 1

    walk(tally)
    for fill, at, listed in ((fill_row, row_at, by_row), (fill_side, side_at, by_side)):
        now = jnp.int32(0)
        for g in range(2 * nblk):
            at[g] = now
            need = (fill[g] + QUAD - 1) // QUAD
            fill[g] = now * QUAD
            now = now + need
            last = jnp.maximum(now * QUAD - QUAD, 0)
            for u in range(QUAD):
                listed[last + u] = nothing
        at[2 * nblk] = now
    walk(place)


def tile_copies(cap, steps, arrived, tiles, sems):
    if steps is None:
        whole = tiles.at[pl.ds(0, arrived[0].shape[0])]
        return [pltpu.make_async_copy(arrived[0], whole, sems.at[0])]
    me = lax.axis_index(PEERS)
    peers = lax.axis_size(PEERS)
    copies = []
    for n, (k, ref) in enumerate(zip(steps, arrived)):
        origin = lax.rem(me + peers - k, peers)
        copies.append(pltpu.make_async_copy(ref, tiles.at[pl.ds(origin * cap, cap)], sems.at[n]))
    return copies


def tile_sums(order, begin, end, tiles, cells, base):
    def quad(q, acc):
        for pair in range(0, QUAD, 2):
            first = order[q * QUAD + pair]
            second = order[q * QUAD + pair + 1]
            weights = jnp.concatenate([tiles[first >> 5], tiles[second >> 5]], axis=1)
            chosen = jnp.concatenate([cells[first & 31], cells[second & 31]], axis=0)
            acc = acc + jnp.dot(weights, chosen, preferred_element_type=F32)
        return acc

    return lax.fori_loop(begin, end, quad, base)


def early_kernel(cap, steps, pieces, nblk, order, at, *refs):
    arrived = refs[:pieces]
    (left, left_twin, h, halves, right, right_twin, base_one, base_two, bases, old) = refs[
        pieces : pieces + 10
    ]
    w_self, bias, agg, cells, own, base_rows, old_rows, tiles, sems = refs[pieces + 10 :]
    sub = lax.axis_index("sub")
    half = agg.shape[1]
    width = h.shape[2]
    lanes = pl.ds(pl.multiple_of(sub * width, width), width)
    others = pl.ds(pl.multiple_of((1 - sub) * width, width), width)
    lines = pl.ds(pl.multiple_of(sub * half, half), half)
    block = [pl.ds(k * nblk, nblk) for k in range(3)]
    low, high = pl.ds(0, half), pl.ds(half, half)
    moves = [
        (left, cells.at[block[0], :, lanes]),
        (left_twin, cells.at[block[0], :, others]),
        (h, cells.at[block[1], :, lanes]),
        (halves.at[block[0]], cells.at[block[1], low, others]),
        (halves.at[block[1]], cells.at[block[1], high, others]),
        (right, cells.at[block[2], :, lanes]),
        (right_twin, cells.at[block[2], :, others]),
        (base_one.at[:, lines], agg.at[:, :, lanes]),
        (bases.at[block[0]], agg.at[:, :, others]),
        (base_two.at[:, lines], base_rows.at[:, :, lanes]),
        (bases.at[block[1]], base_rows.at[:, :, others]),
        (old.at[:, lines], old_rows.at[:, :, lanes]),
        (halves.at[block[2]], old_rows.at[:, :, others]),
    ]
    copies = tile_copies(cap, steps, arrived, tiles, sems)
    for k, (src, dst) in enumerate(moves):
        copies.append(pltpu.make_async_copy(src, dst, sems.at[pieces + k]))
    for copy in copies:
        copy.start()
    tiles[tiles.shape[0] - 1] = jnp.zeros(tiles.shape[1:], tiles.dtype)
    for copy in copies:
        copy.wait()
    for r in range(nblk):
        agg[r] = tile_sums(order, at[r], at[r + 1], tiles, cells, agg[r])
    for r in range(nblk):
        own[r] = (
            jnp.dot(cells[nblk + r, lines], w_self[...], preferred_element_type=F32) + bias[...]
        )


def column(inv, r, sub, half):
    shape = (half, inv.shape[1])
    line = lax.broadcasted_iota(jnp.int32, shape, 0) + sub * half
    lane = lax.broadcasted_iota(jnp.int32, shape, 1)
    spread = jnp.broadcast_to(inv[r : r + 1, :], shape)
    return jnp.sum(jnp.where(line == lane, spread, 0.0), axis=1, keepdims=True)


def late_kernel(cap, steps, pieces, nblk, order, at, affected, *refs):
    arrived = refs[:pieces]
    cells, agg, inv, own, w_neigh, old, out, tiles, means, sems = refs[pieces:]
    half = agg.shape[1]
    sub = lax.axis_index("sub")
    copies = tile_copies(cap, steps, arrived, tiles, sems) if pieces else []
    for copy in copies:
        copy.start()
    tiles[tiles.shape[0] - 1] = jnp.zeros(tiles.shape[1:], tiles.dtype)
    for copy in copies:
        copy.wait()
    for r in range(nblk):
        total = tile_sums(order, at[nblk + r], at[nblk + r + 1], tiles, cells, agg[r])
        means[r] = (total * column(inv, r, sub, half)).astype(BF16)
    for r in range(nblk):
        pre = own[r] + jnp.dot(means[r], w_neigh[...], preferred_element_type=F32)
        pre = jnp.maximum(pre, 0.0)
        keep = jnp.full((half, 1), affected[r], jnp.int32) > 0
        out[r] = jnp.where(keep, pre, old[r].astype(F32)).astype(BF16)


def near_kernel(cap, steps, pieces, nblk, order, at, *refs):
    arrived = refs[:pieces]
    mine, twin, base, w_self, bias, agg, own, hidden, tiles, cells, sems = refs[pieces:]
    width = hidden.shape[2]
    lanes = pl.ds(pl.multiple_of(lax.axis_index("sub") * width, width), width)
    half = base.shape[1]
    sub = lax.axis_index("sub")
    copies = tile_copies(cap, steps, arrived, tiles, sems)
    for k, (ref, side) in enumerate(((mine, sub), (twin, 1 - sub))):
        lines = pl.ds(pl.multiple_of(side * half, half), half)
        copies.append(
            pltpu.make_async_copy(ref, cells.at[pl.ds(nblk, nblk), lines], sems.at[pieces + k])
        )
        copies.append(
            pltpu.make_async_copy(
                ref.at[:, :, lanes], hidden.at[:, lines], sems.at[pieces + 2 + k]
            )
        )
    for copy in copies:
        copy.start()
    tiles[tiles.shape[0] - 1] = jnp.zeros(tiles.shape[1:], tiles.dtype)
    for copy in copies:
        copy.wait()
    for r in range(nblk):
        agg[r] = tile_sums(order, at[r], at[r + 1], tiles, cells, base[r])
    mine_rows = pl.ds(pl.multiple_of(sub * half, half), half)
    for r in range(nblk):
        own[r] = (
            jnp.dot(cells[nblk + r, mine_rows], w_self[...], preferred_element_type=F32) + bias[...]
        )


def far_kernel(cap, steps, pieces, nblk, order, at, *refs):
    arrived = refs[:pieces]
    left, left_twin, right, right_twin, agg, inv, own, w_neigh, keep, send = refs[
        pieces : pieces + 10
    ]
    tiles, cells, means, sems = refs[pieces + 10 :]
    half = agg.shape[1]
    width = keep.shape[2]
    sub = lax.axis_index("sub")
    copies = tile_copies(cap, steps, arrived, tiles, sems)
    sides = ((left, 0, sub), (left_twin, 0, 1 - sub), (right, 2, sub), (right_twin, 2, 1 - sub))
    for k, (ref, third, side) in enumerate(sides):
        lines = pl.ds(pl.multiple_of(side * half, half), half)
        copies.append(
            pltpu.make_async_copy(
                ref, cells.at[pl.ds(third * nblk, nblk), lines], sems.at[pieces + k]
            )
        )
    for copy in copies:
        copy.start()
    tiles[tiles.shape[0] - 1] = jnp.zeros(tiles.shape[1:], tiles.dtype)
    cells[nblk] = jnp.zeros(cells.shape[1:], cells.dtype)
    for copy in copies:
        copy.wait()
    for r in range(nblk):
        total = tile_sums(order, at[nblk + r], at[nblk + r + 1], tiles, cells, agg[r])
        means[r] = (total * column(inv, r, sub, half)).astype(BF16)
    for r in range(nblk):
        pre = own[r] + jnp.dot(means[r], w_neigh[...], preferred_element_type=F32)
        low = pre[:, :width].astype(BF16)
        high = pre[:, width:].astype(BF16)
        first = jnp.full((half, 1), sub, jnp.int32) == 0
        keep[r] = jnp.where(first, low, high)
        send[r] = jnp.where(first, high, low)


def finish_kernel(nblk, affected, kept, came, old, out):
    half = kept.shape[1]
    first = jnp.full((half, 1), lax.axis_index("sub"), jnp.int32) == 0
    for r in range(nblk):
        keep = jnp.full((half, 1), affected[r], jnp.int32) > 0
        low = jnp.where(first, kept[r].astype(F32), came[r].astype(F32))
        high = jnp.where(first, came[r].astype(F32), kept[r].astype(F32))
        out[r, :half] = jnp.where(keep, low, old[r, :half].astype(F32)).astype(BF16)
        out[r, half:] = jnp.where(keep, high, old[r, half:].astype(F32)).astype(BF16)


def swap(x):
    return lax.ppermute(x, "sub", [(0, 1), (1, 0)])


def ring(x, step):
    peers = lax.axis_size(PEERS)
    return lax.ppermute(x, PEERS, [(i, (i + step) % peers) for i in range(peers)])


def on_device(
    h_input,
    inv_degree,
    dest_block,
    row_block,
    block_offset,
    new_tiles,
    base_one,
    affected_one,
    old_one,
    self_one,
    neigh_one,
    bias_one,
    base_two,
    affected_two,
    old_two,
    self_two,
    neigh_two,
    bias_two,
):
    peers = lax.axis_size(PEERS)
    count = dest_block.shape[0]
    cap = max(2, 2 * count // peers)
    slots = peers * cap
    rows_here, width = h_input.shape
    full = width * lax.axis_size("sub")
    nblk = rows_here // BLK
    half = BLK // lax.axis_size("sub")
    direct = 2 < peers <= 16
    shape = jax.ShapeDtypeStruct
    after = lax.optimization_barrier

    order = sorted(range(1, peers), key=lambda k: (abs(k - peers // 2), k))
    lead = order[0] if direct else None
    piece = shape((cap, half, BLK), BF16)
    out_piece, source, fill = pl.pallas_call(
        functools.partial(first_kernel, peers, cap, lead),
        out_shape=[piece, shape((slots,), jnp.int32), shape((peers,), jnp.int32)],
        in_specs=[SMEM, HBM],
        out_specs=[HBM, SMEM, SMEM],
        scratch_shapes=[pltpu.SemaphoreType.DMA((cap,))],
        cost_estimate=TINY,
        name="first",
    )(dest_block.reshape(count), new_tiles)

    if direct:
        others = order[1:] + [0]
        packed = pl.pallas_call(
            functools.partial(rest_kernel, peers, cap, others),
            out_shape=[piece] * len(others),
            in_specs=[SMEM, SMEM, HBM],
            out_specs=[HBM] * len(others),
            scratch_shapes=[pltpu.SemaphoreType.DMA((len(others), cap))],
            cost_estimate=TINY,
            name="rest",
        )(source, fill, new_tiles)
        steps = order + [0]
        got = dict(zip(others, packed))
        got[lead] = out_piece
        got = {k: ring(got[k], k) if k else got[k] for k in steps}
        late = tuple(order[4:]) if peers > 4 else ()
        early = [k for k in steps if k not in late]
        arrived = [got[k] for k in steps]
        arrived_early = [got[k] for k in early]
        arrived_late = [got[k] for k in late]
        flag = got[lead]
        gathered = packed[-1]
    else:
        sent = pl.pallas_call(
            functools.partial(sorted_kernel, peers, cap),
            out_shape=shape((slots, half, BLK), BF16),
            in_specs=[SMEM, SMEM, HBM],
            out_specs=HBM,
            scratch_shapes=[pltpu.SemaphoreType.DMA((count,))],
            cost_estimate=TINY,
            name="rest",
        )(source, fill, new_tiles)
        sent = sent.reshape(peers, cap, half, BLK)
        got = lax.all_to_all(sent, PEERS, split_axis=0, concat_axis=0, tiled=True)
        arrived = [got.reshape(slots, half, BLK)]
        steps = early = None
        late = ()
        arrived_early, arrived_late = arrived, []
        flag = source
        gathered = out_piece

    codes = pl.pallas_call(
        functools.partial(label_kernel, peers, cap),
        out_shape=shape((peers * (cap + 1),), jnp.int32),
        in_specs=[SMEM] * 4 + [ANY],
        out_specs=SMEM,
        compiler_params=SMALL,
        cost_estimate=TINY,
        name="label",
    )(source, fill, row_block, block_offset, gathered)
    got_codes = lax.all_to_all(
        codes.reshape(peers, cap + 1), PEERS, split_axis=0, concat_axis=0, tiled=True
    ).reshape(peers * (cap + 1))

    length = slots + 2 * nblk * QUAD
    by_row, row_at, by_side, side_at = pl.pallas_call(
        functools.partial(plan_kernel, peers, late, nblk),
        out_shape=[shape((length,), jnp.int32), shape((2 * nblk + 1,), jnp.int32)] * 2,
        in_specs=[SMEM],
        out_specs=[SMEM] * 4,
        scratch_shapes=[pltpu.SMEM((2 * nblk,), jnp.int32)] * 2,
        compiler_params=SMALL,
        cost_estimate=TINY,
        name="plan",
    )(got_codes)

    blocks = (nblk, BLK, width)
    h_blocks, old_blocks = h_input.reshape(blocks), old_one.reshape(blocks)
    base_one, base_two = base_one.reshape(blocks), base_two.reshape(blocks)
    bases, halves = pl.pallas_call(
        functools.partial(turn_kernel, nblk),
        out_shape=[shape((2 * nblk, half, width), F32), shape((3 * nblk, half, width), BF16)],
        in_specs=[ANY] * 5,
        out_specs=[ANY] * 2,
        scratch_shapes=[pltpu.SemaphoreType.DMA((5,))],
        compiler_params=SMALL,
        cost_estimate=TINY,
        name="turn",
    )(h_blocks, base_one, base_two, old_blocks, gathered)
    bases, halves = swap(bases), swap(halves)
    h_later, _ = after((h_blocks, flag))
    left, right = ring(h_later, 1), ring(h_later, peers - 1)
    left_twin, right_twin = swap(left), swap(right)

    tile_scratch = pltpu.VMEM((slots + 1, half, BLK), BF16)
    cell_shape = (3 * nblk, BLK, full)
    cell_scratch = pltpu.VMEM(cell_shape, BF16)
    mean_scratch = pltpu.VMEM((nblk, half, full), BF16)
    rows_shape = (nblk, half, full)
    inv = inv_degree.reshape(nblk, BLK)

    many = len(arrived_early)
    agg_early, cells_one, own_one, base_two_rows, old_one_rows = pl.pallas_call(
        functools.partial(early_kernel, cap, early, many, nblk),
        out_shape=[
            shape(rows_shape, F32),
            shape(cell_shape, BF16),
            shape(rows_shape, F32),
            shape(rows_shape, F32),
            shape(rows_shape, BF16),
        ],
        in_specs=[SMEM] * 2 + [ANY] * (many + 10) + [VMEM] * 2,
        out_specs=[VMEM] * 5,
        scratch_shapes=[tile_scratch, pltpu.SemaphoreType.DMA((many + 13,))],
        compiler_params=PARAMS,
        cost_estimate=TINY,
        name="early",
    )(
        by_row,
        row_at,
        *arrived_early,
        left,
        left_twin,
        h_blocks,
        halves,
        right,
        right_twin,
        base_one,
        base_two,
        bases,
        old_blocks,
        self_one,
        bias_one.reshape(1, full),
    )

    many = len(arrived_late)
    hidden_rows = pl.pallas_call(
        functools.partial(late_kernel, cap, late, many, nblk),
        out_shape=shape(rows_shape, BF16),
        in_specs=[SMEM] * 3 + [ANY] * many + [VMEM] * 6,
        out_specs=VMEM,
        scratch_shapes=[tile_scratch, mean_scratch, pltpu.SemaphoreType.DMA((max(1, many),))],
        compiler_params=PARAMS,
        cost_estimate=TINY,
        name="late",
    )(
        by_row,
        row_at,
        affected_one,
        *arrived_late,
        cells_one,
        agg_early,
        inv,
        own_one,
        neigh_one,
        old_one_rows,
    )

    hidden_twin = swap(hidden_rows)
    left = ring(hidden_rows, 1)
    right = ring(hidden_rows, peers - 1)

    many = len(arrived)
    agg_two, own_two, hidden_one = pl.pallas_call(
        functools.partial(near_kernel, cap, steps, many, nblk),
        out_shape=[shape(rows_shape, F32)] * 2 + [shape(blocks, BF16)],
        in_specs=[SMEM] * 2 + [ANY] * (many + 2) + [VMEM] * 3,
        out_specs=[VMEM] * 2 + [ANY],
        scratch_shapes=[tile_scratch, cell_scratch, pltpu.SemaphoreType.DMA((many + 4,))],
        compiler_params=PARAMS,
        cost_estimate=TINY,
        name="near",
    )(
        by_side,
        side_at,
        *arrived,
        hidden_rows,
        hidden_twin,
        base_two_rows,
        self_two,
        bias_two.reshape(1, full),
    )

    left, right, agg_two, own_two = after((left, right, agg_two, own_two))
    left_twin = swap(left)
    right_twin = swap(right)
    kept, sent = pl.pallas_call(
        functools.partial(far_kernel, cap, steps, many, nblk),
        out_shape=[shape((nblk, half, width), BF16)] * 2,
        in_specs=[SMEM] * 2 + [ANY] * (many + 4) + [VMEM] * 4,
        out_specs=[VMEM] * 2,
        scratch_shapes=[
            tile_scratch,
            cell_scratch,
            mean_scratch,
            pltpu.SemaphoreType.DMA((many + 4,)),
        ],
        compiler_params=PARAMS,
        cost_estimate=TINY,
        name="far",
    )(
        by_side,
        side_at,
        *arrived,
        left,
        left_twin,
        right,
        right_twin,
        agg_two,
        inv,
        own_two,
        neigh_two,
    )
    came = swap(sent)
    hidden_two = pl.pallas_call(
        functools.partial(finish_kernel, nblk),
        out_shape=shape(blocks, BF16),
        in_specs=[SMEM] + [VMEM] * 3,
        out_specs=VMEM,
        compiler_params=SMALL,
        cost_estimate=TINY,
        name="finish",
    )(affected_two, kept, came, old_two.reshape(blocks))
    return (hidden_one.reshape(rows_here, width), hidden_two.reshape(rows_here, width))


def solution(mesh):
    rows = P(("groups", "rows", "feat"))
    cells = P(("groups", "rows", "feat"), "sub")
    placed = (
        cells,
        rows,
        P(("groups", "rows", "feat"), None),
        rows,
        rows,
        P(("groups", "rows", "feat"), None, None),
        cells,
        rows,
        cells,
        P(),
        P(),
        P(),
        cells,
        rows,
        cells,
        P(),
        P(),
        P(),
    )
    return jax.shard_map(
        on_device, mesh=mesh, in_specs=placed, out_specs=(cells, cells), check_vma=False
    )
```

```python
import functools

import jax
import jax.numpy as jnp
from jax import lax
from jax.experimental import pallas as pl
from jax.experimental.pallas import tpu as pltpu
from jax.sharding import PartitionSpec as P

PEERS = ("rows", "feat")
BLK = 128
QUAD = 4
F32 = jnp.float32
BF16 = jnp.bfloat16
ANY = pl.BlockSpec(memory_space=pl.ANY)
HBM = pl.BlockSpec(memory_space=pltpu.HBM)
SMEM = pl.BlockSpec(memory_space=pltpu.SMEM)
VMEM = pl.BlockSpec(memory_space=pltpu.VMEM)
PARAMS = pltpu.CompilerParams(vmem_limit_bytes=20 * 1024 * 1024)
SMALL = pltpu.CompilerParams(vmem_limit_bytes=4 * 1024 * 1024)
TINY = pl.CostEstimate(flops=0, bytes_accessed=128, transcendentals=0)


def first_kernel(peers, cap, lead, dest, tiles, out, source, fill, sem):
    count = dest.shape[0]
    half = out.shape[1]
    me = lax.axis_index(PEERS)
    first = pl.multiple_of(lax.axis_index("sub") * half, half)
    for to in range(min(peers, 16)):
        fill[to] = 0
    if peers > 16:

        def clear(i, _):
            fill[i] = 0
            return 0

        lax.fori_loop(16, peers, clear, 0)
    for t in range(count):
        to = dest[t]
        at = fill[to]
        fill[to] = at + 1
        source[to * cap + at] = t
    if lead is None:
        return
    to = lax.rem(me + lead, peers)

    def send(j, _):
        t = source[to * cap + j]
        pltpu.make_async_copy(tiles.at[t, pl.ds(first, half)], out.at[j], sem.at[j]).start()
        return 0

    def finish(j, _):
        pltpu.make_async_copy(tiles.at[0, pl.ds(first, half)], out.at[0], sem.at[j]).wait()
        return 0

    lax.fori_loop(0, fill[to], send, 0)
    lax.fori_loop(0, fill[to], finish, 0)


def rest_kernel(peers, cap, order, source, fill, tiles, *refs):
    outs, sems = refs[:-1], refs[-1]
    half = outs[0].shape[1]
    me = lax.axis_index(PEERS)
    first = pl.multiple_of(lax.axis_index("sub") * half, half)
    begun = []
    for n, k in enumerate(order):
        to = lax.rem(me + k, peers)

        def send(j, _, n=n, to=to):
            t = source[to * cap + j]
            pltpu.make_async_copy(
                tiles.at[t, pl.ds(first, half)], outs[n].at[j], sems.at[n, j]
            ).start()
            return 0

        lax.fori_loop(0, fill[to], send, 0)
        begun.append(fill[to])
    for n, amount in enumerate(begun):

        def finish(j, _, n=n):
            pltpu.make_async_copy(
                tiles.at[0, pl.ds(first, half)], outs[n].at[0], sems.at[n, j]
            ).wait()
            return 0

        lax.fori_loop(0, amount, finish, 0)


def sorted_kernel(peers, cap, source, fill, tiles, out, sems):
    half = out.shape[1]
    first = pl.multiple_of(lax.axis_index("sub") * half, half)

    def each(act):
        def peer(to, _):
            def slot(j, _):
                at = to * cap + j
                act(source[at], at)
                return 0

            return lax.fori_loop(0, fill[to], slot, 0)

        lax.fori_loop(0, peers, peer, 0)

    def copy(t, at):
        return pltpu.make_async_copy(tiles.at[t, pl.ds(first, half)], out.at[at], sems.at[t])

    each(lambda t, at: copy(t, at).start())
    each(lambda t, at: copy(t, at).wait())


def label_kernel(peers, cap, source, fill, row, off, after, codes):
    def peer(to, _):
        def slot(j, _):
            t = source[to * cap + j]
            codes[to * (cap + 1) + j] = row[t] * 32 + off[t] + 8
            return 0

        lax.fori_loop(0, fill[to], slot, 0)
        codes[to * (cap + 1) + cap] = fill[to]
        return 0

    lax.fori_loop(0, peers, peer, 0)


def turn_kernel(nblk, h, base_one, base_two, old, after, bases, halves, sems):
    half = bases.shape[1]
    other = pl.ds(pl.multiple_of((1 - lax.axis_index("sub")) * half, half), half)
    copies = [
        pltpu.make_async_copy(base_one.at[:, other], bases.at[pl.ds(0, nblk)], sems.at[0]),
        pltpu.make_async_copy(base_two.at[:, other], bases.at[pl.ds(nblk, nblk)], sems.at[1]),
        pltpu.make_async_copy(h.at[:, pl.ds(0, half)], halves.at[pl.ds(0, nblk)], sems.at[2]),
        pltpu.make_async_copy(
            h.at[:, pl.ds(half, half)], halves.at[pl.ds(nblk, nblk)], sems.at[3]
        ),
        pltpu.make_async_copy(old.at[:, other], halves.at[pl.ds(2 * nblk, nblk)], sems.at[4]),
    ]
    for copy in copies:
        copy.start()
    for copy in copies:
        copy.wait()


def plan_kernel(peers, late, nblk, codes, by_row, row_at, by_side, side_at, fill_row, fill_side):
    cap = codes.shape[0] // peers - 1
    nothing = peers * cap * 32 + nblk
    me = lax.axis_index(PEERS)
    for g in range(2 * nblk):
        fill_row[g] = 0
        fill_side[g] = 0

    def walk(act):
        def peer(origin, _):
            behind = jnp.int32(0)
            step = lax.rem(me + peers - origin, peers)
            for k in late:
                behind = behind + jnp.where(step == k, nblk, 0)

            def slot(j, _):
                code = codes[origin * (cap + 1) + j]
                row = code >> 5
                col = row + (code & 31)
                own = (col >= nblk) & (col < 2 * nblk)
                act(
                    row + behind,
                    row + jnp.where(own, 0, nblk),
                    (origin * cap + j) * 32 + col,
                )
                return 0

            return lax.fori_loop(0, codes[origin * (cap + 1) + cap], slot, 0)

        lax.fori_loop(0, peers, peer, 0)

    def tally(row, side, entry):
        fill_row[row] = fill_row[row] + 1
        fill_side[side] = fill_side[side] + 1

    def place(row, side, entry):
        to = fill_row[row]
        by_row[to] = entry
        fill_row[row] = to + 1
        to = fill_side[side]
        by_side[to] = entry
        fill_side[side] = to + 1

    walk(tally)
    for fill, at, listed in ((fill_row, row_at, by_row), (fill_side, side_at, by_side)):
        now = jnp.int32(0)
        for g in range(2 * nblk):
            at[g] = now
            need = (fill[g] + QUAD - 1) // QUAD
            fill[g] = now * QUAD
            now = now + need
            last = jnp.maximum(now * QUAD - QUAD, 0)
            for u in range(QUAD):
                listed[last + u] = nothing
        at[2 * nblk] = now
    walk(place)


def tile_copies(cap, steps, arrived, tiles, sems):
    if steps is None:
        whole = tiles.at[pl.ds(0, arrived[0].shape[0])]
        return [pltpu.make_async_copy(arrived[0], whole, sems.at[0])]
    me = lax.axis_index(PEERS)
    peers = lax.axis_size(PEERS)
    copies = []
    for n, (k, ref) in enumerate(zip(steps, arrived)):
        origin = lax.rem(me + peers - k, peers)
        copies.append(pltpu.make_async_copy(ref, tiles.at[pl.ds(origin * cap, cap)], sems.at[n]))
    return copies


def tile_sums(order, begin, end, tiles, cells, base):
    def quad(q, acc):
        for pair in range(0, QUAD, 2):
            first = order[q * QUAD + pair]
            second = order[q * QUAD + pair + 1]
            weights = jnp.concatenate([tiles[first >> 5], tiles[second >> 5]], axis=1)
            chosen = jnp.concatenate([cells[first & 31], cells[second & 31]], axis=0)
            acc = acc + jnp.dot(weights, chosen, preferred_element_type=F32)
        return acc

    return lax.fori_loop(begin, end, quad, base)


def early_kernel(cap, steps, pieces, nblk, order, at, *refs):
    arrived = refs[:pieces]
    (left, left_twin, h, halves, right, right_twin, base_one, base_two, bases, old) = refs[
        pieces : pieces + 10
    ]
    w_self, bias, agg, cells, own, base_rows, old_rows, tiles, sems = refs[pieces + 10 :]
    sub = lax.axis_index("sub")
    half = agg.shape[1]
    width = h.shape[2]
    lanes = pl.ds(pl.multiple_of(sub * width, width), width)
    others = pl.ds(pl.multiple_of((1 - sub) * width, width), width)
    lines = pl.ds(pl.multiple_of(sub * half, half), half)
    block = [pl.ds(k * nblk, nblk) for k in range(3)]
    low, high = pl.ds(0, half), pl.ds(half, half)
    moves = [
        (left, cells.at[block[0], :, lanes]),
        (left_twin, cells.at[block[0], :, others]),
        (h, cells.at[block[1], :, lanes]),
        (halves.at[block[0]], cells.at[block[1], low, others]),
        (halves.at[block[1]], cells.at[block[1], high, others]),
        (right, cells.at[block[2], :, lanes]),
        (right_twin, cells.at[block[2], :, others]),
        (base_one.at[:, lines], agg.at[:, :, lanes]),
        (bases.at[block[0]], agg.at[:, :, others]),
        (base_two.at[:, lines], base_rows.at[:, :, lanes]),
        (bases.at[block[1]], base_rows.at[:, :, others]),
        (old.at[:, lines], old_rows.at[:, :, lanes]),
        (halves.at[block[2]], old_rows.at[:, :, others]),
    ]
    copies = tile_copies(cap, steps, arrived, tiles, sems)
    for k, (src, dst) in enumerate(moves):
        copies.append(pltpu.make_async_copy(src, dst, sems.at[pieces + k]))
    for copy in copies:
        copy.start()
    tiles[tiles.shape[0] - 1] = jnp.zeros(tiles.shape[1:], tiles.dtype)
    for copy in copies:
        copy.wait()
    for r in range(nblk):
        agg[r] = tile_sums(order, at[r], at[r + 1], tiles, cells, agg[r])
    for r in range(nblk):
        own[r] = (
            jnp.dot(cells[nblk + r, lines], w_self[...], preferred_element_type=F32) + bias[...]
        )


def column(inv, r, sub, half):
    shape = (half, inv.shape[1])
    line = lax.broadcasted_iota(jnp.int32, shape, 0) + sub * half
    lane = lax.broadcasted_iota(jnp.int32, shape, 1)
    spread = jnp.broadcast_to(inv[r : r + 1, :], shape)
    return jnp.sum(jnp.where(line == lane, spread, 0.0), axis=1, keepdims=True)


def late_kernel(cap, steps, pieces, nblk, order, at, affected, *refs):
    arrived = refs[:pieces]
    cells, agg, inv, own, w_neigh, old, out, tiles, means, sems = refs[pieces:]
    half = agg.shape[1]
    sub = lax.axis_index("sub")
    copies = tile_copies(cap, steps, arrived, tiles, sems) if pieces else []
    for copy in copies:
        copy.start()
    tiles[tiles.shape[0] - 1] = jnp.zeros(tiles.shape[1:], tiles.dtype)
    for copy in copies:
        copy.wait()
    for r in range(nblk):
        total = tile_sums(order, at[nblk + r], at[nblk + r + 1], tiles, cells, agg[r])
        means[r] = (total * column(inv, r, sub, half)).astype(BF16)
    for r in range(nblk):
        pre = own[r] + jnp.dot(means[r], w_neigh[...], preferred_element_type=F32)
        pre = jnp.maximum(pre, 0.0)
        keep = jnp.full((half, 1), affected[r], jnp.int32) > 0
        out[r] = jnp.where(keep, pre, old[r].astype(F32)).astype(BF16)


def near_kernel(cap, steps, pieces, nblk, order, at, *refs):
    arrived = refs[:pieces]
    mine, twin, base, w_self, bias, agg, own, hidden, tiles, cells, sems = refs[pieces:]
    width = hidden.shape[2]
    lanes = pl.ds(pl.multiple_of(lax.axis_index("sub") * width, width), width)
    half = base.shape[1]
    sub = lax.axis_index("sub")
    copies = tile_copies(cap, steps, arrived, tiles, sems)
    for k, (ref, side) in enumerate(((mine, sub), (twin, 1 - sub))):
        lines = pl.ds(pl.multiple_of(side * half, half), half)
        copies.append(
            pltpu.make_async_copy(ref, cells.at[pl.ds(nblk, nblk), lines], sems.at[pieces + k])
        )
        copies.append(
            pltpu.make_async_copy(
                ref.at[:, :, lanes], hidden.at[:, lines], sems.at[pieces + 2 + k]
            )
        )
    for copy in copies:
        copy.start()
    tiles[tiles.shape[0] - 1] = jnp.zeros(tiles.shape[1:], tiles.dtype)
    for copy in copies:
        copy.wait()
    for r in range(nblk):
        agg[r] = tile_sums(order, at[r], at[r + 1], tiles, cells, base[r])
    mine_rows = pl.ds(pl.multiple_of(sub * half, half), half)
    for r in range(nblk):
        own[r] = (
            jnp.dot(cells[nblk + r, mine_rows], w_self[...], preferred_element_type=F32) + bias[...]
        )


def far_kernel(cap, steps, pieces, nblk, order, at, *refs):
    arrived = refs[:pieces]
    left, left_twin, right, right_twin, agg, inv, own, w_neigh, keep, send = refs[
        pieces : pieces + 10
    ]
    tiles, cells, means, sems = refs[pieces + 10 :]
    half = agg.shape[1]
    width = keep.shape[2]
    sub = lax.axis_index("sub")
    copies = tile_copies(cap, steps, arrived, tiles, sems)
    sides = ((left, 0, sub), (left_twin, 0, 1 - sub), (right, 2, sub), (right_twin, 2, 1 - sub))
    for k, (ref, third, side) in enumerate(sides):
        lines = pl.ds(pl.multiple_of(side * half, half), half)
        copies.append(
            pltpu.make_async_copy(
                ref, cells.at[pl.ds(third * nblk, nblk), lines], sems.at[pieces + k]
            )
        )
    for copy in copies:
        copy.start()
    tiles[tiles.shape[0] - 1] = jnp.zeros(tiles.shape[1:], tiles.dtype)
    cells[nblk] = jnp.zeros(cells.shape[1:], cells.dtype)
    for copy in copies:
        copy.wait()
    for r in range(nblk):
        total = tile_sums(order, at[nblk + r], at[nblk + r + 1], tiles, cells, agg[r])
        means[r] = (total * column(inv, r, sub, half)).astype(BF16)
    for r in range(nblk):
        pre = own[r] + jnp.dot(means[r], w_neigh[...], preferred_element_type=F32)
        low = pre[:, :width].astype(BF16)
        high = pre[:, width:].astype(BF16)
        first = jnp.full((half, 1), sub, jnp.int32) == 0
        keep[r] = jnp.where(first, low, high)
        send[r] = jnp.where(first, high, low)


def finish_kernel(nblk, affected, kept, came, old, out):
    half = kept.shape[1]
    first = jnp.full((half, 1), lax.axis_index("sub"), jnp.int32) == 0
    for r in range(nblk):
        keep = jnp.full((half, 1), affected[r], jnp.int32) > 0
        low = jnp.where(first, kept[r].astype(F32), came[r].astype(F32))
        high = jnp.where(first, came[r].astype(F32), kept[r].astype(F32))
        out[r, :half] = jnp.where(keep, low, old[r, :half].astype(F32)).astype(BF16)
        out[r, half:] = jnp.where(keep, high, old[r, half:].astype(F32)).astype(BF16)


def swap(x):
    return lax.ppermute(x, "sub", [(0, 1), (1, 0)])


def ring(x, step):
    peers = lax.axis_size(PEERS)
    return lax.ppermute(x, PEERS, [(i, (i + step) % peers) for i in range(peers)])


def on_device(
    h_input,
    inv_degree,
    dest_block,
    row_block,
    block_offset,
    new_tiles,
    base_one,
    affected_one,
    old_one,
    self_one,
    neigh_one,
    bias_one,
    base_two,
    affected_two,
    old_two,
    self_two,
    neigh_two,
    bias_two,
):
    peers = lax.axis_size(PEERS)
    count = dest_block.shape[0]
    cap = max(2, 2 * count // peers)
    slots = peers * cap
    rows_here, width = h_input.shape
    full = width * lax.axis_size("sub")
    nblk = rows_here // BLK
    half = BLK // lax.axis_size("sub")
    direct = 2 < peers <= 16
    shape = jax.ShapeDtypeStruct
    after = lax.optimization_barrier

    order = sorted(range(1, peers), key=lambda k: (abs(k - peers // 2), k))
    lead = order[0] if direct else None
    piece = shape((cap, half, BLK), BF16)
    out_piece, source, fill = pl.pallas_call(
        functools.partial(first_kernel, peers, cap, lead),
        out_shape=[piece, shape((slots,), jnp.int32), shape((peers,), jnp.int32)],
        in_specs=[SMEM, HBM],
        out_specs=[VMEM, SMEM, SMEM],
        scratch_shapes=[pltpu.SemaphoreType.DMA((cap,))],
        cost_estimate=TINY,
        name="first",
    )(dest_block.reshape(count), new_tiles)

    if direct:
        others = order[1:] + [0]
        packed = pl.pallas_call(
            functools.partial(rest_kernel, peers, cap, others),
            out_shape=[piece] * len(others),
            in_specs=[SMEM, SMEM, HBM],
            out_specs=[VMEM] * len(others),
            scratch_shapes=[pltpu.SemaphoreType.DMA((len(others), cap))],
            cost_estimate=TINY,
            name="rest",
        )(source, fill, new_tiles)
        steps = order + [0]
        got = dict(zip(others, packed))
        got[lead] = out_piece
        got = {k: ring(got[k], k) if k else got[k] for k in steps}
        late = tuple(order[4:]) if peers > 4 else ()
        early = [k for k in steps if k not in late]
        arrived = [got[k] for k in steps]
        arrived_early = [got[k] for k in early]
        arrived_late = [got[k] for k in late]
        flag = got[lead]
        gathered = packed[-1]
    else:
        sent = pl.pallas_call(
            functools.partial(sorted_kernel, peers, cap),
            out_shape=shape((slots, half, BLK), BF16),
            in_specs=[SMEM, SMEM, HBM],
            out_specs=HBM,
            scratch_shapes=[pltpu.SemaphoreType.DMA((count,))],
            cost_estimate=TINY,
            name="rest",
        )(source, fill, new_tiles)
        sent = sent.reshape(peers, cap, half, BLK)
        got = lax.all_to_all(sent, PEERS, split_axis=0, concat_axis=0, tiled=True)
        arrived = [got.reshape(slots, half, BLK)]
        steps = early = None
        late = ()
        arrived_early, arrived_late = arrived, []
        flag = source
        gathered = out_piece

    codes = pl.pallas_call(
        functools.partial(label_kernel, peers, cap),
        out_shape=shape((peers * (cap + 1),), jnp.int32),
        in_specs=[SMEM] * 4 + [ANY],
        out_specs=SMEM,
        compiler_params=SMALL,
        cost_estimate=TINY,
        name="label",
    )(source, fill, row_block, block_offset, gathered)
    got_codes = lax.all_to_all(
        codes.reshape(peers, cap + 1), PEERS, split_axis=0, concat_axis=0, tiled=True
    ).reshape(peers * (cap + 1))

    length = slots + 2 * nblk * QUAD
    by_row, row_at, by_side, side_at = pl.pallas_call(
        functools.partial(plan_kernel, peers, late, nblk),
        out_shape=[shape((length,), jnp.int32), shape((2 * nblk + 1,), jnp.int32)] * 2,
        in_specs=[SMEM],
        out_specs=[SMEM] * 4,
        scratch_shapes=[pltpu.SMEM((2 * nblk,), jnp.int32)] * 2,
        compiler_params=SMALL,
        cost_estimate=TINY,
        name="plan",
    )(got_codes)

    blocks = (nblk, BLK, width)
    h_blocks, old_blocks = h_input.reshape(blocks), old_one.reshape(blocks)
    base_one, base_two = base_one.reshape(blocks), base_two.reshape(blocks)
    bases, halves = pl.pallas_call(
        functools.partial(turn_kernel, nblk),
        out_shape=[shape((2 * nblk, half, width), F32), shape((3 * nblk, half, width), BF16)],
        in_specs=[ANY] * 5,
        out_specs=[ANY] * 2,
        scratch_shapes=[pltpu.SemaphoreType.DMA((5,))],
        compiler_params=SMALL,
        cost_estimate=TINY,
        name="turn",
    )(h_blocks, base_one, base_two, old_blocks, gathered)
    bases, halves, _ = after((bases, halves, flag))
    bases, halves = swap(bases), swap(halves)
    h_later, _, by_row, by_side = after((h_blocks, flag, by_row, by_side))
    left, right = ring(h_later, 1), ring(h_later, peers - 1)
    left_twin, right_twin = swap(left), swap(right)

    tile_scratch = pltpu.VMEM((slots + 1, half, BLK), BF16)
    cell_shape = (3 * nblk, BLK, full)
    cell_scratch = pltpu.VMEM(cell_shape, BF16)
    mean_scratch = pltpu.VMEM((nblk, half, full), BF16)
    rows_shape = (nblk, half, full)
    inv = inv_degree.reshape(nblk, BLK)

    many = len(arrived_early)
    agg_early, cells_one, own_one, base_two_rows, old_one_rows = pl.pallas_call(
        functools.partial(early_kernel, cap, early, many, nblk),
        out_shape=[
            shape(rows_shape, F32),
            shape(cell_shape, BF16),
            shape(rows_shape, F32),
            shape(rows_shape, F32),
            shape(rows_shape, BF16),
        ],
        in_specs=[SMEM] * 2 + [ANY] * (many + 10) + [VMEM] * 2,
        out_specs=[VMEM] * 5,
        scratch_shapes=[tile_scratch, pltpu.SemaphoreType.DMA((many + 13,))],
        compiler_params=PARAMS,
        cost_estimate=TINY,
        name="early",
    )(
        by_row,
        row_at,
        *arrived_early,
        left,
        left_twin,
        h_blocks,
        halves,
        right,
        right_twin,
        base_one,
        base_two,
        bases,
        old_blocks,
        self_one,
        bias_one.reshape(1, full),
    )

    many = len(arrived_late)
    hidden_rows = pl.pallas_call(
        functools.partial(late_kernel, cap, late, many, nblk),
        out_shape=shape(rows_shape, BF16),
        in_specs=[SMEM] * 3 + [ANY] * many + [VMEM] * 6,
        out_specs=VMEM,
        scratch_shapes=[tile_scratch, mean_scratch, pltpu.SemaphoreType.DMA((max(1, many),))],
        compiler_params=PARAMS,
        cost_estimate=TINY,
        name="late",
    )(
        by_row,
        row_at,
        affected_one,
        *arrived_late,
        cells_one,
        agg_early,
        inv,
        own_one,
        neigh_one,
        old_one_rows,
    )

    hidden_twin = swap(hidden_rows)
    left = ring(hidden_rows, 1)
    right = ring(hidden_rows, peers - 1)

    many = len(arrived)
    agg_two, own_two, hidden_one = pl.pallas_call(
        functools.partial(near_kernel, cap, steps, many, nblk),
        out_shape=[shape(rows_shape, F32)] * 2 + [shape(blocks, BF16)],
        in_specs=[SMEM] * 2 + [ANY] * (many + 2) + [VMEM] * 3,
        out_specs=[VMEM] * 2 + [ANY],
        scratch_shapes=[tile_scratch, cell_scratch, pltpu.SemaphoreType.DMA((many + 4,))],
        compiler_params=PARAMS,
        cost_estimate=TINY,
        name="near",
    )(
        by_side,
        side_at,
        *arrived,
        hidden_rows,
        hidden_twin,
        base_two_rows,
        self_two,
        bias_two.reshape(1, full),
    )

    left, right, agg_two, own_two = after((left, right, agg_two, own_two))
    left_twin = swap(left)
    right_twin = swap(right)
    kept, sent = pl.pallas_call(
        functools.partial(far_kernel, cap, steps, many, nblk),
        out_shape=[shape((nblk, half, width), BF16)] * 2,
        in_specs=[SMEM] * 2 + [ANY] * (many + 4) + [VMEM] * 4,
        out_specs=[VMEM] * 2,
        scratch_shapes=[
            tile_scratch,
            cell_scratch,
            mean_scratch,
            pltpu.SemaphoreType.DMA((many + 4,)),
        ],
        compiler_params=PARAMS,
        cost_estimate=TINY,
        name="far",
    )(
        by_side,
        side_at,
        *arrived,
        left,
        left_twin,
        right,
        right_twin,
        agg_two,
        inv,
        own_two,
        neigh_two,
    )
    came = swap(sent)
    hidden_two = pl.pallas_call(
        functools.partial(finish_kernel, nblk),
        out_shape=shape(blocks, BF16),
        in_specs=[SMEM] + [VMEM] * 3,
        out_specs=VMEM,
        compiler_params=SMALL,
        cost_estimate=TINY,
        name="finish",
    )(affected_two, kept, came, old_two.reshape(blocks))
    return (hidden_one.reshape(rows_here, width), hidden_two.reshape(rows_here, width))


def solution(mesh):
    rows = P(("groups", "rows", "feat"))
    cells = P(("groups", "rows", "feat"), "sub")
    placed = (
        cells,
        rows,
        P(("groups", "rows", "feat"), None),
        rows,
        rows,
        P(("groups", "rows", "feat"), None, None),
        cells,
        rows,
        cells,
        P(),
        P(),
        P(),
        cells,
        rows,
        cells,
        P(),
        P(),
        P(),
    )
    return jax.shard_map(
        on_device, mesh=mesh, in_specs=placed, out_specs=(cells, cells), check_vma=False
    )
```

```python
import functools

import jax
import jax.numpy as jnp
from jax import lax
from jax.experimental import pallas as pl
from jax.experimental.pallas import tpu as pltpu
from jax.sharding import PartitionSpec as P

PEERS = ("rows", "feat")
BLK = 128
QUAD = 4
F32 = jnp.float32
BF16 = jnp.bfloat16
ANY = pl.BlockSpec(memory_space=pl.ANY)
HBM = pl.BlockSpec(memory_space=pltpu.HBM)
SMEM = pl.BlockSpec(memory_space=pltpu.SMEM)
VMEM = pl.BlockSpec(memory_space=pltpu.VMEM)
PARAMS = pltpu.CompilerParams(vmem_limit_bytes=20 * 1024 * 1024)
SMALL = pltpu.CompilerParams(vmem_limit_bytes=4 * 1024 * 1024)
TINY = pl.CostEstimate(flops=0, bytes_accessed=128, transcendentals=0)


def first_kernel(peers, cap, lead, dest, tiles, out, source, fill, sem):
    count = dest.shape[0]
    half = out.shape[1]
    me = lax.axis_index(PEERS)
    first = pl.multiple_of(lax.axis_index("sub") * half, half)
    for to in range(min(peers, 16)):
        fill[to] = 0
    if peers > 16:

        def clear(i, _):
            fill[i] = 0
            return 0

        lax.fori_loop(16, peers, clear, 0)
    for t in range(count):
        to = dest[t]
        at = fill[to]
        fill[to] = at + 1
        source[to * cap + at] = t
    if lead is None:
        return
    to = lax.rem(me + lead, peers)

    def send(j, _):
        t = source[to * cap + j]
        pltpu.make_async_copy(tiles.at[t, pl.ds(first, half)], out.at[j], sem.at[j]).start()
        return 0

    def finish(j, _):
        pltpu.make_async_copy(tiles.at[0, pl.ds(first, half)], out.at[0], sem.at[j]).wait()
        return 0

    lax.fori_loop(0, fill[to], send, 0)
    lax.fori_loop(0, fill[to], finish, 0)


def rest_kernel(peers, cap, order, source, fill, tiles, *refs):
    outs, sems = refs[:-1], refs[-1]
    half = outs[0].shape[1]
    me = lax.axis_index(PEERS)
    first = pl.multiple_of(lax.axis_index("sub") * half, half)
    begun = []
    for n, k in enumerate(order):
        to = lax.rem(me + k, peers)

        def send(j, _, n=n, to=to):
            t = source[to * cap + j]
            pltpu.make_async_copy(
                tiles.at[t, pl.ds(first, half)], outs[n].at[j], sems.at[n, j]
            ).start()
            return 0

        lax.fori_loop(0, fill[to], send, 0)
        begun.append(fill[to])
    for n, amount in enumerate(begun):

        def finish(j, _, n=n):
            pltpu.make_async_copy(
                tiles.at[0, pl.ds(first, half)], outs[n].at[0], sems.at[n, j]
            ).wait()
            return 0

        lax.fori_loop(0, amount, finish, 0)


def sorted_kernel(peers, cap, source, fill, tiles, out, sems):
    half = out.shape[1]
    first = pl.multiple_of(lax.axis_index("sub") * half, half)

    def each(act):
        def peer(to, _):
            def slot(j, _):
                at = to * cap + j
                act(source[at], at)
                return 0

            return lax.fori_loop(0, fill[to], slot, 0)

        lax.fori_loop(0, peers, peer, 0)

    def copy(t, at):
        return pltpu.make_async_copy(tiles.at[t, pl.ds(first, half)], out.at[at], sems.at[t])

    each(lambda t, at: copy(t, at).start())
    each(lambda t, at: copy(t, at).wait())


def label_kernel(peers, cap, source, fill, row, off, after, codes):
    def peer(to, _):
        def slot(j, _):
            t = source[to * cap + j]
            codes[to * (cap + 1) + j] = row[t] * 32 + off[t] + 8
            return 0

        lax.fori_loop(0, fill[to], slot, 0)
        codes[to * (cap + 1) + cap] = fill[to]
        return 0

    lax.fori_loop(0, peers, peer, 0)


def turn_kernel(nblk, h, base_one, base_two, old, after, bases, halves, sems):
    half = bases.shape[1]
    other = pl.ds(pl.multiple_of((1 - lax.axis_index("sub")) * half, half), half)
    copies = [
        pltpu.make_async_copy(base_one.at[:, other], bases.at[pl.ds(0, nblk)], sems.at[0]),
        pltpu.make_async_copy(base_two.at[:, other], bases.at[pl.ds(nblk, nblk)], sems.at[1]),
        pltpu.make_async_copy(h.at[:, pl.ds(0, half)], halves.at[pl.ds(0, nblk)], sems.at[2]),
        pltpu.make_async_copy(
            h.at[:, pl.ds(half, half)], halves.at[pl.ds(nblk, nblk)], sems.at[3]
        ),
        pltpu.make_async_copy(old.at[:, other], halves.at[pl.ds(2 * nblk, nblk)], sems.at[4]),
    ]
    for copy in copies:
        copy.start()
    for copy in copies:
        copy.wait()


def plan_kernel(peers, late, nblk, codes, by_row, row_at, by_side, side_at, fill_row, fill_side):
    cap = codes.shape[0] // peers - 1
    nothing = peers * cap * 32 + nblk
    me = lax.axis_index(PEERS)
    for fill in (fill_row, fill_side):
        for g in range(fill.shape[0]):
            fill[g] = 0

    def walk(act):
        def peer(origin, _):
            behind = jnp.int32(0)
            step = lax.rem(me + peers - origin, peers)
            for k in late:
                behind = behind + jnp.where(step == k, nblk, 0)

            def slot(j, _):
                code = codes[origin * (cap + 1) + j]
                row = code >> 5
                col = row + (code & 31)
                side = jnp.where(col < nblk, nblk, jnp.where(col < 2 * nblk, 0, 2 * nblk))
                act(row + behind, row + side, (row << 16) + (origin * cap + j) * 32 + col)
                return 0

            return lax.fori_loop(0, codes[origin * (cap + 1) + cap], slot, 0)

        lax.fori_loop(0, peers, peer, 0)

    def tally(row, side, entry):
        fill_row[row] = fill_row[row] + 1
        fill_side[side] = fill_side[side] + 1

    def place(row, side, entry):
        to = fill_row[row]
        by_row[to] = entry
        fill_row[row] = to + 1
        to = fill_side[side]
        by_side[to] = entry
        fill_side[side] = to + 1

    walk(tally)
    for fill, at, listed in ((fill_row, row_at, by_row), (fill_side, side_at, by_side)):
        now = jnp.int32(0)
        for g in range(fill.shape[0]):
            at[g] = now
            need = (fill[g] + QUAD - 1) // QUAD
            fill[g] = now * QUAD
            now = now + need
            last = jnp.maximum(now * QUAD - QUAD, 0)
            for u in range(QUAD):
                listed[last + u] = nothing + ((g % nblk) << 16)
        at[fill.shape[0]] = now
    walk(place)


def tile_copies(cap, steps, arrived, tiles, sems):
    if steps is None:
        whole = tiles.at[pl.ds(0, arrived[0].shape[0])]
        return [pltpu.make_async_copy(arrived[0], whole, sems.at[0])]
    me = lax.axis_index(PEERS)
    peers = lax.axis_size(PEERS)
    copies = []
    for n, (k, ref) in enumerate(zip(steps, arrived)):
        origin = lax.rem(me + peers - k, peers)
        copies.append(pltpu.make_async_copy(ref, tiles.at[pl.ds(origin * cap, cap)], sems.at[n]))
    return copies


def tile_sums(order, begin, end, tiles, cells, total):
    nothing = (tiles.shape[0] - 1) * 32 + cells.shape[0] // 3

    def step(n, _):
        for q in (begin + 2 * n, begin + 2 * n + 1):
            entry = [jnp.where(q < end, order[q * QUAD + u], nothing) for u in range(QUAD)]
            row = entry[0] >> 16
            tile = [(e >> 5) & 2047 for e in entry]
            cell = [e & 31 for e in entry]
            acc = None
            for u in range(0, QUAD, 2):
                weights = jnp.concatenate([tiles[tile[u]], tiles[tile[u + 1]]], axis=1)
                chosen = jnp.concatenate([cells[cell[u]], cells[cell[u + 1]]], axis=0)
                part = jnp.dot(weights, chosen, preferred_element_type=F32)
                acc = part if acc is None else acc + part
            total[row] = total[row] + acc
        return 0

    lax.fori_loop(0, (end - begin + 1) >> 1, step, 0)


def early_kernel(cap, steps, pieces, nblk, order, at, *refs):
    arrived = refs[:pieces]
    (left, left_twin, h, halves, right, right_twin, base_one, base_two, bases, old) = refs[
        pieces : pieces + 10
    ]
    w_self, bias, agg, cells, own, base_rows, old_rows, tiles, sems = refs[pieces + 10 :]
    sub = lax.axis_index("sub")
    half = agg.shape[1]
    width = h.shape[2]
    lanes = pl.ds(pl.multiple_of(sub * width, width), width)
    others = pl.ds(pl.multiple_of((1 - sub) * width, width), width)
    lines = pl.ds(pl.multiple_of(sub * half, half), half)
    block = [pl.ds(k * nblk, nblk) for k in range(3)]
    low, high = pl.ds(0, half), pl.ds(half, half)
    moves = [
        (left, cells.at[block[0], :, lanes]),
        (left_twin, cells.at[block[0], :, others]),
        (h, cells.at[block[1], :, lanes]),
        (halves.at[block[0]], cells.at[block[1], low, others]),
        (halves.at[block[1]], cells.at[block[1], high, others]),
        (right, cells.at[block[2], :, lanes]),
        (right_twin, cells.at[block[2], :, others]),
        (base_one.at[:, lines], agg.at[:, :, lanes]),
        (bases.at[block[0]], agg.at[:, :, others]),
        (base_two.at[:, lines], base_rows.at[:, :, lanes]),
        (bases.at[block[1]], base_rows.at[:, :, others]),
        (old.at[:, lines], old_rows.at[:, :, lanes]),
        (halves.at[block[2]], old_rows.at[:, :, others]),
    ]
    copies = tile_copies(cap, steps, arrived, tiles, sems)
    for k, (src, dst) in enumerate(moves):
        copies.append(pltpu.make_async_copy(src, dst, sems.at[pieces + k]))
    for copy in copies:
        copy.start()
    tiles[tiles.shape[0] - 1] = jnp.zeros(tiles.shape[1:], tiles.dtype)
    for copy in copies:
        copy.wait()
    tile_sums(order, at[0], at[nblk], tiles, cells, agg)
    for r in range(nblk):
        own[r] = (
            jnp.dot(cells[nblk + r, lines], w_self[...], preferred_element_type=F32) + bias[...]
        )


def column(inv, r, sub, half):
    shape = (half, inv.shape[1])
    line = lax.broadcasted_iota(jnp.int32, shape, 0) + sub * half
    lane = lax.broadcasted_iota(jnp.int32, shape, 1)
    spread = jnp.broadcast_to(inv[r : r + 1, :], shape)
    return jnp.sum(jnp.where(line == lane, spread, 0.0), axis=1, keepdims=True)


def late_kernel(cap, steps, pieces, nblk, order, at, affected, *refs):
    arrived = refs[:pieces]
    cells, agg, inv, own, w_neigh, old, out, tiles, total, means, sems = refs[pieces:]
    half = agg.shape[1]
    sub = lax.axis_index("sub")
    copies = tile_copies(cap, steps, arrived, tiles, sems) if pieces else []
    for copy in copies:
        copy.start()
    tiles[tiles.shape[0] - 1] = jnp.zeros(tiles.shape[1:], tiles.dtype)
    for r in range(nblk):
        total[r] = agg[r]
    for copy in copies:
        copy.wait()
    tile_sums(order, at[nblk], at[2 * nblk], tiles, cells, total)
    for r in range(nblk):
        means[r] = (total[r] * column(inv, r, sub, half)).astype(BF16)
    for r in range(nblk):
        pre = own[r] + jnp.dot(means[r], w_neigh[...], preferred_element_type=F32)
        pre = jnp.maximum(pre, 0.0)
        keep = jnp.full((half, 1), affected[r], jnp.int32) > 0
        out[r] = jnp.where(keep, pre, old[r].astype(F32)).astype(BF16)


def near_kernel(cap, steps, pieces, nblk, order, at, *refs):
    arrived = refs[:pieces]
    mine, twin, base, w_self, bias, agg, own, hidden, tiles, cells, sems = refs[pieces:]
    half = base.shape[1]
    width = hidden.shape[2]
    sub = lax.axis_index("sub")
    lanes = pl.ds(pl.multiple_of(sub * width, width), width)
    copies = tile_copies(cap, steps, arrived, tiles, sems)
    for k, (ref, side) in enumerate(((mine, sub), (twin, 1 - sub))):
        lines = pl.ds(pl.multiple_of(side * half, half), half)
        to = cells.at[pl.ds(nblk, nblk), lines]
        copies.append(pltpu.make_async_copy(ref, to, sems.at[pieces + k]))
        to = hidden.at[:, lines]
        copies.append(pltpu.make_async_copy(ref.at[:, :, lanes], to, sems.at[pieces + 2 + k]))
    for copy in copies:
        copy.start()
    tiles[tiles.shape[0] - 1] = jnp.zeros(tiles.shape[1:], tiles.dtype)
    for r in range(nblk):
        agg[r] = base[r]
    for copy in copies:
        copy.wait()
    tile_sums(order, at[0], at[nblk], tiles, cells, agg)
    mine_rows = pl.ds(pl.multiple_of(sub * half, half), half)
    for r in range(nblk):
        own[r] = (
            jnp.dot(cells[nblk + r, mine_rows], w_self[...], preferred_element_type=F32) + bias[...]
        )


def far_kernel(nblk, order, at, tiles, left, left_twin, right, right_twin, *refs):
    agg, inv, own, w_neigh, keep, send, cells, total, means, sems = refs
    half = agg.shape[1]
    width = keep.shape[2]
    sub = lax.axis_index("sub")
    sides = ((left, 0, sub), (left_twin, 0, 1 - sub), (right, 2, sub), (right_twin, 2, 1 - sub))
    copies = []
    for k, (ref, third, side) in enumerate(sides):
        lines = pl.ds(pl.multiple_of(side * half, half), half)
        to = cells.at[pl.ds(third * nblk, nblk), lines]
        copies.append(pltpu.make_async_copy(ref, to, sems.at[k]))
    for copy in copies:
        copy.start()
    cells[nblk] = jnp.zeros(cells.shape[1:], cells.dtype)
    for r in range(nblk):
        total[r] = agg[r]
    for copy in copies:
        copy.wait()
    tile_sums(order, at[nblk], at[3 * nblk], tiles, cells, total)
    for r in range(nblk):
        means[r] = (total[r] * column(inv, r, sub, half)).astype(BF16)
    for r in range(nblk):
        pre = own[r] + jnp.dot(means[r], w_neigh[...], preferred_element_type=F32)
        low = pre[:, :width]
        high = pre[:, width:]
        first = jnp.full((half, 1), sub, jnp.int32) == 0
        keep[r] = jnp.where(first, low, high).astype(BF16)
        send[r] = jnp.where(first, high, low).astype(BF16)


def finish_kernel(nblk, affected, kept, came, old, out):
    half = kept.shape[1]
    first = jnp.full((half, 1), lax.axis_index("sub"), jnp.int32) == 0
    for r in range(nblk):
        keep = jnp.full((half, 1), affected[r], jnp.int32) > 0
        low = jnp.where(first, kept[r].astype(F32), came[r].astype(F32))
        high = jnp.where(first, came[r].astype(F32), kept[r].astype(F32))
        out[r, :half] = jnp.where(keep, low, old[r, :half].astype(F32)).astype(BF16)
        out[r, half:] = jnp.where(keep, high, old[r, half:].astype(F32)).astype(BF16)


def swap(x):
    return lax.ppermute(x, "sub", [(0, 1), (1, 0)])


def ring(x, step):
    peers = lax.axis_size(PEERS)
    return lax.ppermute(x, PEERS, [(i, (i + step) % peers) for i in range(peers)])


def on_device(
    h_input,
    inv_degree,
    dest_block,
    row_block,
    block_offset,
    new_tiles,
    base_one,
    affected_one,
    old_one,
    self_one,
    neigh_one,
    bias_one,
    base_two,
    affected_two,
    old_two,
    self_two,
    neigh_two,
    bias_two,
):
    peers = lax.axis_size(PEERS)
    count = dest_block.shape[0]
    cap = max(2, 2 * count // peers)
    slots = peers * cap
    rows_here, width = h_input.shape
    full = width * lax.axis_size("sub")
    nblk = rows_here // BLK
    half = BLK // lax.axis_size("sub")
    direct = 2 < peers <= 16
    shape = jax.ShapeDtypeStruct
    after = lax.optimization_barrier

    order = sorted(range(1, peers), key=lambda k: (abs(k - peers // 2), k))
    lead = order[0] if direct else None
    piece = shape((cap, half, BLK), BF16)
    out_piece, source, fill = pl.pallas_call(
        functools.partial(first_kernel, peers, cap, lead),
        out_shape=[piece, shape((slots,), jnp.int32), shape((peers,), jnp.int32)],
        in_specs=[SMEM, HBM],
        out_specs=[VMEM, SMEM, SMEM],
        scratch_shapes=[pltpu.SemaphoreType.DMA((cap,))],
        cost_estimate=TINY,
        name="first",
    )(dest_block.reshape(count), new_tiles)

    if direct:
        others = order[1:] + [0]
        packed = pl.pallas_call(
            functools.partial(rest_kernel, peers, cap, others),
            out_shape=[piece] * len(others),
            in_specs=[SMEM, SMEM, HBM],
            out_specs=[VMEM] * len(others),
            scratch_shapes=[pltpu.SemaphoreType.DMA((len(others), cap))],
            cost_estimate=TINY,
            name="rest",
        )(source, fill, new_tiles)
        steps = order + [0]
        got = dict(zip(others, packed))
        got[lead] = out_piece
        got = {k: ring(got[k], k) if k else got[k] for k in steps}
        late = tuple(order[4:]) if peers > 4 else ()
        early = [k for k in steps if k not in late]
        arrived = [got[k] for k in steps]
        arrived_early = [got[k] for k in early]
        arrived_late = [got[k] for k in late]
        flag = got[lead]
        gathered = packed[-1]
    else:
        sent = pl.pallas_call(
            functools.partial(sorted_kernel, peers, cap),
            out_shape=shape((slots, half, BLK), BF16),
            in_specs=[SMEM, SMEM, HBM],
            out_specs=HBM,
            scratch_shapes=[pltpu.SemaphoreType.DMA((count,))],
            cost_estimate=TINY,
            name="rest",
        )(source, fill, new_tiles)
        sent = sent.reshape(peers, cap, half, BLK)
        got = lax.all_to_all(sent, PEERS, split_axis=0, concat_axis=0, tiled=True)
        arrived = [got.reshape(slots, half, BLK)]
        steps = early = None
        late = ()
        arrived_early, arrived_late = arrived, []
        flag = source
        gathered = out_piece

    codes = pl.pallas_call(
        functools.partial(label_kernel, peers, cap),
        out_shape=shape((peers * (cap + 1),), jnp.int32),
        in_specs=[SMEM] * 4 + [ANY],
        out_specs=SMEM,
        compiler_params=SMALL,
        cost_estimate=TINY,
        name="label",
    )(source, fill, row_block, block_offset, gathered)
    got_codes = lax.all_to_all(
        codes.reshape(peers, cap + 1), PEERS, split_axis=0, concat_axis=0, tiled=True
    ).reshape(peers * (cap + 1))

    sizes = (2 * nblk, 3 * nblk)
    counts = [pltpu.SMEM((size,), jnp.int32) for size in sizes]
    lists = []
    for size in sizes:
        lists += [shape((slots + size * QUAD,), jnp.int32), shape((size + 1,), jnp.int32)]
    by_row, row_at, by_side, side_at = pl.pallas_call(
        functools.partial(plan_kernel, peers, late, nblk),
        out_shape=lists,
        in_specs=[SMEM],
        out_specs=[SMEM] * 4,
        scratch_shapes=counts,
        compiler_params=SMALL,
        cost_estimate=TINY,
        name="plan",
    )(got_codes)

    blocks = (nblk, BLK, width)
    h_blocks, old_blocks = h_input.reshape(blocks), old_one.reshape(blocks)
    base_one, base_two = base_one.reshape(blocks), base_two.reshape(blocks)
    bases, halves = pl.pallas_call(
        functools.partial(turn_kernel, nblk),
        out_shape=[shape((2 * nblk, half, width), F32), shape((3 * nblk, half, width), BF16)],
        in_specs=[ANY] * 5,
        out_specs=[ANY] * 2,
        scratch_shapes=[pltpu.SemaphoreType.DMA((5,))],
        compiler_params=SMALL,
        cost_estimate=TINY,
        name="turn",
    )(h_blocks, base_one, base_two, old_blocks, gathered)
    bases, halves, _ = after((bases, halves, flag))
    bases, halves = swap(bases), swap(halves)
    h_later, _, by_row, by_side = after((h_blocks, flag, by_row, by_side))
    left, right = ring(h_later, 1), ring(h_later, peers - 1)
    left, right, _ = after((left, right, tuple(arrived_early[1:4])))
    left_twin, right_twin = swap(left), swap(right)

    tile_scratch = pltpu.VMEM((slots + 1, half, BLK), BF16)
    cell_shape = (3 * nblk, BLK, full)
    cell_scratch = pltpu.VMEM(cell_shape, BF16)
    mean_scratch = pltpu.VMEM((nblk, half, full), BF16)
    rows_shape = (nblk, half, full)
    total_scratch = pltpu.VMEM(rows_shape, F32)
    inv = inv_degree.reshape(nblk, BLK)

    many = len(arrived_early)
    agg_early, cells_one, own_one, base_two_rows, old_one_rows = pl.pallas_call(
        functools.partial(early_kernel, cap, early, many, nblk),
        out_shape=[
            shape(rows_shape, F32),
            shape(cell_shape, BF16),
            shape(rows_shape, F32),
            shape(rows_shape, F32),
            shape(rows_shape, BF16),
        ],
        in_specs=[SMEM] * 2 + [ANY] * (many + 10) + [VMEM] * 2,
        out_specs=[VMEM] * 5,
        scratch_shapes=[tile_scratch, pltpu.SemaphoreType.DMA((many + 13,))],
        compiler_params=PARAMS,
        cost_estimate=TINY,
        name="early",
    )(
        by_row,
        row_at,
        *arrived_early,
        left,
        left_twin,
        h_blocks,
        halves,
        right,
        right_twin,
        base_one,
        base_two,
        bases,
        old_blocks,
        self_one,
        bias_one.reshape(1, full),
    )

    many = len(arrived_late)
    hidden_rows = pl.pallas_call(
        functools.partial(late_kernel, cap, late, many, nblk),
        out_shape=shape(rows_shape, BF16),
        in_specs=[SMEM] * 3 + [ANY] * many + [VMEM] * 6,
        out_specs=VMEM,
        scratch_shapes=[
            tile_scratch,
            total_scratch,
            mean_scratch,
            pltpu.SemaphoreType.DMA((max(1, many),)),
        ],
        compiler_params=PARAMS,
        cost_estimate=TINY,
        name="late",
    )(
        by_row,
        row_at,
        affected_one,
        *arrived_late,
        cells_one,
        agg_early,
        inv,
        own_one,
        neigh_one,
        old_one_rows,
    )

    hidden_twin = swap(hidden_rows)
    left = ring(hidden_rows, 1)
    right = ring(hidden_rows, peers - 1)

    many = len(arrived)
    agg_two, own_two, hidden_one, tiles_all = pl.pallas_call(
        functools.partial(near_kernel, cap, steps, many, nblk),
        out_shape=[shape(rows_shape, F32)] * 2
        + [shape(blocks, BF16), shape((slots + 1, half, BLK), BF16)],
        in_specs=[SMEM] * 2 + [ANY] * (many + 2) + [VMEM] * 3,
        out_specs=[VMEM] * 2 + [ANY, VMEM],
        scratch_shapes=[cell_scratch, pltpu.SemaphoreType.DMA((many + 4,))],
        compiler_params=PARAMS,
        cost_estimate=TINY,
        name="near",
    )(
        by_side,
        side_at,
        *arrived,
        hidden_rows,
        hidden_twin,
        base_two_rows,
        self_two,
        bias_two.reshape(1, full),
    )

    left, right, agg_two, own_two = after((left, right, agg_two, own_two))
    left_twin = swap(left)
    right_twin = swap(right)
    kept, sent = pl.pallas_call(
        functools.partial(far_kernel, nblk),
        out_shape=[shape((nblk, half, width), BF16)] * 2,
        in_specs=[SMEM] * 2 + [VMEM] + [ANY] * 4 + [VMEM] * 4,
        out_specs=[VMEM] * 2,
        scratch_shapes=[
            cell_scratch,
            total_scratch,
            mean_scratch,
            pltpu.SemaphoreType.DMA((4,)),
        ],
        compiler_params=PARAMS,
        cost_estimate=TINY,
        name="far",
    )(
        by_side,
        side_at,
        tiles_all,
        left,
        left_twin,
        right,
        right_twin,
        agg_two,
        inv,
        own_two,
        neigh_two,
    )
    came = swap(sent)
    hidden_two = pl.pallas_call(
        functools.partial(finish_kernel, nblk),
        out_shape=shape(blocks, BF16),
        in_specs=[SMEM] + [VMEM] * 3,
        out_specs=VMEM,
        compiler_params=SMALL,
        cost_estimate=TINY,
        name="finish",
    )(affected_two, kept, came, old_two.reshape(blocks))
    return (hidden_one.reshape(rows_here, width), hidden_two.reshape(rows_here, width))


def solution(mesh):
    rows = P(("groups", "rows", "feat"))
    cells = P(("groups", "rows", "feat"), "sub")
    placed = (
        cells,
        rows,
        P(("groups", "rows", "feat"), None),
        rows,
        rows,
        P(("groups", "rows", "feat"), None, None),
        cells,
        rows,
        cells,
        P(),
        P(),
        P(),
        cells,
        rows,
        cells,
        P(),
        P(),
        P(),
    )
    return jax.shard_map(
        on_device, mesh=mesh, in_specs=placed, out_specs=(cells, cells), check_vma=False
    )
```

```python
import functools

import jax
import jax.numpy as jnp
from jax import lax
from jax.experimental import pallas as pl
from jax.experimental.pallas import tpu as pltpu
from jax.sharding import PartitionSpec as P

PEERS = ("rows", "feat")
BLK = 128
QUAD = 4
F32 = jnp.float32
BF16 = jnp.bfloat16
ANY = pl.BlockSpec(memory_space=pl.ANY)
HBM = pl.BlockSpec(memory_space=pltpu.HBM)
SMEM = pl.BlockSpec(memory_space=pltpu.SMEM)
VMEM = pl.BlockSpec(memory_space=pltpu.VMEM)
PARAMS = pltpu.CompilerParams(vmem_limit_bytes=20 * 1024 * 1024)
SMALL = pltpu.CompilerParams(vmem_limit_bytes=4 * 1024 * 1024)
TINY = pl.CostEstimate(flops=0, bytes_accessed=128, transcendentals=0)


def first_kernel(peers, cap, lead, dest, tiles, out, source, fill, sem):
    count = dest.shape[0]
    half = out.shape[1]
    me = lax.axis_index(PEERS)
    first = pl.multiple_of(lax.axis_index("sub") * half, half)
    for to in range(min(peers, 16)):
        fill[to] = 0
    if peers > 16:

        def clear(i, _):
            fill[i] = 0
            return 0

        lax.fori_loop(16, peers, clear, 0)
    for t in range(count):
        to = dest[t]
        at = fill[to]
        fill[to] = at + 1
        source[to * cap + at] = t
    if lead is None:
        return
    to = lax.rem(me + lead, peers)

    def send(j, _):
        t = source[to * cap + j]
        pltpu.make_async_copy(tiles.at[t, pl.ds(first, half)], out.at[j], sem.at[j]).start()
        return 0

    def finish(j, _):
        pltpu.make_async_copy(tiles.at[0, pl.ds(first, half)], out.at[0], sem.at[j]).wait()
        return 0

    lax.fori_loop(0, fill[to], send, 0)
    lax.fori_loop(0, fill[to], finish, 0)


def rest_kernel(peers, cap, order, source, fill, tiles, *refs):
    outs, sems = refs[:-1], refs[-1]
    half = outs[0].shape[1]
    me = lax.axis_index(PEERS)
    first = pl.multiple_of(lax.axis_index("sub") * half, half)
    begun = []
    for n, k in enumerate(order):
        to = lax.rem(me + k, peers)

        def send(j, _, n=n, to=to):
            t = source[to * cap + j]
            pltpu.make_async_copy(
                tiles.at[t, pl.ds(first, half)], outs[n].at[j], sems.at[n, j]
            ).start()
            return 0

        lax.fori_loop(0, fill[to], send, 0)
        begun.append(fill[to])
    for n, amount in enumerate(begun):

        def finish(j, _, n=n):
            pltpu.make_async_copy(
                tiles.at[0, pl.ds(first, half)], outs[n].at[0], sems.at[n, j]
            ).wait()
            return 0

        lax.fori_loop(0, amount, finish, 0)


def sorted_kernel(peers, cap, source, fill, tiles, out, sems):
    half = out.shape[1]
    first = pl.multiple_of(lax.axis_index("sub") * half, half)

    def each(act):
        def peer(to, _):
            def slot(j, _):
                at = to * cap + j
                act(source[at], at)
                return 0

            return lax.fori_loop(0, fill[to], slot, 0)

        lax.fori_loop(0, peers, peer, 0)

    def copy(t, at):
        return pltpu.make_async_copy(tiles.at[t, pl.ds(first, half)], out.at[at], sems.at[t])

    each(lambda t, at: copy(t, at).start())
    each(lambda t, at: copy(t, at).wait())


def label_kernel(peers, cap, source, fill, row, off, after, codes):
    def peer(to, _):
        def slot(j, _):
            t = source[to * cap + j]
            codes[to * (cap + 1) + j] = row[t] * 32 + off[t] + 8
            return 0

        lax.fori_loop(0, fill[to], slot, 0)
        codes[to * (cap + 1) + cap] = fill[to]
        return 0

    lax.fori_loop(0, peers, peer, 0)


def turn_kernel(nblk, h, base_one, base_two, old, after, bases, halves, sems):
    half = bases.shape[1]
    other = pl.ds(pl.multiple_of((1 - lax.axis_index("sub")) * half, half), half)
    copies = [
        pltpu.make_async_copy(base_one.at[:, other], bases.at[pl.ds(0, nblk)], sems.at[0]),
        pltpu.make_async_copy(base_two.at[:, other], bases.at[pl.ds(nblk, nblk)], sems.at[1]),
        pltpu.make_async_copy(h.at[:, pl.ds(0, half)], halves.at[pl.ds(0, nblk)], sems.at[2]),
        pltpu.make_async_copy(
            h.at[:, pl.ds(half, half)], halves.at[pl.ds(nblk, nblk)], sems.at[3]
        ),
        pltpu.make_async_copy(old.at[:, other], halves.at[pl.ds(2 * nblk, nblk)], sems.at[4]),
    ]
    for copy in copies:
        copy.start()
    for copy in copies:
        copy.wait()


def plan_kernel(peers, late, nblk, codes, by_row, row_at, by_side, side_at, fill_row, fill_side):
    cap = codes.shape[0] // peers - 1
    nothing = peers * cap * 32 + nblk
    me = lax.axis_index(PEERS)
    for fill in (fill_row, fill_side):
        for g in range(fill.shape[0]):
            fill[g] = 0

    def walk(act):
        def peer(origin, _):
            behind = jnp.int32(0)
            step = lax.rem(me + peers - origin, peers)
            for k in late:
                behind = behind + jnp.where(step == k, nblk, 0)

            def slot(j, _):
                code = codes[origin * (cap + 1) + j]
                row = code >> 5
                col = row + (code & 31)
                side = jnp.where(col < nblk, nblk, jnp.where(col < 2 * nblk, 0, 2 * nblk))
                act(row + behind, row + side, (row << 16) + (origin * cap + j) * 32 + col)
                return 0

            return lax.fori_loop(0, codes[origin * (cap + 1) + cap], slot, 0)

        lax.fori_loop(0, peers, peer, 0)

    def tally(row, side, entry):
        fill_row[row] = fill_row[row] + 1
        fill_side[side] = fill_side[side] + 1

    def place(row, side, entry):
        to = fill_row[row]
        by_row[to] = entry
        fill_row[row] = to + 1
        to = fill_side[side]
        by_side[to] = entry
        fill_side[side] = to + 1

    walk(tally)
    for fill, at, listed in ((fill_row, row_at, by_row), (fill_side, side_at, by_side)):
        now = jnp.int32(0)
        for g in range(fill.shape[0]):
            at[g] = now
            need = (fill[g] + QUAD - 1) // QUAD
            fill[g] = now * QUAD
            now = now + need
            last = jnp.maximum(now * QUAD - QUAD, 0)
            for u in range(QUAD):
                listed[last + u] = nothing + ((g % nblk) << 16)
        at[fill.shape[0]] = now
    walk(place)


def tile_copies(cap, steps, arrived, tiles, sems):
    if steps is None:
        whole = tiles.at[pl.ds(0, arrived[0].shape[0])]
        return [pltpu.make_async_copy(arrived[0], whole, sems.at[0])]
    me = lax.axis_index(PEERS)
    peers = lax.axis_size(PEERS)
    copies = []
    for n, (k, ref) in enumerate(zip(steps, arrived)):
        origin = lax.rem(me + peers - k, peers)
        copies.append(pltpu.make_async_copy(ref, tiles.at[pl.ds(origin * cap, cap)], sems.at[n]))
    return copies


def tile_sums(order, begin, end, tiles, cells, total):
    nothing = (tiles.shape[0] - 1) * 32 + cells.shape[0] // 3

    def step(n, _):
        for q in (begin + 2 * n, begin + 2 * n + 1):
            entry = [jnp.where(q < end, order[q * QUAD + u], nothing) for u in range(QUAD)]
            row = entry[0] >> 16
            tile = [(e >> 5) & 2047 for e in entry]
            cell = [e & 31 for e in entry]
            acc = None
            for u in range(0, QUAD, 2):
                weights = jnp.concatenate([tiles[tile[u]], tiles[tile[u + 1]]], axis=1)
                chosen = jnp.concatenate([cells[cell[u]], cells[cell[u + 1]]], axis=0)
                part = jnp.dot(weights, chosen, preferred_element_type=F32)
                acc = part if acc is None else acc + part
            total[row] = total[row] + acc
        return 0

    lax.fori_loop(0, (end - begin + 1) >> 1, step, 0)


def early_kernel(cap, steps, pieces, nblk, order, at, *refs):
    arrived = refs[:pieces]
    (left, left_twin, h, halves, right, right_twin, base_one, base_two, bases, old) = refs[
        pieces : pieces + 10
    ]
    w_self, bias, agg, cells, own, base_rows, old_rows, tiles, sems = refs[pieces + 10 :]
    sub = lax.axis_index("sub")
    half = agg.shape[1]
    width = h.shape[2]
    lanes = pl.ds(pl.multiple_of(sub * width, width), width)
    others = pl.ds(pl.multiple_of((1 - sub) * width, width), width)
    lines = pl.ds(pl.multiple_of(sub * half, half), half)
    block = [pl.ds(k * nblk, nblk) for k in range(3)]
    low, high = pl.ds(0, half), pl.ds(half, half)
    moves = [
        (left, cells.at[block[0], :, lanes]),
        (left_twin, cells.at[block[0], :, others]),
        (h, cells.at[block[1], :, lanes]),
        (halves.at[block[0]], cells.at[block[1], low, others]),
        (halves.at[block[1]], cells.at[block[1], high, others]),
        (right, cells.at[block[2], :, lanes]),
        (right_twin, cells.at[block[2], :, others]),
        (base_one.at[:, lines], agg.at[:, :, lanes]),
        (bases.at[block[0]], agg.at[:, :, others]),
        (base_two.at[:, lines], base_rows.at[:, :, lanes]),
        (bases.at[block[1]], base_rows.at[:, :, others]),
        (old.at[:, lines], old_rows.at[:, :, lanes]),
        (halves.at[block[2]], old_rows.at[:, :, others]),
    ]
    copies = tile_copies(cap, steps, arrived, tiles, sems)
    for k, (src, dst) in enumerate(moves):
        copies.append(pltpu.make_async_copy(src, dst, sems.at[pieces + k]))
    for copy in copies:
        copy.start()
    tiles[tiles.shape[0] - 1] = jnp.zeros(tiles.shape[1:], tiles.dtype)
    for copy in copies:
        copy.wait()
    tile_sums(order, at[0], at[nblk], tiles, cells, agg)
    for r in range(nblk):
        own[r] = (
            jnp.dot(cells[nblk + r, lines], w_self[...], preferred_element_type=F32) + bias[...]
        )


def column(inv, r, sub, half):
    shape = (half, inv.shape[1])
    line = lax.broadcasted_iota(jnp.int32, shape, 0) + sub * half
    lane = lax.broadcasted_iota(jnp.int32, shape, 1)
    spread = jnp.broadcast_to(inv[r : r + 1, :], shape)
    return jnp.sum(jnp.where(line == lane, spread, 0.0), axis=1, keepdims=True)


def late_kernel(cap, steps, pieces, nblk, order, at, affected, *refs):
    arrived = refs[:pieces]
    cells, agg, inv, own, w_neigh, old, out, tiles, total, means, sems = refs[pieces:]
    half = agg.shape[1]
    sub = lax.axis_index("sub")
    copies = tile_copies(cap, steps, arrived, tiles, sems) if pieces else []
    for copy in copies:
        copy.start()
    tiles[tiles.shape[0] - 1] = jnp.zeros(tiles.shape[1:], tiles.dtype)
    for r in range(nblk):
        total[r] = agg[r]
    for copy in copies:
        copy.wait()
    tile_sums(order, at[nblk], at[2 * nblk], tiles, cells, total)
    for r in range(nblk):
        means[r] = (total[r] * column(inv, r, sub, half)).astype(BF16)
    for r in range(nblk):
        pre = own[r] + jnp.dot(means[r], w_neigh[...], preferred_element_type=F32)
        pre = jnp.maximum(pre, 0.0)
        keep = jnp.full((half, 1), affected[r], jnp.int32) > 0
        out[r] = jnp.where(keep, pre, old[r].astype(F32)).astype(BF16)


def near_kernel(cap, steps, pieces, nblk, order, at, *refs):
    arrived = refs[:pieces]
    mine, twin, base, w_self, bias, agg, own, hidden, tiles, cells, sems = refs[pieces:]
    half = base.shape[1]
    width = hidden.shape[2]
    sub = lax.axis_index("sub")
    lanes = pl.ds(pl.multiple_of(sub * width, width), width)
    copies = tile_copies(cap, steps, arrived, tiles, sems)
    for k, (ref, side) in enumerate(((mine, sub), (twin, 1 - sub))):
        lines = pl.ds(pl.multiple_of(side * half, half), half)
        to = cells.at[pl.ds(nblk, nblk), lines]
        copies.append(pltpu.make_async_copy(ref, to, sems.at[pieces + k]))
        to = hidden.at[:, lines]
        copies.append(pltpu.make_async_copy(ref.at[:, :, lanes], to, sems.at[pieces + 2 + k]))
    for copy in copies:
        copy.start()
    tiles[tiles.shape[0] - 1] = jnp.zeros(tiles.shape[1:], tiles.dtype)
    for r in range(nblk):
        agg[r] = base[r]
    for copy in copies:
        copy.wait()
    tile_sums(order, at[0], at[nblk], tiles, cells, agg)
    mine_rows = pl.ds(pl.multiple_of(sub * half, half), half)
    for r in range(nblk):
        own[r] = (
            jnp.dot(cells[nblk + r, mine_rows], w_self[...], preferred_element_type=F32) + bias[...]
        )


def far_kernel(nblk, order, at, tiles, left, left_twin, right, right_twin, *refs):
    agg, inv, own, w_neigh, keep, send, cells, total, means, sems = refs
    half = agg.shape[1]
    width = keep.shape[2]
    sub = lax.axis_index("sub")
    sides = ((left, 0, sub), (left_twin, 0, 1 - sub), (right, 2, sub), (right_twin, 2, 1 - sub))
    copies = []
    for k, (ref, third, side) in enumerate(sides):
        lines = pl.ds(pl.multiple_of(side * half, half), half)
        to = cells.at[pl.ds(third * nblk, nblk), lines]
        copies.append(pltpu.make_async_copy(ref, to, sems.at[k]))
    for copy in copies:
        copy.start()
    cells[nblk] = jnp.zeros(cells.shape[1:], cells.dtype)
    for r in range(nblk):
        total[r] = agg[r]
    for copy in copies:
        copy.wait()
    tile_sums(order, at[nblk], at[3 * nblk], tiles, cells, total)
    for r in range(nblk):
        means[r] = (total[r] * column(inv, r, sub, half)).astype(BF16)
    for r in range(nblk):
        pre = own[r] + jnp.dot(means[r], w_neigh[...], preferred_element_type=F32)
        low = pre[:, :width]
        high = pre[:, width:]
        first = jnp.full((half, 1), sub, jnp.int32) == 0
        keep[r] = jnp.where(first, low, high).astype(BF16)
        send[r] = jnp.where(first, high, low).astype(BF16)


def finish_kernel(nblk, affected, kept, came, old, out):
    half = kept.shape[1]
    first = jnp.full((half, 1), lax.axis_index("sub"), jnp.int32) == 0
    for r in range(nblk):
        keep = jnp.full((half, 1), affected[r], jnp.int32) > 0
        low = jnp.where(first, kept[r].astype(F32), came[r].astype(F32))
        high = jnp.where(first, came[r].astype(F32), kept[r].astype(F32))
        out[r, :half] = jnp.where(keep, low, old[r, :half].astype(F32)).astype(BF16)
        out[r, half:] = jnp.where(keep, high, old[r, half:].astype(F32)).astype(BF16)


def swap(x):
    return lax.ppermute(x, "sub", [(0, 1), (1, 0)])


def ring(x, step):
    peers = lax.axis_size(PEERS)
    return lax.ppermute(x, PEERS, [(i, (i + step) % peers) for i in range(peers)])


def on_device(
    h_input,
    inv_degree,
    dest_block,
    row_block,
    block_offset,
    new_tiles,
    base_one,
    affected_one,
    old_one,
    self_one,
    neigh_one,
    bias_one,
    base_two,
    affected_two,
    old_two,
    self_two,
    neigh_two,
    bias_two,
):
    peers = lax.axis_size(PEERS)
    count = dest_block.shape[0]
    cap = max(2, 2 * count // peers)
    slots = peers * cap
    rows_here, width = h_input.shape
    full = width * lax.axis_size("sub")
    nblk = rows_here // BLK
    half = BLK // lax.axis_size("sub")
    direct = 2 < peers <= 16
    shape = jax.ShapeDtypeStruct
    after = lax.optimization_barrier
    blocks = (nblk, BLK, width)
    h_blocks = h_input.reshape(blocks)
    left, right = ring(h_blocks, 1), ring(h_blocks, peers - 1)

    order = sorted(range(1, peers), key=lambda k: (abs(k - peers // 2), k))
    lead = order[0] if direct else None
    piece = shape((cap, half, BLK), BF16)
    out_piece, source, fill = pl.pallas_call(
        functools.partial(first_kernel, peers, cap, lead),
        out_shape=[piece, shape((slots,), jnp.int32), shape((peers,), jnp.int32)],
        in_specs=[SMEM, HBM],
        out_specs=[VMEM, SMEM, SMEM],
        scratch_shapes=[pltpu.SemaphoreType.DMA((cap,))],
        cost_estimate=TINY,
        name="first",
    )(dest_block.reshape(count), new_tiles)

    if direct:
        others = order[1:] + [0]
        packed = pl.pallas_call(
            functools.partial(rest_kernel, peers, cap, others),
            out_shape=[piece] * len(others),
            in_specs=[SMEM, SMEM, HBM],
            out_specs=[VMEM] * len(others),
            scratch_shapes=[pltpu.SemaphoreType.DMA((len(others), cap))],
            cost_estimate=TINY,
            name="rest",
        )(source, fill, new_tiles)
        steps = order + [0]
        got = dict(zip(others, packed))
        got[lead] = out_piece
        got = {k: ring(got[k], k) if k else got[k] for k in steps}
        late = tuple(order[4:]) if peers > 4 else ()
        early = [k for k in steps if k not in late]
        arrived = [got[k] for k in steps]
        arrived_early = [got[k] for k in early]
        arrived_late = [got[k] for k in late]
        flag = got[lead]
        gathered = packed[-1]
    else:
        sent = pl.pallas_call(
            functools.partial(sorted_kernel, peers, cap),
            out_shape=shape((slots, half, BLK), BF16),
            in_specs=[SMEM, SMEM, HBM],
            out_specs=HBM,
            scratch_shapes=[pltpu.SemaphoreType.DMA((count,))],
            cost_estimate=TINY,
            name="rest",
        )(source, fill, new_tiles)
        sent = sent.reshape(peers, cap, half, BLK)
        got = lax.all_to_all(sent, PEERS, split_axis=0, concat_axis=0, tiled=True)
        arrived = [got.reshape(slots, half, BLK)]
        steps = early = None
        late = ()
        arrived_early, arrived_late = arrived, []
        flag = source
        gathered = out_piece

    codes = pl.pallas_call(
        functools.partial(label_kernel, peers, cap),
        out_shape=shape((peers * (cap + 1),), jnp.int32),
        in_specs=[SMEM] * 4 + [ANY],
        out_specs=SMEM,
        compiler_params=SMALL,
        cost_estimate=TINY,
        name="label",
    )(source, fill, row_block, block_offset, gathered)
    got_codes = lax.all_to_all(
        codes.reshape(peers, cap + 1), PEERS, split_axis=0, concat_axis=0, tiled=True
    ).reshape(peers * (cap + 1))

    left, right, codes_later = after((left, right, got_codes))
    sizes = (2 * nblk, 3 * nblk)
    counts = [pltpu.SMEM((size,), jnp.int32) for size in sizes]
    lists = []
    for size in sizes:
        lists += [shape((slots + size * QUAD,), jnp.int32), shape((size + 1,), jnp.int32)]
    by_row, row_at, by_side, side_at = pl.pallas_call(
        functools.partial(plan_kernel, peers, late, nblk),
        out_shape=lists,
        in_specs=[SMEM],
        out_specs=[SMEM] * 4,
        scratch_shapes=counts,
        compiler_params=SMALL,
        cost_estimate=TINY,
        name="plan",
    )(codes_later)

    old_blocks = old_one.reshape(blocks)
    base_one, base_two = base_one.reshape(blocks), base_two.reshape(blocks)
    bases, halves = pl.pallas_call(
        functools.partial(turn_kernel, nblk),
        out_shape=[shape((2 * nblk, half, width), F32), shape((3 * nblk, half, width), BF16)],
        in_specs=[ANY] * 5,
        out_specs=[ANY] * 2,
        scratch_shapes=[pltpu.SemaphoreType.DMA((5,))],
        compiler_params=SMALL,
        cost_estimate=TINY,
        name="turn",
    )(h_blocks, base_one, base_two, old_blocks, gathered)
    bases, halves, _ = after((bases, halves, flag))
    bases, halves = swap(bases), swap(halves)
    left, right, _ = after((left, right, flag))
    left_twin, right_twin = swap(left), swap(right)

    tile_scratch = pltpu.VMEM((slots + 1, half, BLK), BF16)
    cell_shape = (3 * nblk, BLK, full)
    cell_scratch = pltpu.VMEM(cell_shape, BF16)
    mean_scratch = pltpu.VMEM((nblk, half, full), BF16)
    rows_shape = (nblk, half, full)
    total_scratch = pltpu.VMEM(rows_shape, F32)
    inv = inv_degree.reshape(nblk, BLK)

    many = len(arrived_early)
    agg_early, cells_one, own_one, base_two_rows, old_one_rows = pl.pallas_call(
        functools.partial(early_kernel, cap, early, many, nblk),
        out_shape=[
            shape(rows_shape, F32),
            shape(cell_shape, BF16),
            shape(rows_shape, F32),
            shape(rows_shape, F32),
            shape(rows_shape, BF16),
        ],
        in_specs=[SMEM] * 2 + [ANY] * (many + 10) + [VMEM] * 2,
        out_specs=[VMEM] * 5,
        scratch_shapes=[tile_scratch, pltpu.SemaphoreType.DMA((many + 13,))],
        compiler_params=PARAMS,
        cost_estimate=TINY,
        name="early",
    )(
        by_row,
        row_at,
        *arrived_early,
        left,
        left_twin,
        h_blocks,
        halves,
        right,
        right_twin,
        base_one,
        base_two,
        bases,
        old_blocks,
        self_one,
        bias_one.reshape(1, full),
    )

    many = len(arrived_late)
    hidden_rows = pl.pallas_call(
        functools.partial(late_kernel, cap, late, many, nblk),
        out_shape=shape(rows_shape, BF16),
        in_specs=[SMEM] * 3 + [ANY] * many + [VMEM] * 6,
        out_specs=VMEM,
        scratch_shapes=[
            tile_scratch,
            total_scratch,
            mean_scratch,
            pltpu.SemaphoreType.DMA((max(1, many),)),
        ],
        compiler_params=PARAMS,
        cost_estimate=TINY,
        name="late",
    )(
        by_row,
        row_at,
        affected_one,
        *arrived_late,
        cells_one,
        agg_early,
        inv,
        own_one,
        neigh_one,
        old_one_rows,
    )

    hidden_twin = swap(hidden_rows)
    left = ring(hidden_rows, 1)
    right = ring(hidden_rows, peers - 1)

    many = len(arrived)
    agg_two, own_two, hidden_one, tiles_all = pl.pallas_call(
        functools.partial(near_kernel, cap, steps, many, nblk),
        out_shape=[shape(rows_shape, F32)] * 2
        + [shape(blocks, BF16), shape((slots + 1, half, BLK), BF16)],
        in_specs=[SMEM] * 2 + [ANY] * (many + 2) + [VMEM] * 3,
        out_specs=[VMEM] * 2 + [ANY, VMEM],
        scratch_shapes=[cell_scratch, pltpu.SemaphoreType.DMA((many + 4,))],
        compiler_params=PARAMS,
        cost_estimate=TINY,
        name="near",
    )(
        by_side,
        side_at,
        *arrived,
        hidden_rows,
        hidden_twin,
        base_two_rows,
        self_two,
        bias_two.reshape(1, full),
    )

    left, right, agg_two, own_two = after((left, right, agg_two, own_two))
    left_twin = swap(left)
    right_twin = swap(right)
    kept, sent = pl.pallas_call(
        functools.partial(far_kernel, nblk),
        out_shape=[shape((nblk, half, width), BF16)] * 2,
        in_specs=[SMEM] * 2 + [VMEM] + [ANY] * 4 + [VMEM] * 4,
        out_specs=[VMEM] * 2,
        scratch_shapes=[
            cell_scratch,
            total_scratch,
            mean_scratch,
            pltpu.SemaphoreType.DMA((4,)),
        ],
        compiler_params=PARAMS,
        cost_estimate=TINY,
        name="far",
    )(
        by_side,
        side_at,
        tiles_all,
        left,
        left_twin,
        right,
        right_twin,
        agg_two,
        inv,
        own_two,
        neigh_two,
    )
    came = swap(sent)
    hidden_two = pl.pallas_call(
        functools.partial(finish_kernel, nblk),
        out_shape=shape(blocks, BF16),
        in_specs=[SMEM] + [VMEM] * 3,
        out_specs=VMEM,
        compiler_params=SMALL,
        cost_estimate=TINY,
        name="finish",
    )(affected_two, kept, came, old_two.reshape(blocks))
    return (hidden_one.reshape(rows_here, width), hidden_two.reshape(rows_here, width))


def solution(mesh):
    rows = P(("groups", "rows", "feat"))
    cells = P(("groups", "rows", "feat"), "sub")
    placed = (
        cells,
        rows,
        P(("groups", "rows", "feat"), None),
        rows,
        rows,
        P(("groups", "rows", "feat"), None, None),
        cells,
        rows,
        cells,
        P(),
        P(),
        P(),
        cells,
        rows,
        cells,
        P(),
        P(),
        P(),
    )
    return jax.shard_map(
        on_device, mesh=mesh, in_specs=placed, out_specs=(cells, cells), check_vma=False
    )
```

```python
import functools

import jax
import jax.numpy as jnp
from jax import lax
from jax.experimental import pallas as pl
from jax.experimental.pallas import tpu as pltpu
from jax.sharding import PartitionSpec as P

PEERS = ("rows", "feat")
BLK = 128
QUAD = 4
F32 = jnp.float32
BF16 = jnp.bfloat16
ANY = pl.BlockSpec(memory_space=pl.ANY)
HBM = pl.BlockSpec(memory_space=pltpu.HBM)
SMEM = pl.BlockSpec(memory_space=pltpu.SMEM)
VMEM = pl.BlockSpec(memory_space=pltpu.VMEM)
PARAMS = pltpu.CompilerParams(vmem_limit_bytes=20 * 1024 * 1024)
SMALL = pltpu.CompilerParams(vmem_limit_bytes=4 * 1024 * 1024)
TINY = pl.CostEstimate(flops=0, bytes_accessed=128, transcendentals=0)


def first_kernel(peers, cap, lead, dest, tiles, out, source, fill, sem):
    count = dest.shape[0]
    half = out.shape[1]
    me = lax.axis_index(PEERS)
    first = pl.multiple_of(lax.axis_index("sub") * half, half)
    for to in range(min(peers, 16)):
        fill[to] = 0
    if peers > 16:

        def clear(i, _):
            fill[i] = 0
            return 0

        lax.fori_loop(16, peers, clear, 0)
    for t in range(count):
        to = dest[t]
        at = fill[to]
        fill[to] = at + 1
        source[to * cap + at] = t
    if lead is None:
        return
    to = lax.rem(me + lead, peers)

    def send(j, _):
        t = source[to * cap + j]
        pltpu.make_async_copy(tiles.at[t, pl.ds(first, half)], out.at[j], sem.at[j]).start()
        return 0

    def finish(j, _):
        pltpu.make_async_copy(tiles.at[0, pl.ds(first, half)], out.at[0], sem.at[j]).wait()
        return 0

    lax.fori_loop(0, fill[to], send, 0)
    lax.fori_loop(0, fill[to], finish, 0)


def rest_kernel(peers, cap, order, source, fill, tiles, *refs):
    outs, sems = refs[:-1], refs[-1]
    half = outs[0].shape[1]
    me = lax.axis_index(PEERS)
    first = pl.multiple_of(lax.axis_index("sub") * half, half)
    begun = []
    for n, k in enumerate(order):
        to = lax.rem(me + k, peers)

        def send(j, _, n=n, to=to):
            t = source[to * cap + j]
            pltpu.make_async_copy(
                tiles.at[t, pl.ds(first, half)], outs[n].at[j], sems.at[n, j]
            ).start()
            return 0

        lax.fori_loop(0, fill[to], send, 0)
        begun.append(fill[to])
    for n, amount in enumerate(begun):

        def finish(j, _, n=n):
            pltpu.make_async_copy(
                tiles.at[0, pl.ds(first, half)], outs[n].at[0], sems.at[n, j]
            ).wait()
            return 0

        lax.fori_loop(0, amount, finish, 0)


def sorted_kernel(peers, cap, source, fill, tiles, out, sems):
    half = out.shape[1]
    first = pl.multiple_of(lax.axis_index("sub") * half, half)

    def each(act):
        def peer(to, _):
            def slot(j, _):
                at = to * cap + j
                act(source[at], at)
                return 0

            return lax.fori_loop(0, fill[to], slot, 0)

        lax.fori_loop(0, peers, peer, 0)

    def copy(t, at):
        return pltpu.make_async_copy(tiles.at[t, pl.ds(first, half)], out.at[at], sems.at[t])

    each(lambda t, at: copy(t, at).start())
    each(lambda t, at: copy(t, at).wait())


def turn_kernel(nblk, h, base_one, base_two, old, after, bases, halves, sems):
    half = bases.shape[1]
    other = pl.ds(pl.multiple_of((1 - lax.axis_index("sub")) * half, half), half)
    copies = [
        pltpu.make_async_copy(base_one.at[:, other], bases.at[pl.ds(0, nblk)], sems.at[0]),
        pltpu.make_async_copy(base_two.at[:, other], bases.at[pl.ds(nblk, nblk)], sems.at[1]),
        pltpu.make_async_copy(h.at[:, pl.ds(0, half)], halves.at[pl.ds(0, nblk)], sems.at[2]),
        pltpu.make_async_copy(
            h.at[:, pl.ds(half, half)], halves.at[pl.ds(nblk, nblk)], sems.at[3]
        ),
        pltpu.make_async_copy(old.at[:, other], halves.at[pl.ds(2 * nblk, nblk)], sems.at[4]),
    ]
    for copy in copies:
        copy.start()
    for copy in copies:
        copy.wait()


def plan_kernel(peers, cap, late, nblk, sent, *refs):
    by_row, row_at, by_side, side_at, fill_row, fill_side, codes, number = refs
    count = sent.shape[0] // peers
    nothing = peers * cap * 32 + nblk
    me = lax.axis_index(PEERS)
    for fill in (fill_row, fill_side):
        for g in range(fill.shape[0]):
            fill[g] = 0

    def pick(origin, _):
        def one(t, n):
            code = sent[origin * count + t]
            codes[origin * cap + n] = code & 255
            return n + ((code >> 8) == me).astype(jnp.int32)

        number[origin] = lax.fori_loop(0, count, one, jnp.int32(0), unroll=4)
        return 0

    lax.fori_loop(0, peers, pick, 0)

    def walk(act):
        def peer(origin, _):
            behind = jnp.int32(0)
            step = lax.rem(me + peers - origin, peers)
            for k in late:
                behind = behind + jnp.where(step == k, nblk, 0)

            def slot(j, _):
                code = codes[origin * cap + j]
                row = code >> 5
                col = row + (code & 31)
                side = jnp.where(col < nblk, nblk, jnp.where(col < 2 * nblk, 0, 2 * nblk))
                act(row + behind, row + side, (row << 16) + (origin * cap + j) * 32 + col)
                return 0

            return lax.fori_loop(0, number[origin], slot, 0)

        lax.fori_loop(0, peers, peer, 0)

    def tally(row, side, entry):
        fill_row[row] = fill_row[row] + 1
        fill_side[side] = fill_side[side] + 1

    def place(row, side, entry):
        to = fill_row[row]
        by_row[to] = entry
        fill_row[row] = to + 1
        to = fill_side[side]
        by_side[to] = entry
        fill_side[side] = to + 1

    walk(tally)
    for fill, at, listed in ((fill_row, row_at, by_row), (fill_side, side_at, by_side)):
        now = jnp.int32(0)
        for g in range(fill.shape[0]):
            at[g] = now
            need = (fill[g] + QUAD - 1) // QUAD
            fill[g] = now * QUAD
            now = now + need
            last = jnp.maximum(now * QUAD - QUAD, 0)
            for u in range(QUAD):
                listed[last + u] = nothing + ((g % nblk) << 16)
        at[fill.shape[0]] = now
    walk(place)


def tile_copies(cap, steps, arrived, tiles, sems):
    if steps is None:
        whole = tiles.at[pl.ds(0, arrived[0].shape[0])]
        return [pltpu.make_async_copy(arrived[0], whole, sems.at[0])]
    me = lax.axis_index(PEERS)
    peers = lax.axis_size(PEERS)
    copies = []
    for n, (k, ref) in enumerate(zip(steps, arrived)):
        origin = lax.rem(me + peers - k, peers)
        copies.append(pltpu.make_async_copy(ref, tiles.at[pl.ds(origin * cap, cap)], sems.at[n]))
    return copies


def tile_sums(order, begin, end, tiles, cells, total):
    nothing = (tiles.shape[0] - 1) * 32 + cells.shape[0] // 3

    def step(n, _):
        for q in (begin + 2 * n, begin + 2 * n + 1):
            entry = [jnp.where(q < end, order[q * QUAD + u], nothing) for u in range(QUAD)]
            row = entry[0] >> 16
            tile = [(e >> 5) & 2047 for e in entry]
            cell = [e & 31 for e in entry]
            acc = None
            for u in range(0, QUAD, 2):
                weights = jnp.concatenate([tiles[tile[u]], tiles[tile[u + 1]]], axis=1)
                chosen = jnp.concatenate([cells[cell[u]], cells[cell[u + 1]]], axis=0)
                part = jnp.dot(weights, chosen, preferred_element_type=F32)
                acc = part if acc is None else acc + part
            total[row] = total[row] + acc
        return 0

    lax.fori_loop(0, (end - begin + 1) >> 1, step, 0)


def early_kernel(cap, steps, pieces, nblk, order, at, *refs):
    arrived = refs[:pieces]
    (left, left_twin, h, halves, right, right_twin, base_one, base_two, bases, old) = refs[
        pieces : pieces + 10
    ]
    w_self, bias, agg, cells, own, base_rows, old_rows, tiles, sems = refs[pieces + 10 :]
    sub = lax.axis_index("sub")
    half = agg.shape[1]
    width = h.shape[2]
    lanes = pl.ds(pl.multiple_of(sub * width, width), width)
    others = pl.ds(pl.multiple_of((1 - sub) * width, width), width)
    lines = pl.ds(pl.multiple_of(sub * half, half), half)
    block = [pl.ds(k * nblk, nblk) for k in range(3)]
    low, high = pl.ds(0, half), pl.ds(half, half)
    moves = [
        (left, cells.at[block[0], :, lanes]),
        (left_twin, cells.at[block[0], :, others]),
        (h, cells.at[block[1], :, lanes]),
        (halves.at[block[0]], cells.at[block[1], low, others]),
        (halves.at[block[1]], cells.at[block[1], high, others]),
        (right, cells.at[block[2], :, lanes]),
        (right_twin, cells.at[block[2], :, others]),
        (base_one.at[:, lines], agg.at[:, :, lanes]),
        (bases.at[block[0]], agg.at[:, :, others]),
        (base_two.at[:, lines], base_rows.at[:, :, lanes]),
        (bases.at[block[1]], base_rows.at[:, :, others]),
        (old.at[:, lines], old_rows.at[:, :, lanes]),
        (halves.at[block[2]], old_rows.at[:, :, others]),
    ]
    copies = tile_copies(cap, steps, arrived, tiles, sems)
    for k, (src, dst) in enumerate(moves):
        copies.append(pltpu.make_async_copy(src, dst, sems.at[pieces + k]))
    for copy in copies:
        copy.start()
    tiles[tiles.shape[0] - 1] = jnp.zeros(tiles.shape[1:], tiles.dtype)
    for copy in copies:
        copy.wait()
    tile_sums(order, at[0], at[nblk], tiles, cells, agg)
    for r in range(nblk):
        own[r] = (
            jnp.dot(cells[nblk + r, lines], w_self[...], preferred_element_type=F32) + bias[...]
        )


def column(inv, r, sub, half):
    shape = (half, inv.shape[1])
    line = lax.broadcasted_iota(jnp.int32, shape, 0) + sub * half
    lane = lax.broadcasted_iota(jnp.int32, shape, 1)
    spread = jnp.broadcast_to(inv[r : r + 1, :], shape)
    return jnp.sum(jnp.where(line == lane, spread, 0.0), axis=1, keepdims=True)


def late_kernel(cap, steps, pieces, nblk, order, at, affected, *refs):
    arrived = refs[:pieces]
    cells, agg, inv, own, w_neigh, old, out, tiles, total, means, sems = refs[pieces:]
    half = agg.shape[1]
    sub = lax.axis_index("sub")
    copies = tile_copies(cap, steps, arrived, tiles, sems) if pieces else []
    for copy in copies:
        copy.start()
    tiles[tiles.shape[0] - 1] = jnp.zeros(tiles.shape[1:], tiles.dtype)
    for r in range(nblk):
        total[r] = agg[r]
    for copy in copies:
        copy.wait()
    tile_sums(order, at[nblk], at[2 * nblk], tiles, cells, total)
    for r in range(nblk):
        means[r] = (total[r] * column(inv, r, sub, half)).astype(BF16)
    for r in range(nblk):
        pre = own[r] + jnp.dot(means[r], w_neigh[...], preferred_element_type=F32)
        pre = jnp.maximum(pre, 0.0)
        keep = jnp.full((half, 1), affected[r], jnp.int32) > 0
        out[r] = jnp.where(keep, pre, old[r].astype(F32)).astype(BF16)


def near_kernel(cap, steps, pieces, nblk, order, at, *refs):
    arrived = refs[:pieces]
    mine, twin, base, w_self, bias, agg, own, hidden, tiles, cells, sems = refs[pieces:]
    half = base.shape[1]
    width = hidden.shape[2]
    sub = lax.axis_index("sub")
    lanes = pl.ds(pl.multiple_of(sub * width, width), width)
    copies = tile_copies(cap, steps, arrived, tiles, sems)
    for k, (ref, side) in enumerate(((mine, sub), (twin, 1 - sub))):
        lines = pl.ds(pl.multiple_of(side * half, half), half)
        to = cells.at[pl.ds(nblk, nblk), lines]
        copies.append(pltpu.make_async_copy(ref, to, sems.at[pieces + k]))
        to = hidden.at[:, lines]
        copies.append(pltpu.make_async_copy(ref.at[:, :, lanes], to, sems.at[pieces + 2 + k]))
    for copy in copies:
        copy.start()
    tiles[tiles.shape[0] - 1] = jnp.zeros(tiles.shape[1:], tiles.dtype)
    for r in range(nblk):
        agg[r] = base[r]
    for copy in copies:
        copy.wait()
    tile_sums(order, at[0], at[nblk], tiles, cells, agg)
    mine_rows = pl.ds(pl.multiple_of(sub * half, half), half)
    for r in range(nblk):
        own[r] = (
            jnp.dot(cells[nblk + r, mine_rows], w_self[...], preferred_element_type=F32) + bias[...]
        )


def far_kernel(nblk, order, at, tiles, left, left_twin, right, right_twin, *refs):
    agg, inv, own, w_neigh, keep, send, cells, total, means, sems = refs
    half = agg.shape[1]
    width = keep.shape[2]
    sub = lax.axis_index("sub")
    sides = ((left, 0, sub), (left_twin, 0, 1 - sub), (right, 2, sub), (right_twin, 2, 1 - sub))
    copies = []
    for k, (ref, third, side) in enumerate(sides):
        lines = pl.ds(pl.multiple_of(side * half, half), half)
        to = cells.at[pl.ds(third * nblk, nblk), lines]
        copies.append(pltpu.make_async_copy(ref, to, sems.at[k]))
    for copy in copies:
        copy.start()
    cells[nblk] = jnp.zeros(cells.shape[1:], cells.dtype)
    for r in range(nblk):
        total[r] = agg[r]
    for copy in copies:
        copy.wait()
    tile_sums(order, at[nblk], at[3 * nblk], tiles, cells, total)
    for r in range(nblk):
        means[r] = (total[r] * column(inv, r, sub, half)).astype(BF16)
    for r in range(nblk):
        pre = own[r] + jnp.dot(means[r], w_neigh[...], preferred_element_type=F32)
        low = pre[:, :width]
        high = pre[:, width:]
        first = jnp.full((half, 1), sub, jnp.int32) == 0
        keep[r] = jnp.where(first, low, high).astype(BF16)
        send[r] = jnp.where(first, high, low).astype(BF16)


def finish_kernel(nblk, affected, kept, came, old, out):
    half = kept.shape[1]
    first = jnp.full((half, 1), lax.axis_index("sub"), jnp.int32) == 0
    for r in range(nblk):
        keep = jnp.full((half, 1), affected[r], jnp.int32) > 0
        low = jnp.where(first, kept[r].astype(F32), came[r].astype(F32))
        high = jnp.where(first, came[r].astype(F32), kept[r].astype(F32))
        out[r, :half] = jnp.where(keep, low, old[r, :half].astype(F32)).astype(BF16)
        out[r, half:] = jnp.where(keep, high, old[r, half:].astype(F32)).astype(BF16)


def swap(x):
    return lax.ppermute(x, "sub", [(0, 1), (1, 0)])


def ring(x, step):
    peers = lax.axis_size(PEERS)
    return lax.ppermute(x, PEERS, [(i, (i + step) % peers) for i in range(peers)])


def on_device(
    h_input,
    inv_degree,
    dest_block,
    row_block,
    block_offset,
    new_tiles,
    base_one,
    affected_one,
    old_one,
    self_one,
    neigh_one,
    bias_one,
    base_two,
    affected_two,
    old_two,
    self_two,
    neigh_two,
    bias_two,
):
    peers = lax.axis_size(PEERS)
    count = dest_block.shape[0]
    cap = max(2, 2 * count // peers)
    slots = peers * cap
    rows_here, width = h_input.shape
    full = width * lax.axis_size("sub")
    nblk = rows_here // BLK
    half = BLK // lax.axis_size("sub")
    direct = 2 < peers <= 16
    shape = jax.ShapeDtypeStruct
    after = lax.optimization_barrier
    blocks = (nblk, BLK, width)
    h_blocks = h_input.reshape(blocks)
    left, right = ring(h_blocks, 1), ring(h_blocks, peers - 1)

    order = sorted(range(1, peers), key=lambda k: (abs(k - peers // 2), k))
    lead = order[0] if direct else None
    piece = shape((cap, half, BLK), BF16)
    out_piece, source, fill = pl.pallas_call(
        functools.partial(first_kernel, peers, cap, lead),
        out_shape=[piece, shape((slots,), jnp.int32), shape((peers,), jnp.int32)],
        in_specs=[SMEM, HBM],
        out_specs=[VMEM, SMEM, SMEM],
        scratch_shapes=[pltpu.SemaphoreType.DMA((cap,))],
        cost_estimate=TINY,
        name="first",
    )(dest_block.reshape(count), new_tiles)

    labels = dest_block.reshape(count) * 256 + row_block * 32 + block_offset + 8
    got_codes = lax.all_to_all(
        jnp.broadcast_to(labels, (peers, count)),
        PEERS,
        split_axis=0,
        concat_axis=0,
        tiled=True,
    ).reshape(peers * count)
    got_codes, fill = after((got_codes, fill))
    if direct:
        others = order[1:] + [0]
        packed = pl.pallas_call(
            functools.partial(rest_kernel, peers, cap, others),
            out_shape=[piece] * len(others),
            in_specs=[SMEM, SMEM, HBM],
            out_specs=[VMEM] * len(others),
            scratch_shapes=[pltpu.SemaphoreType.DMA((len(others), cap))],
            cost_estimate=TINY,
            name="rest",
        )(source, fill, new_tiles)
        steps = order + [0]
        got = dict(zip(others, packed))
        got[lead] = out_piece
        got = {k: ring(got[k], k) if k else got[k] for k in steps}
        late = tuple(order[4:]) if peers > 4 else ()
        early = [k for k in steps if k not in late]
        arrived = [got[k] for k in steps]
        arrived_early = [got[k] for k in early]
        arrived_late = [got[k] for k in late]
        flag = got[lead]
        gathered = packed[-1]
    else:
        sent = pl.pallas_call(
            functools.partial(sorted_kernel, peers, cap),
            out_shape=shape((slots, half, BLK), BF16),
            in_specs=[SMEM, SMEM, HBM],
            out_specs=HBM,
            scratch_shapes=[pltpu.SemaphoreType.DMA((count,))],
            cost_estimate=TINY,
            name="rest",
        )(source, fill, new_tiles)
        sent = sent.reshape(peers, cap, half, BLK)
        got = lax.all_to_all(sent, PEERS, split_axis=0, concat_axis=0, tiled=True)
        arrived = [got.reshape(slots, half, BLK)]
        steps = early = None
        late = ()
        arrived_early, arrived_late = arrived, []
        flag = source
        gathered = out_piece

    left, right, got_codes = after((left, right, got_codes))
    sizes = (2 * nblk, 3 * nblk)
    counts = [pltpu.SMEM((size,), jnp.int32) for size in sizes]
    lists = []
    for size in sizes:
        lists += [shape((slots + size * QUAD,), jnp.int32), shape((size + 1,), jnp.int32)]
    by_row, row_at, by_side, side_at = pl.pallas_call(
        functools.partial(plan_kernel, peers, cap, late, nblk),
        out_shape=lists,
        in_specs=[SMEM],
        out_specs=[SMEM] * 4,
        scratch_shapes=counts
        + [pltpu.SMEM((slots + 1,), jnp.int32), pltpu.SMEM((peers,), jnp.int32)],
        compiler_params=SMALL,
        cost_estimate=TINY,
        name="plan",
    )(got_codes)

    old_blocks = old_one.reshape(blocks)
    base_one, base_two = base_one.reshape(blocks), base_two.reshape(blocks)
    bases, halves = pl.pallas_call(
        functools.partial(turn_kernel, nblk),
        out_shape=[shape((2 * nblk, half, width), F32), shape((3 * nblk, half, width), BF16)],
        in_specs=[ANY] * 5,
        out_specs=[ANY] * 2,
        scratch_shapes=[pltpu.SemaphoreType.DMA((5,))],
        compiler_params=SMALL,
        cost_estimate=TINY,
        name="turn",
    )(h_blocks, base_one, base_two, old_blocks, gathered)
    bases, halves, _ = after((bases, halves, flag))
    bases, halves = swap(bases), swap(halves)
    left, right, _ = after((left, right, flag))
    left_twin, right_twin = swap(left), swap(right)

    tile_scratch = pltpu.VMEM((slots + 1, half, BLK), BF16)
    cell_shape = (3 * nblk, BLK, full)
    cell_scratch = pltpu.VMEM(cell_shape, BF16)
    mean_scratch = pltpu.VMEM((nblk, half, full), BF16)
    rows_shape = (nblk, half, full)
    total_scratch = pltpu.VMEM(rows_shape, F32)
    inv = inv_degree.reshape(nblk, BLK)

    many = len(arrived_early)
    agg_early, cells_one, own_one, base_two_rows, old_one_rows = pl.pallas_call(
        functools.partial(early_kernel, cap, early, many, nblk),
        out_shape=[
            shape(rows_shape, F32),
            shape(cell_shape, BF16),
            shape(rows_shape, F32),
            shape(rows_shape, F32),
            shape(rows_shape, BF16),
        ],
        in_specs=[SMEM] * 2 + [ANY] * (many + 10) + [VMEM] * 2,
        out_specs=[VMEM] * 5,
        scratch_shapes=[tile_scratch, pltpu.SemaphoreType.DMA((many + 13,))],
        compiler_params=PARAMS,
        cost_estimate=TINY,
        name="early",
    )(
        by_row,
        row_at,
        *arrived_early,
        left,
        left_twin,
        h_blocks,
        halves,
        right,
        right_twin,
        base_one,
        base_two,
        bases,
        old_blocks,
        self_one,
        bias_one.reshape(1, full),
    )

    many = len(arrived_late)
    hidden_rows = pl.pallas_call(
        functools.partial(late_kernel, cap, late, many, nblk),
        out_shape=shape(rows_shape, BF16),
        in_specs=[SMEM] * 3 + [ANY] * many + [VMEM] * 6,
        out_specs=VMEM,
        scratch_shapes=[
            tile_scratch,
            total_scratch,
            mean_scratch,
            pltpu.SemaphoreType.DMA((max(1, many),)),
        ],
        compiler_params=PARAMS,
        cost_estimate=TINY,
        name="late",
    )(
        by_row,
        row_at,
        affected_one,
        *arrived_late,
        cells_one,
        agg_early,
        inv,
        own_one,
        neigh_one,
        old_one_rows,
    )

    hidden_twin = swap(hidden_rows)
    left = ring(hidden_rows, 1)
    right = ring(hidden_rows, peers - 1)

    many = len(arrived)
    agg_two, own_two, hidden_one, tiles_all = pl.pallas_call(
        functools.partial(near_kernel, cap, steps, many, nblk),
        out_shape=[shape(rows_shape, F32)] * 2
        + [shape(blocks, BF16), shape((slots + 1, half, BLK), BF16)],
        in_specs=[SMEM] * 2 + [ANY] * (many + 2) + [VMEM] * 3,
        out_specs=[VMEM] * 2 + [ANY, VMEM],
        scratch_shapes=[cell_scratch, pltpu.SemaphoreType.DMA((many + 4,))],
        compiler_params=PARAMS,
        cost_estimate=TINY,
        name="near",
    )(
        by_side,
        side_at,
        *arrived,
        hidden_rows,
        hidden_twin,
        base_two_rows,
        self_two,
        bias_two.reshape(1, full),
    )

    left, right, agg_two, own_two = after((left, right, agg_two, own_two))
    left_twin = swap(left)
    right_twin = swap(right)
    kept, sent = pl.pallas_call(
        functools.partial(far_kernel, nblk),
        out_shape=[shape((nblk, half, width), BF16)] * 2,
        in_specs=[SMEM] * 2 + [VMEM] + [ANY] * 4 + [VMEM] * 4,
        out_specs=[VMEM] * 2,
        scratch_shapes=[
            cell_scratch,
            total_scratch,
            mean_scratch,
            pltpu.SemaphoreType.DMA((4,)),
        ],
        compiler_params=PARAMS,
        cost_estimate=TINY,
        name="far",
    )(
        by_side,
        side_at,
        tiles_all,
        left,
        left_twin,
        right,
        right_twin,
        agg_two,
        inv,
        own_two,
        neigh_two,
    )
    came = swap(sent)
    hidden_two = pl.pallas_call(
        functools.partial(finish_kernel, nblk),
        out_shape=shape(blocks, BF16),
        in_specs=[SMEM] + [VMEM] * 3,
        out_specs=VMEM,
        compiler_params=SMALL,
        cost_estimate=TINY,
        name="finish",
    )(affected_two, kept, came, old_two.reshape(blocks))
    return (hidden_one.reshape(rows_here, width), hidden_two.reshape(rows_here, width))


def solution(mesh):
    rows = P(("groups", "rows", "feat"))
    cells = P(("groups", "rows", "feat"), "sub")
    placed = (
        cells,
        rows,
        P(("groups", "rows", "feat"), None),
        rows,
        rows,
        P(("groups", "rows", "feat"), None, None),
        cells,
        rows,
        cells,
        P(),
        P(),
        P(),
        cells,
        rows,
        cells,
        P(),
        P(),
        P(),
    )
    return jax.shard_map(
        on_device, mesh=mesh, in_specs=placed, out_specs=(cells, cells), check_vma=False
    )
```

```python
import functools

import jax
import jax.numpy as jnp
from jax import lax
from jax.experimental import pallas as pl
from jax.experimental.pallas import tpu as pltpu
from jax.sharding import PartitionSpec as P

PEERS = ("rows", "feat")
BLK = 128
QUAD = 4
F32 = jnp.float32
BF16 = jnp.bfloat16
ANY = pl.BlockSpec(memory_space=pl.ANY)
HBM = pl.BlockSpec(memory_space=pltpu.HBM)
SMEM = pl.BlockSpec(memory_space=pltpu.SMEM)
VMEM = pl.BlockSpec(memory_space=pltpu.VMEM)
PARAMS = pltpu.CompilerParams(vmem_limit_bytes=20 * 1024 * 1024)
SMALL = pltpu.CompilerParams(vmem_limit_bytes=4 * 1024 * 1024)
TINY = pl.CostEstimate(flops=0, bytes_accessed=128, transcendentals=0)


def first_kernel(peers, cap, lead, dest, tiles, out, source, fill, sem):
    count = dest.shape[0]
    half = out.shape[1]
    me = lax.axis_index(PEERS)
    first = pl.multiple_of(lax.axis_index("sub") * half, half)
    for to in range(min(peers, 16)):
        fill[to] = 0
    if peers > 16:

        def clear(i, _):
            fill[i] = 0
            return 0

        lax.fori_loop(16, peers, clear, 0)
    for t in range(count):
        to = dest[t]
        at = fill[to]
        fill[to] = at + 1
        source[to * cap + at] = t
    if lead is None:
        return
    to = lax.rem(me + lead, peers)

    def send(j, _):
        t = source[to * cap + j]
        pltpu.make_async_copy(tiles.at[t, pl.ds(first, half)], out.at[j], sem.at[j]).start()
        return 0

    def finish(j, _):
        pltpu.make_async_copy(tiles.at[0, pl.ds(first, half)], out.at[0], sem.at[j]).wait()
        return 0

    lax.fori_loop(0, fill[to], send, 0)
    lax.fori_loop(0, fill[to], finish, 0)


def rest_kernel(peers, cap, order, source, fill, tiles, *refs):
    outs, sems = refs[:-1], refs[-1]
    half = outs[0].shape[1]
    me = lax.axis_index(PEERS)
    first = pl.multiple_of(lax.axis_index("sub") * half, half)
    begun = []
    for n, k in enumerate(order):
        to = lax.rem(me + k, peers)

        def send(j, _, n=n, to=to):
            t = source[to * cap + j]
            pltpu.make_async_copy(
                tiles.at[t, pl.ds(first, half)], outs[n].at[j], sems.at[n, j]
            ).start()
            return 0

        lax.fori_loop(0, fill[to], send, 0)
        begun.append(fill[to])
    for n, amount in enumerate(begun):

        def finish(j, _, n=n):
            pltpu.make_async_copy(
                tiles.at[0, pl.ds(first, half)], outs[n].at[0], sems.at[n, j]
            ).wait()
            return 0

        lax.fori_loop(0, amount, finish, 0)


def sorted_kernel(peers, cap, source, fill, tiles, out, sems):
    half = out.shape[1]
    first = pl.multiple_of(lax.axis_index("sub") * half, half)

    def each(act):
        def peer(to, _):
            def slot(j, _):
                at = to * cap + j
                act(source[at], at)
                return 0

            return lax.fori_loop(0, fill[to], slot, 0)

        lax.fori_loop(0, peers, peer, 0)

    def copy(t, at):
        return pltpu.make_async_copy(tiles.at[t, pl.ds(first, half)], out.at[at], sems.at[t])

    each(lambda t, at: copy(t, at).start())
    each(lambda t, at: copy(t, at).wait())


def label_kernel(peers, cap, source, fill, row, off, after, codes):
    def peer(to, _):
        def slot(j, _):
            t = source[to * cap + j]
            codes[to * (cap + 1) + j] = row[t] * 32 + off[t] + 8
            return 0

        lax.fori_loop(0, fill[to], slot, 0)
        codes[to * (cap + 1) + cap] = fill[to]
        return 0

    lax.fori_loop(0, peers, peer, 0)


def turn_kernel(nblk, h, base_one, base_two, old, after, bases, halves, sems):
    half = bases.shape[1]
    other = pl.ds(pl.multiple_of((1 - lax.axis_index("sub")) * half, half), half)
    copies = [
        pltpu.make_async_copy(base_one.at[:, other], bases.at[pl.ds(0, nblk)], sems.at[0]),
        pltpu.make_async_copy(base_two.at[:, other], bases.at[pl.ds(nblk, nblk)], sems.at[1]),
        pltpu.make_async_copy(h.at[:, pl.ds(0, half)], halves.at[pl.ds(0, nblk)], sems.at[2]),
        pltpu.make_async_copy(
            h.at[:, pl.ds(half, half)], halves.at[pl.ds(nblk, nblk)], sems.at[3]
        ),
        pltpu.make_async_copy(old.at[:, other], halves.at[pl.ds(2 * nblk, nblk)], sems.at[4]),
    ]
    for copy in copies:
        copy.start()
    for copy in copies:
        copy.wait()


def plan_kernel(peers, late, nblk, codes, by_row, row_at, by_side, side_at, fill_row, fill_side):
    cap = codes.shape[0] // peers - 1
    nothing = peers * cap * 32 + nblk
    me = lax.axis_index(PEERS)
    for fill in (fill_row, fill_side):
        for g in range(fill.shape[0]):
            fill[g] = 0

    def walk(act):
        def peer(origin, _):
            behind = jnp.int32(0)
            step = lax.rem(me + peers - origin, peers)
            for k in late:
                behind = behind + jnp.where(step == k, nblk, 0)

            def slot(j, _):
                code = codes[origin * (cap + 1) + j]
                row = code >> 5
                col = row + (code & 31)
                side = jnp.where(col < nblk, nblk, jnp.where(col < 2 * nblk, 0, 2 * nblk))
                act(row + behind, row + side, (row << 16) + (origin * cap + j) * 32 + col)
                return 0

            return lax.fori_loop(0, codes[origin * (cap + 1) + cap], slot, 0)

        lax.fori_loop(0, peers, peer, 0)

    def tally(row, side, entry):
        fill_row[row] = fill_row[row] + 1
        fill_side[side] = fill_side[side] + 1

    def place(row, side, entry):
        to = fill_row[row]
        by_row[to] = entry
        fill_row[row] = to + 1
        to = fill_side[side]
        by_side[to] = entry
        fill_side[side] = to + 1

    walk(tally)
    for fill, at, listed in ((fill_row, row_at, by_row), (fill_side, side_at, by_side)):
        now = jnp.int32(0)
        for g in range(fill.shape[0]):
            at[g] = now
            need = (fill[g] + QUAD - 1) // QUAD
            fill[g] = now * QUAD
            now = now + need
            last = jnp.maximum(now * QUAD - QUAD, 0)
            for u in range(QUAD):
                listed[last + u] = nothing + ((g % nblk) << 16)
        at[fill.shape[0]] = now
    walk(place)


def tile_copies(cap, steps, arrived, tiles, sems):
    if steps is None:
        whole = tiles.at[pl.ds(0, arrived[0].shape[0])]
        return [pltpu.make_async_copy(arrived[0], whole, sems.at[0])]
    me = lax.axis_index(PEERS)
    peers = lax.axis_size(PEERS)
    copies = []
    for n, (k, ref) in enumerate(zip(steps, arrived)):
        origin = lax.rem(me + peers - k, peers)
        copies.append(pltpu.make_async_copy(ref, tiles.at[pl.ds(origin * cap, cap)], sems.at[n]))
    return copies


def tile_sums(order, begin, end, tiles, cells, total):
    nothing = (tiles.shape[0] - 1) * 32 + cells.shape[0] // 3

    def step(n, _):
        for q in (begin + 2 * n, begin + 2 * n + 1):
            entry = [jnp.where(q < end, order[q * QUAD + u], nothing) for u in range(QUAD)]
            row = entry[0] >> 16
            tile = [(e >> 5) & 2047 for e in entry]
            cell = [e & 31 for e in entry]
            acc = None
            for u in range(0, QUAD, 2):
                weights = jnp.concatenate([tiles[tile[u]], tiles[tile[u + 1]]], axis=1)
                chosen = jnp.concatenate([cells[cell[u]], cells[cell[u + 1]]], axis=0)
                part = jnp.dot(weights, chosen, preferred_element_type=F32)
                acc = part if acc is None else acc + part
            total[row] = total[row] + acc
        return 0

    lax.fori_loop(0, (end - begin + 1) >> 1, step, 0)


def early_kernel(cap, steps, pieces, nblk, order, at, *refs):
    arrived = refs[:pieces]
    (left, left_twin, h, halves, right, right_twin, base_one, base_two, bases, old) = refs[
        pieces : pieces + 10
    ]
    w_self, bias, agg, cells, own, base_rows, old_rows, tiles, sems = refs[pieces + 10 :]
    sub = lax.axis_index("sub")
    half = agg.shape[1]
    width = h.shape[2]
    lanes = pl.ds(pl.multiple_of(sub * width, width), width)
    others = pl.ds(pl.multiple_of((1 - sub) * width, width), width)
    lines = pl.ds(pl.multiple_of(sub * half, half), half)
    block = [pl.ds(k * nblk, nblk) for k in range(3)]
    low, high = pl.ds(0, half), pl.ds(half, half)
    moves = [
        (left, cells.at[block[0], :, lanes]),
        (left_twin, cells.at[block[0], :, others]),
        (h, cells.at[block[1], :, lanes]),
        (halves.at[block[0]], cells.at[block[1], low, others]),
        (halves.at[block[1]], cells.at[block[1], high, others]),
        (right, cells.at[block[2], :, lanes]),
        (right_twin, cells.at[block[2], :, others]),
        (base_one.at[:, lines], agg.at[:, :, lanes]),
        (bases.at[block[0]], agg.at[:, :, others]),
        (base_two.at[:, lines], base_rows.at[:, :, lanes]),
        (bases.at[block[1]], base_rows.at[:, :, others]),
        (old.at[:, lines], old_rows.at[:, :, lanes]),
        (halves.at[block[2]], old_rows.at[:, :, others]),
    ]
    copies = tile_copies(cap, steps, arrived, tiles, sems)
    for k, (src, dst) in enumerate(moves):
        copies.append(pltpu.make_async_copy(src, dst, sems.at[pieces + k]))
    for copy in copies:
        copy.start()
    tiles[tiles.shape[0] - 1] = jnp.zeros(tiles.shape[1:], tiles.dtype)
    for copy in copies:
        copy.wait()
    tile_sums(order, at[0], at[nblk], tiles, cells, agg)
    for r in range(nblk):
        own[r] = (
            jnp.dot(cells[nblk + r, lines], w_self[...], preferred_element_type=F32) + bias[...]
        )


def column(inv, r, sub, half):
    shape = (half, inv.shape[1])
    line = lax.broadcasted_iota(jnp.int32, shape, 0) + sub * half
    lane = lax.broadcasted_iota(jnp.int32, shape, 1)
    spread = jnp.broadcast_to(inv[r : r + 1, :], shape)
    return jnp.sum(jnp.where(line == lane, spread, 0.0), axis=1, keepdims=True)


def late_kernel(cap, steps, pieces, nblk, order, at, affected, *refs):
    arrived = refs[:pieces]
    cells, agg, inv, own, w_neigh, old, out, tiles, total, means, sems = refs[pieces:]
    half = agg.shape[1]
    sub = lax.axis_index("sub")
    copies = tile_copies(cap, steps, arrived, tiles, sems) if pieces else []
    for copy in copies:
        copy.start()
    tiles[tiles.shape[0] - 1] = jnp.zeros(tiles.shape[1:], tiles.dtype)
    for r in range(nblk):
        total[r] = agg[r]
    for copy in copies:
        copy.wait()
    tile_sums(order, at[nblk], at[2 * nblk], tiles, cells, total)
    for r in range(nblk):
        means[r] = (total[r] * column(inv, r, sub, half)).astype(BF16)
    for r in range(nblk):
        pre = own[r] + jnp.dot(means[r], w_neigh[...], preferred_element_type=F32)
        pre = jnp.maximum(pre, 0.0)
        keep = jnp.full((half, 1), affected[r], jnp.int32) > 0
        out[r] = jnp.where(keep, pre, old[r].astype(F32)).astype(BF16)


def near_kernel(cap, steps, pieces, nblk, order, at, *refs):
    arrived = refs[:pieces]
    mine, twin, base, w_self, bias, agg, own, hidden, tiles, cells, sems = refs[pieces:]
    half = base.shape[1]
    width = hidden.shape[2]
    sub = lax.axis_index("sub")
    lanes = pl.ds(pl.multiple_of(sub * width, width), width)
    copies = tile_copies(cap, steps, arrived, tiles, sems)
    for k, (ref, side) in enumerate(((mine, sub), (twin, 1 - sub))):
        lines = pl.ds(pl.multiple_of(side * half, half), half)
        to = cells.at[pl.ds(nblk, nblk), lines]
        copies.append(pltpu.make_async_copy(ref, to, sems.at[pieces + k]))
        to = hidden.at[:, lines]
        copies.append(pltpu.make_async_copy(ref.at[:, :, lanes], to, sems.at[pieces + 2 + k]))
    for copy in copies:
        copy.start()
    tiles[tiles.shape[0] - 1] = jnp.zeros(tiles.shape[1:], tiles.dtype)
    for r in range(nblk):
        agg[r] = base[r]
    for copy in copies:
        copy.wait()
    tile_sums(order, at[0], at[nblk], tiles, cells, agg)
    mine_rows = pl.ds(pl.multiple_of(sub * half, half), half)
    for r in range(nblk):
        own[r] = (
            jnp.dot(cells[nblk + r, mine_rows], w_self[...], preferred_element_type=F32) + bias[...]
        )


def far_kernel(nblk, order, at, tiles, left, left_twin, right, right_twin, *refs):
    agg, inv, own, w_neigh, keep, send, cells, total, means, sems = refs
    half = agg.shape[1]
    width = keep.shape[2]
    sub = lax.axis_index("sub")
    sides = ((left, 0, sub), (left_twin, 0, 1 - sub), (right, 2, sub), (right_twin, 2, 1 - sub))
    copies = []
    for k, (ref, third, side) in enumerate(sides):
        lines = pl.ds(pl.multiple_of(side * half, half), half)
        to = cells.at[pl.ds(third * nblk, nblk), lines]
        copies.append(pltpu.make_async_copy(ref, to, sems.at[k]))
    for copy in copies:
        copy.start()
    cells[nblk] = jnp.zeros(cells.shape[1:], cells.dtype)
    for r in range(nblk):
        total[r] = agg[r]
    for copy in copies:
        copy.wait()
    tile_sums(order, at[nblk], at[3 * nblk], tiles, cells, total)
    for r in range(nblk):
        means[r] = (total[r] * column(inv, r, sub, half)).astype(BF16)
    for r in range(nblk):
        pre = own[r] + jnp.dot(means[r], w_neigh[...], preferred_element_type=F32)
        low = pre[:, :width]
        high = pre[:, width:]
        first = jnp.full((half, 1), sub, jnp.int32) == 0
        keep[r] = jnp.where(first, low, high).astype(BF16)
        send[r] = jnp.where(first, high, low).astype(BF16)


def finish_kernel(nblk, affected, kept, came, old, out):
    half = kept.shape[1]
    first = jnp.full((half, 1), lax.axis_index("sub"), jnp.int32) == 0
    for r in range(nblk):
        keep = jnp.full((half, 1), affected[r], jnp.int32) > 0
        low = jnp.where(first, kept[r].astype(F32), came[r].astype(F32))
        high = jnp.where(first, came[r].astype(F32), kept[r].astype(F32))
        out[r, :half] = jnp.where(keep, low, old[r, :half].astype(F32)).astype(BF16)
        out[r, half:] = jnp.where(keep, high, old[r, half:].astype(F32)).astype(BF16)


def swap(x):
    return lax.ppermute(x, "sub", [(0, 1), (1, 0)])


def ring(x, step):
    peers = lax.axis_size(PEERS)
    return lax.ppermute(x, PEERS, [(i, (i + step) % peers) for i in range(peers)])


def on_device(
    h_input,
    inv_degree,
    dest_block,
    row_block,
    block_offset,
    new_tiles,
    base_one,
    affected_one,
    old_one,
    self_one,
    neigh_one,
    bias_one,
    base_two,
    affected_two,
    old_two,
    self_two,
    neigh_two,
    bias_two,
):
    peers = lax.axis_size(PEERS)
    count = dest_block.shape[0]
    cap = max(2, 2 * count // peers)
    slots = peers * cap
    rows_here, width = h_input.shape
    full = width * lax.axis_size("sub")
    nblk = rows_here // BLK
    half = BLK // lax.axis_size("sub")
    direct = 2 < peers <= 16
    shape = jax.ShapeDtypeStruct
    after = lax.optimization_barrier

    order = sorted(range(1, peers), key=lambda k: (abs(k - peers // 2), k))
    lead = order[0] if direct else None
    piece = shape((cap, half, BLK), BF16)
    out_piece, source, fill = pl.pallas_call(
        functools.partial(first_kernel, peers, cap, lead),
        out_shape=[piece, shape((slots,), jnp.int32), shape((peers,), jnp.int32)],
        in_specs=[SMEM, HBM],
        out_specs=[VMEM, SMEM, SMEM],
        scratch_shapes=[pltpu.SemaphoreType.DMA((cap,))],
        cost_estimate=TINY,
        name="first",
    )(dest_block.reshape(count), new_tiles)

    if direct:
        others = order[1:] + [0]
        packed = pl.pallas_call(
            functools.partial(rest_kernel, peers, cap, others),
            out_shape=[piece] * len(others),
            in_specs=[SMEM, SMEM, HBM],
            out_specs=[VMEM] * len(others),
            scratch_shapes=[pltpu.SemaphoreType.DMA((len(others), cap))],
            cost_estimate=TINY,
            name="rest",
        )(source, fill, new_tiles)
        steps = order + [0]
        got = dict(zip(others, packed))
        got[lead] = out_piece
        got = {k: ring(got[k], k) if k else got[k] for k in steps}
        late = tuple(order[4:]) if peers > 4 else ()
        early = [k for k in steps if k not in late]
        arrived = [got[k] for k in steps]
        arrived_early = [got[k] for k in early]
        arrived_late = [got[k] for k in late]
        flag = got[lead]
        gathered = packed[-1]
    else:
        sent = pl.pallas_call(
            functools.partial(sorted_kernel, peers, cap),
            out_shape=shape((slots, half, BLK), BF16),
            in_specs=[SMEM, SMEM, HBM],
            out_specs=HBM,
            scratch_shapes=[pltpu.SemaphoreType.DMA((count,))],
            cost_estimate=TINY,
            name="rest",
        )(source, fill, new_tiles)
        sent = sent.reshape(peers, cap, half, BLK)
        got = lax.all_to_all(sent, PEERS, split_axis=0, concat_axis=0, tiled=True)
        arrived = [got.reshape(slots, half, BLK)]
        steps = early = None
        late = ()
        arrived_early, arrived_late = arrived, []
        flag = source
        gathered = out_piece

    codes = pl.pallas_call(
        functools.partial(label_kernel, peers, cap),
        out_shape=shape((peers * (cap + 1),), jnp.int32),
        in_specs=[SMEM] * 4 + [ANY],
        out_specs=SMEM,
        compiler_params=SMALL,
        cost_estimate=TINY,
        name="label",
    )(source, fill, row_block, block_offset, gathered)
    got_codes = lax.all_to_all(
        codes.reshape(peers, cap + 1), PEERS, split_axis=0, concat_axis=0, tiled=True
    ).reshape(peers * (cap + 1))

    sizes = (2 * nblk, 3 * nblk)
    counts = [pltpu.SMEM((size,), jnp.int32) for size in sizes]
    lists = []
    for size in sizes:
        lists += [shape((slots + size * QUAD,), jnp.int32), shape((size + 1,), jnp.int32)]
    by_row, row_at, by_side, side_at = pl.pallas_call(
        functools.partial(plan_kernel, peers, late, nblk),
        out_shape=lists,
        in_specs=[SMEM],
        out_specs=[SMEM] * 4,
        scratch_shapes=counts,
        compiler_params=SMALL,
        cost_estimate=TINY,
        name="plan",
    )(got_codes)

    blocks = (nblk, BLK, width)
    h_blocks, old_blocks = h_input.reshape(blocks), old_one.reshape(blocks)
    base_one, base_two = base_one.reshape(blocks), base_two.reshape(blocks)
    bases, halves = pl.pallas_call(
        functools.partial(turn_kernel, nblk),
        out_shape=[shape((2 * nblk, half, width), F32), shape((3 * nblk, half, width), BF16)],
        in_specs=[ANY] * 5,
        out_specs=[ANY] * 2,
        scratch_shapes=[pltpu.SemaphoreType.DMA((5,))],
        compiler_params=SMALL,
        cost_estimate=TINY,
        name="turn",
    )(h_blocks, base_one, base_two, old_blocks, gathered)
    bases, halves, _ = after((bases, halves, flag))
    bases, halves = swap(bases), swap(halves)
    h_later, _, by_row, by_side = after((h_blocks, flag, by_row, by_side))
    left, right = ring(h_later, 1), ring(h_later, peers - 1)
    left_twin, right_twin = swap(left), swap(right)

    tile_scratch = pltpu.VMEM((slots + 1, half, BLK), BF16)
    cell_shape = (3 * nblk, BLK, full)
    cell_scratch = pltpu.VMEM(cell_shape, BF16)
    mean_scratch = pltpu.VMEM((nblk, half, full), BF16)
    rows_shape = (nblk, half, full)
    total_scratch = pltpu.VMEM(rows_shape, F32)
    inv = inv_degree.reshape(nblk, BLK)

    many = len(arrived_early)
    agg_early, cells_one, own_one, base_two_rows, old_one_rows = pl.pallas_call(
        functools.partial(early_kernel, cap, early, many, nblk),
        out_shape=[
            shape(rows_shape, F32),
            shape(cell_shape, BF16),
            shape(rows_shape, F32),
            shape(rows_shape, F32),
            shape(rows_shape, BF16),
        ],
        in_specs=[SMEM] * 2 + [ANY] * (many + 10) + [VMEM] * 2,
        out_specs=[VMEM] * 5,
        scratch_shapes=[tile_scratch, pltpu.SemaphoreType.DMA((many + 13,))],
        compiler_params=PARAMS,
        cost_estimate=TINY,
        name="early",
    )(
        by_row,
        row_at,
        *arrived_early,
        left,
        left_twin,
        h_blocks,
        halves,
        right,
        right_twin,
        base_one,
        base_two,
        bases,
        old_blocks,
        self_one,
        bias_one.reshape(1, full),
    )

    many = len(arrived_late)
    hidden_rows = pl.pallas_call(
        functools.partial(late_kernel, cap, late, many, nblk),
        out_shape=shape(rows_shape, BF16),
        in_specs=[SMEM] * 3 + [ANY] * many + [VMEM] * 6,
        out_specs=VMEM,
        scratch_shapes=[
            tile_scratch,
            total_scratch,
            mean_scratch,
            pltpu.SemaphoreType.DMA((max(1, many),)),
        ],
        compiler_params=PARAMS,
        cost_estimate=TINY,
        name="late",
    )(
        by_row,
        row_at,
        affected_one,
        *arrived_late,
        cells_one,
        agg_early,
        inv,
        own_one,
        neigh_one,
        old_one_rows,
    )

    hidden_twin = swap(hidden_rows)
    left = ring(hidden_rows, 1)
    right = ring(hidden_rows, peers - 1)

    many = len(arrived)
    agg_two, own_two, hidden_one, tiles_all = pl.pallas_call(
        functools.partial(near_kernel, cap, steps, many, nblk),
        out_shape=[shape(rows_shape, F32)] * 2
        + [shape(blocks, BF16), shape((slots + 1, half, BLK), BF16)],
        in_specs=[SMEM] * 2 + [ANY] * (many + 2) + [VMEM] * 3,
        out_specs=[VMEM] * 2 + [ANY, VMEM],
        scratch_shapes=[cell_scratch, pltpu.SemaphoreType.DMA((many + 4,))],
        compiler_params=PARAMS,
        cost_estimate=TINY,
        name="near",
    )(
        by_side,
        side_at,
        *arrived,
        hidden_rows,
        hidden_twin,
        base_two_rows,
        self_two,
        bias_two.reshape(1, full),
    )

    left, right, agg_two, own_two = after((left, right, agg_two, own_two))
    left_twin = swap(left)
    right_twin = swap(right)
    kept, sent = pl.pallas_call(
        functools.partial(far_kernel, nblk),
        out_shape=[shape((nblk, half, width), BF16)] * 2,
        in_specs=[SMEM] * 2 + [VMEM] + [ANY] * 4 + [VMEM] * 4,
        out_specs=[VMEM] * 2,
        scratch_shapes=[
            cell_scratch,
            total_scratch,
            mean_scratch,
            pltpu.SemaphoreType.DMA((4,)),
        ],
        compiler_params=PARAMS,
        cost_estimate=TINY,
        name="far",
    )(
        by_side,
        side_at,
        tiles_all,
        left,
        left_twin,
        right,
        right_twin,
        agg_two,
        inv,
        own_two,
        neigh_two,
    )
    came = swap(sent)
    hidden_two = pl.pallas_call(
        functools.partial(finish_kernel, nblk),
        out_shape=shape(blocks, BF16),
        in_specs=[SMEM] + [VMEM] * 3,
        out_specs=VMEM,
        compiler_params=SMALL,
        cost_estimate=TINY,
        name="finish",
    )(affected_two, kept, came, old_two.reshape(blocks))
    return (hidden_one.reshape(rows_here, width), hidden_two.reshape(rows_here, width))


def solution(mesh):
    rows = P(("groups", "rows", "feat"))
    cells = P(("groups", "rows", "feat"), "sub")
    placed = (
        cells,
        rows,
        P(("groups", "rows", "feat"), None),
        rows,
        rows,
        P(("groups", "rows", "feat"), None, None),
        cells,
        rows,
        cells,
        P(),
        P(),
        P(),
        cells,
        rows,
        cells,
        P(),
        P(),
        P(),
    )
    return jax.shard_map(
        on_device, mesh=mesh, in_specs=placed, out_specs=(cells, cells), check_vma=False
    )
```

```python
import functools

import jax
import jax.numpy as jnp
from jax import lax
from jax.experimental import pallas as pl
from jax.experimental.pallas import tpu as pltpu
from jax.sharding import PartitionSpec as P

PEERS = ("rows", "feat")
BLK = 128
QUAD = 4
F32 = jnp.float32
BF16 = jnp.bfloat16
ANY = pl.BlockSpec(memory_space=pl.ANY)
HBM = pl.BlockSpec(memory_space=pltpu.HBM)
SMEM = pl.BlockSpec(memory_space=pltpu.SMEM)
VMEM = pl.BlockSpec(memory_space=pltpu.VMEM)
PARAMS = pltpu.CompilerParams(vmem_limit_bytes=20 * 1024 * 1024)
SMALL = pltpu.CompilerParams(vmem_limit_bytes=4 * 1024 * 1024)
TINY = pl.CostEstimate(flops=0, bytes_accessed=128, transcendentals=0)


def first_kernel(peers, cap, lead, dest, tiles, out, source, fill, sem):
    count = dest.shape[0]
    half = out.shape[1]
    me = lax.axis_index(PEERS)
    first = pl.multiple_of(lax.axis_index("sub") * half, half)
    for to in range(min(peers, 16)):
        fill[to] = 0
    if peers > 16:

        def clear(i, _):
            fill[i] = 0
            return 0

        lax.fori_loop(16, peers, clear, 0)
    for t in range(count):
        to = dest[t]
        at = fill[to]
        fill[to] = at + 1
        source[to * cap + at] = t
    if lead is None:
        return
    to = lax.rem(me + lead, peers)

    def send(j, _):
        t = source[to * cap + j]
        pltpu.make_async_copy(tiles.at[t, pl.ds(first, half)], out.at[j], sem.at[j]).start()
        return 0

    def finish(j, _):
        pltpu.make_async_copy(tiles.at[0, pl.ds(first, half)], out.at[0], sem.at[j]).wait()
        return 0

    lax.fori_loop(0, fill[to], send, 0)
    lax.fori_loop(0, fill[to], finish, 0)


def rest_kernel(peers, cap, order, source, fill, tiles, *refs):
    outs, sems = refs[:-1], refs[-1]
    half = outs[0].shape[1]
    me = lax.axis_index(PEERS)
    first = pl.multiple_of(lax.axis_index("sub") * half, half)
    begun = []
    for n, k in enumerate(order):
        to = lax.rem(me + k, peers)

        def send(j, _, n=n, to=to):
            t = source[to * cap + j]
            pltpu.make_async_copy(
                tiles.at[t, pl.ds(first, half)], outs[n].at[j], sems.at[n, j]
            ).start()
            return 0

        lax.fori_loop(0, fill[to], send, 0)
        begun.append(fill[to])
    for n, amount in enumerate(begun):

        def finish(j, _, n=n):
            pltpu.make_async_copy(
                tiles.at[0, pl.ds(first, half)], outs[n].at[0], sems.at[n, j]
            ).wait()
            return 0

        lax.fori_loop(0, amount, finish, 0)


def sorted_kernel(peers, cap, source, fill, tiles, out, sems):
    half = out.shape[1]
    first = pl.multiple_of(lax.axis_index("sub") * half, half)

    def each(act):
        def peer(to, _):
            def slot(j, _):
                at = to * cap + j
                act(source[at], at)
                return 0

            return lax.fori_loop(0, fill[to], slot, 0)

        lax.fori_loop(0, peers, peer, 0)

    def copy(t, at):
        return pltpu.make_async_copy(tiles.at[t, pl.ds(first, half)], out.at[at], sems.at[t])

    each(lambda t, at: copy(t, at).start())
    each(lambda t, at: copy(t, at).wait())


def label_kernel(peers, cap, source, fill, row, off, codes):
    def peer(to, _):
        def slot(j, _):
            t = source[to * cap + j]
            codes[to * (cap + 1) + j] = row[t] * 32 + off[t] + 8
            return 0

        lax.fori_loop(0, fill[to], slot, 0)
        codes[to * (cap + 1) + cap] = fill[to]
        return 0

    lax.fori_loop(0, peers, peer, 0)


def turn_kernel(nblk, h, base_one, base_two, old, after, bases, halves, sems):
    half = bases.shape[1]
    other = pl.ds(pl.multiple_of((1 - lax.axis_index("sub")) * half, half), half)
    copies = [
        pltpu.make_async_copy(base_one.at[:, other], bases.at[pl.ds(0, nblk)], sems.at[0]),
        pltpu.make_async_copy(base_two.at[:, other], bases.at[pl.ds(nblk, nblk)], sems.at[1]),
        pltpu.make_async_copy(h.at[:, pl.ds(0, half)], halves.at[pl.ds(0, nblk)], sems.at[2]),
        pltpu.make_async_copy(
            h.at[:, pl.ds(half, half)], halves.at[pl.ds(nblk, nblk)], sems.at[3]
        ),
        pltpu.make_async_copy(old.at[:, other], halves.at[pl.ds(2 * nblk, nblk)], sems.at[4]),
    ]
    for copy in copies:
        copy.start()
    for copy in copies:
        copy.wait()


def plan_kernel(peers, late, nblk, codes, by_row, row_at, by_side, side_at, fill_row, fill_side):
    cap = codes.shape[0] // peers - 1
    nothing = peers * cap * 32 + nblk
    me = lax.axis_index(PEERS)
    for fill in (fill_row, fill_side):
        for g in range(fill.shape[0]):
            fill[g] = 0

    def walk(act):
        def peer(origin, _):
            behind = jnp.int32(0)
            step = lax.rem(me + peers - origin, peers)
            for k in late:
                behind = behind + jnp.where(step == k, nblk, 0)

            def slot(j, _):
                code = codes[origin * (cap + 1) + j]
                row = code >> 5
                col = row + (code & 31)
                side = jnp.where(col < nblk, nblk, jnp.where(col < 2 * nblk, 0, 2 * nblk))
                act(row + behind, row + side, (row << 16) + (origin * cap + j) * 32 + col)
                return 0

            return lax.fori_loop(0, codes[origin * (cap + 1) + cap], slot, 0)

        lax.fori_loop(0, peers, peer, 0)

    def tally(row, side, entry):
        fill_row[row] = fill_row[row] + 1
        fill_side[side] = fill_side[side] + 1

    def place(row, side, entry):
        to = fill_row[row]
        by_row[to] = entry
        fill_row[row] = to + 1
        to = fill_side[side]
        by_side[to] = entry
        fill_side[side] = to + 1

    walk(tally)
    for fill, at, listed in ((fill_row, row_at, by_row), (fill_side, side_at, by_side)):
        now = jnp.int32(0)
        for g in range(fill.shape[0]):
            at[g] = now
            need = (fill[g] + QUAD - 1) // QUAD
            fill[g] = now * QUAD
            now = now + need
            last = jnp.maximum(now * QUAD - QUAD, 0)
            for u in range(QUAD):
                listed[last + u] = nothing + ((g % nblk) << 16)
        at[fill.shape[0]] = now
    walk(place)


def tile_copies(cap, steps, arrived, tiles, sems):
    if steps is None:
        whole = tiles.at[pl.ds(0, arrived[0].shape[0])]
        return [pltpu.make_async_copy(arrived[0], whole, sems.at[0])]
    me = lax.axis_index(PEERS)
    peers = lax.axis_size(PEERS)
    copies = []
    for n, (k, ref) in enumerate(zip(steps, arrived)):
        origin = lax.rem(me + peers - k, peers)
        copies.append(pltpu.make_async_copy(ref, tiles.at[pl.ds(origin * cap, cap)], sems.at[n]))
    return copies


def tile_sums(order, begin, end, tiles, cells, total):
    nothing = (tiles.shape[0] - 1) * 32 + cells.shape[0] // 3

    def step(n, _):
        for q in (begin + 2 * n, begin + 2 * n + 1):
            entry = [jnp.where(q < end, order[q * QUAD + u], nothing) for u in range(QUAD)]
            row = entry[0] >> 16
            tile = [(e >> 5) & 2047 for e in entry]
            cell = [e & 31 for e in entry]
            acc = None
            for u in range(0, QUAD, 2):
                weights = jnp.concatenate([tiles[tile[u]], tiles[tile[u + 1]]], axis=1)
                chosen = jnp.concatenate([cells[cell[u]], cells[cell[u + 1]]], axis=0)
                part = jnp.dot(weights, chosen, preferred_element_type=F32)
                acc = part if acc is None else acc + part
            total[row] = total[row] + acc
        return 0

    lax.fori_loop(0, (end - begin + 1) >> 1, step, 0)


def early_kernel(cap, steps, pieces, nblk, order, at, *refs):
    arrived = refs[:pieces]
    (left, left_twin, h, halves, right, right_twin, base_one, base_two, bases, old) = refs[
        pieces : pieces + 10
    ]
    w_self, bias, agg, cells, own, base_rows, old_rows, tiles, sems = refs[pieces + 10 :]
    sub = lax.axis_index("sub")
    half = agg.shape[1]
    width = h.shape[2]
    lanes = pl.ds(pl.multiple_of(sub * width, width), width)
    others = pl.ds(pl.multiple_of((1 - sub) * width, width), width)
    lines = pl.ds(pl.multiple_of(sub * half, half), half)
    block = [pl.ds(k * nblk, nblk) for k in range(3)]
    low, high = pl.ds(0, half), pl.ds(half, half)
    moves = [
        (left, cells.at[block[0], :, lanes]),
        (left_twin, cells.at[block[0], :, others]),
        (h, cells.at[block[1], :, lanes]),
        (halves.at[block[0]], cells.at[block[1], low, others]),
        (halves.at[block[1]], cells.at[block[1], high, others]),
        (right, cells.at[block[2], :, lanes]),
        (right_twin, cells.at[block[2], :, others]),
        (base_one.at[:, lines], agg.at[:, :, lanes]),
        (bases.at[block[0]], agg.at[:, :, others]),
        (base_two.at[:, lines], base_rows.at[:, :, lanes]),
        (bases.at[block[1]], base_rows.at[:, :, others]),
        (old.at[:, lines], old_rows.at[:, :, lanes]),
        (halves.at[block[2]], old_rows.at[:, :, others]),
    ]
    copies = tile_copies(cap, steps, arrived, tiles, sems)
    for k, (src, dst) in enumerate(moves):
        copies.append(pltpu.make_async_copy(src, dst, sems.at[pieces + k]))
    for copy in copies:
        copy.start()
    tiles[tiles.shape[0] - 1] = jnp.zeros(tiles.shape[1:], tiles.dtype)
    for copy in copies:
        copy.wait()
    tile_sums(order, at[0], at[nblk], tiles, cells, agg)
    for r in range(nblk):
        own[r] = (
            jnp.dot(cells[nblk + r, lines], w_self[...], preferred_element_type=F32) + bias[...]
        )


def column(inv, r, sub, half):
    shape = (half, inv.shape[1])
    line = lax.broadcasted_iota(jnp.int32, shape, 0) + sub * half
    lane = lax.broadcasted_iota(jnp.int32, shape, 1)
    spread = jnp.broadcast_to(inv[r : r + 1, :], shape)
    return jnp.sum(jnp.where(line == lane, spread, 0.0), axis=1, keepdims=True)


def late_kernel(cap, steps, pieces, nblk, order, at, affected, *refs):
    arrived = refs[:pieces]
    cells, agg, inv, own, w_neigh, old, out, tiles, total, means, sems = refs[pieces:]
    half = agg.shape[1]
    sub = lax.axis_index("sub")
    copies = tile_copies(cap, steps, arrived, tiles, sems) if pieces else []
    for copy in copies:
        copy.start()
    tiles[tiles.shape[0] - 1] = jnp.zeros(tiles.shape[1:], tiles.dtype)
    for r in range(nblk):
        total[r] = agg[r]
    for copy in copies:
        copy.wait()
    tile_sums(order, at[nblk], at[2 * nblk], tiles, cells, total)
    for r in range(nblk):
        means[r] = (total[r] * column(inv, r, sub, half)).astype(BF16)
    for r in range(nblk):
        pre = own[r] + jnp.dot(means[r], w_neigh[...], preferred_element_type=F32)
        pre = jnp.maximum(pre, 0.0)
        keep = jnp.full((half, 1), affected[r], jnp.int32) > 0
        out[r] = jnp.where(keep, pre, old[r].astype(F32)).astype(BF16)


def near_kernel(cap, steps, pieces, nblk, order, at, *refs):
    arrived = refs[:pieces]
    mine, twin, base, w_self, bias, agg, own, hidden, tiles, cells, sems = refs[pieces:]
    half = base.shape[1]
    width = hidden.shape[2]
    sub = lax.axis_index("sub")
    lanes = pl.ds(pl.multiple_of(sub * width, width), width)
    copies = tile_copies(cap, steps, arrived, tiles, sems)
    for k, (ref, side) in enumerate(((mine, sub), (twin, 1 - sub))):
        lines = pl.ds(pl.multiple_of(side * half, half), half)
        to = cells.at[pl.ds(nblk, nblk), lines]
        copies.append(pltpu.make_async_copy(ref, to, sems.at[pieces + k]))
        to = hidden.at[:, lines]
        copies.append(pltpu.make_async_copy(ref.at[:, :, lanes], to, sems.at[pieces + 2 + k]))
    for copy in copies:
        copy.start()
    tiles[tiles.shape[0] - 1] = jnp.zeros(tiles.shape[1:], tiles.dtype)
    for r in range(nblk):
        agg[r] = base[r]
    for copy in copies:
        copy.wait()
    tile_sums(order, at[0], at[nblk], tiles, cells, agg)
    mine_rows = pl.ds(pl.multiple_of(sub * half, half), half)
    for r in range(nblk):
        own[r] = (
            jnp.dot(cells[nblk + r, mine_rows], w_self[...], preferred_element_type=F32) + bias[...]
        )


def far_kernel(nblk, order, at, tiles, left, left_twin, right, right_twin, *refs):
    agg, inv, own, w_neigh, keep, send, cells, total, means, sems = refs
    half = agg.shape[1]
    width = keep.shape[2]
    sub = lax.axis_index("sub")
    sides = ((left, 0, sub), (left_twin, 0, 1 - sub), (right, 2, sub), (right_twin, 2, 1 - sub))
    copies = []
    for k, (ref, third, side) in enumerate(sides):
        lines = pl.ds(pl.multiple_of(side * half, half), half)
        to = cells.at[pl.ds(third * nblk, nblk), lines]
        copies.append(pltpu.make_async_copy(ref, to, sems.at[k]))
    for copy in copies:
        copy.start()
    cells[nblk] = jnp.zeros(cells.shape[1:], cells.dtype)
    for r in range(nblk):
        total[r] = agg[r]
    for copy in copies:
        copy.wait()
    tile_sums(order, at[nblk], at[3 * nblk], tiles, cells, total)
    for r in range(nblk):
        means[r] = (total[r] * column(inv, r, sub, half)).astype(BF16)
    for r in range(nblk):
        pre = own[r] + jnp.dot(means[r], w_neigh[...], preferred_element_type=F32)
        low = pre[:, :width]
        high = pre[:, width:]
        first = jnp.full((half, 1), sub, jnp.int32) == 0
        keep[r] = jnp.where(first, low, high).astype(BF16)
        send[r] = jnp.where(first, high, low).astype(BF16)


def finish_kernel(nblk, affected, kept, came, old, out):
    half = kept.shape[1]
    first = jnp.full((half, 1), lax.axis_index("sub"), jnp.int32) == 0
    for r in range(nblk):
        keep = jnp.full((half, 1), affected[r], jnp.int32) > 0
        low = jnp.where(first, kept[r].astype(F32), came[r].astype(F32))
        high = jnp.where(first, came[r].astype(F32), kept[r].astype(F32))
        out[r, :half] = jnp.where(keep, low, old[r, :half].astype(F32)).astype(BF16)
        out[r, half:] = jnp.where(keep, high, old[r, half:].astype(F32)).astype(BF16)


def swap(x):
    return lax.ppermute(x, "sub", [(0, 1), (1, 0)])


def ring(x, step):
    peers = lax.axis_size(PEERS)
    return lax.ppermute(x, PEERS, [(i, (i + step) % peers) for i in range(peers)])


def on_device(
    h_input,
    inv_degree,
    dest_block,
    row_block,
    block_offset,
    new_tiles,
    base_one,
    affected_one,
    old_one,
    self_one,
    neigh_one,
    bias_one,
    base_two,
    affected_two,
    old_two,
    self_two,
    neigh_two,
    bias_two,
):
    peers = lax.axis_size(PEERS)
    count = dest_block.shape[0]
    cap = max(2, 2 * count // peers)
    slots = peers * cap
    rows_here, width = h_input.shape
    full = width * lax.axis_size("sub")
    nblk = rows_here // BLK
    half = BLK // lax.axis_size("sub")
    direct = 2 < peers <= 16
    shape = jax.ShapeDtypeStruct
    after = lax.optimization_barrier

    order = sorted(range(1, peers), key=lambda k: (abs(k - peers // 2), k))
    lead = order[0] if direct else None
    piece = shape((cap, half, BLK), BF16)
    out_piece, source, fill = pl.pallas_call(
        functools.partial(first_kernel, peers, cap, lead),
        out_shape=[piece, shape((slots,), jnp.int32), shape((peers,), jnp.int32)],
        in_specs=[SMEM, HBM],
        out_specs=[VMEM, SMEM, SMEM],
        scratch_shapes=[pltpu.SemaphoreType.DMA((cap,))],
        cost_estimate=TINY,
        name="first",
    )(dest_block.reshape(count), new_tiles)

    if direct:
        others = order[1:] + [0]
        packed = pl.pallas_call(
            functools.partial(rest_kernel, peers, cap, others),
            out_shape=[piece] * len(others),
            in_specs=[SMEM, SMEM, HBM],
            out_specs=[VMEM] * len(others),
            scratch_shapes=[pltpu.SemaphoreType.DMA((len(others), cap))],
            cost_estimate=TINY,
            name="rest",
        )(source, fill, new_tiles)
        steps = order + [0]
        got = dict(zip(others, packed))
        got[lead] = out_piece
        got = {k: ring(got[k], k) if k else got[k] for k in steps}
        late = tuple(order[4:]) if peers > 4 else ()
        early = [k for k in steps if k not in late]
        arrived = [got[k] for k in steps]
        arrived_early = [got[k] for k in early]
        arrived_late = [got[k] for k in late]
        flag = got[lead]
        gathered = packed[-1]
    else:
        sent = pl.pallas_call(
            functools.partial(sorted_kernel, peers, cap),
            out_shape=shape((slots, half, BLK), BF16),
            in_specs=[SMEM, SMEM, HBM],
            out_specs=HBM,
            scratch_shapes=[pltpu.SemaphoreType.DMA((count,))],
            cost_estimate=TINY,
            name="rest",
        )(source, fill, new_tiles)
        sent = sent.reshape(peers, cap, half, BLK)
        got = lax.all_to_all(sent, PEERS, split_axis=0, concat_axis=0, tiled=True)
        arrived = [got.reshape(slots, half, BLK)]
        steps = early = None
        late = ()
        arrived_early, arrived_late = arrived, []
        flag = source
        gathered = out_piece

    codes = pl.pallas_call(
        functools.partial(label_kernel, peers, cap),
        out_shape=shape((peers * (cap + 1),), jnp.int32),
        in_specs=[SMEM] * 4,
        out_specs=SMEM,
        compiler_params=SMALL,
        cost_estimate=TINY,
        name="label",
    )(source, fill, row_block, block_offset)
    got_codes = lax.all_to_all(
        codes.reshape(peers, cap + 1), PEERS, split_axis=0, concat_axis=0, tiled=True
    ).reshape(peers * (cap + 1))

    sizes = (2 * nblk, 3 * nblk)
    counts = [pltpu.SMEM((size,), jnp.int32) for size in sizes]
    lists = []
    for size in sizes:
        lists += [shape((slots + size * QUAD,), jnp.int32), shape((size + 1,), jnp.int32)]
    by_row, row_at, by_side, side_at = pl.pallas_call(
        functools.partial(plan_kernel, peers, late, nblk),
        out_shape=lists,
        in_specs=[SMEM],
        out_specs=[SMEM] * 4,
        scratch_shapes=counts,
        compiler_params=SMALL,
        cost_estimate=TINY,
        name="plan",
    )(got_codes)

    blocks = (nblk, BLK, width)
    h_blocks, old_blocks = h_input.reshape(blocks), old_one.reshape(blocks)
    base_one, base_two = base_one.reshape(blocks), base_two.reshape(blocks)
    bases, halves = pl.pallas_call(
        functools.partial(turn_kernel, nblk),
        out_shape=[shape((2 * nblk, half, width), F32), shape((3 * nblk, half, width), BF16)],
        in_specs=[ANY] * 5,
        out_specs=[ANY] * 2,
        scratch_shapes=[pltpu.SemaphoreType.DMA((5,))],
        compiler_params=SMALL,
        cost_estimate=TINY,
        name="turn",
    )(h_blocks, base_one, base_two, old_blocks, gathered)
    bases, halves, _ = after((bases, halves, flag))
    bases, halves = swap(bases), swap(halves)
    h_later, _, by_row, by_side = after((h_blocks, flag, by_row, by_side))
    left, right = ring(h_later, 1), ring(h_later, peers - 1)
    left_twin, right_twin = swap(left), swap(right)

    tile_scratch = pltpu.VMEM((slots + 1, half, BLK), BF16)
    cell_shape = (3 * nblk, BLK, full)
    cell_scratch = pltpu.VMEM(cell_shape, BF16)
    mean_scratch = pltpu.VMEM((nblk, half, full), BF16)
    rows_shape = (nblk, half, full)
    total_scratch = pltpu.VMEM(rows_shape, F32)
    inv = inv_degree.reshape(nblk, BLK)

    many = len(arrived_early)
    agg_early, cells_one, own_one, base_two_rows, old_one_rows = pl.pallas_call(
        functools.partial(early_kernel, cap, early, many, nblk),
        out_shape=[
            shape(rows_shape, F32),
            shape(cell_shape, BF16),
            shape(rows_shape, F32),
            shape(rows_shape, F32),
            shape(rows_shape, BF16),
        ],
        in_specs=[SMEM] * 2 + [ANY] * (many + 10) + [VMEM] * 2,
        out_specs=[VMEM] * 5,
        scratch_shapes=[tile_scratch, pltpu.SemaphoreType.DMA((many + 13,))],
        compiler_params=PARAMS,
        cost_estimate=TINY,
        name="early",
    )(
        by_row,
        row_at,
        *arrived_early,
        left,
        left_twin,
        h_blocks,
        halves,
        right,
        right_twin,
        base_one,
        base_two,
        bases,
        old_blocks,
        self_one,
        bias_one.reshape(1, full),
    )

    many = len(arrived_late)
    hidden_rows = pl.pallas_call(
        functools.partial(late_kernel, cap, late, many, nblk),
        out_shape=shape(rows_shape, BF16),
        in_specs=[SMEM] * 3 + [ANY] * many + [VMEM] * 6,
        out_specs=VMEM,
        scratch_shapes=[
            tile_scratch,
            total_scratch,
            mean_scratch,
            pltpu.SemaphoreType.DMA((max(1, many),)),
        ],
        compiler_params=PARAMS,
        cost_estimate=TINY,
        name="late",
    )(
        by_row,
        row_at,
        affected_one,
        *arrived_late,
        cells_one,
        agg_early,
        inv,
        own_one,
        neigh_one,
        old_one_rows,
    )

    hidden_twin = swap(hidden_rows)
    left = ring(hidden_rows, 1)
    right = ring(hidden_rows, peers - 1)

    many = len(arrived)
    agg_two, own_two, hidden_one, tiles_all = pl.pallas_call(
        functools.partial(near_kernel, cap, steps, many, nblk),
        out_shape=[shape(rows_shape, F32)] * 2
        + [shape(blocks, BF16), shape((slots + 1, half, BLK), BF16)],
        in_specs=[SMEM] * 2 + [ANY] * (many + 2) + [VMEM] * 3,
        out_specs=[VMEM] * 2 + [ANY, VMEM],
        scratch_shapes=[cell_scratch, pltpu.SemaphoreType.DMA((many + 4,))],
        compiler_params=PARAMS,
        cost_estimate=TINY,
        name="near",
    )(
        by_side,
        side_at,
        *arrived,
        hidden_rows,
        hidden_twin,
        base_two_rows,
        self_two,
        bias_two.reshape(1, full),
    )

    left, right, agg_two, own_two = after((left, right, agg_two, own_two))
    left_twin = swap(left)
    right_twin = swap(right)
    kept, sent = pl.pallas_call(
        functools.partial(far_kernel, nblk),
        out_shape=[shape((nblk, half, width), BF16)] * 2,
        in_specs=[SMEM] * 2 + [VMEM] + [ANY] * 4 + [VMEM] * 4,
        out_specs=[VMEM] * 2,
        scratch_shapes=[
            cell_scratch,
            total_scratch,
            mean_scratch,
            pltpu.SemaphoreType.DMA((4,)),
        ],
        compiler_params=PARAMS,
        cost_estimate=TINY,
        name="far",
    )(
        by_side,
        side_at,
        tiles_all,
        left,
        left_twin,
        right,
        right_twin,
        agg_two,
        inv,
        own_two,
        neigh_two,
    )
    came = swap(sent)
    hidden_two = pl.pallas_call(
        functools.partial(finish_kernel, nblk),
        out_shape=shape(blocks, BF16),
        in_specs=[SMEM] + [VMEM] * 3,
        out_specs=VMEM,
        compiler_params=SMALL,
        cost_estimate=TINY,
        name="finish",
    )(affected_two, kept, came, old_two.reshape(blocks))
    return (hidden_one.reshape(rows_here, width), hidden_two.reshape(rows_here, width))


def solution(mesh):
    rows = P(("groups", "rows", "feat"))
    cells = P(("groups", "rows", "feat"), "sub")
    placed = (
        cells,
        rows,
        P(("groups", "rows", "feat"), None),
        rows,
        rows,
        P(("groups", "rows", "feat"), None, None),
        cells,
        rows,
        cells,
        P(),
        P(),
        P(),
        cells,
        rows,
        cells,
        P(),
        P(),
        P(),
    )
    return jax.shard_map(
        on_device, mesh=mesh, in_specs=placed, out_specs=(cells, cells), check_vma=False
    )
```

```python
import functools

import jax
import jax.numpy as jnp
from jax import lax
from jax.experimental import pallas as pl
from jax.experimental.pallas import tpu as pltpu
from jax.sharding import PartitionSpec as P

PEERS = ("rows", "feat")
BLK = 128
QUAD = 4
F32 = jnp.float32
BF16 = jnp.bfloat16
ANY = pl.BlockSpec(memory_space=pl.ANY)
HBM = pl.BlockSpec(memory_space=pltpu.HBM)
SMEM = pl.BlockSpec(memory_space=pltpu.SMEM)
VMEM = pl.BlockSpec(memory_space=pltpu.VMEM)
PARAMS = pltpu.CompilerParams(vmem_limit_bytes=20 * 1024 * 1024)
SMALL = pltpu.CompilerParams(vmem_limit_bytes=4 * 1024 * 1024)
TINY = pl.CostEstimate(flops=0, bytes_accessed=128, transcendentals=0)


def first_kernel(peers, cap, lead, dest, tiles, out, source, fill, sem):
    count = dest.shape[0]
    half = out.shape[1]
    me = lax.axis_index(PEERS)
    first = pl.multiple_of(lax.axis_index("sub") * half, half)
    for to in range(min(peers, 16)):
        fill[to] = 0
    if peers > 16:

        def clear(i, _):
            fill[i] = 0
            return 0

        lax.fori_loop(16, peers, clear, 0)
    for t in range(count):
        to = dest[t]
        at = fill[to]
        fill[to] = at + 1
        source[to * cap + at] = t
    if lead is None:
        return
    to = lax.rem(me + lead, peers)

    def send(j, _):
        t = source[to * cap + j]
        pltpu.make_async_copy(tiles.at[t, pl.ds(first, half)], out.at[j], sem.at[j]).start()
        return 0

    def finish(j, _):
        pltpu.make_async_copy(tiles.at[0, pl.ds(first, half)], out.at[0], sem.at[j]).wait()
        return 0

    lax.fori_loop(0, fill[to], send, 0)
    lax.fori_loop(0, fill[to], finish, 0)


def rest_kernel(peers, cap, order, source, fill, tiles, *refs):
    outs, sems = refs[:-1], refs[-1]
    half = outs[0].shape[1]
    me = lax.axis_index(PEERS)
    first = pl.multiple_of(lax.axis_index("sub") * half, half)
    begun = []
    for n, k in enumerate(order):
        to = lax.rem(me + k, peers)

        def send(j, _, n=n, to=to):
            t = source[to * cap + j]
            pltpu.make_async_copy(
                tiles.at[t, pl.ds(first, half)], outs[n].at[j], sems.at[n, j]
            ).start()
            return 0

        lax.fori_loop(0, fill[to], send, 0)
        begun.append(fill[to])
    for n, amount in enumerate(begun):

        def finish(j, _, n=n):
            pltpu.make_async_copy(
                tiles.at[0, pl.ds(first, half)], outs[n].at[0], sems.at[n, j]
            ).wait()
            return 0

        lax.fori_loop(0, amount, finish, 0)


def sorted_kernel(peers, cap, source, fill, tiles, out, sems):
    half = out.shape[1]
    first = pl.multiple_of(lax.axis_index("sub") * half, half)

    def each(act):
        def peer(to, _):
            def slot(j, _):
                at = to * cap + j
                act(source[at], at)
                return 0

            return lax.fori_loop(0, fill[to], slot, 0)

        lax.fori_loop(0, peers, peer, 0)

    def copy(t, at):
        return pltpu.make_async_copy(tiles.at[t, pl.ds(first, half)], out.at[at], sems.at[t])

    each(lambda t, at: copy(t, at).start())
    each(lambda t, at: copy(t, at).wait())


def label_kernel(peers, cap, source, fill, row, off, codes):
    def peer(to, _):
        def slot(j, _):
            t = source[to * cap + j]
            codes[to * (cap + 1) + j] = row[t] * 32 + off[t] + 8
            return 0

        lax.fori_loop(0, fill[to], slot, 0)
        codes[to * (cap + 1) + cap] = fill[to]
        return 0

    lax.fori_loop(0, peers, peer, 0)


def turn_kernel(nblk, h, base_one, base_two, old, after, bases, halves, sems):
    half = bases.shape[1]
    other = pl.ds(pl.multiple_of((1 - lax.axis_index("sub")) * half, half), half)
    copies = [
        pltpu.make_async_copy(base_one.at[:, other], bases.at[pl.ds(0, nblk)], sems.at[0]),
        pltpu.make_async_copy(base_two.at[:, other], bases.at[pl.ds(nblk, nblk)], sems.at[1]),
        pltpu.make_async_copy(h.at[:, pl.ds(0, half)], halves.at[pl.ds(0, nblk)], sems.at[2]),
        pltpu.make_async_copy(
            h.at[:, pl.ds(half, half)], halves.at[pl.ds(nblk, nblk)], sems.at[3]
        ),
        pltpu.make_async_copy(old.at[:, other], halves.at[pl.ds(2 * nblk, nblk)], sems.at[4]),
    ]
    for copy in copies:
        copy.start()
    for copy in copies:
        copy.wait()


def plan_kernel(peers, late, nblk, codes, by_row, row_at, by_side, side_at, fill_row, fill_side):
    cap = codes.shape[0] // peers - 1
    nothing = peers * cap * 32 + nblk
    me = lax.axis_index(PEERS)
    for fill in (fill_row, fill_side):
        for g in range(fill.shape[0]):
            fill[g] = 0

    def walk(act):
        def peer(origin, _):
            behind = jnp.int32(0)
            step = lax.rem(me + peers - origin, peers)
            for k in late:
                behind = behind + jnp.where(step == k, nblk, 0)

            def slot(j, _):
                code = codes[origin * (cap + 1) + j]
                row = code >> 5
                col = row + (code & 31)
                side = jnp.where(col < nblk, nblk, jnp.where(col < 2 * nblk, 0, 2 * nblk))
                act(row + behind, row + side, (row << 16) + (origin * cap + j) * 32 + col)
                return 0

            return lax.fori_loop(0, codes[origin * (cap + 1) + cap], slot, 0)

        lax.fori_loop(0, peers, peer, 0)

    def tally(row, side, entry):
        fill_row[row] = fill_row[row] + 1
        fill_side[side] = fill_side[side] + 1

    def place(row, side, entry):
        to = fill_row[row]
        by_row[to] = entry
        fill_row[row] = to + 1
        to = fill_side[side]
        by_side[to] = entry
        fill_side[side] = to + 1

    walk(tally)
    for fill, at, listed in ((fill_row, row_at, by_row), (fill_side, side_at, by_side)):
        now = jnp.int32(0)
        for g in range(fill.shape[0]):
            at[g] = now
            need = (fill[g] + QUAD - 1) // QUAD
            fill[g] = now * QUAD
            now = now + need
            last = jnp.maximum(now * QUAD - QUAD, 0)
            for u in range(QUAD):
                listed[last + u] = nothing + ((g % nblk) << 16)
        at[fill.shape[0]] = now
    walk(place)


def tile_copies(cap, steps, arrived, tiles, sems):
    if steps is None:
        whole = tiles.at[pl.ds(0, arrived[0].shape[0])]
        return [pltpu.make_async_copy(arrived[0], whole, sems.at[0])]
    me = lax.axis_index(PEERS)
    peers = lax.axis_size(PEERS)
    copies = []
    for n, (k, ref) in enumerate(zip(steps, arrived)):
        origin = lax.rem(me + peers - k, peers)
        copies.append(pltpu.make_async_copy(ref, tiles.at[pl.ds(origin * cap, cap)], sems.at[n]))
    return copies


def tile_sums(order, begin, end, tiles, cells, total):
    nothing = (tiles.shape[0] - 1) * 32 + cells.shape[0] // 3

    def step(n, _):
        for q in (begin + 2 * n, begin + 2 * n + 1):
            entry = [jnp.where(q < end, order[q * QUAD + u], nothing) for u in range(QUAD)]
            row = entry[0] >> 16
            tile = [(e >> 5) & 2047 for e in entry]
            cell = [e & 31 for e in entry]
            acc = None
            for u in range(0, QUAD, 2):
                weights = jnp.concatenate([tiles[tile[u]], tiles[tile[u + 1]]], axis=1)
                chosen = jnp.concatenate([cells[cell[u]], cells[cell[u + 1]]], axis=0)
                part = jnp.dot(weights, chosen, preferred_element_type=F32)
                acc = part if acc is None else acc + part
            total[row] = total[row] + acc
        return 0

    lax.fori_loop(0, (end - begin + 1) >> 1, step, 0)


def early_kernel(cap, steps, pieces, nblk, order, at, *refs):
    arrived = refs[:pieces]
    (left, left_twin, h, halves, right, right_twin, base_one, base_two, bases, old) = refs[
        pieces : pieces + 10
    ]
    w_self, bias, agg, cells, own, base_rows, old_rows, tiles, sems = refs[pieces + 10 :]
    sub = lax.axis_index("sub")
    half = agg.shape[1]
    width = h.shape[2]
    lanes = pl.ds(pl.multiple_of(sub * width, width), width)
    others = pl.ds(pl.multiple_of((1 - sub) * width, width), width)
    lines = pl.ds(pl.multiple_of(sub * half, half), half)
    block = [pl.ds(k * nblk, nblk) for k in range(3)]
    low, high = pl.ds(0, half), pl.ds(half, half)
    moves = [
        (left, cells.at[block[0], :, lanes]),
        (left_twin, cells.at[block[0], :, others]),
        (h, cells.at[block[1], :, lanes]),
        (halves.at[block[0]], cells.at[block[1], low, others]),
        (halves.at[block[1]], cells.at[block[1], high, others]),
        (right, cells.at[block[2], :, lanes]),
        (right_twin, cells.at[block[2], :, others]),
        (base_one.at[:, lines], agg.at[:, :, lanes]),
        (bases.at[block[0]], agg.at[:, :, others]),
        (base_two.at[:, lines], base_rows.at[:, :, lanes]),
        (bases.at[block[1]], base_rows.at[:, :, others]),
        (old.at[:, lines], old_rows.at[:, :, lanes]),
        (halves.at[block[2]], old_rows.at[:, :, others]),
    ]
    copies = tile_copies(cap, steps, arrived, tiles, sems)
    for k, (src, dst) in enumerate(moves):
        copies.append(pltpu.make_async_copy(src, dst, sems.at[pieces + k]))
    for copy in copies:
        copy.start()
    tiles[tiles.shape[0] - 1] = jnp.zeros(tiles.shape[1:], tiles.dtype)
    for copy in copies:
        copy.wait()
    tile_sums(order, at[0], at[nblk], tiles, cells, agg)
    for r in range(nblk):
        own[r] = (
            jnp.dot(cells[nblk + r, lines], w_self[...], preferred_element_type=F32) + bias[...]
        )


def column(inv, r, sub, half):
    shape = (half, inv.shape[1])
    line = lax.broadcasted_iota(jnp.int32, shape, 0) + sub * half
    lane = lax.broadcasted_iota(jnp.int32, shape, 1)
    spread = jnp.broadcast_to(inv[r : r + 1, :], shape)
    return jnp.sum(jnp.where(line == lane, spread, 0.0), axis=1, keepdims=True)


def late_kernel(cap, steps, pieces, nblk, order, at, affected, *refs):
    arrived = refs[:pieces]
    cells, agg, inv, own, w_neigh, old, out, tiles, total, means, sems = refs[pieces:]
    half = agg.shape[1]
    sub = lax.axis_index("sub")
    copies = tile_copies(cap, steps, arrived, tiles, sems) if pieces else []
    for copy in copies:
        copy.start()
    tiles[tiles.shape[0] - 1] = jnp.zeros(tiles.shape[1:], tiles.dtype)
    for r in range(nblk):
        total[r] = agg[r]
    for copy in copies:
        copy.wait()
    tile_sums(order, at[nblk], at[2 * nblk], tiles, cells, total)
    for r in range(nblk):
        means[r] = (total[r] * column(inv, r, sub, half)).astype(BF16)
    for r in range(nblk):
        pre = own[r] + jnp.dot(means[r], w_neigh[...], preferred_element_type=F32)
        pre = jnp.maximum(pre, 0.0)
        keep = jnp.full((half, 1), affected[r], jnp.int32) > 0
        out[r] = jnp.where(keep, pre, old[r].astype(F32)).astype(BF16)


def near_kernel(cap, steps, pieces, nblk, order, at, *refs):
    arrived = refs[:pieces]
    mine, twin, base, w_self, bias, agg, own, hidden, tiles, cells, sems = refs[pieces:]
    half = base.shape[1]
    width = hidden.shape[2]
    sub = lax.axis_index("sub")
    lanes = pl.ds(pl.multiple_of(sub * width, width), width)
    copies = tile_copies(cap, steps, arrived, tiles, sems)
    for k, (ref, side) in enumerate(((mine, sub), (twin, 1 - sub))):
        lines = pl.ds(pl.multiple_of(side * half, half), half)
        to = cells.at[pl.ds(nblk, nblk), lines]
        copies.append(pltpu.make_async_copy(ref, to, sems.at[pieces + k]))
        to = hidden.at[:, lines]
        copies.append(pltpu.make_async_copy(ref.at[:, :, lanes], to, sems.at[pieces + 2 + k]))
    for copy in copies:
        copy.start()
    tiles[tiles.shape[0] - 1] = jnp.zeros(tiles.shape[1:], tiles.dtype)
    for r in range(nblk):
        agg[r] = base[r]
    for copy in copies:
        copy.wait()
    tile_sums(order, at[0], at[nblk], tiles, cells, agg)
    mine_rows = pl.ds(pl.multiple_of(sub * half, half), half)
    for r in range(nblk):
        own[r] = (
            jnp.dot(cells[nblk + r, mine_rows], w_self[...], preferred_element_type=F32) + bias[...]
        )


def far_kernel(nblk, order, at, tiles, left, left_twin, right, right_twin, *refs):
    agg, inv, own, w_neigh, keep, send, cells, total, means, sems = refs
    half = agg.shape[1]
    width = keep.shape[2]
    sub = lax.axis_index("sub")
    sides = ((left, 0, sub), (left_twin, 0, 1 - sub), (right, 2, sub), (right_twin, 2, 1 - sub))
    copies = []
    for k, (ref, third, side) in enumerate(sides):
        lines = pl.ds(pl.multiple_of(side * half, half), half)
        to = cells.at[pl.ds(third * nblk, nblk), lines]
        copies.append(pltpu.make_async_copy(ref, to, sems.at[k]))
    for copy in copies:
        copy.start()
    cells[nblk] = jnp.zeros(cells.shape[1:], cells.dtype)
    for r in range(nblk):
        total[r] = agg[r]
    for copy in copies:
        copy.wait()
    tile_sums(order, at[nblk], at[3 * nblk], tiles, cells, total)
    for r in range(nblk):
        means[r] = (total[r] * column(inv, r, sub, half)).astype(BF16)
    for r in range(nblk):
        pre = own[r] + jnp.dot(means[r], w_neigh[...], preferred_element_type=F32)
        low = pre[:, :width]
        high = pre[:, width:]
        first = jnp.full((half, 1), sub, jnp.int32) == 0
        keep[r] = jnp.where(first, low, high).astype(BF16)
        send[r] = jnp.where(first, high, low).astype(BF16)


def finish_kernel(nblk, affected, kept, came, old, out):
    half = kept.shape[1]
    first = jnp.full((half, 1), lax.axis_index("sub"), jnp.int32) == 0
    for r in range(nblk):
        keep = jnp.full((half, 1), affected[r], jnp.int32) > 0
        low = jnp.where(first, kept[r].astype(F32), came[r].astype(F32))
        high = jnp.where(first, came[r].astype(F32), kept[r].astype(F32))
        out[r, :half] = jnp.where(keep, low, old[r, :half].astype(F32)).astype(BF16)
        out[r, half:] = jnp.where(keep, high, old[r, half:].astype(F32)).astype(BF16)


def swap(x):
    return lax.ppermute(x, "sub", [(0, 1), (1, 0)])


def ring(x, step):
    peers = lax.axis_size(PEERS)
    return lax.ppermute(x, PEERS, [(i, (i + step) % peers) for i in range(peers)])


def on_device(
    h_input,
    inv_degree,
    dest_block,
    row_block,
    block_offset,
    new_tiles,
    base_one,
    affected_one,
    old_one,
    self_one,
    neigh_one,
    bias_one,
    base_two,
    affected_two,
    old_two,
    self_two,
    neigh_two,
    bias_two,
):
    peers = lax.axis_size(PEERS)
    count = dest_block.shape[0]
    cap = max(2, 2 * count // peers)
    slots = peers * cap
    rows_here, width = h_input.shape
    full = width * lax.axis_size("sub")
    nblk = rows_here // BLK
    half = BLK // lax.axis_size("sub")
    direct = 2 < peers <= 16
    shape = jax.ShapeDtypeStruct
    after = lax.optimization_barrier
    blocks = (nblk, BLK, width)
    h_blocks = h_input.reshape(blocks)
    left, right = ring(h_blocks, 1), ring(h_blocks, peers - 1)

    order = sorted(range(1, peers), key=lambda k: (abs(k - peers // 2), k))
    lead = order[0] if direct else None
    piece = shape((cap, half, BLK), BF16)
    out_piece, source, fill = pl.pallas_call(
        functools.partial(first_kernel, peers, cap, lead),
        out_shape=[piece, shape((slots,), jnp.int32), shape((peers,), jnp.int32)],
        in_specs=[SMEM, HBM],
        out_specs=[VMEM, SMEM, SMEM],
        scratch_shapes=[pltpu.SemaphoreType.DMA((cap,))],
        cost_estimate=TINY,
        name="first",
    )(dest_block.reshape(count), new_tiles)

    if direct:
        others = order[1:] + [0]
        packed = pl.pallas_call(
            functools.partial(rest_kernel, peers, cap, others),
            out_shape=[piece] * len(others),
            in_specs=[SMEM, SMEM, HBM],
            out_specs=[VMEM] * len(others),
            scratch_shapes=[pltpu.SemaphoreType.DMA((len(others), cap))],
            cost_estimate=TINY,
            name="rest",
        )(source, fill, new_tiles)
        steps = order + [0]
        got = dict(zip(others, packed))
        got[lead] = out_piece
        got = {k: ring(got[k], k) if k else got[k] for k in steps}
        late = tuple(order[4:]) if peers > 4 else ()
        early = [k for k in steps if k not in late]
        arrived = [got[k] for k in steps]
        arrived_early = [got[k] for k in early]
        arrived_late = [got[k] for k in late]
        flag = got[lead]
        gathered = packed[-1]
    else:
        sent = pl.pallas_call(
            functools.partial(sorted_kernel, peers, cap),
            out_shape=shape((slots, half, BLK), BF16),
            in_specs=[SMEM, SMEM, HBM],
            out_specs=HBM,
            scratch_shapes=[pltpu.SemaphoreType.DMA((count,))],
            cost_estimate=TINY,
            name="rest",
        )(source, fill, new_tiles)
        sent = sent.reshape(peers, cap, half, BLK)
        got = lax.all_to_all(sent, PEERS, split_axis=0, concat_axis=0, tiled=True)
        arrived = [got.reshape(slots, half, BLK)]
        steps = early = None
        late = ()
        arrived_early, arrived_late = arrived, []
        flag = source
        gathered = out_piece

    left, right, fill_later = after((left, right, fill))
    codes = pl.pallas_call(
        functools.partial(label_kernel, peers, cap),
        out_shape=shape((peers * (cap + 1),), jnp.int32),
        in_specs=[SMEM] * 4,
        out_specs=SMEM,
        compiler_params=SMALL,
        cost_estimate=TINY,
        name="label",
    )(source, fill_later, row_block, block_offset)
    got_codes = lax.all_to_all(
        codes.reshape(peers, cap + 1), PEERS, split_axis=0, concat_axis=0, tiled=True
    ).reshape(peers * (cap + 1))

    sizes = (2 * nblk, 3 * nblk)
    counts = [pltpu.SMEM((size,), jnp.int32) for size in sizes]
    lists = []
    for size in sizes:
        lists += [shape((slots + size * QUAD,), jnp.int32), shape((size + 1,), jnp.int32)]
    by_row, row_at, by_side, side_at = pl.pallas_call(
        functools.partial(plan_kernel, peers, late, nblk),
        out_shape=lists,
        in_specs=[SMEM],
        out_specs=[SMEM] * 4,
        scratch_shapes=counts,
        compiler_params=SMALL,
        cost_estimate=TINY,
        name="plan",
    )(got_codes)

    old_blocks = old_one.reshape(blocks)
    base_one, base_two = base_one.reshape(blocks), base_two.reshape(blocks)
    bases, halves = pl.pallas_call(
        functools.partial(turn_kernel, nblk),
        out_shape=[shape((2 * nblk, half, width), F32), shape((3 * nblk, half, width), BF16)],
        in_specs=[ANY] * 5,
        out_specs=[ANY] * 2,
        scratch_shapes=[pltpu.SemaphoreType.DMA((5,))],
        compiler_params=SMALL,
        cost_estimate=TINY,
        name="turn",
    )(h_blocks, base_one, base_two, old_blocks, gathered)
    bases, halves, _ = after((bases, halves, flag))
    bases, halves = swap(bases), swap(halves)
    left, right, _ = after((left, right, flag))
    right, by_row = after((right, by_row))
    left_twin, right_twin = swap(left), swap(right)

    tile_scratch = pltpu.VMEM((slots + 1, half, BLK), BF16)
    cell_shape = (3 * nblk, BLK, full)
    cell_scratch = pltpu.VMEM(cell_shape, BF16)
    mean_scratch = pltpu.VMEM((nblk, half, full), BF16)
    rows_shape = (nblk, half, full)
    total_scratch = pltpu.VMEM(rows_shape, F32)
    inv = inv_degree.reshape(nblk, BLK)

    many = len(arrived_early)
    agg_early, cells_one, own_one, base_two_rows, old_one_rows = pl.pallas_call(
        functools.partial(early_kernel, cap, early, many, nblk),
        out_shape=[
            shape(rows_shape, F32),
            shape(cell_shape, BF16),
            shape(rows_shape, F32),
            shape(rows_shape, F32),
            shape(rows_shape, BF16),
        ],
        in_specs=[SMEM] * 2 + [ANY] * (many + 10) + [VMEM] * 2,
        out_specs=[VMEM] * 5,
        scratch_shapes=[tile_scratch, pltpu.SemaphoreType.DMA((many + 13,))],
        compiler_params=PARAMS,
        cost_estimate=TINY,
        name="early",
    )(
        by_row,
        row_at,
        *arrived_early,
        left,
        left_twin,
        h_blocks,
        halves,
        right,
        right_twin,
        base_one,
        base_two,
        bases,
        old_blocks,
        self_one,
        bias_one.reshape(1, full),
    )

    many = len(arrived_late)
    hidden_rows = pl.pallas_call(
        functools.partial(late_kernel, cap, late, many, nblk),
        out_shape=shape(rows_shape, BF16),
        in_specs=[SMEM] * 3 + [ANY] * many + [VMEM] * 6,
        out_specs=VMEM,
        scratch_shapes=[
            tile_scratch,
            total_scratch,
            mean_scratch,
            pltpu.SemaphoreType.DMA((max(1, many),)),
        ],
        compiler_params=PARAMS,
        cost_estimate=TINY,
        name="late",
    )(
        by_row,
        row_at,
        affected_one,
        *arrived_late,
        cells_one,
        agg_early,
        inv,
        own_one,
        neigh_one,
        old_one_rows,
    )

    hidden_twin = swap(hidden_rows)
    left = ring(hidden_rows, 1)
    right = ring(hidden_rows, peers - 1)

    many = len(arrived)
    agg_two, own_two, hidden_one, tiles_all = pl.pallas_call(
        functools.partial(near_kernel, cap, steps, many, nblk),
        out_shape=[shape(rows_shape, F32)] * 2
        + [shape(blocks, BF16), shape((slots + 1, half, BLK), BF16)],
        in_specs=[SMEM] * 2 + [ANY] * (many + 2) + [VMEM] * 3,
        out_specs=[VMEM] * 2 + [ANY, VMEM],
        scratch_shapes=[cell_scratch, pltpu.SemaphoreType.DMA((many + 4,))],
        compiler_params=PARAMS,
        cost_estimate=TINY,
        name="near",
    )(
        by_side,
        side_at,
        *arrived,
        hidden_rows,
        hidden_twin,
        base_two_rows,
        self_two,
        bias_two.reshape(1, full),
    )

    left, right, agg_two, own_two = after((left, right, agg_two, own_two))
    left_twin = swap(left)
    right_twin = swap(right)
    kept, sent = pl.pallas_call(
        functools.partial(far_kernel, nblk),
        out_shape=[shape((nblk, half, width), BF16)] * 2,
        in_specs=[SMEM] * 2 + [VMEM] + [ANY] * 4 + [VMEM] * 4,
        out_specs=[VMEM] * 2,
        scratch_shapes=[
            cell_scratch,
            total_scratch,
            mean_scratch,
            pltpu.SemaphoreType.DMA((4,)),
        ],
        compiler_params=PARAMS,
        cost_estimate=TINY,
        name="far",
    )(
        by_side,
        side_at,
        tiles_all,
        left,
        left_twin,
        right,
        right_twin,
        agg_two,
        inv,
        own_two,
        neigh_two,
    )
    came = swap(sent)
    hidden_two = pl.pallas_call(
        functools.partial(finish_kernel, nblk),
        out_shape=shape(blocks, BF16),
        in_specs=[SMEM] + [VMEM] * 3,
        out_specs=VMEM,
        compiler_params=SMALL,
        cost_estimate=TINY,
        name="finish",
    )(affected_two, kept, came, old_two.reshape(blocks))
    return (hidden_one.reshape(rows_here, width), hidden_two.reshape(rows_here, width))


def solution(mesh):
    rows = P(("groups", "rows", "feat"))
    cells = P(("groups", "rows", "feat"), "sub")
    placed = (
        cells,
        rows,
        P(("groups", "rows", "feat"), None),
        rows,
        rows,
        P(("groups", "rows", "feat"), None, None),
        cells,
        rows,
        cells,
        P(),
        P(),
        P(),
        cells,
        rows,
        cells,
        P(),
        P(),
        P(),
    )
    return jax.shard_map(
        on_device, mesh=mesh, in_specs=placed, out_specs=(cells, cells), check_vma=False
    )
```

```python
import functools

import jax
import jax.numpy as jnp
from jax import lax
from jax.experimental import pallas as pl
from jax.experimental.pallas import tpu as pltpu
from jax.sharding import PartitionSpec as P

PEERS = ("rows", "feat")
BLK = 128
QUAD = 4
F32 = jnp.float32
BF16 = jnp.bfloat16
ANY = pl.BlockSpec(memory_space=pl.ANY)
HBM = pl.BlockSpec(memory_space=pltpu.HBM)
SMEM = pl.BlockSpec(memory_space=pltpu.SMEM)
VMEM = pl.BlockSpec(memory_space=pltpu.VMEM)
PARAMS = pltpu.CompilerParams(vmem_limit_bytes=20 * 1024 * 1024)
SMALL = pltpu.CompilerParams(vmem_limit_bytes=4 * 1024 * 1024)
TINY = pl.CostEstimate(flops=0, bytes_accessed=128, transcendentals=0)


def first_kernel(peers, cap, lead, dest, row, off, tiles, out, source, fill, codes, sem):
    count = dest.shape[0]
    half = out.shape[1]
    me = lax.axis_index(PEERS)
    first = pl.multiple_of(lax.axis_index("sub") * half, half)
    for to in range(min(peers, 16)):
        fill[to] = 0
    if peers > 16:

        def clear(i, _):
            fill[i] = 0
            return 0

        lax.fori_loop(16, peers, clear, 0)
    for t in range(count):
        to = dest[t]
        at = fill[to]
        fill[to] = at + 1
        source[to * cap + at] = t
    leading = lax.rem(me + lead, peers) if lead else 0

    def send(j, _):
        t = source[leading * cap + j]
        pltpu.make_async_copy(tiles.at[t, pl.ds(first, half)], out.at[j], sem.at[j]).start()
        return 0

    def finish(j, _):
        pltpu.make_async_copy(tiles.at[0, pl.ds(first, half)], out.at[0], sem.at[j]).wait()
        return 0

    def label(to, _):
        def slot(j, _):
            t = source[to * cap + j]
            codes[to * (cap + 1) + j] = row[t] * 32 + off[t] + 8
            return 0

        lax.fori_loop(0, fill[to], slot, 0)
        codes[to * (cap + 1) + cap] = fill[to]
        return 0

    if lead:
        lax.fori_loop(0, fill[leading], send, 0)
    lax.fori_loop(0, peers, label, 0)
    if lead:
        lax.fori_loop(0, fill[leading], finish, 0)


def rest_kernel(peers, cap, order, source, fill, tiles, *refs):
    outs, sems = refs[:-1], refs[-1]
    half = outs[0].shape[1]
    me = lax.axis_index(PEERS)
    first = pl.multiple_of(lax.axis_index("sub") * half, half)
    begun = []
    for n, k in enumerate(order):
        to = lax.rem(me + k, peers)

        def send(j, _, n=n, to=to):
            t = source[to * cap + j]
            pltpu.make_async_copy(
                tiles.at[t, pl.ds(first, half)], outs[n].at[j], sems.at[n, j]
            ).start()
            return 0

        lax.fori_loop(0, fill[to], send, 0)
        begun.append(fill[to])
    for n, amount in enumerate(begun):

        def finish(j, _, n=n):
            pltpu.make_async_copy(
                tiles.at[0, pl.ds(first, half)], outs[n].at[0], sems.at[n, j]
            ).wait()
            return 0

        lax.fori_loop(0, amount, finish, 0)


def sorted_kernel(peers, cap, source, fill, tiles, out, sems):
    half = out.shape[1]
    first = pl.multiple_of(lax.axis_index("sub") * half, half)

    def each(act):
        def peer(to, _):
            def slot(j, _):
                at = to * cap + j
                act(source[at], at)
                return 0

            return lax.fori_loop(0, fill[to], slot, 0)

        lax.fori_loop(0, peers, peer, 0)

    def copy(t, at):
        return pltpu.make_async_copy(tiles.at[t, pl.ds(first, half)], out.at[at], sems.at[t])

    each(lambda t, at: copy(t, at).start())
    each(lambda t, at: copy(t, at).wait())


def turn_kernel(nblk, h, base_one, base_two, old, after, bases, halves, sems):
    half = bases.shape[1]
    other = pl.ds(pl.multiple_of((1 - lax.axis_index("sub")) * half, half), half)
    copies = [
        pltpu.make_async_copy(base_one.at[:, other], bases.at[pl.ds(0, nblk)], sems.at[0]),
        pltpu.make_async_copy(base_two.at[:, other], bases.at[pl.ds(nblk, nblk)], sems.at[1]),
        pltpu.make_async_copy(h.at[:, pl.ds(0, half)], halves.at[pl.ds(0, nblk)], sems.at[2]),
        pltpu.make_async_copy(
            h.at[:, pl.ds(half, half)], halves.at[pl.ds(nblk, nblk)], sems.at[3]
        ),
        pltpu.make_async_copy(old.at[:, other], halves.at[pl.ds(2 * nblk, nblk)], sems.at[4]),
    ]
    for copy in copies:
        copy.start()
    for copy in copies:
        copy.wait()


def plan_kernel(peers, late, nblk, codes, by_row, row_at, by_side, side_at, fill_row, fill_side):
    cap = codes.shape[0] // peers - 1
    nothing = peers * cap * 32 + nblk
    me = lax.axis_index(PEERS)
    for fill in (fill_row, fill_side):
        for g in range(fill.shape[0]):
            fill[g] = 0

    def walk(act):
        def peer(origin, _):
            behind = jnp.int32(0)
            step = lax.rem(me + peers - origin, peers)
            for k in late:
                behind = behind + jnp.where(step == k, nblk, 0)

            def slot(j, _):
                code = codes[origin * (cap + 1) + j]
                row = code >> 5
                col = row + (code & 31)
                side = jnp.where(col < nblk, nblk, jnp.where(col < 2 * nblk, 0, 2 * nblk))
                act(row + behind, row + side, (row << 16) + (origin * cap + j) * 32 + col)
                return 0

            return lax.fori_loop(0, codes[origin * (cap + 1) + cap], slot, 0)

        lax.fori_loop(0, peers, peer, 0)

    def tally(row, side, entry):
        fill_row[row] = fill_row[row] + 1
        fill_side[side] = fill_side[side] + 1

    def place(row, side, entry):
        to = fill_row[row]
        by_row[to] = entry
        fill_row[row] = to + 1
        to = fill_side[side]
        by_side[to] = entry
        fill_side[side] = to + 1

    walk(tally)
    for fill, at, listed in ((fill_row, row_at, by_row), (fill_side, side_at, by_side)):
        now = jnp.int32(0)
        for g in range(fill.shape[0]):
            at[g] = now
            need = (fill[g] + QUAD - 1) // QUAD
            fill[g] = now * QUAD
            now = now + need
            last = jnp.maximum(now * QUAD - QUAD, 0)
            for u in range(QUAD):
                listed[last + u] = nothing + ((g % nblk) << 16)
        at[fill.shape[0]] = now
    walk(place)


def tile_copies(cap, steps, arrived, tiles, sems):
    if steps is None:
        whole = tiles.at[pl.ds(0, arrived[0].shape[0])]
        return [pltpu.make_async_copy(arrived[0], whole, sems.at[0])]
    me = lax.axis_index(PEERS)
    peers = lax.axis_size(PEERS)
    copies = []
    for n, (k, ref) in enumerate(zip(steps, arrived)):
        origin = lax.rem(me + peers - k, peers)
        copies.append(pltpu.make_async_copy(ref, tiles.at[pl.ds(origin * cap, cap)], sems.at[n]))
    return copies


def tile_sums(order, begin, end, tiles, cells, total):
    nothing = (tiles.shape[0] - 1) * 32 + cells.shape[0] // 3

    def step(n, _):
        for q in (begin + 2 * n, begin + 2 * n + 1):
            entry = [jnp.where(q < end, order[q * QUAD + u], nothing) for u in range(QUAD)]
            row = entry[0] >> 16
            tile = [(e >> 5) & 2047 for e in entry]
            cell = [e & 31 for e in entry]
            acc = None
            for u in range(0, QUAD, 2):
                weights = jnp.concatenate([tiles[tile[u]], tiles[tile[u + 1]]], axis=1)
                chosen = jnp.concatenate([cells[cell[u]], cells[cell[u + 1]]], axis=0)
                part = jnp.dot(weights, chosen, preferred_element_type=F32)
                acc = part if acc is None else acc + part
            total[row] = total[row] + acc
        return 0

    lax.fori_loop(0, (end - begin + 1) >> 1, step, 0)


def early_kernel(cap, steps, pieces, nblk, order, at, *refs):
    arrived = refs[:pieces]
    (left, left_twin, h, halves, right, right_twin, base_one, base_two, bases, old) = refs[
        pieces : pieces + 10
    ]
    w_self, bias, agg, cells, own, base_rows, old_rows, tiles, sems = refs[pieces + 10 :]
    sub = lax.axis_index("sub")
    half = agg.shape[1]
    width = h.shape[2]
    lanes = pl.ds(pl.multiple_of(sub * width, width), width)
    others = pl.ds(pl.multiple_of((1 - sub) * width, width), width)
    lines = pl.ds(pl.multiple_of(sub * half, half), half)
    block = [pl.ds(k * nblk, nblk) for k in range(3)]
    low, high = pl.ds(0, half), pl.ds(half, half)
    moves = [
        (left, cells.at[block[0], :, lanes]),
        (left_twin, cells.at[block[0], :, others]),
        (h, cells.at[block[1], :, lanes]),
        (halves.at[block[0]], cells.at[block[1], low, others]),
        (halves.at[block[1]], cells.at[block[1], high, others]),
        (right, cells.at[block[2], :, lanes]),
        (right_twin, cells.at[block[2], :, others]),
        (base_one.at[:, lines], agg.at[:, :, lanes]),
        (bases.at[block[0]], agg.at[:, :, others]),
        (base_two.at[:, lines], base_rows.at[:, :, lanes]),
        (bases.at[block[1]], base_rows.at[:, :, others]),
        (old.at[:, lines], old_rows.at[:, :, lanes]),
        (halves.at[block[2]], old_rows.at[:, :, others]),
    ]
    copies = tile_copies(cap, steps, arrived, tiles, sems)
    for k, (src, dst) in enumerate(moves):
        copies.append(pltpu.make_async_copy(src, dst, sems.at[pieces + k]))
    for copy in copies:
        copy.start()
    tiles[tiles.shape[0] - 1] = jnp.zeros(tiles.shape[1:], tiles.dtype)
    for copy in copies:
        copy.wait()
    tile_sums(order, at[0], at[nblk], tiles, cells, agg)
    for r in range(nblk):
        own[r] = (
            jnp.dot(cells[nblk + r, lines], w_self[...], preferred_element_type=F32) + bias[...]
        )


def column(inv, r, sub, half):
    shape = (half, inv.shape[1])
    line = lax.broadcasted_iota(jnp.int32, shape, 0) + sub * half
    lane = lax.broadcasted_iota(jnp.int32, shape, 1)
    spread = jnp.broadcast_to(inv[r : r + 1, :], shape)
    return jnp.sum(jnp.where(line == lane, spread, 0.0), axis=1, keepdims=True)


def late_kernel(cap, steps, pieces, nblk, order, at, affected, *refs):
    arrived = refs[:pieces]
    cells, agg, inv, own, w_neigh, old, out, tiles, total, means, sems = refs[pieces:]
    half = agg.shape[1]
    sub = lax.axis_index("sub")
    copies = tile_copies(cap, steps, arrived, tiles, sems) if pieces else []
    for copy in copies:
        copy.start()
    tiles[tiles.shape[0] - 1] = jnp.zeros(tiles.shape[1:], tiles.dtype)
    for r in range(nblk):
        total[r] = agg[r]
    for copy in copies:
        copy.wait()
    tile_sums(order, at[nblk], at[2 * nblk], tiles, cells, total)
    for r in range(nblk):
        means[r] = (total[r] * column(inv, r, sub, half)).astype(BF16)
    for r in range(nblk):
        pre = own[r] + jnp.dot(means[r], w_neigh[...], preferred_element_type=F32)
        pre = jnp.maximum(pre, 0.0)
        keep = jnp.full((half, 1), affected[r], jnp.int32) > 0
        out[r] = jnp.where(keep, pre, old[r].astype(F32)).astype(BF16)


def near_kernel(cap, steps, pieces, nblk, order, at, *refs):
    arrived = refs[:pieces]
    mine, twin, base, w_self, bias, agg, own, hidden, tiles, cells, sems = refs[pieces:]
    half = base.shape[1]
    width = hidden.shape[2]
    sub = lax.axis_index("sub")
    lanes = pl.ds(pl.multiple_of(sub * width, width), width)
    copies = tile_copies(cap, steps, arrived, tiles, sems)
    for k, (ref, side) in enumerate(((mine, sub), (twin, 1 - sub))):
        lines = pl.ds(pl.multiple_of(side * half, half), half)
        to = cells.at[pl.ds(nblk, nblk), lines]
        copies.append(pltpu.make_async_copy(ref, to, sems.at[pieces + k]))
        to = hidden.at[:, lines]
        copies.append(pltpu.make_async_copy(ref.at[:, :, lanes], to, sems.at[pieces + 2 + k]))
    for copy in copies:
        copy.start()
    tiles[tiles.shape[0] - 1] = jnp.zeros(tiles.shape[1:], tiles.dtype)
    for r in range(nblk):
        agg[r] = base[r]
    for copy in copies:
        copy.wait()
    tile_sums(order, at[0], at[nblk], tiles, cells, agg)
    mine_rows = pl.ds(pl.multiple_of(sub * half, half), half)
    for r in range(nblk):
        own[r] = (
            jnp.dot(cells[nblk + r, mine_rows], w_self[...], preferred_element_type=F32) + bias[...]
        )


def far_kernel(nblk, order, at, tiles, left, left_twin, right, right_twin, *refs):
    agg, inv, own, w_neigh, keep, send, cells, total, means, sems = refs
    half = agg.shape[1]
    width = keep.shape[2]
    sub = lax.axis_index("sub")
    sides = ((left, 0, sub), (left_twin, 0, 1 - sub), (right, 2, sub), (right_twin, 2, 1 - sub))
    copies = []
    for k, (ref, third, side) in enumerate(sides):
        lines = pl.ds(pl.multiple_of(side * half, half), half)
        to = cells.at[pl.ds(third * nblk, nblk), lines]
        copies.append(pltpu.make_async_copy(ref, to, sems.at[k]))
    for copy in copies:
        copy.start()
    cells[nblk] = jnp.zeros(cells.shape[1:], cells.dtype)
    for r in range(nblk):
        total[r] = agg[r]
    for copy in copies:
        copy.wait()
    tile_sums(order, at[nblk], at[3 * nblk], tiles, cells, total)
    for r in range(nblk):
        means[r] = (total[r] * column(inv, r, sub, half)).astype(BF16)
    for r in range(nblk):
        pre = own[r] + jnp.dot(means[r], w_neigh[...], preferred_element_type=F32)
        low = pre[:, :width]
        high = pre[:, width:]
        first = jnp.full((half, 1), sub, jnp.int32) == 0
        keep[r] = jnp.where(first, low, high).astype(BF16)
        send[r] = jnp.where(first, high, low).astype(BF16)


def finish_kernel(nblk, affected, kept, came, old, out):
    half = kept.shape[1]
    first = jnp.full((half, 1), lax.axis_index("sub"), jnp.int32) == 0
    for r in range(nblk):
        keep = jnp.full((half, 1), affected[r], jnp.int32) > 0
        low = jnp.where(first, kept[r].astype(F32), came[r].astype(F32))
        high = jnp.where(first, came[r].astype(F32), kept[r].astype(F32))
        out[r, :half] = jnp.where(keep, low, old[r, :half].astype(F32)).astype(BF16)
        out[r, half:] = jnp.where(keep, high, old[r, half:].astype(F32)).astype(BF16)


def swap(x):
    return lax.ppermute(x, "sub", [(0, 1), (1, 0)])


def ring(x, step):
    peers = lax.axis_size(PEERS)
    return lax.ppermute(x, PEERS, [(i, (i + step) % peers) for i in range(peers)])


def on_device(
    h_input,
    inv_degree,
    dest_block,
    row_block,
    block_offset,
    new_tiles,
    base_one,
    affected_one,
    old_one,
    self_one,
    neigh_one,
    bias_one,
    base_two,
    affected_two,
    old_two,
    self_two,
    neigh_two,
    bias_two,
):
    peers = lax.axis_size(PEERS)
    count = dest_block.shape[0]
    cap = max(2, 2 * count // peers)
    slots = peers * cap
    rows_here, width = h_input.shape
    full = width * lax.axis_size("sub")
    nblk = rows_here // BLK
    half = BLK // lax.axis_size("sub")
    direct = 2 < peers <= 16
    shape = jax.ShapeDtypeStruct
    after = lax.optimization_barrier

    order = sorted(range(1, peers), key=lambda k: (abs(k - peers // 2), k))
    lead = order[0] if direct else None
    piece = shape((cap, half, BLK), BF16)
    out_piece, source, fill, codes = pl.pallas_call(
        functools.partial(first_kernel, peers, cap, lead),
        out_shape=[
            piece,
            shape((slots,), jnp.int32),
            shape((peers,), jnp.int32),
            shape((peers * (cap + 1),), jnp.int32),
        ],
        in_specs=[SMEM] * 3 + [HBM],
        out_specs=[VMEM] + [SMEM] * 3,
        scratch_shapes=[pltpu.SemaphoreType.DMA((cap,))],
        cost_estimate=TINY,
        name="first",
    )(dest_block.reshape(count), row_block, block_offset, new_tiles)

    if direct:
        others = order[1:] + [0]
        packed = pl.pallas_call(
            functools.partial(rest_kernel, peers, cap, others),
            out_shape=[piece] * len(others),
            in_specs=[SMEM, SMEM, HBM],
            out_specs=[VMEM] * len(others),
            scratch_shapes=[pltpu.SemaphoreType.DMA((len(others), cap))],
            cost_estimate=TINY,
            name="rest",
        )(source, fill, new_tiles)
        steps = order + [0]
        got = dict(zip(others, packed))
        got[lead] = out_piece
        got = {k: ring(got[k], k) if k else got[k] for k in steps}
        late = tuple(order[4:]) if peers > 4 else ()
        early = [k for k in steps if k not in late]
        arrived = [got[k] for k in steps]
        arrived_early = [got[k] for k in early]
        arrived_late = [got[k] for k in late]
        flag = got[lead]
        gathered = packed[-1]
    else:
        sent = pl.pallas_call(
            functools.partial(sorted_kernel, peers, cap),
            out_shape=shape((slots, half, BLK), BF16),
            in_specs=[SMEM, SMEM, HBM],
            out_specs=HBM,
            scratch_shapes=[pltpu.SemaphoreType.DMA((count,))],
            cost_estimate=TINY,
            name="rest",
        )(source, fill, new_tiles)
        sent = sent.reshape(peers, cap, half, BLK)
        got = lax.all_to_all(sent, PEERS, split_axis=0, concat_axis=0, tiled=True)
        arrived = [got.reshape(slots, half, BLK)]
        steps = early = None
        late = ()
        arrived_early, arrived_late = arrived, []
        flag = source
        gathered = out_piece

    got_codes = lax.all_to_all(
        codes.reshape(peers, cap + 1), PEERS, split_axis=0, concat_axis=0, tiled=True
    ).reshape(peers * (cap + 1))

    sizes = (2 * nblk, 3 * nblk)
    counts = [pltpu.SMEM((size,), jnp.int32) for size in sizes]
    lists = []
    for size in sizes:
        lists += [shape((slots + size * QUAD,), jnp.int32), shape((size + 1,), jnp.int32)]
    by_row, row_at, by_side, side_at = pl.pallas_call(
        functools.partial(plan_kernel, peers, late, nblk),
        out_shape=lists,
        in_specs=[SMEM],
        out_specs=[SMEM] * 4,
        scratch_shapes=counts,
        compiler_params=SMALL,
        cost_estimate=TINY,
        name="plan",
    )(got_codes)

    blocks = (nblk, BLK, width)
    h_blocks, old_blocks = h_input.reshape(blocks), old_one.reshape(blocks)
    base_one, base_two = base_one.reshape(blocks), base_two.reshape(blocks)
    bases, halves = pl.pallas_call(
        functools.partial(turn_kernel, nblk),
        out_shape=[shape((2 * nblk, half, width), F32), shape((3 * nblk, half, width), BF16)],
        in_specs=[ANY] * 5,
        out_specs=[ANY] * 2,
        scratch_shapes=[pltpu.SemaphoreType.DMA((5,))],
        compiler_params=SMALL,
        cost_estimate=TINY,
        name="turn",
    )(h_blocks, base_one, base_two, old_blocks, gathered)
    bases, halves, _ = after((bases, halves, flag))
    bases, halves = swap(bases), swap(halves)
    h_later, _, by_row, by_side = after((h_blocks, flag, by_row, by_side))
    left, right = ring(h_later, 1), ring(h_later, peers - 1)
    left_twin, right_twin = swap(left), swap(right)

    tile_scratch = pltpu.VMEM((slots + 1, half, BLK), BF16)
    cell_shape = (3 * nblk, BLK, full)
    cell_scratch = pltpu.VMEM(cell_shape, BF16)
    mean_scratch = pltpu.VMEM((nblk, half, full), BF16)
    rows_shape = (nblk, half, full)
    total_scratch = pltpu.VMEM(rows_shape, F32)
    inv = inv_degree.reshape(nblk, BLK)

    many = len(arrived_early)
    agg_early, cells_one, own_one, base_two_rows, old_one_rows = pl.pallas_call(
        functools.partial(early_kernel, cap, early, many, nblk),
        out_shape=[
            shape(rows_shape, F32),
            shape(cell_shape, BF16),
            shape(rows_shape, F32),
            shape(rows_shape, F32),
            shape(rows_shape, BF16),
        ],
        in_specs=[SMEM] * 2 + [ANY] * (many + 10) + [VMEM] * 2,
        out_specs=[VMEM] * 5,
        scratch_shapes=[tile_scratch, pltpu.SemaphoreType.DMA((many + 13,))],
        compiler_params=PARAMS,
        cost_estimate=TINY,
        name="early",
    )(
        by_row,
        row_at,
        *arrived_early,
        left,
        left_twin,
        h_blocks,
        halves,
        right,
        right_twin,
        base_one,
        base_two,
        bases,
        old_blocks,
        self_one,
        bias_one.reshape(1, full),
    )

    many = len(arrived_late)
    hidden_rows = pl.pallas_call(
        functools.partial(late_kernel, cap, late, many, nblk),
        out_shape=shape(rows_shape, BF16),
        in_specs=[SMEM] * 3 + [ANY] * many + [VMEM] * 6,
        out_specs=VMEM,
        scratch_shapes=[
            tile_scratch,
            total_scratch,
            mean_scratch,
            pltpu.SemaphoreType.DMA((max(1, many),)),
        ],
        compiler_params=PARAMS,
        cost_estimate=TINY,
        name="late",
    )(
        by_row,
        row_at,
        affected_one,
        *arrived_late,
        cells_one,
        agg_early,
        inv,
        own_one,
        neigh_one,
        old_one_rows,
    )

    hidden_twin = swap(hidden_rows)
    left = ring(hidden_rows, 1)
    right = ring(hidden_rows, peers - 1)

    many = len(arrived)
    agg_two, own_two, hidden_one, tiles_all = pl.pallas_call(
        functools.partial(near_kernel, cap, steps, many, nblk),
        out_shape=[shape(rows_shape, F32)] * 2
        + [shape(blocks, BF16), shape((slots + 1, half, BLK), BF16)],
        in_specs=[SMEM] * 2 + [ANY] * (many + 2) + [VMEM] * 3,
        out_specs=[VMEM] * 2 + [ANY, VMEM],
        scratch_shapes=[cell_scratch, pltpu.SemaphoreType.DMA((many + 4,))],
        compiler_params=PARAMS,
        cost_estimate=TINY,
        name="near",
    )(
        by_side,
        side_at,
        *arrived,
        hidden_rows,
        hidden_twin,
        base_two_rows,
        self_two,
        bias_two.reshape(1, full),
    )

    left, right, agg_two, own_two = after((left, right, agg_two, own_two))
    left_twin = swap(left)
    right_twin = swap(right)
    kept, sent = pl.pallas_call(
        functools.partial(far_kernel, nblk),
        out_shape=[shape((nblk, half, width), BF16)] * 2,
        in_specs=[SMEM] * 2 + [VMEM] + [ANY] * 4 + [VMEM] * 4,
        out_specs=[VMEM] * 2,
        scratch_shapes=[
            cell_scratch,
            total_scratch,
            mean_scratch,
            pltpu.SemaphoreType.DMA((4,)),
        ],
        compiler_params=PARAMS,
        cost_estimate=TINY,
        name="far",
    )(
        by_side,
        side_at,
        tiles_all,
        left,
        left_twin,
        right,
        right_twin,
        agg_two,
        inv,
        own_two,
        neigh_two,
    )
    came = swap(sent)
    hidden_two = pl.pallas_call(
        functools.partial(finish_kernel, nblk),
        out_shape=shape(blocks, BF16),
        in_specs=[SMEM] + [VMEM] * 3,
        out_specs=VMEM,
        compiler_params=SMALL,
        cost_estimate=TINY,
        name="finish",
    )(affected_two, kept, came, old_two.reshape(blocks))
    return (hidden_one.reshape(rows_here, width), hidden_two.reshape(rows_here, width))


def solution(mesh):
    rows = P(("groups", "rows", "feat"))
    cells = P(("groups", "rows", "feat"), "sub")
    placed = (
        cells,
        rows,
        P(("groups", "rows", "feat"), None),
        rows,
        rows,
        P(("groups", "rows", "feat"), None, None),
        cells,
        rows,
        cells,
        P(),
        P(),
        P(),
        cells,
        rows,
        cells,
        P(),
        P(),
        P(),
    )
    return jax.shard_map(
        on_device, mesh=mesh, in_specs=placed, out_specs=(cells, cells), check_vma=False
    )
```

```python
import functools
import math

import jax
import jax.numpy as jnp
from jax import lax
from jax.experimental import pallas as pl
from jax.experimental.pallas import tpu as pltpu
from jax.sharding import PartitionSpec as P

PEERS = ("rows", "feat")
BLK = 128
QUAD = 4
F32 = jnp.float32
BF16 = jnp.bfloat16
ANY = pl.BlockSpec(memory_space=pl.ANY)
HBM = pl.BlockSpec(memory_space=pltpu.HBM)
SMEM = pl.BlockSpec(memory_space=pltpu.SMEM)
VMEM = pl.BlockSpec(memory_space=pltpu.VMEM)
PARAMS = pltpu.CompilerParams(vmem_limit_bytes=20 * 1024 * 1024)
SMALL = pltpu.CompilerParams(vmem_limit_bytes=4 * 1024 * 1024)
TINY = pl.CostEstimate(flops=0, bytes_accessed=128, transcendentals=0)


def first_kernel(peers, cap, lead, dest, row, off, tiles, out, source, fill, codes, sem):
    count = dest.shape[0]
    half = out.shape[1]
    me = lax.axis_index(PEERS)
    first = pl.multiple_of(lax.axis_index("sub") * half, half)
    for to in range(min(peers, 16)):
        fill[to] = 0
    if peers > 16:

        def clear(i, _):
            fill[i] = 0
            return 0

        lax.fori_loop(16, peers, clear, 0)
    for t in range(count):
        to = dest[t]
        at = fill[to]
        fill[to] = at + 1
        source[to * cap + at] = t
    leading = lax.rem(me + lead, peers) if lead else 0

    def send(j, _):
        t = source[leading * cap + j]
        pltpu.make_async_copy(tiles.at[t, pl.ds(first, half)], out.at[j], sem.at[j]).start()
        return 0

    def finish(j, _):
        pltpu.make_async_copy(tiles.at[0, pl.ds(first, half)], out.at[0], sem.at[j]).wait()
        return 0

    def label(to, _):
        def slot(j, _):
            t = source[to * cap + j]
            codes[to * (cap + 1) + j] = row[t] * 32 + off[t] + 8
            return 0

        lax.fori_loop(0, fill[to], slot, 0)
        codes[to * (cap + 1) + cap] = fill[to]
        return 0

    if lead:
        lax.fori_loop(0, fill[leading], send, 0)
    lax.fori_loop(0, peers, label, 0)
    if lead:
        lax.fori_loop(0, fill[leading], finish, 0)


def rest_kernel(peers, cap, order, source, fill, tiles, *refs):
    outs, sems = refs[:-1], refs[-1]
    half = outs[0].shape[1]
    me = lax.axis_index(PEERS)
    first = pl.multiple_of(lax.axis_index("sub") * half, half)
    begun = []
    for n, k in enumerate(order):
        to = lax.rem(me + k, peers)

        def send(j, _, n=n, to=to):
            t = source[to * cap + j]
            pltpu.make_async_copy(
                tiles.at[t, pl.ds(first, half)], outs[n].at[j], sems.at[n, j]
            ).start()
            return 0

        lax.fori_loop(0, fill[to], send, 0)
        begun.append(fill[to])
    for n, amount in enumerate(begun):

        def finish(j, _, n=n):
            pltpu.make_async_copy(
                tiles.at[0, pl.ds(first, half)], outs[n].at[0], sems.at[n, j]
            ).wait()
            return 0

        lax.fori_loop(0, amount, finish, 0)


def sorted_kernel(peers, cap, source, fill, tiles, out, sems):
    half = out.shape[1]
    first = pl.multiple_of(lax.axis_index("sub") * half, half)

    def each(act):
        def peer(to, _):
            def slot(j, _):
                at = to * cap + j
                act(source[at], at)
                return 0

            return lax.fori_loop(0, fill[to], slot, 0)

        lax.fori_loop(0, peers, peer, 0)

    def copy(t, at):
        return pltpu.make_async_copy(tiles.at[t, pl.ds(first, half)], out.at[at], sems.at[t])

    each(lambda t, at: copy(t, at).start())
    each(lambda t, at: copy(t, at).wait())


def turn_kernel(nblk, h, base_one, base_two, old, after, bases, halves, sems):
    half = bases.shape[1]
    other = pl.ds(pl.multiple_of((1 - lax.axis_index("sub")) * half, half), half)
    copies = [
        pltpu.make_async_copy(base_one.at[:, other], bases.at[pl.ds(0, nblk)], sems.at[0]),
        pltpu.make_async_copy(base_two.at[:, other], bases.at[pl.ds(nblk, nblk)], sems.at[1]),
        pltpu.make_async_copy(h.at[:, pl.ds(0, half)], halves.at[pl.ds(0, nblk)], sems.at[2]),
        pltpu.make_async_copy(
            h.at[:, pl.ds(half, half)], halves.at[pl.ds(nblk, nblk)], sems.at[3]
        ),
        pltpu.make_async_copy(old.at[:, other], halves.at[pl.ds(2 * nblk, nblk)], sems.at[4]),
    ]
    for copy in copies:
        copy.start()
    for copy in copies:
        copy.wait()


def plan_kernel(peers, late, nblk, codes, by_row, row_at, by_side, side_at, fill_row, fill_side):
    cap = codes.shape[0] // peers - 1
    nothing = peers * cap * 32 + nblk
    me = lax.axis_index(PEERS)
    for fill in (fill_row, fill_side):
        for g in range(fill.shape[0]):
            fill[g] = 0

    def walk(act):
        def peer(origin, _):
            behind = jnp.int32(0)
            step = lax.rem(me + peers - origin, peers)
            for k in late:
                behind = behind + jnp.where(step == k, nblk, 0)

            def slot(j, _):
                code = codes[origin * (cap + 1) + j]
                row = code >> 5
                col = row + (code & 31)
                side = jnp.where(col < nblk, nblk, jnp.where(col < 2 * nblk, 0, 2 * nblk))
                act(row + behind, row + side, (row << 16) + (origin * cap + j) * 32 + col)
                return 0

            return lax.fori_loop(0, codes[origin * (cap + 1) + cap], slot, 0)

        lax.fori_loop(0, peers, peer, 0)

    def tally(row, side, entry):
        fill_row[row] = fill_row[row] + 1
        fill_side[side] = fill_side[side] + 1

    def place(row, side, entry):
        to = fill_row[row]
        by_row[to] = entry
        fill_row[row] = to + 1
        to = fill_side[side]
        by_side[to] = entry
        fill_side[side] = to + 1

    walk(tally)
    for fill, at, listed in ((fill_row, row_at, by_row), (fill_side, side_at, by_side)):
        now = jnp.int32(0)
        for g in range(fill.shape[0]):
            at[g] = now
            need = (fill[g] + QUAD - 1) // QUAD
            fill[g] = now * QUAD
            now = now + need
            last = jnp.maximum(now * QUAD - QUAD, 0)
            for u in range(QUAD):
                listed[last + u] = nothing + ((g % nblk) << 16)
        at[fill.shape[0]] = now
    walk(place)


def tile_copies(cap, steps, arrived, tiles, sems):
    if steps is None:
        whole = tiles.at[pl.ds(0, arrived[0].shape[0])]
        return [pltpu.make_async_copy(arrived[0], whole, sems.at[0])]
    me = lax.axis_index(PEERS)
    peers = lax.axis_size(PEERS)
    copies = []
    for n, (k, ref) in enumerate(zip(steps, arrived)):
        origin = lax.rem(me + peers - k, peers)
        copies.append(pltpu.make_async_copy(ref, tiles.at[pl.ds(origin * cap, cap)], sems.at[n]))
    return copies


def tile_sums(order, begin, end, tiles, cells, total):
    nothing = (tiles.shape[0] - 1) * 32 + cells.shape[0] // 3

    def step(n, _):
        for q in (begin + 2 * n, begin + 2 * n + 1):
            entry = [jnp.where(q < end, order[q * QUAD + u], nothing) for u in range(QUAD)]
            row = entry[0] >> 16
            tile = [(e >> 5) & 2047 for e in entry]
            cell = [e & 31 for e in entry]
            acc = None
            for u in range(0, QUAD, 2):
                weights = jnp.concatenate([tiles[tile[u]], tiles[tile[u + 1]]], axis=1)
                chosen = jnp.concatenate([cells[cell[u]], cells[cell[u + 1]]], axis=0)
                part = jnp.dot(weights, chosen, preferred_element_type=F32)
                acc = part if acc is None else acc + part
            total[row] = total[row] + acc
        return 0

    lax.fori_loop(0, (end - begin + 1) >> 1, step, 0)


def early_kernel(cap, steps, pieces, nblk, order, at, *refs):
    arrived = refs[:pieces]
    (left, left_twin, h, halves, right, right_twin, base_one, base_two, bases, old) = refs[
        pieces : pieces + 10
    ]
    w_self, bias, agg, cells, own, base_rows, old_rows, tiles, sems = refs[pieces + 10 :]
    sub = lax.axis_index("sub")
    half = agg.shape[1]
    width = h.shape[2]
    lanes = pl.ds(pl.multiple_of(sub * width, width), width)
    others = pl.ds(pl.multiple_of((1 - sub) * width, width), width)
    lines = pl.ds(pl.multiple_of(sub * half, half), half)
    block = [pl.ds(k * nblk, nblk) for k in range(3)]
    low, high = pl.ds(0, half), pl.ds(half, half)
    moves = [
        (left, cells.at[block[0], :, lanes]),
        (left_twin, cells.at[block[0], :, others]),
        (h, cells.at[block[1], :, lanes]),
        (halves.at[block[0]], cells.at[block[1], low, others]),
        (halves.at[block[1]], cells.at[block[1], high, others]),
        (right, cells.at[block[2], :, lanes]),
        (right_twin, cells.at[block[2], :, others]),
        (base_one.at[:, lines], agg.at[:, :, lanes]),
        (bases.at[block[0]], agg.at[:, :, others]),
        (base_two.at[:, lines], base_rows.at[:, :, lanes]),
        (bases.at[block[1]], base_rows.at[:, :, others]),
        (old.at[:, lines], old_rows.at[:, :, lanes]),
        (halves.at[block[2]], old_rows.at[:, :, others]),
    ]
    copies = tile_copies(cap, steps, arrived, tiles, sems)
    for k, (src, dst) in enumerate(moves):
        copies.append(pltpu.make_async_copy(src, dst, sems.at[pieces + k]))
    for copy in copies:
        copy.start()
    tiles[tiles.shape[0] - 1] = jnp.zeros(tiles.shape[1:], tiles.dtype)
    for copy in copies:
        copy.wait()
    tile_sums(order, at[0], at[nblk], tiles, cells, agg)
    for r in range(nblk):
        own[r] = (
            jnp.dot(cells[nblk + r, lines], w_self[...], preferred_element_type=F32) + bias[...]
        )


def column(inv, r, sub, half):
    shape = (half, inv.shape[1])
    line = lax.broadcasted_iota(jnp.int32, shape, 0) + sub * half
    lane = lax.broadcasted_iota(jnp.int32, shape, 1)
    spread = jnp.broadcast_to(inv[r : r + 1, :], shape)
    return jnp.sum(jnp.where(line == lane, spread, 0.0), axis=1, keepdims=True)


def products(means, weight):
    nblk, half, full = means.shape
    few = math.gcd(nblk, 4)
    for g in range(0, nblk, few):
        rows = means[g : g + few].reshape(few * half, full)
        part = jnp.dot(rows, weight[...], preferred_element_type=F32)
        for r in range(few):
            yield g + r, part[r * half : (r + 1) * half]


def late_kernel(cap, steps, pieces, nblk, order, at, affected, *refs):
    arrived = refs[:pieces]
    cells, agg, inv, own, w_neigh, old, out, tiles, total, means, sems = refs[pieces:]
    half = agg.shape[1]
    sub = lax.axis_index("sub")
    copies = tile_copies(cap, steps, arrived, tiles, sems) if pieces else []
    for copy in copies:
        copy.start()
    tiles[tiles.shape[0] - 1] = jnp.zeros(tiles.shape[1:], tiles.dtype)
    for r in range(nblk):
        total[r] = agg[r]
    for copy in copies:
        copy.wait()
    tile_sums(order, at[nblk], at[2 * nblk], tiles, cells, total)
    for r in range(nblk):
        means[r] = (total[r] * column(inv, r, sub, half)).astype(BF16)
    for r, part in products(means, w_neigh):
        pre = jnp.maximum(own[r] + part, 0.0)
        keep = jnp.full((half, 1), affected[r], jnp.int32) > 0
        out[r] = jnp.where(keep, pre, old[r].astype(F32)).astype(BF16)


def near_kernel(cap, steps, pieces, nblk, order, at, *refs):
    arrived = refs[:pieces]
    mine, twin, base, w_self, bias, agg, own, hidden, tiles, cells, sems = refs[pieces:]
    half = base.shape[1]
    width = hidden.shape[2]
    sub = lax.axis_index("sub")
    lanes = pl.ds(pl.multiple_of(sub * width, width), width)
    copies = tile_copies(cap, steps, arrived, tiles, sems)
    for k, (ref, side) in enumerate(((mine, sub), (twin, 1 - sub))):
        lines = pl.ds(pl.multiple_of(side * half, half), half)
        to = cells.at[pl.ds(nblk, nblk), lines]
        copies.append(pltpu.make_async_copy(ref, to, sems.at[pieces + k]))
        to = hidden.at[:, lines]
        copies.append(pltpu.make_async_copy(ref.at[:, :, lanes], to, sems.at[pieces + 2 + k]))
    for copy in copies:
        copy.start()
    tiles[tiles.shape[0] - 1] = jnp.zeros(tiles.shape[1:], tiles.dtype)
    for r in range(nblk):
        agg[r] = base[r]
    for copy in copies:
        copy.wait()
    tile_sums(order, at[0], at[nblk], tiles, cells, agg)
    mine_rows = pl.ds(pl.multiple_of(sub * half, half), half)
    for r in range(nblk):
        own[r] = (
            jnp.dot(cells[nblk + r, mine_rows], w_self[...], preferred_element_type=F32) + bias[...]
        )


def far_kernel(nblk, order, at, tiles, left, left_twin, right, right_twin, *refs):
    agg, inv, own, w_neigh, keep, send, cells, total, means, sems = refs
    half = agg.shape[1]
    width = keep.shape[2]
    sub = lax.axis_index("sub")
    sides = ((left, 0, sub), (left_twin, 0, 1 - sub), (right, 2, sub), (right_twin, 2, 1 - sub))
    copies = []
    for k, (ref, third, side) in enumerate(sides):
        lines = pl.ds(pl.multiple_of(side * half, half), half)
        to = cells.at[pl.ds(third * nblk, nblk), lines]
        copies.append(pltpu.make_async_copy(ref, to, sems.at[k]))
    for copy in copies:
        copy.start()
    cells[nblk] = jnp.zeros(cells.shape[1:], cells.dtype)
    for r in range(nblk):
        total[r] = agg[r]
    for copy in copies:
        copy.wait()
    tile_sums(order, at[nblk], at[3 * nblk], tiles, cells, total)
    for r in range(nblk):
        means[r] = (total[r] * column(inv, r, sub, half)).astype(BF16)
    for r, part in products(means, w_neigh):
        pre = own[r] + part
        low = pre[:, :width]
        high = pre[:, width:]
        first = jnp.full((half, 1), sub, jnp.int32) == 0
        keep[r] = jnp.where(first, low, high).astype(BF16)
        send[r] = jnp.where(first, high, low).astype(BF16)


def finish_kernel(nblk, affected, kept, came, old, out):
    half = kept.shape[1]
    first = jnp.full((half, 1), lax.axis_index("sub"), jnp.int32) == 0
    for r in range(nblk):
        keep = jnp.full((half, 1), affected[r], jnp.int32) > 0
        low = jnp.where(first, kept[r].astype(F32), came[r].astype(F32))
        high = jnp.where(first, came[r].astype(F32), kept[r].astype(F32))
        out[r, :half] = jnp.where(keep, low, old[r, :half].astype(F32)).astype(BF16)
        out[r, half:] = jnp.where(keep, high, old[r, half:].astype(F32)).astype(BF16)


def swap(x):
    return lax.ppermute(x, "sub", [(0, 1), (1, 0)])


def ring(x, step):
    peers = lax.axis_size(PEERS)
    return lax.ppermute(x, PEERS, [(i, (i + step) % peers) for i in range(peers)])


def on_device(
    h_input,
    inv_degree,
    dest_block,
    row_block,
    block_offset,
    new_tiles,
    base_one,
    affected_one,
    old_one,
    self_one,
    neigh_one,
    bias_one,
    base_two,
    affected_two,
    old_two,
    self_two,
    neigh_two,
    bias_two,
):
    peers = lax.axis_size(PEERS)
    count = dest_block.shape[0]
    cap = max(2, 2 * count // peers)
    slots = peers * cap
    rows_here, width = h_input.shape
    full = width * lax.axis_size("sub")
    nblk = rows_here // BLK
    half = BLK // lax.axis_size("sub")
    direct = 2 < peers <= 16
    shape = jax.ShapeDtypeStruct
    after = lax.optimization_barrier

    order = sorted(range(1, peers), key=lambda k: (abs(k - peers // 2), k))
    lead = order[0] if direct else None
    piece = shape((cap, half, BLK), BF16)
    out_piece, source, fill, codes = pl.pallas_call(
        functools.partial(first_kernel, peers, cap, lead),
        out_shape=[
            piece,
            shape((slots,), jnp.int32),
            shape((peers,), jnp.int32),
            shape((peers * (cap + 1),), jnp.int32),
        ],
        in_specs=[SMEM] * 3 + [HBM],
        out_specs=[VMEM] + [SMEM] * 3,
        scratch_shapes=[pltpu.SemaphoreType.DMA((cap,))],
        cost_estimate=TINY,
        name="first",
    )(dest_block.reshape(count), row_block, block_offset, new_tiles)

    if direct:
        others = order[1:] + [0]
        packed = pl.pallas_call(
            functools.partial(rest_kernel, peers, cap, others),
            out_shape=[piece] * len(others),
            in_specs=[SMEM, SMEM, HBM],
            out_specs=[VMEM] * len(others),
            scratch_shapes=[pltpu.SemaphoreType.DMA((len(others), cap))],
            cost_estimate=TINY,
            name="rest",
        )(source, fill, new_tiles)
        steps = order + [0]
        got = dict(zip(others, packed))
        got[lead] = out_piece
        got = {k: ring(got[k], k) if k else got[k] for k in steps}
        late = tuple(order[4:]) if peers > 4 else ()
        early = [k for k in steps if k not in late]
        arrived = [got[k] for k in steps]
        arrived_early = [got[k] for k in early]
        arrived_late = [got[k] for k in late]
        flag = got[lead]
        gathered = packed[-1]
    else:
        sent = pl.pallas_call(
            functools.partial(sorted_kernel, peers, cap),
            out_shape=shape((slots, half, BLK), BF16),
            in_specs=[SMEM, SMEM, HBM],
            out_specs=HBM,
            scratch_shapes=[pltpu.SemaphoreType.DMA((count,))],
            cost_estimate=TINY,
            name="rest",
        )(source, fill, new_tiles)
        sent = sent.reshape(peers, cap, half, BLK)
        got = lax.all_to_all(sent, PEERS, split_axis=0, concat_axis=0, tiled=True)
        arrived = [got.reshape(slots, half, BLK)]
        steps = early = None
        late = ()
        arrived_early, arrived_late = arrived, []
        flag = source
        gathered = out_piece

    got_codes = lax.all_to_all(
        codes.reshape(peers, cap + 1), PEERS, split_axis=0, concat_axis=0, tiled=True
    ).reshape(peers * (cap + 1))

    sizes = (2 * nblk, 3 * nblk)
    counts = [pltpu.SMEM((size,), jnp.int32) for size in sizes]
    lists = []
    for size in sizes:
        lists += [shape((slots + size * QUAD,), jnp.int32), shape((size + 1,), jnp.int32)]
    by_row, row_at, by_side, side_at = pl.pallas_call(
        functools.partial(plan_kernel, peers, late, nblk),
        out_shape=lists,
        in_specs=[SMEM],
        out_specs=[SMEM] * 4,
        scratch_shapes=counts,
        compiler_params=SMALL,
        cost_estimate=TINY,
        name="plan",
    )(got_codes)

    blocks = (nblk, BLK, width)
    h_blocks, old_blocks = h_input.reshape(blocks), old_one.reshape(blocks)
    base_one, base_two = base_one.reshape(blocks), base_two.reshape(blocks)
    bases, halves = pl.pallas_call(
        functools.partial(turn_kernel, nblk),
        out_shape=[shape((2 * nblk, half, width), F32), shape((3 * nblk, half, width), BF16)],
        in_specs=[ANY] * 5,
        out_specs=[ANY] * 2,
        scratch_shapes=[pltpu.SemaphoreType.DMA((5,))],
        compiler_params=SMALL,
        cost_estimate=TINY,
        name="turn",
    )(h_blocks, base_one, base_two, old_blocks, gathered)
    bases, halves, _ = after((bases, halves, flag))
    bases, halves = swap(bases), swap(halves)
    h_later, _, by_row, by_side = after((h_blocks, flag, by_row, by_side))
    left, right = ring(h_later, 1), ring(h_later, peers - 1)
    left_twin, right_twin = swap(left), swap(right)

    tile_scratch = pltpu.VMEM((slots + 1, half, BLK), BF16)
    cell_shape = (3 * nblk, BLK, full)
    cell_scratch = pltpu.VMEM(cell_shape, BF16)
    mean_scratch = pltpu.VMEM((nblk, half, full), BF16)
    rows_shape = (nblk, half, full)
    total_scratch = pltpu.VMEM(rows_shape, F32)
    inv = inv_degree.reshape(nblk, BLK)

    many = len(arrived_early)
    agg_early, cells_one, own_one, base_two_rows, old_one_rows = pl.pallas_call(
        functools.partial(early_kernel, cap, early, many, nblk),
        out_shape=[
            shape(rows_shape, F32),
            shape(cell_shape, BF16),
            shape(rows_shape, F32),
            shape(rows_shape, F32),
            shape(rows_shape, BF16),
        ],
        in_specs=[SMEM] * 2 + [ANY] * (many + 10) + [VMEM] * 2,
        out_specs=[VMEM] * 5,
        scratch_shapes=[tile_scratch, pltpu.SemaphoreType.DMA((many + 13,))],
        compiler_params=PARAMS,
        cost_estimate=TINY,
        name="early",
    )(
        by_row,
        row_at,
        *arrived_early,
        left,
        left_twin,
        h_blocks,
        halves,
        right,
        right_twin,
        base_one,
        base_two,
        bases,
        old_blocks,
        self_one,
        bias_one.reshape(1, full),
    )

    many = len(arrived_late)
    hidden_rows = pl.pallas_call(
        functools.partial(late_kernel, cap, late, many, nblk),
        out_shape=shape(rows_shape, BF16),
        in_specs=[SMEM] * 3 + [ANY] * many + [VMEM] * 6,
        out_specs=VMEM,
        scratch_shapes=[
            tile_scratch,
            total_scratch,
            mean_scratch,
            pltpu.SemaphoreType.DMA((max(1, many),)),
        ],
        compiler_params=PARAMS,
        cost_estimate=TINY,
        name="late",
    )(
        by_row,
        row_at,
        affected_one,
        *arrived_late,
        cells_one,
        agg_early,
        inv,
        own_one,
        neigh_one,
        old_one_rows,
    )

    hidden_twin = swap(hidden_rows)
    left = ring(hidden_rows, 1)
    right = ring(hidden_rows, peers - 1)

    many = len(arrived)
    agg_two, own_two, hidden_one, tiles_all = pl.pallas_call(
        functools.partial(near_kernel, cap, steps, many, nblk),
        out_shape=[shape(rows_shape, F32)] * 2
        + [shape(blocks, BF16), shape((slots + 1, half, BLK), BF16)],
        in_specs=[SMEM] * 2 + [ANY] * (many + 2) + [VMEM] * 3,
        out_specs=[VMEM] * 2 + [ANY, VMEM],
        scratch_shapes=[cell_scratch, pltpu.SemaphoreType.DMA((many + 4,))],
        compiler_params=PARAMS,
        cost_estimate=TINY,
        name="near",
    )(
        by_side,
        side_at,
        *arrived,
        hidden_rows,
        hidden_twin,
        base_two_rows,
        self_two,
        bias_two.reshape(1, full),
    )

    left, right, agg_two, own_two = after((left, right, agg_two, own_two))
    left_twin = swap(left)
    right_twin = swap(right)
    kept, sent = pl.pallas_call(
        functools.partial(far_kernel, nblk),
        out_shape=[shape((nblk, half, width), BF16)] * 2,
        in_specs=[SMEM] * 2 + [VMEM] + [ANY] * 4 + [VMEM] * 4,
        out_specs=[VMEM] * 2,
        scratch_shapes=[
            cell_scratch,
            total_scratch,
            mean_scratch,
            pltpu.SemaphoreType.DMA((4,)),
        ],
        compiler_params=PARAMS,
        cost_estimate=TINY,
        name="far",
    )(
        by_side,
        side_at,
        tiles_all,
        left,
        left_twin,
        right,
        right_twin,
        agg_two,
        inv,
        own_two,
        neigh_two,
    )
    came = swap(sent)
    hidden_two = pl.pallas_call(
        functools.partial(finish_kernel, nblk),
        out_shape=shape(blocks, BF16),
        in_specs=[SMEM] + [VMEM] * 3,
        out_specs=VMEM,
        compiler_params=SMALL,
        cost_estimate=TINY,
        name="finish",
    )(affected_two, kept, came, old_two.reshape(blocks))
    return (hidden_one.reshape(rows_here, width), hidden_two.reshape(rows_here, width))


def solution(mesh):
    rows = P(("groups", "rows", "feat"))
    cells = P(("groups", "rows", "feat"), "sub")
    placed = (
        cells,
        rows,
        P(("groups", "rows", "feat"), None),
        rows,
        rows,
        P(("groups", "rows", "feat"), None, None),
        cells,
        rows,
        cells,
        P(),
        P(),
        P(),
        cells,
        rows,
        cells,
        P(),
        P(),
        P(),
    )
    return jax.shard_map(
        on_device, mesh=mesh, in_specs=placed, out_specs=(cells, cells), check_vma=False
    )
```

```python
import functools
import math

import jax
import jax.numpy as jnp
from jax import lax
from jax.experimental import pallas as pl
from jax.experimental.pallas import tpu as pltpu
from jax.sharding import PartitionSpec as P

PEERS = ("rows", "feat")
BLK = 128
QUAD = 4
F32 = jnp.float32
BF16 = jnp.bfloat16
ANY = pl.BlockSpec(memory_space=pl.ANY)
HBM = pl.BlockSpec(memory_space=pltpu.HBM)
SMEM = pl.BlockSpec(memory_space=pltpu.SMEM)
VMEM = pl.BlockSpec(memory_space=pltpu.VMEM)
PARAMS = pltpu.CompilerParams(vmem_limit_bytes=20 * 1024 * 1024)
SMALL = pltpu.CompilerParams(vmem_limit_bytes=4 * 1024 * 1024)
TINY = pl.CostEstimate(flops=0, bytes_accessed=128, transcendentals=0)


def first_kernel(peers, cap, lead, dest, row, off, tiles, out, source, fill, codes, sem):
    count = dest.shape[0]
    half = out.shape[1]
    me = lax.axis_index(PEERS)
    first = pl.multiple_of(lax.axis_index("sub") * half, half)
    for to in range(min(peers, 16)):
        fill[to] = 0
    if peers > 16:

        def clear(i, _):
            fill[i] = 0
            return 0

        lax.fori_loop(16, peers, clear, 0)
    for t in range(count):
        to = dest[t]
        at = fill[to]
        fill[to] = at + 1
        source[to * cap + at] = t
    leading = lax.rem(me + lead, peers) if lead else 0

    def send(j, _):
        t = source[leading * cap + j]
        pltpu.make_async_copy(tiles.at[t, pl.ds(first, half)], out.at[j], sem.at[j]).start()
        return 0

    def finish(j, _):
        pltpu.make_async_copy(tiles.at[0, pl.ds(first, half)], out.at[0], sem.at[j]).wait()
        return 0

    def label(to, _):
        def slot(j, _):
            t = source[to * cap + j]
            codes[to * (cap + 1) + j] = row[t] * 32 + off[t] + 8
            return 0

        lax.fori_loop(0, fill[to], slot, 0)
        codes[to * (cap + 1) + cap] = fill[to]
        return 0

    if lead:
        lax.fori_loop(0, fill[leading], send, 0)
    lax.fori_loop(0, peers, label, 0)
    if lead:
        lax.fori_loop(0, fill[leading], finish, 0)


def rest_kernel(peers, cap, order, source, fill, tiles, *refs):
    outs, sems = refs[:-1], refs[-1]
    half = outs[0].shape[1]
    me = lax.axis_index(PEERS)
    first = pl.multiple_of(lax.axis_index("sub") * half, half)
    begun = []
    for n, k in enumerate(order):
        to = lax.rem(me + k, peers)

        def send(j, _, n=n, to=to):
            t = source[to * cap + j]
            pltpu.make_async_copy(
                tiles.at[t, pl.ds(first, half)], outs[n].at[j], sems.at[n, j]
            ).start()
            return 0

        lax.fori_loop(0, fill[to], send, 0)
        begun.append(fill[to])
    for n, amount in enumerate(begun):

        def finish(j, _, n=n):
            pltpu.make_async_copy(
                tiles.at[0, pl.ds(first, half)], outs[n].at[0], sems.at[n, j]
            ).wait()
            return 0

        lax.fori_loop(0, amount, finish, 0)


def sorted_kernel(peers, cap, source, fill, tiles, out, sems):
    half = out.shape[1]
    first = pl.multiple_of(lax.axis_index("sub") * half, half)

    def each(act):
        def peer(to, _):
            def slot(j, _):
                at = to * cap + j
                act(source[at], at)
                return 0

            return lax.fori_loop(0, fill[to], slot, 0)

        lax.fori_loop(0, peers, peer, 0)

    def copy(t, at):
        return pltpu.make_async_copy(tiles.at[t, pl.ds(first, half)], out.at[at], sems.at[t])

    each(lambda t, at: copy(t, at).start())
    each(lambda t, at: copy(t, at).wait())


def turn_kernel(nblk, h, base_one, base_two, old, after, bases, halves, sems):
    half = bases.shape[1]
    other = pl.ds(pl.multiple_of((1 - lax.axis_index("sub")) * half, half), half)
    copies = [
        pltpu.make_async_copy(base_one.at[:, other], bases.at[pl.ds(0, nblk)], sems.at[0]),
        pltpu.make_async_copy(base_two.at[:, other], bases.at[pl.ds(nblk, nblk)], sems.at[1]),
        pltpu.make_async_copy(h.at[:, pl.ds(0, half)], halves.at[pl.ds(0, nblk)], sems.at[2]),
        pltpu.make_async_copy(
            h.at[:, pl.ds(half, half)], halves.at[pl.ds(nblk, nblk)], sems.at[3]
        ),
        pltpu.make_async_copy(old.at[:, other], halves.at[pl.ds(2 * nblk, nblk)], sems.at[4]),
    ]
    for copy in copies:
        copy.start()
    for copy in copies:
        copy.wait()


def plan_kernel(peers, late, nblk, codes, by_row, row_at, by_side, side_at, fill_row, fill_side):
    cap = codes.shape[0] // peers - 1
    nothing = peers * cap * 32 + nblk
    me = lax.axis_index(PEERS)
    for fill in (fill_row, fill_side):
        for g in range(fill.shape[0]):
            fill[g] = 0

    def walk(act):
        def peer(origin, _):
            behind = jnp.int32(0)
            step = lax.rem(me + peers - origin, peers)
            for k in late:
                behind = behind + jnp.where(step == k, nblk, 0)

            def slot(j, _):
                code = codes[origin * (cap + 1) + j]
                row = code >> 5
                col = row + (code & 31)
                side = jnp.where(col < nblk, nblk, jnp.where(col < 2 * nblk, 0, 2 * nblk))
                act(row + behind, row + side, (row << 16) + (origin * cap + j) * 32 + col)
                return 0

            return lax.fori_loop(0, codes[origin * (cap + 1) + cap], slot, 0)

        lax.fori_loop(0, peers, peer, 0)

    def tally(row, side, entry):
        fill_row[row] = fill_row[row] + 1
        fill_side[side] = fill_side[side] + 1

    def place(row, side, entry):
        to = fill_row[row]
        by_row[to] = entry
        fill_row[row] = to + 1
        to = fill_side[side]
        by_side[to] = entry
        fill_side[side] = to + 1

    walk(tally)
    for fill, at, listed in ((fill_row, row_at, by_row), (fill_side, side_at, by_side)):
        now = jnp.int32(0)
        for g in range(fill.shape[0]):
            at[g] = now
            need = (fill[g] + QUAD - 1) // QUAD
            fill[g] = now * QUAD
            now = now + need
            last = jnp.maximum(now * QUAD - QUAD, 0)
            for u in range(QUAD):
                listed[last + u] = nothing + ((g % nblk) << 16)
        at[fill.shape[0]] = now
    walk(place)


def tile_copies(cap, steps, arrived, tiles, sems):
    if steps is None:
        whole = tiles.at[pl.ds(0, arrived[0].shape[0])]
        return [pltpu.make_async_copy(arrived[0], whole, sems.at[0])]
    me = lax.axis_index(PEERS)
    peers = lax.axis_size(PEERS)
    copies = []
    for n, (k, ref) in enumerate(zip(steps, arrived)):
        origin = lax.rem(me + peers - k, peers)
        copies.append(pltpu.make_async_copy(ref, tiles.at[pl.ds(origin * cap, cap)], sems.at[n]))
    return copies


def tile_sums(order, begin, end, tiles, cells, total):
    nothing = (tiles.shape[0] - 1) * 32 + cells.shape[0] // 3

    def step(n, _):
        for q in (begin + 2 * n, begin + 2 * n + 1):
            entry = [jnp.where(q < end, order[q * QUAD + u], nothing) for u in range(QUAD)]
            row = entry[0] >> 16
            tile = [(e >> 5) & 2047 for e in entry]
            cell = [e & 31 for e in entry]
            acc = None
            for u in range(0, QUAD, 2):
                weights = jnp.concatenate([tiles[tile[u]], tiles[tile[u + 1]]], axis=1)
                chosen = jnp.concatenate([cells[cell[u]], cells[cell[u + 1]]], axis=0)
                part = jnp.dot(weights, chosen, preferred_element_type=F32)
                acc = part if acc is None else acc + part
            total[row] = total[row] + acc
        return 0

    lax.fori_loop(0, (end - begin + 1) >> 1, step, 0)


def early_kernel(cap, steps, pieces, nblk, order, at, *refs):
    arrived = refs[:pieces]
    (left, left_twin, h, halves, right, right_twin, base_one, base_two, bases, old) = refs[
        pieces : pieces + 10
    ]
    w_self, bias, agg, cells, own, base_rows, old_rows, tiles, sems = refs[pieces + 10 :]
    sub = lax.axis_index("sub")
    half = agg.shape[1]
    width = h.shape[2]
    lanes = pl.ds(pl.multiple_of(sub * width, width), width)
    others = pl.ds(pl.multiple_of((1 - sub) * width, width), width)
    lines = pl.ds(pl.multiple_of(sub * half, half), half)
    block = [pl.ds(k * nblk, nblk) for k in range(3)]
    low, high = pl.ds(0, half), pl.ds(half, half)
    moves = [
        (left, cells.at[block[0], :, lanes]),
        (left_twin, cells.at[block[0], :, others]),
        (h, cells.at[block[1], :, lanes]),
        (halves.at[block[0]], cells.at[block[1], low, others]),
        (halves.at[block[1]], cells.at[block[1], high, others]),
        (right, cells.at[block[2], :, lanes]),
        (right_twin, cells.at[block[2], :, others]),
        (base_one.at[:, lines], agg.at[:, :, lanes]),
        (bases.at[block[0]], agg.at[:, :, others]),
        (base_two.at[:, lines], base_rows.at[:, :, lanes]),
        (bases.at[block[1]], base_rows.at[:, :, others]),
        (old.at[:, lines], old_rows.at[:, :, lanes]),
        (halves.at[block[2]], old_rows.at[:, :, others]),
    ]
    copies = tile_copies(cap, steps, arrived, tiles, sems)
    for k, (src, dst) in enumerate(moves):
        copies.append(pltpu.make_async_copy(src, dst, sems.at[pieces + k]))
    for copy in copies:
        copy.start()
    tiles[tiles.shape[0] - 1] = jnp.zeros(tiles.shape[1:], tiles.dtype)
    for copy in copies:
        copy.wait()
    tile_sums(order, at[0], at[nblk], tiles, cells, agg)
    for r in range(nblk):
        own[r] = (
            jnp.dot(cells[nblk + r, lines], w_self[...], preferred_element_type=F32) + bias[...]
        )


def column(inv, r, sub, half):
    shape = (half, inv.shape[1])
    line = lax.broadcasted_iota(jnp.int32, shape, 0) + sub * half
    lane = lax.broadcasted_iota(jnp.int32, shape, 1)
    spread = jnp.broadcast_to(inv[r : r + 1, :], shape)
    return jnp.sum(jnp.where(line == lane, spread, 0.0), axis=1, keepdims=True)


def products(means, weight):
    nblk, half, full = means.shape
    few = math.gcd(nblk, 4)
    for g in range(0, nblk, few):
        rows = means[g : g + few].reshape(few * half, full)
        part = jnp.dot(rows, weight[...], preferred_element_type=F32)
        for r in range(few):
            yield g + r, part[r * half : (r + 1) * half]


def late_kernel(cap, steps, pieces, nblk, order, at, affected, *refs):
    arrived = refs[:pieces]
    cells, agg, inv, own, w_neigh, old, out, tiles, total, means, sems = refs[pieces:]
    half = agg.shape[1]
    sub = lax.axis_index("sub")
    copies = tile_copies(cap, steps, arrived, tiles, sems) if pieces else []
    for copy in copies:
        copy.start()
    tiles[tiles.shape[0] - 1] = jnp.zeros(tiles.shape[1:], tiles.dtype)
    for r in range(nblk):
        total[r] = agg[r]
    for copy in copies:
        copy.wait()
    tile_sums(order, at[nblk], at[2 * nblk], tiles, cells, total)
    for r in range(nblk):
        means[r] = (total[r] * column(inv, r, sub, half)).astype(BF16)
    for r, part in products(means, w_neigh):
        pre = jnp.maximum(own[r] + part, 0.0)
        keep = jnp.full((half, 1), affected[r], jnp.int32) > 0
        out[r] = jnp.where(keep, pre, old[r].astype(F32)).astype(BF16)


def near_kernel(cap, steps, pieces, nblk, order, at, *refs):
    arrived = refs[:pieces]
    mine, twin, base, w_self, bias, agg, own, hidden, tiles, cells, sems = refs[pieces:]
    half = base.shape[1]
    width = hidden.shape[2]
    sub = lax.axis_index("sub")
    lanes = pl.ds(pl.multiple_of(sub * width, width), width)
    copies = tile_copies(cap, steps, arrived, tiles, sems)
    for k, (ref, side) in enumerate(((mine, sub), (twin, 1 - sub))):
        lines = pl.ds(pl.multiple_of(side * half, half), half)
        to = cells.at[pl.ds(nblk, nblk), lines]
        copies.append(pltpu.make_async_copy(ref, to, sems.at[pieces + k]))
        to = hidden.at[:, lines]
        copies.append(pltpu.make_async_copy(ref.at[:, :, lanes], to, sems.at[pieces + 2 + k]))
    for copy in copies:
        copy.start()
    tiles[tiles.shape[0] - 1] = jnp.zeros(tiles.shape[1:], tiles.dtype)
    for r in range(nblk):
        agg[r] = base[r]
    for copy in copies:
        copy.wait()
    tile_sums(order, at[0], at[nblk], tiles, cells, agg)
    mine_rows = pl.ds(pl.multiple_of(sub * half, half), half)
    for r in range(nblk):
        own[r] = (
            jnp.dot(cells[nblk + r, mine_rows], w_self[...], preferred_element_type=F32) + bias[...]
        )


def far_kernel(nblk, order, at, tiles, left, left_twin, right, right_twin, *refs):
    agg, inv, own, w_neigh, keep, send, cells, total, means, sems = refs
    half = agg.shape[1]
    width = keep.shape[2]
    sub = lax.axis_index("sub")
    sides = ((left, 0, sub), (left_twin, 0, 1 - sub), (right, 2, sub), (right_twin, 2, 1 - sub))
    copies = []
    for k, (ref, third, side) in enumerate(sides):
        lines = pl.ds(pl.multiple_of(side * half, half), half)
        to = cells.at[pl.ds(third * nblk, nblk), lines]
        copies.append(pltpu.make_async_copy(ref, to, sems.at[k]))
    for copy in copies:
        copy.start()
    cells[nblk] = jnp.zeros(cells.shape[1:], cells.dtype)
    for r in range(nblk):
        total[r] = agg[r]
    for copy in copies:
        copy.wait()
    tile_sums(order, at[nblk], at[3 * nblk], tiles, cells, total)
    for r in range(nblk):
        means[r] = (total[r] * column(inv, r, sub, half)).astype(BF16)
    for r, part in products(means, w_neigh):
        pre = own[r] + part
        low = pre[:, :width]
        high = pre[:, width:]
        first = jnp.full((half, 1), sub, jnp.int32) == 0
        keep[r] = jnp.where(first, low, high).astype(BF16)
        send[r] = jnp.where(first, high, low).astype(BF16)


def finish_kernel(nblk, affected, kept, came, old, out):
    half = kept.shape[1]
    first = jnp.full((half, 1), lax.axis_index("sub"), jnp.int32) == 0
    for r in range(nblk):
        keep = jnp.full((half, 1), affected[r], jnp.int32) > 0
        low = jnp.where(first, kept[r].astype(F32), came[r].astype(F32))
        high = jnp.where(first, came[r].astype(F32), kept[r].astype(F32))
        out[r, :half] = jnp.where(keep, low, old[r, :half].astype(F32)).astype(BF16)
        out[r, half:] = jnp.where(keep, high, old[r, half:].astype(F32)).astype(BF16)


def swap(x):
    return lax.ppermute(x, "sub", [(0, 1), (1, 0)])


def ring(x, step):
    peers = lax.axis_size(PEERS)
    return lax.ppermute(x, PEERS, [(i, (i + step) % peers) for i in range(peers)])


def on_device(
    h_input,
    inv_degree,
    dest_block,
    row_block,
    block_offset,
    new_tiles,
    base_one,
    affected_one,
    old_one,
    self_one,
    neigh_one,
    bias_one,
    base_two,
    affected_two,
    old_two,
    self_two,
    neigh_two,
    bias_two,
):
    peers = lax.axis_size(PEERS)
    count = dest_block.shape[0]
    cap = max(2, 2 * count // peers)
    slots = peers * cap
    rows_here, width = h_input.shape
    full = width * lax.axis_size("sub")
    nblk = rows_here // BLK
    half = BLK // lax.axis_size("sub")
    direct = 2 < peers <= 16
    shape = jax.ShapeDtypeStruct
    after = lax.optimization_barrier

    order = sorted(range(1, peers), key=lambda k: (abs(k - peers // 2), k))
    lead = order[0] if direct else None
    piece = shape((cap, half, BLK), BF16)
    out_piece, source, fill, codes = pl.pallas_call(
        functools.partial(first_kernel, peers, cap, lead),
        out_shape=[
            piece,
            shape((slots,), jnp.int32),
            shape((peers,), jnp.int32),
            shape((peers * (cap + 1),), jnp.int32),
        ],
        in_specs=[SMEM] * 3 + [HBM],
        out_specs=[VMEM] + [SMEM] * 3,
        scratch_shapes=[pltpu.SemaphoreType.DMA((cap,))],
        cost_estimate=TINY,
        name="first",
    )(dest_block.reshape(count), row_block, block_offset, new_tiles)

    if direct:
        got = {lead: out_piece}
        for name, some in (("second", order[1:3]), ("third", order[3:] + [0])):
            packed = pl.pallas_call(
                functools.partial(rest_kernel, peers, cap, some),
                out_shape=[piece] * len(some),
                in_specs=[SMEM, SMEM, HBM],
                out_specs=[VMEM] * len(some),
                scratch_shapes=[pltpu.SemaphoreType.DMA((len(some), cap))],
                cost_estimate=TINY,
                name=name,
            )(source, fill, new_tiles)
            got.update(zip(some, packed))
        steps = order + [0]
        got = {k: ring(got[k], k) if k else got[k] for k in steps}
        late = tuple(order[4:]) if peers > 4 else ()
        early = [k for k in steps if k not in late]
        arrived = [got[k] for k in steps]
        arrived_early = [got[k] for k in early]
        arrived_late = [got[k] for k in late]
        flag = got[lead]
        gathered = packed[-1]
    else:
        sent = pl.pallas_call(
            functools.partial(sorted_kernel, peers, cap),
            out_shape=shape((slots, half, BLK), BF16),
            in_specs=[SMEM, SMEM, HBM],
            out_specs=HBM,
            scratch_shapes=[pltpu.SemaphoreType.DMA((count,))],
            cost_estimate=TINY,
            name="rest",
        )(source, fill, new_tiles)
        sent = sent.reshape(peers, cap, half, BLK)
        got = lax.all_to_all(sent, PEERS, split_axis=0, concat_axis=0, tiled=True)
        arrived = [got.reshape(slots, half, BLK)]
        steps = early = None
        late = ()
        arrived_early, arrived_late = arrived, []
        flag = source
        gathered = out_piece

    got_codes = lax.all_to_all(
        codes.reshape(peers, cap + 1), PEERS, split_axis=0, concat_axis=0, tiled=True
    ).reshape(peers * (cap + 1))

    sizes = (2 * nblk, 3 * nblk)
    counts = [pltpu.SMEM((size,), jnp.int32) for size in sizes]
    lists = []
    for size in sizes:
        lists += [shape((slots + size * QUAD,), jnp.int32), shape((size + 1,), jnp.int32)]
    by_row, row_at, by_side, side_at = pl.pallas_call(
        functools.partial(plan_kernel, peers, late, nblk),
        out_shape=lists,
        in_specs=[SMEM],
        out_specs=[SMEM] * 4,
        scratch_shapes=counts,
        compiler_params=SMALL,
        cost_estimate=TINY,
        name="plan",
    )(got_codes)

    blocks = (nblk, BLK, width)
    h_blocks, old_blocks = h_input.reshape(blocks), old_one.reshape(blocks)
    base_one, base_two = base_one.reshape(blocks), base_two.reshape(blocks)
    bases, halves = pl.pallas_call(
        functools.partial(turn_kernel, nblk),
        out_shape=[shape((2 * nblk, half, width), F32), shape((3 * nblk, half, width), BF16)],
        in_specs=[ANY] * 5,
        out_specs=[ANY] * 2,
        scratch_shapes=[pltpu.SemaphoreType.DMA((5,))],
        compiler_params=SMALL,
        cost_estimate=TINY,
        name="turn",
    )(h_blocks, base_one, base_two, old_blocks, gathered)
    bases, halves, _ = after((bases, halves, flag))
    bases, halves = swap(bases), swap(halves)
    h_later, _, by_row, by_side = after((h_blocks, flag, by_row, by_side))
    left, right = ring(h_later, 1), ring(h_later, peers - 1)
    left_twin, right_twin = swap(left), swap(right)

    tile_scratch = pltpu.VMEM((slots + 1, half, BLK), BF16)
    cell_shape = (3 * nblk, BLK, full)
    cell_scratch = pltpu.VMEM(cell_shape, BF16)
    mean_scratch = pltpu.VMEM((nblk, half, full), BF16)
    rows_shape = (nblk, half, full)
    total_scratch = pltpu.VMEM(rows_shape, F32)
    inv = inv_degree.reshape(nblk, BLK)

    many = len(arrived_early)
    agg_early, cells_one, own_one, base_two_rows, old_one_rows = pl.pallas_call(
        functools.partial(early_kernel, cap, early, many, nblk),
        out_shape=[
            shape(rows_shape, F32),
            shape(cell_shape, BF16),
            shape(rows_shape, F32),
            shape(rows_shape, F32),
            shape(rows_shape, BF16),
        ],
        in_specs=[SMEM] * 2 + [ANY] * (many + 10) + [VMEM] * 2,
        out_specs=[VMEM] * 5,
        scratch_shapes=[tile_scratch, pltpu.SemaphoreType.DMA((many + 13,))],
        compiler_params=PARAMS,
        cost_estimate=TINY,
        name="early",
    )(
        by_row,
        row_at,
        *arrived_early,
        left,
        left_twin,
        h_blocks,
        halves,
        right,
        right_twin,
        base_one,
        base_two,
        bases,
        old_blocks,
        self_one,
        bias_one.reshape(1, full),
    )

    many = len(arrived_late)
    hidden_rows = pl.pallas_call(
        functools.partial(late_kernel, cap, late, many, nblk),
        out_shape=shape(rows_shape, BF16),
        in_specs=[SMEM] * 3 + [ANY] * many + [VMEM] * 6,
        out_specs=VMEM,
        scratch_shapes=[
            tile_scratch,
            total_scratch,
            mean_scratch,
            pltpu.SemaphoreType.DMA((max(1, many),)),
        ],
        compiler_params=PARAMS,
        cost_estimate=TINY,
        name="late",
    )(
        by_row,
        row_at,
        affected_one,
        *arrived_late,
        cells_one,
        agg_early,
        inv,
        own_one,
        neigh_one,
        old_one_rows,
    )

    hidden_twin = swap(hidden_rows)
    left = ring(hidden_rows, 1)
    right = ring(hidden_rows, peers - 1)

    many = len(arrived)
    agg_two, own_two, hidden_one, tiles_all = pl.pallas_call(
        functools.partial(near_kernel, cap, steps, many, nblk),
        out_shape=[shape(rows_shape, F32)] * 2
        + [shape(blocks, BF16), shape((slots + 1, half, BLK), BF16)],
        in_specs=[SMEM] * 2 + [ANY] * (many + 2) + [VMEM] * 3,
        out_specs=[VMEM] * 2 + [ANY, VMEM],
        scratch_shapes=[cell_scratch, pltpu.SemaphoreType.DMA((many + 4,))],
        compiler_params=PARAMS,
        cost_estimate=TINY,
        name="near",
    )(
        by_side,
        side_at,
        *arrived,
        hidden_rows,
        hidden_twin,
        base_two_rows,
        self_two,
        bias_two.reshape(1, full),
    )

    left, right, agg_two, own_two = after((left, right, agg_two, own_two))
    left_twin = swap(left)
    right_twin = swap(right)
    kept, sent = pl.pallas_call(
        functools.partial(far_kernel, nblk),
        out_shape=[shape((nblk, half, width), BF16)] * 2,
        in_specs=[SMEM] * 2 + [VMEM] + [ANY] * 4 + [VMEM] * 4,
        out_specs=[VMEM] * 2,
        scratch_shapes=[
            cell_scratch,
            total_scratch,
            mean_scratch,
            pltpu.SemaphoreType.DMA((4,)),
        ],
        compiler_params=PARAMS,
        cost_estimate=TINY,
        name="far",
    )(
        by_side,
        side_at,
        tiles_all,
        left,
        left_twin,
        right,
        right_twin,
        agg_two,
        inv,
        own_two,
        neigh_two,
    )
    came = swap(sent)
    hidden_two = pl.pallas_call(
        functools.partial(finish_kernel, nblk),
        out_shape=shape(blocks, BF16),
        in_specs=[SMEM] + [VMEM] * 3,
        out_specs=VMEM,
        compiler_params=SMALL,
        cost_estimate=TINY,
        name="finish",
    )(affected_two, kept, came, old_two.reshape(blocks))
    return (hidden_one.reshape(rows_here, width), hidden_two.reshape(rows_here, width))


def solution(mesh):
    rows = P(("groups", "rows", "feat"))
    cells = P(("groups", "rows", "feat"), "sub")
    placed = (
        cells,
        rows,
        P(("groups", "rows", "feat"), None),
        rows,
        rows,
        P(("groups", "rows", "feat"), None, None),
        cells,
        rows,
        cells,
        P(),
        P(),
        P(),
        cells,
        rows,
        cells,
        P(),
        P(),
        P(),
    )
    return jax.shard_map(
        on_device, mesh=mesh, in_specs=placed, out_specs=(cells, cells), check_vma=False
    )
```

```python
import functools
import math

import jax
import jax.numpy as jnp
from jax import lax
from jax.experimental import pallas as pl
from jax.experimental.pallas import tpu as pltpu
from jax.sharding import PartitionSpec as P

PEERS = ("rows", "feat")
BLK = 128
QUAD = 4
F32 = jnp.float32
BF16 = jnp.bfloat16
ANY = pl.BlockSpec(memory_space=pl.ANY)
HBM = pl.BlockSpec(memory_space=pltpu.HBM)
SMEM = pl.BlockSpec(memory_space=pltpu.SMEM)
VMEM = pl.BlockSpec(memory_space=pltpu.VMEM)
PARAMS = pltpu.CompilerParams(vmem_limit_bytes=20 * 1024 * 1024)
SMALL = pltpu.CompilerParams(vmem_limit_bytes=4 * 1024 * 1024)
TINY = pl.CostEstimate(flops=0, bytes_accessed=128, transcendentals=0)


def first_kernel(peers, cap, lead, dest, row, off, tiles, out, source, fill, codes, sem):
    count = dest.shape[0]
    half = out.shape[1]
    me = lax.axis_index(PEERS)
    first = pl.multiple_of(lax.axis_index("sub") * half, half)
    for to in range(min(peers, 16)):
        fill[to] = 0
    if peers > 16:

        def clear(i, _):
            fill[i] = 0
            return 0

        lax.fori_loop(16, peers, clear, 0)
    for t in range(count):
        to = dest[t]
        at = fill[to]
        fill[to] = at + 1
        source[to * cap + at] = t
    leading = lax.rem(me + lead, peers) if lead else 0

    def send(j, _):
        t = source[leading * cap + j]
        pltpu.make_async_copy(tiles.at[t, pl.ds(first, half)], out.at[j], sem.at[j]).start()
        return 0

    def finish(j, _):
        pltpu.make_async_copy(tiles.at[0, pl.ds(first, half)], out.at[0], sem.at[j]).wait()
        return 0

    def label(to, _):
        def slot(j, _):
            t = source[to * cap + j]
            codes[to * (cap + 1) + j] = row[t] * 32 + off[t] + 8
            return 0

        lax.fori_loop(0, fill[to], slot, 0)
        codes[to * (cap + 1) + cap] = fill[to]
        return 0

    if lead:
        lax.fori_loop(0, fill[leading], send, 0)
    lax.fori_loop(0, peers, label, 0)
    if lead:
        lax.fori_loop(0, fill[leading], finish, 0)


def rest_kernel(peers, cap, order, source, fill, tiles, *refs):
    outs, sems = refs[:-1], refs[-1]
    half = outs[0].shape[1]
    me = lax.axis_index(PEERS)
    first = pl.multiple_of(lax.axis_index("sub") * half, half)
    begun = []
    for n, k in enumerate(order):
        to = lax.rem(me + k, peers)

        def send(j, _, n=n, to=to):
            t = source[to * cap + j]
            pltpu.make_async_copy(
                tiles.at[t, pl.ds(first, half)], outs[n].at[j], sems.at[n, j]
            ).start()
            return 0

        lax.fori_loop(0, fill[to], send, 0)
        begun.append(fill[to])
    for n, amount in enumerate(begun):

        def finish(j, _, n=n):
            pltpu.make_async_copy(
                tiles.at[0, pl.ds(first, half)], outs[n].at[0], sems.at[n, j]
            ).wait()
            return 0

        lax.fori_loop(0, amount, finish, 0)


def sorted_kernel(peers, cap, source, fill, tiles, out, sems):
    half = out.shape[1]
    first = pl.multiple_of(lax.axis_index("sub") * half, half)

    def each(act):
        def peer(to, _):
            def slot(j, _):
                at = to * cap + j
                act(source[at], at)
                return 0

            return lax.fori_loop(0, fill[to], slot, 0)

        lax.fori_loop(0, peers, peer, 0)

    def copy(t, at):
        return pltpu.make_async_copy(tiles.at[t, pl.ds(first, half)], out.at[at], sems.at[t])

    each(lambda t, at: copy(t, at).start())
    each(lambda t, at: copy(t, at).wait())


def turn_kernel(nblk, h, base_one, base_two, old, after, bases, halves, sems):
    half = bases.shape[1]
    other = pl.ds(pl.multiple_of((1 - lax.axis_index("sub")) * half, half), half)
    copies = [
        pltpu.make_async_copy(base_one.at[:, other], bases.at[pl.ds(0, nblk)], sems.at[0]),
        pltpu.make_async_copy(base_two.at[:, other], bases.at[pl.ds(nblk, nblk)], sems.at[1]),
        pltpu.make_async_copy(h.at[:, pl.ds(0, half)], halves.at[pl.ds(0, nblk)], sems.at[2]),
        pltpu.make_async_copy(
            h.at[:, pl.ds(half, half)], halves.at[pl.ds(nblk, nblk)], sems.at[3]
        ),
        pltpu.make_async_copy(old.at[:, other], halves.at[pl.ds(2 * nblk, nblk)], sems.at[4]),
    ]
    for copy in copies:
        copy.start()
    for copy in copies:
        copy.wait()


def plan_kernel(peers, late, nblk, codes, by_row, row_at, by_side, side_at, fill_row, fill_side):
    cap = codes.shape[0] // peers - 1
    nothing = peers * cap * 32 + nblk
    me = lax.axis_index(PEERS)
    for fill in (fill_row, fill_side):
        for g in range(fill.shape[0]):
            fill[g] = 0

    def walk(act):
        def peer(origin, _):
            behind = jnp.int32(0)
            step = lax.rem(me + peers - origin, peers)
            for k in late:
                behind = behind + jnp.where(step == k, nblk, 0)

            def slot(j, _):
                code = codes[origin * (cap + 1) + j]
                row = code >> 5
                col = row + (code & 31)
                side = jnp.where(col < nblk, nblk, jnp.where(col < 2 * nblk, 0, 2 * nblk))
                act(row + behind, row + side, (row << 16) + (origin * cap + j) * 32 + col)
                return 0

            return lax.fori_loop(0, codes[origin * (cap + 1) + cap], slot, 0)

        lax.fori_loop(0, peers, peer, 0)

    def tally(row, side, entry):
        fill_row[row] = fill_row[row] + 1
        fill_side[side] = fill_side[side] + 1

    def place(row, side, entry):
        to = fill_row[row]
        by_row[to] = entry
        fill_row[row] = to + 1
        to = fill_side[side]
        by_side[to] = entry
        fill_side[side] = to + 1

    walk(tally)
    for fill, at, listed in ((fill_row, row_at, by_row), (fill_side, side_at, by_side)):
        now = jnp.int32(0)
        for g in range(fill.shape[0]):
            at[g] = now
            need = (fill[g] + QUAD - 1) // QUAD
            fill[g] = now * QUAD
            now = now + need
            last = jnp.maximum(now * QUAD - QUAD, 0)
            for u in range(QUAD):
                listed[last + u] = nothing + ((g % nblk) << 16)
        at[fill.shape[0]] = now
    walk(place)


def tile_copies(cap, steps, arrived, tiles, sems):
    if steps is None:
        whole = tiles.at[pl.ds(0, arrived[0].shape[0])]
        return [pltpu.make_async_copy(arrived[0], whole, sems.at[0])]
    me = lax.axis_index(PEERS)
    peers = lax.axis_size(PEERS)
    copies = []
    for n, (k, ref) in enumerate(zip(steps, arrived)):
        origin = lax.rem(me + peers - k, peers)
        copies.append(pltpu.make_async_copy(ref, tiles.at[pl.ds(origin * cap, cap)], sems.at[n]))
    return copies


def tile_sums(order, begin, end, tiles, cells, total):
    nothing = (tiles.shape[0] - 1) * 32 + cells.shape[0] // 3

    def step(n, _):
        for q in (begin + 2 * n, begin + 2 * n + 1):
            entry = [jnp.where(q < end, order[q * QUAD + u], nothing) for u in range(QUAD)]
            row = entry[0] >> 16
            tile = [(e >> 5) & 2047 for e in entry]
            cell = [e & 31 for e in entry]
            acc = None
            for u in range(0, QUAD, 2):
                weights = jnp.concatenate([tiles[tile[u]], tiles[tile[u + 1]]], axis=1)
                chosen = jnp.concatenate([cells[cell[u]], cells[cell[u + 1]]], axis=0)
                part = jnp.dot(weights, chosen, preferred_element_type=F32)
                acc = part if acc is None else acc + part
            total[row] = total[row] + acc
        return 0

    lax.fori_loop(0, (end - begin + 1) >> 1, step, 0)


def early_kernel(cap, steps, pieces, nblk, order, at, *refs):
    arrived = refs[:pieces]
    (left, left_twin, h, halves, right, right_twin, base_one, base_two, bases, old) = refs[
        pieces : pieces + 10
    ]
    w_self, bias, agg, cells, own, base_rows, old_rows, tiles, sems = refs[pieces + 10 :]
    sub = lax.axis_index("sub")
    half = agg.shape[1]
    width = h.shape[2]
    lanes = pl.ds(pl.multiple_of(sub * width, width), width)
    others = pl.ds(pl.multiple_of((1 - sub) * width, width), width)
    lines = pl.ds(pl.multiple_of(sub * half, half), half)
    block = [pl.ds(k * nblk, nblk) for k in range(3)]
    low, high = pl.ds(0, half), pl.ds(half, half)
    moves = [
        (left, cells.at[block[0], :, lanes]),
        (left_twin, cells.at[block[0], :, others]),
        (h, cells.at[block[1], :, lanes]),
        (halves.at[block[0]], cells.at[block[1], low, others]),
        (halves.at[block[1]], cells.at[block[1], high, others]),
        (right, cells.at[block[2], :, lanes]),
        (right_twin, cells.at[block[2], :, others]),
        (base_one.at[:, lines], agg.at[:, :, lanes]),
        (bases.at[block[0]], agg.at[:, :, others]),
        (base_two.at[:, lines], base_rows.at[:, :, lanes]),
        (bases.at[block[1]], base_rows.at[:, :, others]),
        (old.at[:, lines], old_rows.at[:, :, lanes]),
        (halves.at[block[2]], old_rows.at[:, :, others]),
    ]
    copies = tile_copies(cap, steps, arrived, tiles, sems)
    for k, (src, dst) in enumerate(moves):
        copies.append(pltpu.make_async_copy(src, dst, sems.at[pieces + k]))
    for copy in copies:
        copy.start()
    tiles[tiles.shape[0] - 1] = jnp.zeros(tiles.shape[1:], tiles.dtype)
    for copy in copies:
        copy.wait()
    tile_sums(order, at[0], at[nblk], tiles, cells, agg)
    for r in range(nblk):
        own[r] = (
            jnp.dot(cells[nblk + r, lines], w_self[...], preferred_element_type=F32) + bias[...]
        )


def column(inv, r, sub, half):
    shape = (half, inv.shape[1])
    line = lax.broadcasted_iota(jnp.int32, shape, 0) + sub * half
    lane = lax.broadcasted_iota(jnp.int32, shape, 1)
    spread = jnp.broadcast_to(inv[r : r + 1, :], shape)
    return jnp.sum(jnp.where(line == lane, spread, 0.0), axis=1, keepdims=True)


def products(means, weight):
    nblk, half, full = means.shape
    few = math.gcd(nblk, 4)
    for g in range(0, nblk, few):
        rows = means[g : g + few].reshape(few * half, full)
        part = jnp.dot(rows, weight[...], preferred_element_type=F32)
        for r in range(few):
            yield g + r, part[r * half : (r + 1) * half]


def late_kernel(cap, steps, pieces, nblk, order, at, affected, *refs):
    arrived = refs[:pieces]
    cells, agg, inv, own, w_neigh, old, out, tiles, total, means, sems = refs[pieces:]
    half = agg.shape[1]
    sub = lax.axis_index("sub")
    copies = tile_copies(cap, steps, arrived, tiles, sems) if pieces else []
    for copy in copies:
        copy.start()
    tiles[tiles.shape[0] - 1] = jnp.zeros(tiles.shape[1:], tiles.dtype)
    for r in range(nblk):
        total[r] = agg[r]
    for copy in copies:
        copy.wait()
    tile_sums(order, at[nblk], at[2 * nblk], tiles, cells, total)
    for r in range(nblk):
        means[r] = (total[r] * column(inv, r, sub, half)).astype(BF16)
    for r, part in products(means, w_neigh):
        pre = jnp.maximum(own[r] + part, 0.0)
        keep = jnp.full((half, 1), affected[r], jnp.int32) > 0
        out[r] = jnp.where(keep, pre, old[r].astype(F32)).astype(BF16)


def near_kernel(cap, steps, pieces, nblk, order, at, *refs):
    arrived = refs[:pieces]
    mine, twin, base, w_self, bias, agg, own, hidden, tiles, cells, sems = refs[pieces:]
    half = base.shape[1]
    width = hidden.shape[2]
    sub = lax.axis_index("sub")
    lanes = pl.ds(pl.multiple_of(sub * width, width), width)
    copies = tile_copies(cap, steps, arrived, tiles, sems)
    for k, (ref, side) in enumerate(((mine, sub), (twin, 1 - sub))):
        lines = pl.ds(pl.multiple_of(side * half, half), half)
        to = cells.at[pl.ds(nblk, nblk), lines]
        copies.append(pltpu.make_async_copy(ref, to, sems.at[pieces + k]))
        to = hidden.at[:, lines]
        copies.append(pltpu.make_async_copy(ref.at[:, :, lanes], to, sems.at[pieces + 2 + k]))
    for copy in copies:
        copy.start()
    tiles[tiles.shape[0] - 1] = jnp.zeros(tiles.shape[1:], tiles.dtype)
    for r in range(nblk):
        agg[r] = base[r]
    for copy in copies:
        copy.wait()
    tile_sums(order, at[0], at[nblk], tiles, cells, agg)
    mine_rows = pl.ds(pl.multiple_of(sub * half, half), half)
    for r in range(nblk):
        own[r] = (
            jnp.dot(cells[nblk + r, mine_rows], w_self[...], preferred_element_type=F32) + bias[...]
        )


def far_kernel(nblk, order, at, tiles, left, left_twin, right, right_twin, *refs):
    agg, inv, own, w_neigh, keep, send, cells, total, means, sems = refs
    half = agg.shape[1]
    width = keep.shape[2]
    sub = lax.axis_index("sub")
    sides = ((left, 0, sub), (left_twin, 0, 1 - sub), (right, 2, sub), (right_twin, 2, 1 - sub))
    copies = []
    for k, (ref, third, side) in enumerate(sides):
        lines = pl.ds(pl.multiple_of(side * half, half), half)
        to = cells.at[pl.ds(third * nblk, nblk), lines]
        copies.append(pltpu.make_async_copy(ref, to, sems.at[k]))
    for copy in copies:
        copy.start()
    cells[nblk] = jnp.zeros(cells.shape[1:], cells.dtype)
    for r in range(nblk):
        total[r] = agg[r]
    for copy in copies:
        copy.wait()
    tile_sums(order, at[nblk], at[3 * nblk], tiles, cells, total)
    for r in range(nblk):
        means[r] = (total[r] * column(inv, r, sub, half)).astype(BF16)
    for r, part in products(means, w_neigh):
        pre = own[r] + part
        low = pre[:, :width]
        high = pre[:, width:]
        first = jnp.full((half, 1), sub, jnp.int32) == 0
        keep[r] = jnp.where(first, low, high).astype(BF16)
        send[r] = jnp.where(first, high, low).astype(BF16)


def finish_kernel(nblk, affected, kept, came, old, out):
    half = kept.shape[1]
    first = jnp.full((half, 1), lax.axis_index("sub"), jnp.int32) == 0
    for r in range(nblk):
        keep = jnp.full((half, 1), affected[r], jnp.int32) > 0
        low = jnp.where(first, kept[r].astype(F32), came[r].astype(F32))
        high = jnp.where(first, came[r].astype(F32), kept[r].astype(F32))
        out[r, :half] = jnp.where(keep, low, old[r, :half].astype(F32)).astype(BF16)
        out[r, half:] = jnp.where(keep, high, old[r, half:].astype(F32)).astype(BF16)


def swap(x):
    return lax.ppermute(x, "sub", [(0, 1), (1, 0)])


def ring(x, step):
    peers = lax.axis_size(PEERS)
    return lax.ppermute(x, PEERS, [(i, (i + step) % peers) for i in range(peers)])


def on_device(
    h_input,
    inv_degree,
    dest_block,
    row_block,
    block_offset,
    new_tiles,
    base_one,
    affected_one,
    old_one,
    self_one,
    neigh_one,
    bias_one,
    base_two,
    affected_two,
    old_two,
    self_two,
    neigh_two,
    bias_two,
):
    peers = lax.axis_size(PEERS)
    count = dest_block.shape[0]
    cap = max(2, 2 * count // peers)
    slots = peers * cap
    rows_here, width = h_input.shape
    full = width * lax.axis_size("sub")
    nblk = rows_here // BLK
    half = BLK // lax.axis_size("sub")
    direct = 2 < peers <= 16
    shape = jax.ShapeDtypeStruct
    after = lax.optimization_barrier

    order = sorted(range(1, peers), key=lambda k: (abs(k - peers // 2), k))
    lead = order[0] if direct else None
    piece = shape((cap, half, BLK), BF16)
    out_piece, source, fill, codes = pl.pallas_call(
        functools.partial(first_kernel, peers, cap, lead),
        out_shape=[
            piece,
            shape((slots,), jnp.int32),
            shape((peers,), jnp.int32),
            shape((peers * (cap + 1),), jnp.int32),
        ],
        in_specs=[SMEM] * 3 + [HBM],
        out_specs=[VMEM] + [SMEM] * 3,
        scratch_shapes=[pltpu.SemaphoreType.DMA((cap,))],
        cost_estimate=TINY,
        name="first",
    )(dest_block.reshape(count), row_block, block_offset, new_tiles)

    got_codes = lax.all_to_all(
        codes.reshape(peers, cap + 1), PEERS, split_axis=0, concat_axis=0, tiled=True
    ).reshape(peers * (cap + 1))

    if direct:
        got = {lead: out_piece}
        for name, some in (("second", order[1:3]), ("third", order[3:] + [0])):
            packed = pl.pallas_call(
                functools.partial(rest_kernel, peers, cap, some),
                out_shape=[piece] * len(some),
                in_specs=[SMEM, SMEM, HBM],
                out_specs=[VMEM] * len(some),
                scratch_shapes=[pltpu.SemaphoreType.DMA((len(some), cap))],
                cost_estimate=TINY,
                name=name,
            )(source, fill, new_tiles)
            if name == "second":
                packed, got_codes, fill = after((packed, got_codes, fill))
            got.update(zip(some, packed))
        steps = order + [0]
        got = {k: ring(got[k], k) if k else got[k] for k in steps}
        late = tuple(order[4:]) if peers > 4 else ()
        early = [k for k in steps if k not in late]
        arrived = [got[k] for k in steps]
        arrived_early = [got[k] for k in early]
        arrived_late = [got[k] for k in late]
        flag = got[lead]
        gathered = packed[-1]
    else:
        sent = pl.pallas_call(
            functools.partial(sorted_kernel, peers, cap),
            out_shape=shape((slots, half, BLK), BF16),
            in_specs=[SMEM, SMEM, HBM],
            out_specs=HBM,
            scratch_shapes=[pltpu.SemaphoreType.DMA((count,))],
            cost_estimate=TINY,
            name="rest",
        )(source, fill, new_tiles)
        sent = sent.reshape(peers, cap, half, BLK)
        got = lax.all_to_all(sent, PEERS, split_axis=0, concat_axis=0, tiled=True)
        arrived = [got.reshape(slots, half, BLK)]
        steps = early = None
        late = ()
        arrived_early, arrived_late = arrived, []
        flag = source
        gathered = out_piece

    got_codes, flag = after((got_codes, flag))
    sizes = (2 * nblk, 3 * nblk)
    counts = [pltpu.SMEM((size,), jnp.int32) for size in sizes]
    lists = []
    for size in sizes:
        lists += [shape((slots + size * QUAD,), jnp.int32), shape((size + 1,), jnp.int32)]
    by_row, row_at, by_side, side_at = pl.pallas_call(
        functools.partial(plan_kernel, peers, late, nblk),
        out_shape=lists,
        in_specs=[SMEM],
        out_specs=[SMEM] * 4,
        scratch_shapes=counts,
        compiler_params=SMALL,
        cost_estimate=TINY,
        name="plan",
    )(got_codes)

    blocks = (nblk, BLK, width)
    h_blocks, old_blocks = h_input.reshape(blocks), old_one.reshape(blocks)
    base_one, base_two = base_one.reshape(blocks), base_two.reshape(blocks)
    bases, halves = pl.pallas_call(
        functools.partial(turn_kernel, nblk),
        out_shape=[shape((2 * nblk, half, width), F32), shape((3 * nblk, half, width), BF16)],
        in_specs=[ANY] * 5,
        out_specs=[ANY] * 2,
        scratch_shapes=[pltpu.SemaphoreType.DMA((5,))],
        compiler_params=SMALL,
        cost_estimate=TINY,
        name="turn",
    )(h_blocks, base_one, base_two, old_blocks, gathered)
    bases, halves, _ = after((bases, halves, flag))
    bases, halves = swap(bases), swap(halves)
    h_later, _, by_row, by_side = after((h_blocks, flag, by_row, by_side))
    left, right = ring(h_later, 1), ring(h_later, peers - 1)
    left_twin, right_twin = swap(left), swap(right)

    tile_scratch = pltpu.VMEM((slots + 1, half, BLK), BF16)
    cell_shape = (3 * nblk, BLK, full)
    cell_scratch = pltpu.VMEM(cell_shape, BF16)
    mean_scratch = pltpu.VMEM((nblk, half, full), BF16)
    rows_shape = (nblk, half, full)
    total_scratch = pltpu.VMEM(rows_shape, F32)
    inv = inv_degree.reshape(nblk, BLK)

    many = len(arrived_early)
    agg_early, cells_one, own_one, base_two_rows, old_one_rows = pl.pallas_call(
        functools.partial(early_kernel, cap, early, many, nblk),
        out_shape=[
            shape(rows_shape, F32),
            shape(cell_shape, BF16),
            shape(rows_shape, F32),
            shape(rows_shape, F32),
            shape(rows_shape, BF16),
        ],
        in_specs=[SMEM] * 2 + [ANY] * (many + 10) + [VMEM] * 2,
        out_specs=[VMEM] * 5,
        scratch_shapes=[tile_scratch, pltpu.SemaphoreType.DMA((many + 13,))],
        compiler_params=PARAMS,
        cost_estimate=TINY,
        name="early",
    )(
        by_row,
        row_at,
        *arrived_early,
        left,
        left_twin,
        h_blocks,
        halves,
        right,
        right_twin,
        base_one,
        base_two,
        bases,
        old_blocks,
        self_one,
        bias_one.reshape(1, full),
    )

    many = len(arrived_late)
    hidden_rows = pl.pallas_call(
        functools.partial(late_kernel, cap, late, many, nblk),
        out_shape=shape(rows_shape, BF16),
        in_specs=[SMEM] * 3 + [ANY] * many + [VMEM] * 6,
        out_specs=VMEM,
        scratch_shapes=[
            tile_scratch,
            total_scratch,
            mean_scratch,
            pltpu.SemaphoreType.DMA((max(1, many),)),
        ],
        compiler_params=PARAMS,
        cost_estimate=TINY,
        name="late",
    )(
        by_row,
        row_at,
        affected_one,
        *arrived_late,
        cells_one,
        agg_early,
        inv,
        own_one,
        neigh_one,
        old_one_rows,
    )

    hidden_twin = swap(hidden_rows)
    left = ring(hidden_rows, 1)
    right = ring(hidden_rows, peers - 1)

    many = len(arrived)
    agg_two, own_two, hidden_one, tiles_all = pl.pallas_call(
        functools.partial(near_kernel, cap, steps, many, nblk),
        out_shape=[shape(rows_shape, F32)] * 2
        + [shape(blocks, BF16), shape((slots + 1, half, BLK), BF16)],
        in_specs=[SMEM] * 2 + [ANY] * (many + 2) + [VMEM] * 3,
        out_specs=[VMEM] * 2 + [ANY, VMEM],
        scratch_shapes=[cell_scratch, pltpu.SemaphoreType.DMA((many + 4,))],
        compiler_params=PARAMS,
        cost_estimate=TINY,
        name="near",
    )(
        by_side,
        side_at,
        *arrived,
        hidden_rows,
        hidden_twin,
        base_two_rows,
        self_two,
        bias_two.reshape(1, full),
    )

    left, right, agg_two, own_two = after((left, right, agg_two, own_two))
    left_twin = swap(left)
    right_twin = swap(right)
    kept, sent = pl.pallas_call(
        functools.partial(far_kernel, nblk),
        out_shape=[shape((nblk, half, width), BF16)] * 2,
        in_specs=[SMEM] * 2 + [VMEM] + [ANY] * 4 + [VMEM] * 4,
        out_specs=[VMEM] * 2,
        scratch_shapes=[
            cell_scratch,
            total_scratch,
            mean_scratch,
            pltpu.SemaphoreType.DMA((4,)),
        ],
        compiler_params=PARAMS,
        cost_estimate=TINY,
        name="far",
    )(
        by_side,
        side_at,
        tiles_all,
        left,
        left_twin,
        right,
        right_twin,
        agg_two,
        inv,
        own_two,
        neigh_two,
    )
    came = swap(sent)
    hidden_two = pl.pallas_call(
        functools.partial(finish_kernel, nblk),
        out_shape=shape(blocks, BF16),
        in_specs=[SMEM] + [VMEM] * 3,
        out_specs=VMEM,
        compiler_params=SMALL,
        cost_estimate=TINY,
        name="finish",
    )(affected_two, kept, came, old_two.reshape(blocks))
    return (hidden_one.reshape(rows_here, width), hidden_two.reshape(rows_here, width))


def solution(mesh):
    rows = P(("groups", "rows", "feat"))
    cells = P(("groups", "rows", "feat"), "sub")
    placed = (
        cells,
        rows,
        P(("groups", "rows", "feat"), None),
        rows,
        rows,
        P(("groups", "rows", "feat"), None, None),
        cells,
        rows,
        cells,
        P(),
        P(),
        P(),
        cells,
        rows,
        cells,
        P(),
        P(),
        P(),
    )
    return jax.shard_map(
        on_device, mesh=mesh, in_specs=placed, out_specs=(cells, cells), check_vma=False
    )
```

```python
import functools
import math

import jax
import jax.numpy as jnp
from jax import lax
from jax.experimental import pallas as pl
from jax.experimental.pallas import tpu as pltpu
from jax.sharding import PartitionSpec as P

PEERS = ("rows", "feat")
BLK = 128
QUAD = 4
F32 = jnp.float32
BF16 = jnp.bfloat16
ANY = pl.BlockSpec(memory_space=pl.ANY)
HBM = pl.BlockSpec(memory_space=pltpu.HBM)
SMEM = pl.BlockSpec(memory_space=pltpu.SMEM)
VMEM = pl.BlockSpec(memory_space=pltpu.VMEM)
PARAMS = pltpu.CompilerParams(vmem_limit_bytes=20 * 1024 * 1024)
SMALL = pltpu.CompilerParams(vmem_limit_bytes=4 * 1024 * 1024)
TINY = pl.CostEstimate(flops=0, bytes_accessed=128, transcendentals=0)


def first_kernel(peers, cap, lead, dest, row, off, tiles, out, source, fill, codes, sem):
    count = dest.shape[0]
    half = out.shape[1]
    me = lax.axis_index(PEERS)
    first = pl.multiple_of(lax.axis_index("sub") * half, half)
    for to in range(min(peers, 16)):
        fill[to] = 0
    if peers > 16:

        def clear(i, _):
            fill[i] = 0
            return 0

        lax.fori_loop(16, peers, clear, 0)
    for t in range(count):
        to = dest[t]
        at = fill[to]
        fill[to] = at + 1
        source[to * cap + at] = t
    leading = lax.rem(me + lead, peers) if lead else 0

    def send(j, _):
        t = source[leading * cap + j]
        pltpu.make_async_copy(tiles.at[t, pl.ds(first, half)], out.at[j], sem.at[j]).start()
        return 0

    def finish(j, _):
        pltpu.make_async_copy(tiles.at[0, pl.ds(first, half)], out.at[0], sem.at[j]).wait()
        return 0

    def label(to, _):
        def slot(j, _):
            t = source[to * cap + j]
            codes[to * (cap + 1) + j] = row[t] * 32 + off[t] + 8
            return 0

        lax.fori_loop(0, fill[to], slot, 0)
        codes[to * (cap + 1) + cap] = fill[to]
        return 0

    if lead:
        lax.fori_loop(0, fill[leading], send, 0)
    lax.fori_loop(0, peers, label, 0)
    if lead:
        lax.fori_loop(0, fill[leading], finish, 0)


def rest_kernel(peers, cap, order, source, fill, tiles, *refs):
    outs, sems = refs[:-1], refs[-1]
    half = outs[0].shape[1]
    me = lax.axis_index(PEERS)
    first = pl.multiple_of(lax.axis_index("sub") * half, half)
    begun = []
    for n, k in enumerate(order):
        to = lax.rem(me + k, peers)

        def send(j, _, n=n, to=to):
            t = source[to * cap + j]
            pltpu.make_async_copy(
                tiles.at[t, pl.ds(first, half)], outs[n].at[j], sems.at[n, j]
            ).start()
            return 0

        lax.fori_loop(0, fill[to], send, 0)
        begun.append(fill[to])
    for n, amount in enumerate(begun):

        def finish(j, _, n=n):
            pltpu.make_async_copy(
                tiles.at[0, pl.ds(first, half)], outs[n].at[0], sems.at[n, j]
            ).wait()
            return 0

        lax.fori_loop(0, amount, finish, 0)


def sorted_kernel(peers, cap, source, fill, tiles, out, sems):
    half = out.shape[1]
    first = pl.multiple_of(lax.axis_index("sub") * half, half)

    def each(act):
        def peer(to, _):
            def slot(j, _):
                at = to * cap + j
                act(source[at], at)
                return 0

            return lax.fori_loop(0, fill[to], slot, 0)

        lax.fori_loop(0, peers, peer, 0)

    def copy(t, at):
        return pltpu.make_async_copy(tiles.at[t, pl.ds(first, half)], out.at[at], sems.at[t])

    each(lambda t, at: copy(t, at).start())
    each(lambda t, at: copy(t, at).wait())


def turn_kernel(nblk, h, base_one, base_two, old, after, bases, halves, sems):
    half = bases.shape[1]
    other = pl.ds(pl.multiple_of((1 - lax.axis_index("sub")) * half, half), half)
    copies = [
        pltpu.make_async_copy(base_one.at[:, other], bases.at[pl.ds(0, nblk)], sems.at[0]),
        pltpu.make_async_copy(base_two.at[:, other], bases.at[pl.ds(nblk, nblk)], sems.at[1]),
        pltpu.make_async_copy(h.at[:, pl.ds(0, half)], halves.at[pl.ds(0, nblk)], sems.at[2]),
        pltpu.make_async_copy(
            h.at[:, pl.ds(half, half)], halves.at[pl.ds(nblk, nblk)], sems.at[3]
        ),
        pltpu.make_async_copy(old.at[:, other], halves.at[pl.ds(2 * nblk, nblk)], sems.at[4]),
    ]
    for copy in copies:
        copy.start()
    for copy in copies:
        copy.wait()


def plan_kernel(peers, late, nblk, codes, by_row, row_at, by_side, side_at, fill_row, fill_side):
    cap = codes.shape[0] // peers - 1
    nothing = peers * cap * 32 + nblk
    me = lax.axis_index(PEERS)
    for fill in (fill_row, fill_side):
        for g in range(fill.shape[0]):
            fill[g] = 0

    def walk(act):
        def peer(origin, _):
            behind = jnp.int32(0)
            step = lax.rem(me + peers - origin, peers)
            for k in late:
                behind = behind + jnp.where(step == k, nblk, 0)

            def slot(j, _):
                code = codes[origin * (cap + 1) + j]
                row = code >> 5
                col = row + (code & 31)
                side = jnp.where(col < nblk, nblk, jnp.where(col < 2 * nblk, 0, 2 * nblk))
                act(row + behind, row + side, (row << 16) + (origin * cap + j) * 32 + col)
                return 0

            return lax.fori_loop(0, codes[origin * (cap + 1) + cap], slot, 0)

        lax.fori_loop(0, peers, peer, 0)

    def tally(row, side, entry):
        fill_row[row] = fill_row[row] + 1
        fill_side[side] = fill_side[side] + 1

    def place(row, side, entry):
        to = fill_row[row]
        by_row[to] = entry
        fill_row[row] = to + 1
        to = fill_side[side]
        by_side[to] = entry
        fill_side[side] = to + 1

    walk(tally)
    for fill, at, listed in ((fill_row, row_at, by_row), (fill_side, side_at, by_side)):
        now = jnp.int32(0)
        for g in range(fill.shape[0]):
            at[g] = now
            need = (fill[g] + QUAD - 1) // QUAD
            fill[g] = now * QUAD
            now = now + need
            last = jnp.maximum(now * QUAD - QUAD, 0)
            for u in range(QUAD):
                listed[last + u] = nothing + ((g % nblk) << 16)
        at[fill.shape[0]] = now
    walk(place)


def tile_copies(cap, steps, arrived, tiles, sems):
    if steps is None:
        whole = tiles.at[pl.ds(0, arrived[0].shape[0])]
        return [pltpu.make_async_copy(arrived[0], whole, sems.at[0])]
    me = lax.axis_index(PEERS)
    peers = lax.axis_size(PEERS)
    copies = []
    for n, (k, ref) in enumerate(zip(steps, arrived)):
        origin = lax.rem(me + peers - k, peers)
        copies.append(pltpu.make_async_copy(ref, tiles.at[pl.ds(origin * cap, cap)], sems.at[n]))
    return copies


def tile_sums(order, begin, end, tiles, cells, total):
    nothing = (tiles.shape[0] - 1) * 32 + cells.shape[0] // 3

    def step(n, _):
        for k in range(4):
            q = begin + 4 * n + k
            at = jnp.minimum(q, end - 1) * QUAD
            entry = [jnp.where(q < end, order[at + u], nothing) for u in range(QUAD)]
            row = entry[0] >> 16
            tile = [(e >> 5) & 2047 for e in entry]
            cell = [e & 31 for e in entry]
            acc = None
            for u in range(0, QUAD, 2):
                weights = jnp.concatenate([tiles[tile[u]], tiles[tile[u + 1]]], axis=1)
                chosen = jnp.concatenate([cells[cell[u]], cells[cell[u + 1]]], axis=0)
                part = jnp.dot(weights, chosen, preferred_element_type=F32)
                acc = part if acc is None else acc + part
            total[row] = total[row] + acc
        return 0

    lax.fori_loop(0, (end - begin + 3) >> 2, step, 0)


def early_kernel(cap, steps, pieces, nblk, order, at, *refs):
    arrived = refs[:pieces]
    (left, left_twin, h, halves, right, right_twin, base_one, base_two, bases, old) = refs[
        pieces : pieces + 10
    ]
    w_self, bias, agg, cells, own, base_rows, old_rows, tiles, sems = refs[pieces + 10 :]
    sub = lax.axis_index("sub")
    half = agg.shape[1]
    width = h.shape[2]
    lanes = pl.ds(pl.multiple_of(sub * width, width), width)
    others = pl.ds(pl.multiple_of((1 - sub) * width, width), width)
    lines = pl.ds(pl.multiple_of(sub * half, half), half)
    block = [pl.ds(k * nblk, nblk) for k in range(3)]
    low, high = pl.ds(0, half), pl.ds(half, half)
    moves = [
        (left, cells.at[block[0], :, lanes]),
        (left_twin, cells.at[block[0], :, others]),
        (h, cells.at[block[1], :, lanes]),
        (halves.at[block[0]], cells.at[block[1], low, others]),
        (halves.at[block[1]], cells.at[block[1], high, others]),
        (right, cells.at[block[2], :, lanes]),
        (right_twin, cells.at[block[2], :, others]),
        (base_one.at[:, lines], agg.at[:, :, lanes]),
        (bases.at[block[0]], agg.at[:, :, others]),
        (base_two.at[:, lines], base_rows.at[:, :, lanes]),
        (bases.at[block[1]], base_rows.at[:, :, others]),
        (old.at[:, lines], old_rows.at[:, :, lanes]),
        (halves.at[block[2]], old_rows.at[:, :, others]),
    ]
    copies = tile_copies(cap, steps, arrived, tiles, sems)
    for k, (src, dst) in enumerate(moves):
        copies.append(pltpu.make_async_copy(src, dst, sems.at[pieces + k]))
    for copy in copies:
        copy.start()
    tiles[tiles.shape[0] - 1] = jnp.zeros(tiles.shape[1:], tiles.dtype)
    for copy in copies:
        copy.wait()
    tile_sums(order, at[0], at[nblk], tiles, cells, agg)
    for r in range(nblk):
        own[r] = (
            jnp.dot(cells[nblk + r, lines], w_self[...], preferred_element_type=F32) + bias[...]
        )


def column(inv, r, sub, half):
    shape = (half, inv.shape[1])
    line = lax.broadcasted_iota(jnp.int32, shape, 0) + sub * half
    lane = lax.broadcasted_iota(jnp.int32, shape, 1)
    spread = jnp.broadcast_to(inv[r : r + 1, :], shape)
    return jnp.sum(jnp.where(line == lane, spread, 0.0), axis=1, keepdims=True)


def products(means, weight):
    nblk, half, full = means.shape
    few = math.gcd(nblk, 4)
    for g in range(0, nblk, few):
        rows = means[g : g + few].reshape(few * half, full)
        part = jnp.dot(rows, weight[...], preferred_element_type=F32)
        for r in range(few):
            yield g + r, part[r * half : (r + 1) * half]


def late_kernel(cap, steps, pieces, nblk, order, at, affected, *refs):
    arrived = refs[:pieces]
    cells, agg, inv, own, w_neigh, old, out, tiles, total, means, sems = refs[pieces:]
    half = agg.shape[1]
    sub = lax.axis_index("sub")
    copies = tile_copies(cap, steps, arrived, tiles, sems) if pieces else []
    for copy in copies:
        copy.start()
    tiles[tiles.shape[0] - 1] = jnp.zeros(tiles.shape[1:], tiles.dtype)
    for r in range(nblk):
        total[r] = agg[r]
    for copy in copies:
        copy.wait()
    tile_sums(order, at[nblk], at[2 * nblk], tiles, cells, total)
    for r in range(nblk):
        means[r] = (total[r] * column(inv, r, sub, half)).astype(BF16)
    for r, part in products(means, w_neigh):
        pre = jnp.maximum(own[r] + part, 0.0)
        keep = jnp.full((half, 1), affected[r], jnp.int32) > 0
        out[r] = jnp.where(keep, pre, old[r].astype(F32)).astype(BF16)


def near_kernel(cap, steps, pieces, nblk, order, at, *refs):
    arrived = refs[:pieces]
    mine, twin, base, w_self, bias, agg, own, hidden, tiles, cells, sems = refs[pieces:]
    half = base.shape[1]
    width = hidden.shape[2]
    sub = lax.axis_index("sub")
    lanes = pl.ds(pl.multiple_of(sub * width, width), width)
    copies = tile_copies(cap, steps, arrived, tiles, sems)
    for k, (ref, side) in enumerate(((mine, sub), (twin, 1 - sub))):
        lines = pl.ds(pl.multiple_of(side * half, half), half)
        to = cells.at[pl.ds(nblk, nblk), lines]
        copies.append(pltpu.make_async_copy(ref, to, sems.at[pieces + k]))
        to = hidden.at[:, lines]
        copies.append(pltpu.make_async_copy(ref.at[:, :, lanes], to, sems.at[pieces + 2 + k]))
    for copy in copies:
        copy.start()
    tiles[tiles.shape[0] - 1] = jnp.zeros(tiles.shape[1:], tiles.dtype)
    for r in range(nblk):
        agg[r] = base[r]
    for copy in copies:
        copy.wait()
    tile_sums(order, at[0], at[nblk], tiles, cells, agg)
    mine_rows = pl.ds(pl.multiple_of(sub * half, half), half)
    for r in range(nblk):
        own[r] = (
            jnp.dot(cells[nblk + r, mine_rows], w_self[...], preferred_element_type=F32) + bias[...]
        )


def far_kernel(nblk, order, at, tiles, left, left_twin, right, right_twin, *refs):
    agg, inv, own, w_neigh, keep, send, cells, total, means, sems = refs
    half = agg.shape[1]
    width = keep.shape[2]
    sub = lax.axis_index("sub")
    sides = ((left, 0, sub), (left_twin, 0, 1 - sub), (right, 2, sub), (right_twin, 2, 1 - sub))
    copies = []
    for k, (ref, third, side) in enumerate(sides):
        lines = pl.ds(pl.multiple_of(side * half, half), half)
        to = cells.at[pl.ds(third * nblk, nblk), lines]
        copies.append(pltpu.make_async_copy(ref, to, sems.at[k]))
    for copy in copies:
        copy.start()
    cells[nblk] = jnp.zeros(cells.shape[1:], cells.dtype)
    for r in range(nblk):
        total[r] = agg[r]
    for copy in copies:
        copy.wait()
    tile_sums(order, at[nblk], at[3 * nblk], tiles, cells, total)
    for r in range(nblk):
        means[r] = (total[r] * column(inv, r, sub, half)).astype(BF16)
    for r, part in products(means, w_neigh):
        pre = own[r] + part
        low = pre[:, :width]
        high = pre[:, width:]
        first = jnp.full((half, 1), sub, jnp.int32) == 0
        keep[r] = jnp.where(first, low, high).astype(BF16)
        send[r] = jnp.where(first, high, low).astype(BF16)


def finish_kernel(nblk, affected, kept, came, old, out):
    half = kept.shape[1]
    first = jnp.full((half, 1), lax.axis_index("sub"), jnp.int32) == 0
    for r in range(nblk):
        keep = jnp.full((half, 1), affected[r], jnp.int32) > 0
        low = jnp.where(first, kept[r].astype(F32), came[r].astype(F32))
        high = jnp.where(first, came[r].astype(F32), kept[r].astype(F32))
        out[r, :half] = jnp.where(keep, low, old[r, :half].astype(F32)).astype(BF16)
        out[r, half:] = jnp.where(keep, high, old[r, half:].astype(F32)).astype(BF16)


def swap(x):
    return lax.ppermute(x, "sub", [(0, 1), (1, 0)])


def ring(x, step):
    peers = lax.axis_size(PEERS)
    return lax.ppermute(x, PEERS, [(i, (i + step) % peers) for i in range(peers)])


def on_device(
    h_input,
    inv_degree,
    dest_block,
    row_block,
    block_offset,
    new_tiles,
    base_one,
    affected_one,
    old_one,
    self_one,
    neigh_one,
    bias_one,
    base_two,
    affected_two,
    old_two,
    self_two,
    neigh_two,
    bias_two,
):
    peers = lax.axis_size(PEERS)
    count = dest_block.shape[0]
    cap = max(2, 2 * count // peers)
    slots = peers * cap
    rows_here, width = h_input.shape
    full = width * lax.axis_size("sub")
    nblk = rows_here // BLK
    half = BLK // lax.axis_size("sub")
    direct = 2 < peers <= 16
    shape = jax.ShapeDtypeStruct
    after = lax.optimization_barrier

    order = sorted(range(1, peers), key=lambda k: (abs(k - peers // 2), k))
    lead = order[0] if direct else None
    piece = shape((cap, half, BLK), BF16)
    out_piece, source, fill, codes = pl.pallas_call(
        functools.partial(first_kernel, peers, cap, lead),
        out_shape=[
            piece,
            shape((slots,), jnp.int32),
            shape((peers,), jnp.int32),
            shape((peers * (cap + 1),), jnp.int32),
        ],
        in_specs=[SMEM] * 3 + [HBM],
        out_specs=[VMEM] + [SMEM] * 3,
        scratch_shapes=[pltpu.SemaphoreType.DMA((cap,))],
        cost_estimate=TINY,
        name="first",
    )(dest_block.reshape(count), row_block, block_offset, new_tiles)

    if direct:
        others = order[1:] + [0]
        packed = pl.pallas_call(
            functools.partial(rest_kernel, peers, cap, others),
            out_shape=[piece] * len(others),
            in_specs=[SMEM, SMEM, HBM],
            out_specs=[VMEM] * len(others),
            scratch_shapes=[pltpu.SemaphoreType.DMA((len(others), cap))],
            cost_estimate=TINY,
            name="rest",
        )(source, fill, new_tiles)
        steps = order + [0]
        got = dict(zip(others, packed))
        got[lead] = out_piece
        got = {k: ring(got[k], k) if k else got[k] for k in steps}
        late = tuple(order[4:]) if peers > 4 else ()
        early = [k for k in steps if k not in late]
        arrived = [got[k] for k in steps]
        arrived_early = [got[k] for k in early]
        arrived_late = [got[k] for k in late]
        flag = got[lead]
        gathered = packed[-1]
    else:
        sent = pl.pallas_call(
            functools.partial(sorted_kernel, peers, cap),
            out_shape=shape((slots, half, BLK), BF16),
            in_specs=[SMEM, SMEM, HBM],
            out_specs=HBM,
            scratch_shapes=[pltpu.SemaphoreType.DMA((count,))],
            cost_estimate=TINY,
            name="rest",
        )(source, fill, new_tiles)
        sent = sent.reshape(peers, cap, half, BLK)
        got = lax.all_to_all(sent, PEERS, split_axis=0, concat_axis=0, tiled=True)
        arrived = [got.reshape(slots, half, BLK)]
        steps = early = None
        late = ()
        arrived_early, arrived_late = arrived, []
        flag = source
        gathered = out_piece

    got_codes = lax.all_to_all(
        codes.reshape(peers, cap + 1), PEERS, split_axis=0, concat_axis=0, tiled=True
    ).reshape(peers * (cap + 1))

    sizes = (2 * nblk, 3 * nblk)
    counts = [pltpu.SMEM((size,), jnp.int32) for size in sizes]
    lists = []
    for size in sizes:
        lists += [shape((slots + size * QUAD,), jnp.int32), shape((size + 1,), jnp.int32)]
    by_row, row_at, by_side, side_at = pl.pallas_call(
        functools.partial(plan_kernel, peers, late, nblk),
        out_shape=lists,
        in_specs=[SMEM],
        out_specs=[SMEM] * 4,
        scratch_shapes=counts,
        compiler_params=SMALL,
        cost_estimate=TINY,
        name="plan",
    )(got_codes)

    blocks = (nblk, BLK, width)
    h_blocks, old_blocks = h_input.reshape(blocks), old_one.reshape(blocks)
    base_one, base_two = base_one.reshape(blocks), base_two.reshape(blocks)
    bases, halves = pl.pallas_call(
        functools.partial(turn_kernel, nblk),
        out_shape=[shape((2 * nblk, half, width), F32), shape((3 * nblk, half, width), BF16)],
        in_specs=[ANY] * 5,
        out_specs=[ANY] * 2,
        scratch_shapes=[pltpu.SemaphoreType.DMA((5,))],
        compiler_params=SMALL,
        cost_estimate=TINY,
        name="turn",
    )(h_blocks, base_one, base_two, old_blocks, gathered)
    bases, halves, _ = after((bases, halves, flag))
    bases, halves = swap(bases), swap(halves)
    h_later, _, by_row, by_side = after((h_blocks, flag, by_row, by_side))
    left, right = ring(h_later, 1), ring(h_later, peers - 1)
    left_twin, right_twin = swap(left), swap(right)

    tile_scratch = pltpu.VMEM((slots + 1, half, BLK), BF16)
    cell_shape = (3 * nblk, BLK, full)
    cell_scratch = pltpu.VMEM(cell_shape, BF16)
    mean_scratch = pltpu.VMEM((nblk, half, full), BF16)
    rows_shape = (nblk, half, full)
    total_scratch = pltpu.VMEM(rows_shape, F32)
    inv = inv_degree.reshape(nblk, BLK)

    many = len(arrived_early)
    agg_early, cells_one, own_one, base_two_rows, old_one_rows = pl.pallas_call(
        functools.partial(early_kernel, cap, early, many, nblk),
        out_shape=[
            shape(rows_shape, F32),
            shape(cell_shape, BF16),
            shape(rows_shape, F32),
            shape(rows_shape, F32),
            shape(rows_shape, BF16),
        ],
        in_specs=[SMEM] * 2 + [ANY] * (many + 10) + [VMEM] * 2,
        out_specs=[VMEM] * 5,
        scratch_shapes=[tile_scratch, pltpu.SemaphoreType.DMA((many + 13,))],
        compiler_params=PARAMS,
        cost_estimate=TINY,
        name="early",
    )(
        by_row,
        row_at,
        *arrived_early,
        left,
        left_twin,
        h_blocks,
        halves,
        right,
        right_twin,
        base_one,
        base_two,
        bases,
        old_blocks,
        self_one,
        bias_one.reshape(1, full),
    )

    many = len(arrived_late)
    hidden_rows = pl.pallas_call(
        functools.partial(late_kernel, cap, late, many, nblk),
        out_shape=shape(rows_shape, BF16),
        in_specs=[SMEM] * 3 + [ANY] * many + [VMEM] * 6,
        out_specs=VMEM,
        scratch_shapes=[
            tile_scratch,
            total_scratch,
            mean_scratch,
            pltpu.SemaphoreType.DMA((max(1, many),)),
        ],
        compiler_params=PARAMS,
        cost_estimate=TINY,
        name="late",
    )(
        by_row,
        row_at,
        affected_one,
        *arrived_late,
        cells_one,
        agg_early,
        inv,
        own_one,
        neigh_one,
        old_one_rows,
    )

    hidden_twin = swap(hidden_rows)
    left = ring(hidden_rows, 1)
    right = ring(hidden_rows, peers - 1)

    many = len(arrived)
    agg_two, own_two, hidden_one, tiles_all = pl.pallas_call(
        functools.partial(near_kernel, cap, steps, many, nblk),
        out_shape=[shape(rows_shape, F32)] * 2
        + [shape(blocks, BF16), shape((slots + 1, half, BLK), BF16)],
        in_specs=[SMEM] * 2 + [ANY] * (many + 2) + [VMEM] * 3,
        out_specs=[VMEM] * 2 + [ANY, VMEM],
        scratch_shapes=[cell_scratch, pltpu.SemaphoreType.DMA((many + 4,))],
        compiler_params=PARAMS,
        cost_estimate=TINY,
        name="near",
    )(
        by_side,
        side_at,
        *arrived,
        hidden_rows,
        hidden_twin,
        base_two_rows,
        self_two,
        bias_two.reshape(1, full),
    )

    left, right, agg_two, own_two = after((left, right, agg_two, own_two))
    left_twin = swap(left)
    right_twin = swap(right)
    kept, sent = pl.pallas_call(
        functools.partial(far_kernel, nblk),
        out_shape=[shape((nblk, half, width), BF16)] * 2,
        in_specs=[SMEM] * 2 + [VMEM] + [ANY] * 4 + [VMEM] * 4,
        out_specs=[VMEM] * 2,
        scratch_shapes=[
            cell_scratch,
            total_scratch,
            mean_scratch,
            pltpu.SemaphoreType.DMA((4,)),
        ],
        compiler_params=PARAMS,
        cost_estimate=TINY,
        name="far",
    )(
        by_side,
        side_at,
        tiles_all,
        left,
        left_twin,
        right,
        right_twin,
        agg_two,
        inv,
        own_two,
        neigh_two,
    )
    came = swap(sent)
    hidden_two = pl.pallas_call(
        functools.partial(finish_kernel, nblk),
        out_shape=shape(blocks, BF16),
        in_specs=[SMEM] + [VMEM] * 3,
        out_specs=VMEM,
        compiler_params=SMALL,
        cost_estimate=TINY,
        name="finish",
    )(affected_two, kept, came, old_two.reshape(blocks))
    return (hidden_one.reshape(rows_here, width), hidden_two.reshape(rows_here, width))


def solution(mesh):
    rows = P(("groups", "rows", "feat"))
    cells = P(("groups", "rows", "feat"), "sub")
    placed = (
        cells,
        rows,
        P(("groups", "rows", "feat"), None),
        rows,
        rows,
        P(("groups", "rows", "feat"), None, None),
        cells,
        rows,
        cells,
        P(),
        P(),
        P(),
        cells,
        rows,
        cells,
        P(),
        P(),
        P(),
    )
    return jax.shard_map(
        on_device, mesh=mesh, in_specs=placed, out_specs=(cells, cells), check_vma=False
    )
```

```python
import functools

import jax
import jax.numpy as jnp
from jax import lax
from jax.experimental import pallas as pl
from jax.experimental.pallas import tpu as pltpu
from jax.sharding import PartitionSpec as P

PEERS = ("rows", "feat")
BLK = 128
QUAD = 4
F32 = jnp.float32
BF16 = jnp.bfloat16
ANY = pl.BlockSpec(memory_space=pl.ANY)
HBM = pl.BlockSpec(memory_space=pltpu.HBM)
SMEM = pl.BlockSpec(memory_space=pltpu.SMEM)
VMEM = pl.BlockSpec(memory_space=pltpu.VMEM)
PARAMS = pltpu.CompilerParams(vmem_limit_bytes=20 * 1024 * 1024)
SMALL = pltpu.CompilerParams(vmem_limit_bytes=4 * 1024 * 1024)
TINY = pl.CostEstimate(flops=0, bytes_accessed=128, transcendentals=0)


def first_kernel(peers, cap, lead, dest, row, off, tiles, out, source, fill, codes, sem):
    count = dest.shape[0]
    half = out.shape[1]
    me = lax.axis_index(PEERS)
    first = pl.multiple_of(lax.axis_index("sub") * half, half)
    for to in range(min(peers, 16)):
        fill[to] = 0
    if peers > 16:

        def clear(i, _):
            fill[i] = 0
            return 0

        lax.fori_loop(16, peers, clear, 0)
    for t in range(count):
        to = dest[t]
        at = fill[to]
        fill[to] = at + 1
        source[to * cap + at] = t
    leading = lax.rem(me + lead, peers) if lead else 0

    def send(j, _):
        t = source[leading * cap + j]
        pltpu.make_async_copy(tiles.at[t, pl.ds(first, half)], out.at[j], sem.at[j]).start()
        return 0

    def finish(j, _):
        pltpu.make_async_copy(tiles.at[0, pl.ds(first, half)], out.at[0], sem.at[j]).wait()
        return 0

    def label(to, _):
        def slot(j, _):
            t = source[to * cap + j]
            codes[to * (cap + 1) + j] = row[t] * 32 + off[t] + 8
            return 0

        lax.fori_loop(0, fill[to], slot, 0)
        codes[to * (cap + 1) + cap] = fill[to]
        return 0

    if lead:
        lax.fori_loop(0, fill[leading], send, 0)
    lax.fori_loop(0, peers, label, 0)
    if lead:
        lax.fori_loop(0, fill[leading], finish, 0)


def rest_kernel(peers, cap, order, source, fill, tiles, *refs):
    outs, sems = refs[:-1], refs[-1]
    half = outs[0].shape[1]
    me = lax.axis_index(PEERS)
    first = pl.multiple_of(lax.axis_index("sub") * half, half)
    begun = []
    for n, k in enumerate(order):
        to = lax.rem(me + k, peers)

        def send(j, _, n=n, to=to):
            t = source[to * cap + j]
            pltpu.make_async_copy(
                tiles.at[t, pl.ds(first, half)], outs[n].at[j], sems.at[n, j]
            ).start()
            return 0

        lax.fori_loop(0, fill[to], send, 0)
        begun.append(fill[to])
    for n, amount in enumerate(begun):

        def finish(j, _, n=n):
            pltpu.make_async_copy(
                tiles.at[0, pl.ds(first, half)], outs[n].at[0], sems.at[n, j]
            ).wait()
            return 0

        lax.fori_loop(0, amount, finish, 0)


def sorted_kernel(peers, cap, source, fill, tiles, out, sems):
    half = out.shape[1]
    first = pl.multiple_of(lax.axis_index("sub") * half, half)

    def each(act):
        def peer(to, _):
            def slot(j, _):
                at = to * cap + j
                act(source[at], at)
                return 0

            return lax.fori_loop(0, fill[to], slot, 0)

        lax.fori_loop(0, peers, peer, 0)

    def copy(t, at):
        return pltpu.make_async_copy(tiles.at[t, pl.ds(first, half)], out.at[at], sems.at[t])

    each(lambda t, at: copy(t, at).start())
    each(lambda t, at: copy(t, at).wait())


def turn_kernel(nblk, h, base_one, base_two, old, after, bases, halves, sems):
    half = bases.shape[1]
    other = pl.ds(pl.multiple_of((1 - lax.axis_index("sub")) * half, half), half)
    copies = [
        pltpu.make_async_copy(base_one.at[:, other], bases.at[pl.ds(0, nblk)], sems.at[0]),
        pltpu.make_async_copy(base_two.at[:, other], bases.at[pl.ds(nblk, nblk)], sems.at[1]),
        pltpu.make_async_copy(h.at[:, pl.ds(0, half)], halves.at[pl.ds(0, nblk)], sems.at[2]),
        pltpu.make_async_copy(
            h.at[:, pl.ds(half, half)], halves.at[pl.ds(nblk, nblk)], sems.at[3]
        ),
        pltpu.make_async_copy(old.at[:, other], halves.at[pl.ds(2 * nblk, nblk)], sems.at[4]),
    ]
    for copy in copies:
        copy.start()
    for copy in copies:
        copy.wait()


def plan_kernel(peers, late, nblk, codes, by_row, row_at, by_side, side_at, fill_row, fill_side):
    cap = codes.shape[0] // peers - 1
    nothing = peers * cap * 32 + nblk
    me = lax.axis_index(PEERS)
    for fill in (fill_row, fill_side):
        for g in range(fill.shape[0]):
            fill[g] = 0

    def walk(act):
        def peer(origin, _):
            behind = jnp.int32(0)
            step = lax.rem(me + peers - origin, peers)
            for k in late:
                behind = behind + jnp.where(step == k, nblk, 0)

            def slot(j, _):
                code = codes[origin * (cap + 1) + j]
                row = code >> 5
                col = row + (code & 31)
                side = jnp.where(col < nblk, nblk, jnp.where(col < 2 * nblk, 0, 2 * nblk))
                act(row + behind, row + side, (row << 16) + (origin * cap + j) * 32 + col)
                return 0

            return lax.fori_loop(0, codes[origin * (cap + 1) + cap], slot, 0)

        lax.fori_loop(0, peers, peer, 0)

    def tally(row, side, entry):
        fill_row[row] = fill_row[row] + 1
        fill_side[side] = fill_side[side] + 1

    def place(row, side, entry):
        to = fill_row[row]
        by_row[to] = entry
        fill_row[row] = to + 1
        to = fill_side[side]
        by_side[to] = entry
        fill_side[side] = to + 1

    walk(tally)
    for fill, at, listed in ((fill_row, row_at, by_row), (fill_side, side_at, by_side)):
        now = jnp.int32(0)
        for g in range(fill.shape[0]):
            at[g] = now
            need = (fill[g] + QUAD - 1) // QUAD
            fill[g] = now * QUAD
            now = now + need
            last = jnp.maximum(now * QUAD - QUAD, 0)
            for u in range(QUAD):
                listed[last + u] = nothing + ((g % nblk) << 16)
        at[fill.shape[0]] = now
    walk(place)


def tile_copies(cap, steps, arrived, tiles, sems):
    if steps is None:
        whole = tiles.at[pl.ds(0, arrived[0].shape[0])]
        return [pltpu.make_async_copy(arrived[0], whole, sems.at[0])]
    me = lax.axis_index(PEERS)
    peers = lax.axis_size(PEERS)
    copies = []
    for n, (k, ref) in enumerate(zip(steps, arrived)):
        origin = lax.rem(me + peers - k, peers)
        copies.append(pltpu.make_async_copy(ref, tiles.at[pl.ds(origin * cap, cap)], sems.at[n]))
    return copies


def tile_sums(order, begin, end, tiles, cells, total):
    nothing = (tiles.shape[0] - 1) * 32 + cells.shape[0] // 3

    def step(n, _):
        for k in range(4):
            q = begin + 4 * n + k
            at = jnp.minimum(q, end - 1) * QUAD
            entry = [jnp.where(q < end, order[at + u], nothing) for u in range(QUAD)]
            row = entry[0] >> 16
            tile = [(e >> 5) & 2047 for e in entry]
            cell = [e & 31 for e in entry]
            acc = None
            for u in range(0, QUAD, 2):
                weights = jnp.concatenate([tiles[tile[u]], tiles[tile[u + 1]]], axis=1)
                chosen = jnp.concatenate([cells[cell[u]], cells[cell[u + 1]]], axis=0)
                part = jnp.dot(weights, chosen, preferred_element_type=F32)
                acc = part if acc is None else acc + part
            total[row] = total[row] + acc
        return 0

    lax.fori_loop(0, (end - begin + 3) >> 2, step, 0)


def early_kernel(cap, steps, pieces, nblk, order, at, *refs):
    arrived = refs[:pieces]
    (left, left_twin, h, halves, right, right_twin, base_one, base_two, bases, old) = refs[
        pieces : pieces + 10
    ]
    w_self, bias, agg, cells, own, base_rows, old_rows, tiles, sems = refs[pieces + 10 :]
    sub = lax.axis_index("sub")
    half = agg.shape[1]
    width = h.shape[2]
    lanes = pl.ds(pl.multiple_of(sub * width, width), width)
    others = pl.ds(pl.multiple_of((1 - sub) * width, width), width)
    lines = pl.ds(pl.multiple_of(sub * half, half), half)
    block = [pl.ds(k * nblk, nblk) for k in range(3)]
    low, high = pl.ds(0, half), pl.ds(half, half)
    moves = [
        (left, cells.at[block[0], :, lanes]),
        (left_twin, cells.at[block[0], :, others]),
        (h, cells.at[block[1], :, lanes]),
        (halves.at[block[0]], cells.at[block[1], low, others]),
        (halves.at[block[1]], cells.at[block[1], high, others]),
        (right, cells.at[block[2], :, lanes]),
        (right_twin, cells.at[block[2], :, others]),
        (base_one.at[:, lines], agg.at[:, :, lanes]),
        (bases.at[block[0]], agg.at[:, :, others]),
        (base_two.at[:, lines], base_rows.at[:, :, lanes]),
        (bases.at[block[1]], base_rows.at[:, :, others]),
        (old.at[:, lines], old_rows.at[:, :, lanes]),
        (halves.at[block[2]], old_rows.at[:, :, others]),
    ]
    copies = tile_copies(cap, steps, arrived, tiles, sems)
    for k, (src, dst) in enumerate(moves):
        copies.append(pltpu.make_async_copy(src, dst, sems.at[pieces + k]))
    for copy in copies:
        copy.start()
    tiles[tiles.shape[0] - 1] = jnp.zeros(tiles.shape[1:], tiles.dtype)
    for copy in copies:
        copy.wait()
    tile_sums(order, at[0], at[nblk], tiles, cells, agg)
    for r in range(nblk):
        own[r] = (
            jnp.dot(cells[nblk + r, lines], w_self[...], preferred_element_type=F32) + bias[...]
        )


def column(inv, r, sub, half):
    shape = (half, inv.shape[1])
    line = lax.broadcasted_iota(jnp.int32, shape, 0) + sub * half
    lane = lax.broadcasted_iota(jnp.int32, shape, 1)
    spread = jnp.broadcast_to(inv[r : r + 1, :], shape)
    return jnp.sum(jnp.where(line == lane, spread, 0.0), axis=1, keepdims=True)


def products(means, weight):
    nblk, half, full = means.shape
    few = nblk
    for g in range(0, nblk, few):
        rows = means[g : g + few].reshape(few * half, full)
        part = jnp.dot(rows, weight[...], preferred_element_type=F32)
        for r in range(few):
            yield g + r, part[r * half : (r + 1) * half]


def late_kernel(cap, steps, pieces, nblk, order, at, affected, *refs):
    arrived = refs[:pieces]
    cells, agg, inv, own, w_neigh, old, out, tiles, total, means, sems = refs[pieces:]
    half = agg.shape[1]
    sub = lax.axis_index("sub")
    copies = tile_copies(cap, steps, arrived, tiles, sems) if pieces else []
    for copy in copies:
        copy.start()
    tiles[tiles.shape[0] - 1] = jnp.zeros(tiles.shape[1:], tiles.dtype)
    for r in range(nblk):
        total[r] = agg[r]
    for copy in copies:
        copy.wait()
    tile_sums(order, at[nblk], at[2 * nblk], tiles, cells, total)
    for r in range(nblk):
        means[r] = (total[r] * column(inv, r, sub, half)).astype(BF16)
    for r, part in products(means, w_neigh):
        pre = jnp.maximum(own[r] + part, 0.0)
        keep = jnp.full((half, 1), affected[r], jnp.int32) > 0
        out[r] = jnp.where(keep, pre, old[r].astype(F32)).astype(BF16)


def near_kernel(cap, steps, pieces, nblk, order, at, *refs):
    arrived = refs[:pieces]
    mine, twin, base, w_self, bias, agg, own, hidden, tiles, cells, sems = refs[pieces:]
    half = base.shape[1]
    width = hidden.shape[2]
    sub = lax.axis_index("sub")
    lanes = pl.ds(pl.multiple_of(sub * width, width), width)
    copies = tile_copies(cap, steps, arrived, tiles, sems)
    for k, (ref, side) in enumerate(((mine, sub), (twin, 1 - sub))):
        lines = pl.ds(pl.multiple_of(side * half, half), half)
        to = cells.at[pl.ds(nblk, nblk), lines]
        copies.append(pltpu.make_async_copy(ref, to, sems.at[pieces + k]))
        to = hidden.at[:, lines]
        copies.append(pltpu.make_async_copy(ref.at[:, :, lanes], to, sems.at[pieces + 2 + k]))
    for copy in copies:
        copy.start()
    tiles[tiles.shape[0] - 1] = jnp.zeros(tiles.shape[1:], tiles.dtype)
    for r in range(nblk):
        agg[r] = base[r]
    for copy in copies:
        copy.wait()
    tile_sums(order, at[0], at[nblk], tiles, cells, agg)
    mine_rows = pl.ds(pl.multiple_of(sub * half, half), half)
    for r in range(nblk):
        own[r] = (
            jnp.dot(cells[nblk + r, mine_rows], w_self[...], preferred_element_type=F32) + bias[...]
        )


def far_kernel(nblk, order, at, tiles, left, left_twin, right, right_twin, *refs):
    agg, inv, own, w_neigh, keep, send, cells, total, means, sems = refs
    half = agg.shape[1]
    width = keep.shape[2]
    sub = lax.axis_index("sub")
    sides = ((left, 0, sub), (left_twin, 0, 1 - sub), (right, 2, sub), (right_twin, 2, 1 - sub))
    copies = []
    for k, (ref, third, side) in enumerate(sides):
        lines = pl.ds(pl.multiple_of(side * half, half), half)
        to = cells.at[pl.ds(third * nblk, nblk), lines]
        copies.append(pltpu.make_async_copy(ref, to, sems.at[k]))
    for copy in copies:
        copy.start()
    cells[nblk] = jnp.zeros(cells.shape[1:], cells.dtype)
    for r in range(nblk):
        total[r] = agg[r]
    for copy in copies:
        copy.wait()
    tile_sums(order, at[nblk], at[3 * nblk], tiles, cells, total)
    for r in range(nblk):
        means[r] = (total[r] * column(inv, r, sub, half)).astype(BF16)
    for r, part in products(means, w_neigh):
        pre = own[r] + part
        low = pre[:, :width]
        high = pre[:, width:]
        first = jnp.full((half, 1), sub, jnp.int32) == 0
        keep[r] = jnp.where(first, low, high).astype(BF16)
        send[r] = jnp.where(first, high, low).astype(BF16)


def finish_kernel(nblk, affected, kept, came, old, out):
    half = kept.shape[1]
    first = jnp.full((half, 1), lax.axis_index("sub"), jnp.int32) == 0
    for r in range(nblk):
        keep = jnp.full((half, 1), affected[r], jnp.int32) > 0
        low = jnp.where(first, kept[r].astype(F32), came[r].astype(F32))
        high = jnp.where(first, came[r].astype(F32), kept[r].astype(F32))
        out[r, :half] = jnp.where(keep, low, old[r, :half].astype(F32)).astype(BF16)
        out[r, half:] = jnp.where(keep, high, old[r, half:].astype(F32)).astype(BF16)


def swap(x):
    return lax.ppermute(x, "sub", [(0, 1), (1, 0)])


def ring(x, step):
    peers = lax.axis_size(PEERS)
    return lax.ppermute(x, PEERS, [(i, (i + step) % peers) for i in range(peers)])


def on_device(
    h_input,
    inv_degree,
    dest_block,
    row_block,
    block_offset,
    new_tiles,
    base_one,
    affected_one,
    old_one,
    self_one,
    neigh_one,
    bias_one,
    base_two,
    affected_two,
    old_two,
    self_two,
    neigh_two,
    bias_two,
):
    peers = lax.axis_size(PEERS)
    count = dest_block.shape[0]
    cap = max(2, 2 * count // peers)
    slots = peers * cap
    rows_here, width = h_input.shape
    full = width * lax.axis_size("sub")
    nblk = rows_here // BLK
    half = BLK // lax.axis_size("sub")
    direct = 2 < peers <= 16
    shape = jax.ShapeDtypeStruct
    after = lax.optimization_barrier

    order = sorted(range(1, peers), key=lambda k: (abs(k - peers // 2), k))
    lead = order[0] if direct else None
    piece = shape((cap, half, BLK), BF16)
    out_piece, source, fill, codes = pl.pallas_call(
        functools.partial(first_kernel, peers, cap, lead),
        out_shape=[
            piece,
            shape((slots,), jnp.int32),
            shape((peers,), jnp.int32),
            shape((peers * (cap + 1),), jnp.int32),
        ],
        in_specs=[SMEM] * 3 + [HBM],
        out_specs=[VMEM] + [SMEM] * 3,
        scratch_shapes=[pltpu.SemaphoreType.DMA((cap,))],
        cost_estimate=TINY,
        name="first",
    )(dest_block.reshape(count), row_block, block_offset, new_tiles)

    if direct:
        others = order[1:] + [0]
        packed = pl.pallas_call(
            functools.partial(rest_kernel, peers, cap, others),
            out_shape=[piece] * len(others),
            in_specs=[SMEM, SMEM, HBM],
            out_specs=[VMEM] * len(others),
            scratch_shapes=[pltpu.SemaphoreType.DMA((len(others), cap))],
            cost_estimate=TINY,
            name="rest",
        )(source, fill, new_tiles)
        steps = order + [0]
        got = dict(zip(others, packed))
        got[lead] = out_piece
        got = {k: ring(got[k], k) if k else got[k] for k in steps}
        late = tuple(order[4:]) if peers > 4 else ()
        early = [k for k in steps if k not in late]
        arrived = [got[k] for k in steps]
        arrived_early = [got[k] for k in early]
        arrived_late = [got[k] for k in late]
        flag = got[lead]
        gathered = packed[-1]
    else:
        sent = pl.pallas_call(
            functools.partial(sorted_kernel, peers, cap),
            out_shape=shape((slots, half, BLK), BF16),
            in_specs=[SMEM, SMEM, HBM],
            out_specs=HBM,
            scratch_shapes=[pltpu.SemaphoreType.DMA((count,))],
            cost_estimate=TINY,
            name="rest",
        )(source, fill, new_tiles)
        sent = sent.reshape(peers, cap, half, BLK)
        got = lax.all_to_all(sent, PEERS, split_axis=0, concat_axis=0, tiled=True)
        arrived = [got.reshape(slots, half, BLK)]
        steps = early = None
        late = ()
        arrived_early, arrived_late = arrived, []
        flag = source
        gathered = out_piece

    got_codes = lax.all_to_all(
        codes.reshape(peers, cap + 1), PEERS, split_axis=0, concat_axis=0, tiled=True
    ).reshape(peers * (cap + 1))

    sizes = (2 * nblk, 3 * nblk)
    counts = [pltpu.SMEM((size,), jnp.int32) for size in sizes]
    lists = []
    for size in sizes:
        lists += [shape((slots + size * QUAD,), jnp.int32), shape((size + 1,), jnp.int32)]
    by_row, row_at, by_side, side_at = pl.pallas_call(
        functools.partial(plan_kernel, peers, late, nblk),
        out_shape=lists,
        in_specs=[SMEM],
        out_specs=[SMEM] * 4,
        scratch_shapes=counts,
        compiler_params=SMALL,
        cost_estimate=TINY,
        name="plan",
    )(got_codes)

    blocks = (nblk, BLK, width)
    h_blocks, old_blocks = h_input.reshape(blocks), old_one.reshape(blocks)
    base_one, base_two = base_one.reshape(blocks), base_two.reshape(blocks)
    bases, halves = pl.pallas_call(
        functools.partial(turn_kernel, nblk),
        out_shape=[shape((2 * nblk, half, width), F32), shape((3 * nblk, half, width), BF16)],
        in_specs=[ANY] * 5,
        out_specs=[ANY] * 2,
        scratch_shapes=[pltpu.SemaphoreType.DMA((5,))],
        compiler_params=SMALL,
        cost_estimate=TINY,
        name="turn",
    )(h_blocks, base_one, base_two, old_blocks, gathered)
    bases, halves, _ = after((bases, halves, flag))
    bases, halves = swap(bases), swap(halves)
    h_later, _, by_row, by_side = after((h_blocks, flag, by_row, by_side))
    left, right = ring(h_later, 1), ring(h_later, peers - 1)
    left_twin, right_twin = swap(left), swap(right)

    tile_scratch = pltpu.VMEM((slots + 1, half, BLK), BF16)
    cell_shape = (3 * nblk, BLK, full)
    cell_scratch = pltpu.VMEM(cell_shape, BF16)
    mean_scratch = pltpu.VMEM((nblk, half, full), BF16)
    rows_shape = (nblk, half, full)
    total_scratch = pltpu.VMEM(rows_shape, F32)
    inv = inv_degree.reshape(nblk, BLK)

    many = len(arrived_early)
    agg_early, cells_one, own_one, base_two_rows, old_one_rows = pl.pallas_call(
        functools.partial(early_kernel, cap, early, many, nblk),
        out_shape=[
            shape(rows_shape, F32),
            shape(cell_shape, BF16),
            shape(rows_shape, F32),
            shape(rows_shape, F32),
            shape(rows_shape, BF16),
        ],
        in_specs=[SMEM] * 2 + [ANY] * (many + 10) + [VMEM] * 2,
        out_specs=[VMEM] * 5,
        scratch_shapes=[tile_scratch, pltpu.SemaphoreType.DMA((many + 13,))],
        compiler_params=PARAMS,
        cost_estimate=TINY,
        name="early",
    )(
        by_row,
        row_at,
        *arrived_early,
        left,
        left_twin,
        h_blocks,
        halves,
        right,
        right_twin,
        base_one,
        base_two,
        bases,
        old_blocks,
        self_one,
        bias_one.reshape(1, full),
    )

    many = len(arrived_late)
    hidden_rows = pl.pallas_call(
        functools.partial(late_kernel, cap, late, many, nblk),
        out_shape=shape(rows_shape, BF16),
        in_specs=[SMEM] * 3 + [ANY] * many + [VMEM] * 6,
        out_specs=VMEM,
        scratch_shapes=[
            tile_scratch,
            total_scratch,
            mean_scratch,
            pltpu.SemaphoreType.DMA((max(1, many),)),
        ],
        compiler_params=PARAMS,
        cost_estimate=TINY,
        name="late",
    )(
        by_row,
        row_at,
        affected_one,
        *arrived_late,
        cells_one,
        agg_early,
        inv,
        own_one,
        neigh_one,
        old_one_rows,
    )

    hidden_twin = swap(hidden_rows)
    left = ring(hidden_rows, 1)
    right = ring(hidden_rows, peers - 1)

    many = len(arrived)
    agg_two, own_two, hidden_one, tiles_all = pl.pallas_call(
        functools.partial(near_kernel, cap, steps, many, nblk),
        out_shape=[shape(rows_shape, F32)] * 2
        + [shape(blocks, BF16), shape((slots + 1, half, BLK), BF16)],
        in_specs=[SMEM] * 2 + [ANY] * (many + 2) + [VMEM] * 3,
        out_specs=[VMEM] * 2 + [ANY, VMEM],
        scratch_shapes=[cell_scratch, pltpu.SemaphoreType.DMA((many + 4,))],
        compiler_params=PARAMS,
        cost_estimate=TINY,
        name="near",
    )(
        by_side,
        side_at,
        *arrived,
        hidden_rows,
        hidden_twin,
        base_two_rows,
        self_two,
        bias_two.reshape(1, full),
    )

    left, right, agg_two, own_two = after((left, right, agg_two, own_two))
    left_twin = swap(left)
    right_twin = swap(right)
    kept, sent = pl.pallas_call(
        functools.partial(far_kernel, nblk),
        out_shape=[shape((nblk, half, width), BF16)] * 2,
        in_specs=[SMEM] * 2 + [VMEM] + [ANY] * 4 + [VMEM] * 4,
        out_specs=[VMEM] * 2,
        scratch_shapes=[
            cell_scratch,
            total_scratch,
            mean_scratch,
            pltpu.SemaphoreType.DMA((4,)),
        ],
        compiler_params=PARAMS,
        cost_estimate=TINY,
        name="far",
    )(
        by_side,
        side_at,
        tiles_all,
        left,
        left_twin,
        right,
        right_twin,
        agg_two,
        inv,
        own_two,
        neigh_two,
    )
    came = swap(sent)
    hidden_two = pl.pallas_call(
        functools.partial(finish_kernel, nblk),
        out_shape=shape(blocks, BF16),
        in_specs=[SMEM] + [VMEM] * 3,
        out_specs=VMEM,
        compiler_params=SMALL,
        cost_estimate=TINY,
        name="finish",
    )(affected_two, kept, came, old_two.reshape(blocks))
    return (hidden_one.reshape(rows_here, width), hidden_two.reshape(rows_here, width))


def solution(mesh):
    rows = P(("groups", "rows", "feat"))
    cells = P(("groups", "rows", "feat"), "sub")
    placed = (
        cells,
        rows,
        P(("groups", "rows", "feat"), None),
        rows,
        rows,
        P(("groups", "rows", "feat"), None, None),
        cells,
        rows,
        cells,
        P(),
        P(),
        P(),
        cells,
        rows,
        cells,
        P(),
        P(),
        P(),
    )
    return jax.shard_map(
        on_device, mesh=mesh, in_specs=placed, out_specs=(cells, cells), check_vma=False
    )
```
